32 devices in a mesh: seq: 16 (over z, y, core), head: 2 (over x).
Axes of the slice: x: 2, y: 2, z: 4, core: 2. Of those that a mesh axis runs over, the one named last changes fastest.
Arguments:
- queries: bfloat16 [4096, 4096], P('seq', 'head'), may hold values from -0.29882812 to 0.29882812
- keys: bfloat16 [4096, 4096], P('seq', 'head'), may hold values from -0.29882812 to 0.29882812
- values: bfloat16 [4096, 4096], P('seq', 'head'), may hold values from -0.59765625 to 0.59765625
- out_grad: bfloat16 [4096, 4096], P('seq', 'head'), may hold values from -6 to 6
- doc_lengths: int32 [8], replicated, may hold values from 1 to 1024, 4096 in all
Outputs:
- query_grad: bfloat16 [4096, 4096], P(('seq', 'head'))
- key_grad: bfloat16 [4096, 4096], P(('seq', 'head'))
- value_grad: bfloat16 [4096, 4096], P(('seq', 'head'))
The draws below stay inside these ranges and needn't reach their ends.
Inputs may be any that keep to these rules, and one draw needn't show every extreme that they name: `doc_lengths`: the lengths sum to 4096 and the largest equals 1024.
All inputs are finite; a program needn't handle non-finite values.
Results may differ from the reference program's by a relative error of at most 0.0033.
Values may be sent and summed in bfloat16 or wider, within the bound.
No kernel may reach another device: no remote copies, remote signals or barrier semaphores. Data moves between devices by JAX's collectives and lax.ppermute only.
A program may use at most 128 MiB of HBM per device.

```python
import math
import jax
import jax.numpy as jnp
import numpy as np
from jax import lax

HEADS = 32
HEAD_DIM = 128
D = 4096
TOK_DEV = 256
TOKENS = 4096
MOST = 1024
NDOCS = 8


def levels(own_key, shape, cuts, low, largest):
    loudness = 1.0
    for dim, blocks in cuts:
        draws = jax.random.uniform(jax.random.fold_in(jax.random.fold_in(own_key, 6), dim), (blocks,), jnp.float32, low / len(cuts), largest / len(cuts))
        loudness = loudness * jnp.repeat(jnp.exp(draws), shape[dim] // blocks).reshape((-1,) + (1,) * (len(shape) - 1 - dim))
    return loudness


def profile(number_of, total, reach, slope):
    weights = [(1 << 20) // math.isqrt(rank ** slope) + 1 for rank in range(2, number_of + 1)]
    spare, holding = total - reach - (number_of - 1), [1] * (number_of - 1)
    while spare > 0:
        movable = [i for i in range(number_of - 1) if holding[i] < reach]
        mass, budget = sum([weights[i] for i in movable]), spare
        for i in movable:
            more = min(reach - holding[i], max(1, budget * weights[i] // mass), spare)
            holding[i] = holding[i] + more
            spare = spare - more
    return np.array([reach] + holding)


def ragged(own_key, count, total, most, lean):
    if count == 2:
        one = jax.random.randint(own_key, (), max(1, total - most), min(most, total - 1) + 1)
        return jnp.stack([one, total - one])
    tallies = jnp.asarray(profile(count, total, most, lean), jnp.int32)
    pairs = (count - 1) // 2
    donor, receiver = tallies[1:1 + 2 * pairs:2], tallies[2:2 + 2 * pairs:2]
    margin = jnp.minimum(donor - 1, most - receiver)
    moved = jax.random.randint(jax.random.fold_in(own_key, 1), (pairs,), 0, 1 << 20) % (margin + 1)
    tallies = tallies.at[1:1 + 2 * pairs:2].set(donor - moved).at[2:2 + 2 * pairs:2].set(receiver + moved)
    return tallies[jax.random.permutation(jax.random.fold_in(own_key, 2), count)]


def bell_draw(stream_key, dims, width, bound, cuts=(), kind=jnp.bfloat16):
    gain = levels(stream_key, dims, cuts, -0.22, 0.18) if cuts else 1.0
    entries = jax.random.normal(stream_key, dims, jnp.float32) * width * gain
    return jnp.minimum(jnp.maximum(entries, -bound), bound).astype(kind)


def setup_inputs(seed: int = 0) -> dict:
    seeds = jax.random.split(jax.random.key(seed), 6)
    queries = bell_draw(seeds[0], (TOKENS, D), 0.05, 0.29882812, ((0, 16), (1, 2)))
    keys = bell_draw(seeds[1], (TOKENS, D), 0.05, 0.29882812, ((0, 16), (1, 2)))
    values = bell_draw(seeds[2], (TOKENS, D), 0.1, 0.59765625, ((0, 16), (1, 2)))
    out_grad = bell_draw(seeds[3], (TOKENS, D), 1.0, 6.0, ((0, 16), (1, 2)))
    doc_lengths = ragged(seeds[4], NDOCS, TOKENS, MOST, 2).astype(jnp.int32)
    return dict(queries=queries, keys=keys, values=values, out_grad=out_grad, doc_lengths=doc_lengths)


def doc_tables(doc_lengths):
    starts = jnp.cumsum(doc_lengths) - doc_lengths
    position = jnp.arange(TOKENS, dtype=jnp.int32)
    before = starts[None, :] <= position[:, None]
    doc_index = jnp.sum(before.astype(jnp.int32), axis=1) - 1
    doc_begin = jnp.max(jnp.where(before, starts[None, :], 0), axis=1)
    return doc_index, doc_begin


def block_grads(item):
    query_block, key_block, value_block, grad_block, doc_block, first_rows, last_rows, state_in, grad_in = item
    query_f = query_block.astype(jnp.float32)
    key_f = key_block.astype(jnp.float32)
    value_f = value_block.astype(jnp.float32)
    grad_f = grad_block.astype(jnp.float32)
    order = jnp.arange(TOK_DEV, dtype=jnp.int32)
    pair_mask = (doc_block[:, None] == doc_block[None, :]) & (order[:, None] >= order[None, :])
    score_qk = jnp.einsum("thd,shd->hts", query_f, key_f)
    weight_qk = jnp.where(pair_mask[None], score_qk, 0.0).astype(jnp.bfloat16).astype(jnp.float32)
    score_gv = jnp.einsum("the,she->hts", grad_f, value_f)
    weight_gv = jnp.where(pair_mask[None], score_gv, 0.0).astype(jnp.bfloat16).astype(jnp.float32)
    high = lax.Precision.HIGHEST
    carry_query = jnp.einsum("hde,the->thd", state_in, grad_f, precision=high)
    carry_key = jnp.einsum("hde,she->shd", grad_in, value_f, precision=high)
    carry_value = jnp.einsum("hde,shd->she", grad_in, key_f, precision=high)
    query_out = jnp.einsum("hts,shd->thd", weight_gv, key_f) + jnp.where(first_rows[:, None, None], carry_query, 0.0)
    key_out = jnp.einsum("hts,thd->shd", weight_gv, query_f) + jnp.where(last_rows[:, None, None], carry_key, 0.0)
    value_out = jnp.einsum("hts,the->she", weight_qk, grad_f) + jnp.where(last_rows[:, None, None], carry_value, 0.0)
    return (query_out.reshape(TOK_DEV, D).astype(jnp.bfloat16),
            key_out.reshape(TOK_DEV, D).astype(jnp.bfloat16),
            value_out.reshape(TOK_DEV, D).astype(jnp.bfloat16))


def reference(queries, keys, values, out_grad, doc_lengths):
    blocks = TOKENS // TOK_DEV
    doc_index, doc_begin = doc_tables(doc_lengths)
    doc_blocks = doc_index.reshape(blocks, TOK_DEV)
    begin_blocks = doc_begin.reshape(blocks, TOK_DEV)
    block_start = jnp.arange(blocks, dtype=jnp.int32) * TOK_DEV
    first_rows = begin_blocks < block_start[:, None]
    last_rows = doc_blocks == doc_blocks[:, TOK_DEV - 1:TOK_DEV]
    has_start = jnp.any(begin_blocks >= block_start[:, None], axis=1).astype(jnp.float32)
    shape4 = (blocks, TOK_DEV, HEADS, HEAD_DIM)
    query_b = queries.reshape(shape4)
    key_b = keys.reshape(shape4)
    value_b = values.reshape(shape4)
    grad_b = out_grad.reshape(shape4)
    empty = jnp.zeros((HEADS, HEAD_DIM, HEAD_DIM), jnp.float32)

    def forward_step(state, item):
        key_block, value_block, rows, started = item
        picked = jnp.where(rows[:, None, None], key_block.astype(jnp.float32), 0.0)
        tail_state = jnp.einsum("lhd,lhe->hde", picked, value_block.astype(jnp.float32))
        return (1.0 - started) * state + tail_state, state

    def backward_step(state, item):
        query_block, grad_block, rows, started = item
        picked = jnp.where(rows[:, None, None], query_block.astype(jnp.float32), 0.0)
        head_state = jnp.einsum("lhd,lhe->hde", picked, grad_block.astype(jnp.float32))
        return head_state + (1.0 - started) * state, state

    _, states_in = lax.scan(forward_step, empty, (key_b, value_b, last_rows, has_start))
    _, grads_in = lax.scan(backward_step, empty, (query_b, grad_b, first_rows, has_start), reverse=True)
    query_grad, key_grad, value_grad = lax.map(block_grads, (query_b, key_b, value_b, grad_b, doc_blocks, first_rows, last_rows, states_in, grads_in))
    return (query_grad.reshape(TOKENS, D), key_grad.reshape(TOKENS, D), value_grad.reshape(TOKENS, D))
```

```python
import functools

import jax
import jax.numpy as jnp
from jax import lax
from jax.experimental import pallas as pl
from jax.experimental.pallas import tpu as pltpu
from jax.sharding import PartitionSpec as P

HEAD_DIM = 128
MOST = 1024
CHUNKS = 2
VMEM_LIMIT = 48 * 1024 * 1024
NT = (((1,), (1,)), ((), ()))
TN = (((0,), (0,)), ((), ()))
NN = (((1,), (0,)), ((), ()))


def dot(a, b, dims):
    return lax.dot_general(a, b, dims, preferred_element_type=jnp.float32)


def doc_at(meta, ndocs, position):
    start, begin, end = jnp.int32(0), jnp.int32(0), jnp.int32(0)
    for i in range(ndocs):
        stop = start + meta[i]
        begin = jnp.where(start <= position, start, begin)
        end = jnp.where(start <= position, stop, end)
        start = stop
    return begin, end


def block_range(meta, ndocs, base, rows):
    begin0, end0 = doc_at(meta, ndocs, base)
    begin1, end1 = doc_at(meta, ndocs, base + rows - 1)
    first = jnp.where(begin0 < base, end0, base) - base
    return begin0, end0, begin1, end1, first, begin1 - base


def pack_kernel(meta, q, k, v, g, out, sems, *, ndocs, half):
    other = 1 - lax.rem(meta[ndocs], 2)
    copies = []
    for i, ref in enumerate((q, k, v, g)):
        src = ref.at[:, pl.ds(pl.multiple_of(other * half, 128), half)]
        copies.append(pltpu.make_async_copy(src, out.at[i], sems.at[i]))
        copies[-1].start()
    for copy in copies:
        copy.wait()


def state_kernel(meta, q, k, v, g, pair, tail_out, head_out, even_tail, odd_head, *, ndocs, rows, heads):
    place = meta[ndocs]
    odd_here = lax.rem(place, 2) == 1
    even = (place - lax.rem(place, 2)) * rows
    odd = even + rows
    even_b0, even_e0, _, _, even_first, even_last = block_range(meta, ndocs, even, rows)
    _, _, odd_b1, _, odd_first, odd_last = block_range(meta, ndocs, odd, rows)
    order = lax.broadcasted_iota(jnp.int32, (rows, HEAD_DIM), 0)
    own_first = jnp.where(odd_here, odd_first, even_first)
    own_last = jnp.where(odd_here, odd_last, even_last)
    far_first = jnp.where(odd_here, even_first, odd_first)
    far_last = jnp.where(odd_here, even_last, odd_last)
    tail_joins = jnp.where(odd_b1 < odd, 1.0, 0.0)
    head_joins = jnp.where(even_e0 > odd, 1.0, 0.0)
    zero = jnp.zeros((), q.dtype)
    for h in range(heads):
        cols = slice(h * HEAD_DIM, (h + 1) * HEAD_DIM)
        own_tail = dot(jnp.where(order >= own_last, k[:, cols], zero), v[:, cols], TN)
        far_tail = dot(jnp.where(order >= far_last, pair[1, :, cols], zero), pair[2, :, cols], TN)
        own_head = dot(jnp.where(order < own_first, q[:, cols], zero), g[:, cols], TN)
        far_head = dot(jnp.where(order < far_first, pair[0, :, cols], zero), pair[3, :, cols], TN)
        tail_even = jnp.where(odd_here, far_tail, own_tail)
        tail_odd = jnp.where(odd_here, own_tail, far_tail)
        head_even = jnp.where(odd_here, far_head, own_head)
        head_odd = jnp.where(odd_here, own_head, far_head)
        tail_out[h] = tail_odd + tail_joins * tail_even
        head_out[h] = head_even + head_joins * head_odd
        even_tail[h] = tail_even
        odd_head[h] = head_odd


def split(a):
    high = a.astype(jnp.bfloat16)
    return high, (a - high.astype(jnp.float32)).astype(jnp.bfloat16)


def grad_kernel(meta, q, k, v, g, pair, even_tail, odd_head, tails, heads_in, *rest, ndocs, rows, heads, groups, hops):
    outs, (done,) = rest[:-1], rest[-1:]
    place, column = meta[ndocs], meta[ndocs + 1]
    odd_here = lax.rem(place, 2) == 1
    even = (place - lax.rem(place, 2)) * rows
    odd = even + rows
    even_range = block_range(meta, ndocs, even, rows)
    odd_range = block_range(meta, ndocs, odd, rows)
    even_b0, even_e1 = even_range[0], even_range[3]
    odd_b0, odd_e1 = odd_range[0], odd_range[3]

    def one(flag):
        return jnp.where(flag, 1.0, 0.0)

    tail_w = [one(even - hop * 2 * rows > even_b0) for hop in range(hops)]
    head_w = [one(odd + rows + hop * 2 * rows < odd_e1) for hop in range(hops)]
    state_from_tail, state_from_pair = one(odd > odd_b0), one(even > odd_b0)
    grad_from_head, grad_from_pair = one(odd < even_e1), one(odd + rows < even_e1)
    order = lax.broadcasted_iota(jnp.int32, (rows, HEAD_DIM), 0)
    line = lax.broadcasted_iota(jnp.int32, (rows, rows), 0)
    across = lax.broadcasted_iota(jnp.int32, (rows, rows), 1)
    sides = []
    for base, first, last in (
        (jnp.where(odd_here, odd, even), jnp.where(odd_here, odd_range[4], even_range[4]), jnp.where(odd_here, odd_range[5], even_range[5])),
        (jnp.where(odd_here, even, odd), jnp.where(odd_here, even_range[4], odd_range[4]), jnp.where(odd_here, even_range[5], odd_range[5])),
    ):
        begin_line = jnp.zeros((rows, rows), jnp.int32)
        begin_across = jnp.zeros((rows, rows), jnp.int32)
        start = jnp.int32(0) - base
        for i in range(ndocs):
            begin_line = jnp.where(line >= start, start, begin_line)
            begin_across = jnp.where(across >= start, start, begin_across)
            start = start + meta[i]
        lower = (across <= line) & (across >= begin_line)
        upper = (line <= across) & (line >= begin_across)
        sides.append((lower, upper, order < first, order >= last))
    for h in range(heads):
        cols = slice(h * HEAD_DIM, (h + 1) * HEAD_DIM)
        state_even = tail_w[0] * tails[0, h]
        grad_odd = head_w[0] * heads_in[0, h]
        for hop in range(1, hops):
            state_even = state_even + tail_w[hop] * tails[hop, h]
            grad_odd = grad_odd + head_w[hop] * heads_in[hop, h]
        state_odd = state_from_tail * even_tail[h] + state_from_pair * state_even
        grad_even = grad_from_head * odd_head[h] + grad_from_pair * grad_odd
        states = (jnp.where(odd_here, state_odd, state_even), jnp.where(odd_here, state_even, state_odd))
        grads = (jnp.where(odd_here, grad_odd, grad_even), jnp.where(odd_here, grad_even, grad_odd))
        for side in range(2):
            lower, upper, first_rows, last_rows = sides[side]
            if side == 0:
                qh, kh, vh, gh = (ref[:, cols] for ref in (q, k, v, g))
            else:
                qh, kh, vh, gh = (pair[i, :, cols] for i in range(4))
            state_hi, state_lo = split(states[side])
            grad_hi, grad_lo = split(grads[side])
            weight_gv = jnp.where(lower, dot(gh, vh, NT), 0.0).astype(jnp.bfloat16)
            weight_vg = jnp.where(upper, dot(vh, gh, NT), 0.0).astype(jnp.bfloat16)
            weight_kq = jnp.where(upper, dot(kh, qh, NT), 0.0).astype(jnp.bfloat16)
            carry_q = dot(gh, state_hi, NT) + dot(gh, state_lo, NT)
            carry_k = dot(vh, grad_hi, NT) + dot(vh, grad_lo, NT)
            carry_v = dot(kh, grad_hi, NN) + dot(kh, grad_lo, NN)
            q_out = dot(weight_gv, kh, NN) + jnp.where(first_rows, carry_q, 0.0)
            k_out = dot(weight_vg, qh, NN) + jnp.where(last_rows, carry_k, 0.0)
            v_out = dot(weight_kq, gh, NN) + jnp.where(last_rows, carry_v, 0.0)
            done[side, 0, :, cols] = q_out.astype(jnp.bfloat16)
            done[side, 1, :, cols] = k_out.astype(jnp.bfloat16)
            done[side, 2, :, cols] = v_out.astype(jnp.bfloat16)
    part = rows // groups
    for side in range(2):
        for j in range(groups):
            target = lax.rem(column + j, groups)
            at = pl.ds(pl.multiple_of(target * part, part), part)
            for i in range(3):
                outs[side * groups + j][i] = done[side, i, at, :]


def place_kernel(meta, *refs, ndocs, groups, chunks, width, half, cw):
    count = 2 * groups * chunks
    parts, outs, sems = refs[:count], refs[count:count + 3], refs[count + 3]
    side_here, column = lax.rem(meta[ndocs], 2), meta[ndocs + 1]
    copies = []
    for c in range(chunks):
        for side in range(2):
            for j in range(groups):
                source = lax.rem(column + groups - j, groups)
                side_from = side_here if side == 0 else 1 - side_here
                start = pl.multiple_of(source * width + side_from * half + c * cw, 128)
                ref = parts[(c * 2 + side) * groups + j]
                for i in range(3):
                    copy = pltpu.make_async_copy(ref.at[i], outs[i].at[:, pl.ds(start, cw)], sems.at[len(copies)])
                    copy.start()
                    copies.append(copy)
    for copy in copies:
        copy.wait()


def shards(queries, keys, values, out_grad, doc_lengths):
    rows, width = queries.shape
    half = width // 2
    ndocs = doc_lengths.shape[0]
    seq, groups = lax.axis_size("seq"), lax.axis_size("head")
    hops = -(-MOST // (2 * rows))
    chunks = min(CHUNKS, half // HEAD_DIM)
    cw = half // chunks
    heads = cw // HEAD_DIM
    part = rows // groups
    meta = jnp.concatenate(
        [doc_lengths, jnp.stack([lax.axis_index("seq"), lax.axis_index("head")]).astype(jnp.int32)]
    )
    params = pltpu.CompilerParams(vmem_limit_bytes=VMEM_LIMIT)
    anywhere = pl.BlockSpec(memory_space=pl.ANY)
    f32, bf16 = jnp.float32, jnp.bfloat16

    packed = pl.pallas_call(
        functools.partial(pack_kernel, ndocs=ndocs, half=half),
        grid_spec=pltpu.PrefetchScalarGridSpec(
            num_scalar_prefetch=1, grid=(1,), in_specs=[anywhere] * 4, out_specs=anywhere,
            scratch_shapes=[pltpu.SemaphoreType.DMA((4,))],
        ),
        out_shape=jax.ShapeDtypeStruct((4, rows, half), bf16),
        cost_estimate=pl.CostEstimate(flops=0, bytes_accessed=16 * rows * half, transcendentals=0),
        compiler_params=params, name="pack",
    )(meta, queries, keys, values, out_grad)
    pair = lax.ppermute(packed, "seq", [(b, b ^ 1) for b in range(seq)])

    square = (heads, HEAD_DIM, HEAD_DIM)
    state_spec = pl.BlockSpec(square, lambda s, meta: (0, 0, 0))
    results = []
    stage = []
    for c in range(chunks):
        own = pl.BlockSpec((rows, cw), lambda s, meta, c=c: (0, lax.rem(meta[ndocs], 2) * chunks + c))
        far = pl.BlockSpec((4, rows, cw), lambda s, meta, c=c: (0, 0, c))
        tail, head, even_tail, odd_head = pl.pallas_call(
            functools.partial(state_kernel, ndocs=ndocs, rows=rows, heads=heads),
            grid_spec=pltpu.PrefetchScalarGridSpec(
                num_scalar_prefetch=1, grid=(1,), in_specs=[own] * 4 + [far], out_specs=[state_spec] * 4,
            ),
            out_shape=[jax.ShapeDtypeStruct(square, f32)] * 4,
            cost_estimate=pl.CostEstimate(
                flops=8 * heads * rows * HEAD_DIM * HEAD_DIM, bytes_accessed=16 * rows * cw + 16 * heads * HEAD_DIM**2, transcendentals=0
            ),
            compiler_params=params, name="states",
        )(meta, queries, keys, values, out_grad, pair)
        tails, heads_in = [], []
        for hop in range(1, hops + 1):
            far_by = 2 * hop
            tails.append(lax.ppermute(tail, "seq", [(b, b + far_by) for b in range(seq - far_by)]))
            heads_in.append(lax.ppermute(head, "seq", [(b + far_by, b) for b in range(seq - far_by)]))
        stage.append((own, far, even_tail, odd_head, tails, heads_in))

    def grads(meta, q, k, v, g, pair, even_tail, odd_head, *rest, **sizes):
        tails, heads_in, rest = rest[:hops], rest[hops:2 * hops], rest[2 * hops:]
        grad_kernel(meta, q, k, v, g, pair, even_tail, odd_head, Pick(tails), Pick(heads_in), *rest, **sizes)

    arrived = []
    for c in range(chunks):
        own, far, even_tail, odd_head, tails, heads_in = stage[c]
        slot = pl.BlockSpec((3, part, cw), lambda s, meta: (0, 0, 0))
        outs = pl.pallas_call(
            functools.partial(grads, ndocs=ndocs, rows=rows, heads=heads, groups=groups, hops=hops),
            grid_spec=pltpu.PrefetchScalarGridSpec(
                num_scalar_prefetch=1, grid=(1,),
                in_specs=[own] * 4 + [far] + [state_spec] * (2 + 2 * hops),
                out_specs=[slot] * (2 * groups),
                scratch_shapes=[pltpu.VMEM((2, 3, rows, cw), bf16)],
            ),
            out_shape=[jax.ShapeDtypeStruct((3, part, cw), bf16)] * (2 * groups),
            cost_estimate=pl.CostEstimate(
                flops=2 * heads * (12 * rows * rows * HEAD_DIM + 12 * rows * HEAD_DIM**2),
                bytes_accessed=16 * rows * cw + 8 * (1 + hops) * heads * HEAD_DIM**2 + 12 * rows * cw, transcendentals=0,
            ),
            compiler_params=params, name="grads",
        )(meta, queries, keys, values, out_grad, pair, even_tail, odd_head, *tails, *heads_in)
        for side in range(2):
            for j in range(groups):
                out = outs[side * groups + j]
                if side or j:
                    perm = [
                        (b * groups + x, (b ^ side) * groups + (x + j) % groups) for b in range(seq) for x in range(groups)
                    ]
                    out = lax.ppermute(out, ("seq", "head"), perm)
                arrived.append(out)

    return tuple(
        pl.pallas_call(
            functools.partial(place_kernel, ndocs=ndocs, groups=groups, chunks=chunks, width=width, half=half, cw=cw),
            grid_spec=pltpu.PrefetchScalarGridSpec(
                num_scalar_prefetch=1, grid=(1,), in_specs=[anywhere] * len(arrived), out_specs=[anywhere] * 3,
                scratch_shapes=[pltpu.SemaphoreType.DMA((3 * len(arrived),))],
            ),
            out_shape=[jax.ShapeDtypeStruct((part, width * groups), bf16)] * 3,
            cost_estimate=pl.CostEstimate(flops=0, bytes_accessed=12 * part * width * groups, transcendentals=0),
            compiler_params=params, name="place",
        )(meta, *arrived)
    )


class Pick:
    def __init__(self, refs):
        self.refs = refs

    def __getitem__(self, at):
        return self.refs[at[0]][at[1]]


def solution(mesh):
    return jax.shard_map(
        shards,
        mesh=mesh,
        in_specs=(P("seq", "head"), P("seq", "head"), P("seq", "head"), P("seq", "head"), P()),
        out_specs=(P(("seq", "head"), None), P(("seq", "head"), None), P(("seq", "head"), None)),
        check_vma=False,
    )
```

```python
import functools

import jax
import jax.numpy as jnp
from jax import lax
from jax.experimental import pallas as pl
from jax.experimental.pallas import tpu as pltpu
from jax.sharding import PartitionSpec as P

HEAD_DIM = 128
MOST = 1024
CUTS = (8, 8)
VMEM_LIMIT = 32 * 1024 * 1024
FIRST_LIMIT = 60 * 1024 * 1024
NT = (((1,), (1,)), ((), ()))
TN = (((0,), (0,)), ((), ()))
NN = (((1,), (0,)), ((), ()))


def dot(a, b, dims):
    return lax.dot_general(a, b, dims, preferred_element_type=jnp.float32)


def doc_at(meta, ndocs, position):
    start, begin, end = jnp.int32(0), jnp.int32(0), jnp.int32(0)
    for i in range(ndocs):
        stop = start + meta[i]
        begin = jnp.where(start <= position, start, begin)
        end = jnp.where(start <= position, stop, end)
        start = stop
    return begin, end


def block_range(meta, ndocs, base, rows):
    begin0, end0 = doc_at(meta, ndocs, base)
    begin1, end1 = doc_at(meta, ndocs, base + rows - 1)
    first = jnp.where(begin0 < base, end0, base) - base
    return begin0, end0, begin1, end1, first, begin1 - base


def goes_up(place, hop):
    return lax.rem(lax.div(lax.div(place, 2), hop), 2) == 0


def state_kernel(lengths, q, k, v, g, *rest, ndocs, rows, heads):
    kept, sent = rest[-2:]
    place = lax.axis_index("seq")
    first_core = lax.rem(place, 2) == 0
    _, _, _, _, first, last = block_range(lengths, ndocs, place * rows, rows)
    order = lax.broadcasted_iota(jnp.int32, (rows, HEAD_DIM), 0)
    first_rows, last_rows = order < first, order >= last
    zero = jnp.zeros((), q.dtype)

    def one(h):
        cols = slice(h * HEAD_DIM, (h + 1) * HEAD_DIM)
        tail = dot(jnp.where(last_rows, k[:, cols], zero), v[:, cols], TN)
        return tail, dot(jnp.where(first_rows, q[:, cols], zero), g[:, cols], TN)

    for i in range(heads // 2):
        for which, (low, high) in enumerate(zip(one(i), one(i + heads // 2))):
            kept[which, i] = jnp.where(first_core, low, high)
            sent[which, i] = jnp.where(first_core, high, low)


def pair_parts(kept, got, first_core, i):
    tail_even = jnp.where(first_core, kept[0, i], got[0, i])
    tail_odd = jnp.where(first_core, got[0, i], kept[0, i])
    head_even = jnp.where(first_core, kept[1, i], got[1, i])
    head_odd = jnp.where(first_core, got[1, i], kept[1, i])
    return tail_even, tail_odd, head_even, head_odd


def pair_kernel(lengths, kept, got, *rest, ndocs, rows, count, hops):
    sent = rest[-2 * hops:]
    place = lax.axis_index("seq")
    first_core = lax.rem(place, 2) == 0
    even = (place - lax.rem(place, 2)) * rows
    odd = even + rows
    _, even_e0 = doc_at(lengths, ndocs, even)
    odd_b1, _ = doc_at(lengths, ndocs, odd + rows - 1)
    tail_joins = jnp.where(odd_b1 < odd, 1.0, 0.0)
    head_joins = jnp.where(even_e0 > odd, 1.0, 0.0)
    ups = [goes_up(place, hop) for hop in range(1, hops + 1)]
    for i in range(count):
        tail_even, tail_odd, head_even, head_odd = pair_parts(kept, got, first_core, i)
        tail = tail_odd + tail_joins * tail_even
        head = head_even + head_joins * head_odd
        for hop in range(hops):
            sent[2 * hop][i] = jnp.where(ups[hop], tail, head)
            sent[2 * hop + 1][i] = jnp.where(ups[hop], head, tail)


def join_kernel(lengths, kept, got, *rest, ndocs, rows, count, hops):
    came, (mine, theirs) = rest[:2 * hops], rest[-2:]
    place = lax.axis_index("seq")
    first_core = lax.rem(place, 2) == 0
    even = (place - lax.rem(place, 2)) * rows
    odd = even + rows
    even_b0, _ = doc_at(lengths, ndocs, even)
    _, even_e1 = doc_at(lengths, ndocs, odd - 1)
    odd_b0, _ = doc_at(lengths, ndocs, odd)
    _, odd_e1 = doc_at(lengths, ndocs, odd + rows - 1)

    def one(flag):
        return jnp.where(flag, 1.0, 0.0)

    ups = [goes_up(place, hop) for hop in range(1, hops + 1)]
    tail_w = [one(even - hop * 2 * rows > even_b0) for hop in range(hops)]
    head_w = [one(odd + rows + hop * 2 * rows < odd_e1) for hop in range(hops)]
    state_from_tail, state_from_pair = one(odd > odd_b0), one(even > odd_b0)
    grad_from_head, grad_from_pair = one(odd < even_e1), one(odd + rows < even_e1)
    for i in range(count):
        tail_even, _, _, head_odd = pair_parts(kept, got, first_core, i)
        state_even, grad_odd = 0.0, 0.0
        for hop in range(hops):
            a, b = came[2 * hop][i], came[2 * hop + 1][i]
            state_even = state_even + tail_w[hop] * jnp.where(ups[hop], b, a)
            grad_odd = grad_odd + head_w[hop] * jnp.where(ups[hop], a, b)
        state_odd = state_from_tail * tail_even + state_from_pair * state_even
        grad_even = grad_from_head * head_odd + grad_from_pair * grad_odd
        mine[0, i] = jnp.where(first_core, state_even, state_odd)
        mine[1, i] = jnp.where(first_core, grad_even, grad_odd)
        theirs[0, i] = jnp.where(first_core, state_odd, state_even)
        theirs[1, i] = jnp.where(first_core, grad_odd, grad_even)


def split(a, axis):
    high = a.astype(jnp.bfloat16)
    return jnp.concatenate([high, (a - high.astype(jnp.float32)).astype(jnp.bfloat16)], axis=axis)


def local_kernel(lengths, q, k, v, g, *rest, ndocs, rows, heads):
    out = rest[-1]
    line = lax.broadcasted_iota(jnp.int32, (rows, rows), 0)
    across = lax.broadcasted_iota(jnp.int32, (rows, rows), 1)
    begin_line = jnp.zeros((rows, rows), jnp.int32)
    begin_across = jnp.zeros((rows, rows), jnp.int32)
    start = jnp.int32(0) - lax.axis_index("seq") * rows
    for i in range(ndocs):
        begin_line = jnp.where(line >= start, start, begin_line)
        begin_across = jnp.where(across >= start, start, begin_across)
        start = start + lengths[i]
    lower = (across <= line) & (across >= begin_line)
    upper = (line <= across) & (line >= begin_across)
    for h in range(heads):
        cols = slice(h * HEAD_DIM, (h + 1) * HEAD_DIM)
        qh, kh, vh, gh = (ref[:, cols] for ref in (q, k, v, g))
        weight_gv = jnp.where(lower, dot(gh, vh, NT), 0.0).astype(jnp.bfloat16)
        weight_vg = jnp.where(upper, dot(vh, gh, NT), 0.0).astype(jnp.bfloat16)
        weight_kq = jnp.where(upper, dot(kh, qh, NT), 0.0).astype(jnp.bfloat16)
        out[0, :, cols] = dot(weight_gv, kh, NN)
        out[1, :, cols] = dot(weight_vg, qh, NN)
        out[2, :, cols] = dot(weight_kq, gh, NN)


def carry_kernel(lengths, k, v, g, local, mine, got, *rest, ndocs, rows, heads, groups):
    outs, done = rest[-1 - groups:-1], rest[-1]
    place, column = lax.axis_index("seq"), lax.axis_index("head")
    first_core = lax.rem(place, 2) == 0
    _, _, _, _, first, last = block_range(lengths, ndocs, place * rows, rows)
    order = lax.broadcasted_iota(jnp.int32, (rows, HEAD_DIM), 0)
    first_rows, last_rows = order < first, order >= last
    count = heads // 2
    for h in range(heads):
        cols = slice(h * HEAD_DIM, (h + 1) * HEAD_DIM)
        here = first_core if h < count else jnp.logical_not(first_core)
        state, grad = (jnp.where(here, mine[which, h % count], got[which, h % count]) for which in range(2))
        kh, vh, gh = (jnp.concatenate([ref[:, cols]] * 2, axis=1) for ref in (k, v, g))
        carry_q = jnp.where(first_rows, dot(gh, split(state, 1), NT), 0.0)
        carry_k = jnp.where(last_rows, dot(vh, split(grad, 1), NT), 0.0)
        carry_v = jnp.where(last_rows, dot(kh, split(grad, 0), NN), 0.0)
        for i, carry in enumerate((carry_q, carry_k, carry_v)):
            done[i, :, cols] = (local[i, :, cols] + carry).astype(jnp.bfloat16)
    part = rows // groups
    for j in range(groups):
        at = pl.ds(pl.multiple_of(lax.rem(column + j, groups) * part, part), part)
        for i in range(3):
            outs[j][i] = done[i, at, :]


def place_kernel(*refs, groups, cuts, width):
    total = groups * len(cuts)
    parts, outs, sems = refs[:total], refs[total:total + 3], refs[total + 3]
    column = lax.axis_index("head")
    copies = []
    for c, (offset, cw) in enumerate(cuts):
        for j in range(groups):
            start = pl.multiple_of(lax.rem(column + groups - j, groups) * width + offset, 128)
            for i in range(3):
                dst = outs[i].at[:, pl.ds(start, cw)]
                copies.append(pltpu.make_async_copy(parts[c * groups + j].at[i], dst, sems.at[len(copies)]))
                copies[-1].start()
    for copy in copies:
        copy.wait()


def cuts_of(width):
    heads = width // HEAD_DIM
    sizes = CUTS if sum(CUTS) == heads else (2,) * (heads // 2)
    offsets = [sum(sizes[:c]) for c in range(len(sizes))]
    return [(o * HEAD_DIM, s * HEAD_DIM) for o, s in zip(offsets, sizes)]


def shards(queries, keys, values, out_grad, doc_lengths):
    rows, width = queries.shape
    ndocs = doc_lengths.shape[0]
    seq, groups = lax.axis_size("seq"), lax.axis_size("head")
    pairs = seq // 2
    hops = -(-MOST // (2 * rows))
    cuts = cuts_of(width)
    part = rows // groups
    anywhere = pl.BlockSpec(memory_space=pl.ANY)
    f32, bf16 = jnp.float32, jnp.bfloat16
    inputs = (queries, keys, values, out_grad)

    def whole(shape):
        return pl.BlockSpec(shape, lambda s, lengths: (0,) * len(shape))

    def call(name, kernel, args, in_specs, outs, after=(), flops=0, scratch=(), limit=VMEM_LIMIT):
        moved = sum(a.size * a.dtype.itemsize for a in outs) * 2
        return pl.pallas_call(
            kernel,
            grid_spec=pltpu.PrefetchScalarGridSpec(
                num_scalar_prefetch=1, grid=(1,), in_specs=list(in_specs) + [anywhere] * len(after),
                out_specs=[whole(a.shape) for a in outs], scratch_shapes=list(scratch),
            ),
            out_shape=outs,
            cost_estimate=pl.CostEstimate(flops=0, bytes_accessed=1024, transcendentals=0),
            compiler_params=pltpu.CompilerParams(vmem_limit_bytes=limit), name=name,
        )(doc_lengths, *args, *after)

    def swap_cores(a):
        return lax.ppermute(a, "seq", [(b, b ^ 1) for b in range(seq)])

    def swap_pairs(sent):
        came = []
        for hop in range(1, hops + 1):
            for turn in range(2):
                lower = [m for m in range(pairs - hop) if (m // hop) % 2 == turn]
                perm = [(2 * m + core, 2 * (m + hop) + core) for m in lower for core in range(2)]
                came.append(lax.ppermute(sent[2 * (hop - 1) + turn], "seq", perm + [(b, a) for a, b in perm]))
        return came

    def send_rows(outs):
        arrived = list(outs[:1])
        for j in range(1, groups):
            arrived.append(lax.ppermute(outs[j], "head", [(x, (x + j) % groups) for x in range(groups)]))
        return arrived

    class Chunk:
        def __init__(self, offset, cw):
            self.cw, self.heads = cw, cw // HEAD_DIM
            self.count = self.heads // 2
            self.own = pl.BlockSpec((rows, cw), lambda s, lengths: (0, offset // cw))
            self.square = (self.count, HEAD_DIM, HEAD_DIM)
            self.both = jax.ShapeDtypeStruct((2,) + self.square, f32)
            self.sizes = dict(ndocs=ndocs, rows=rows)

        def states(self, after=(), limit=VMEM_LIMIT):
            kernel = functools.partial(state_kernel, heads=self.heads, **self.sizes)
            flops = 4 * self.heads * rows * HEAD_DIM**2
            self.kept, sent = call("states", kernel, inputs, [self.own] * 4, [self.both] * 2, after, flops, limit=limit)
            self.got = swap_cores(sent)

        def pair_up(self, after=()):
            kernel = functools.partial(pair_kernel, count=self.count, hops=hops, **self.sizes)
            sent = call(
                "pair", kernel, (self.kept, self.got), [whole(self.both.shape)] * 2,
                [jax.ShapeDtypeStruct(self.square, f32)] * (2 * hops), after,
            )
            self.sent = sent
            self.came = swap_pairs(sent)

        def join(self, after=()):
            kernel = functools.partial(join_kernel, count=self.count, hops=hops, **self.sizes)
            specs = [whole(self.both.shape)] * 2 + [whole(self.square)] * (2 * hops)
            self.mine, theirs = call("join", kernel, (self.kept, self.got, *self.came), specs, [self.both] * 2, after)
            self.state = swap_cores(theirs)

        def local(self, after=()):
            kernel = functools.partial(local_kernel, heads=self.heads, **self.sizes)
            flops = 12 * self.heads * rows * rows * HEAD_DIM
            out = jax.ShapeDtypeStruct((3, rows, self.cw), f32)
            self.near = call("local", kernel, inputs, [self.own] * 4, [out], after, flops)[0]

        def carry(self, after=()):
            kernel = functools.partial(carry_kernel, heads=self.heads, groups=groups, **self.sizes)
            specs = [self.own] * 3 + [whole((3, rows, self.cw))] + [whole(self.both.shape)] * 2
            self.outs = call(
                "carry", kernel, (keys, values, out_grad, self.near, self.mine, self.state), specs,
                [jax.ShapeDtypeStruct((3, part, self.cw), bf16)] * groups, after,
                12 * self.heads * rows * HEAD_DIM**2, [pltpu.VMEM((3, rows, self.cw), bf16)],
            )
            self.arrived = send_rows(self.outs)

    chunks = [Chunk(*cut) for cut in cuts]
    chunks[0].states(limit=FIRST_LIMIT)
    for before, chunk in zip(chunks, chunks[1:]):
        chunk.states([before.kept])
    last = chunks[-1].kept
    chunks[0].pair_up([last])
    last = chunks[0].sent[0]
    for chunk in chunks:
        chunk.local([last])
        last = chunk.near
        chunk.join([last])
        last = chunk.mine
        behind = chunks.index(chunk) + 1
        if behind < len(chunks):
            chunks[behind].pair_up([last])
        chunk.carry()
        last = chunk.outs[0]

    parts = [a for chunk in chunks for a in chunk.arrived]
    return tuple(
        pl.pallas_call(
            functools.partial(place_kernel, groups=groups, cuts=cuts, width=width),
            grid_spec=pl.GridSpec(
                grid=(1,), in_specs=[anywhere] * len(parts), out_specs=[anywhere] * 3,
                scratch_shapes=[pltpu.SemaphoreType.DMA((3 * len(parts),))],
            ),
            out_shape=[jax.ShapeDtypeStruct((part, width * groups), bf16)] * 3,
            cost_estimate=pl.CostEstimate(flops=0, bytes_accessed=12 * part * width * groups, transcendentals=0),
            compiler_params=pltpu.CompilerParams(vmem_limit_bytes=VMEM_LIMIT), name="place",
        )(*parts)
    )


def solution(mesh):
    return jax.shard_map(
        shards,
        mesh=mesh,
        in_specs=(P("seq", "head"), P("seq", "head"), P("seq", "head"), P("seq", "head"), P()),
        out_specs=(P(("seq", "head"), None), P(("seq", "head"), None), P(("seq", "head"), None)),
        check_vma=False,
    )
```

```python
import functools

import jax
import jax.numpy as jnp
from jax import lax
from jax.experimental import pallas as pl
from jax.experimental.pallas import tpu as pltpu
from jax.sharding import PartitionSpec as P

HEAD_DIM = 128
MOST = 1024
GROUP = 4
CUTS = (4, 4, 4, 4)
LINK = jnp.bfloat16
VMEM_LIMIT = 16 * 1024 * 1024
GRAD_LIMIT = 48 * 1024 * 1024
FIRST_LIMIT = 52 * 1024 * 1024
NT = (((1,), (1,)), ((), ()))
TN = (((0,), (0,)), ((), ()))
NN = (((1,), (0,)), ((), ()))


def dot(a, b, dims):
    return lax.dot_general(a, b, dims, preferred_element_type=jnp.float32)


def doc_at(meta, ndocs, position):
    start, begin, end = jnp.int32(0), jnp.int32(0), jnp.int32(0)
    for i in range(ndocs):
        stop = start + meta[i]
        begin = jnp.where(start <= position, start, begin)
        end = jnp.where(start <= position, stop, end)
        start = stop
    return begin, end


def block_range(meta, ndocs, base, rows):
    begin0, end0 = doc_at(meta, ndocs, base)
    begin1, end1 = doc_at(meta, ndocs, base + rows - 1)
    first = jnp.where(begin0 < base, end0, base) - base
    return begin0, end0, begin1, end1, first, begin1 - base


def goes_up(place, hop):
    return lax.rem(lax.div(lax.div(place, 2), hop), 2) == 0


def state_kernel(lengths, q, k, v, g, kept, sent, *, ndocs, rows, heads):
    place = lax.axis_index("seq")
    first_core = lax.rem(place, 2) == 0
    _, _, _, _, first, last = block_range(lengths, ndocs, place * rows, rows)
    order = lax.broadcasted_iota(jnp.int32, (rows, HEAD_DIM), 0)
    first_rows, last_rows = order < first, order >= last
    zero = jnp.zeros((), q.dtype)

    def one(h):
        cols = slice(h * HEAD_DIM, (h + 1) * HEAD_DIM)
        tail = dot(jnp.where(last_rows, k[:, cols], zero), v[:, cols], TN)
        return tail, dot(jnp.where(first_rows, q[:, cols], zero), g[:, cols], TN)

    for i in range(heads // 2):
        for which, (low, high) in enumerate(zip(one(2 * i), one(2 * i + 1))):
            kept[which, i] = jnp.where(first_core, low, high)
            sent[which, i] = jnp.where(first_core, high, low)


def pair_parts(kept, got, first_core, i):
    tail_even = jnp.where(first_core, kept[0, i], got[0, i])
    tail_odd = jnp.where(first_core, got[0, i], kept[0, i])
    head_even = jnp.where(first_core, kept[1, i], got[1, i])
    head_odd = jnp.where(first_core, got[1, i], kept[1, i])
    return tail_even, tail_odd, head_even, head_odd


def pair_kernel(lengths, kept, got, *sent, ndocs, rows, count, hops):
    place = lax.axis_index("seq")
    first_core = lax.rem(place, 2) == 0
    even = (place - lax.rem(place, 2)) * rows
    odd = even + rows
    _, even_e0 = doc_at(lengths, ndocs, even)
    odd_b1, _ = doc_at(lengths, ndocs, odd + rows - 1)
    tail_joins = jnp.where(odd_b1 < odd, 1.0, 0.0)
    head_joins = jnp.where(even_e0 > odd, 1.0, 0.0)
    ups = [goes_up(place, hop) for hop in range(1, hops + 1)]
    for i in range(count):
        tail_even, tail_odd, head_even, head_odd = pair_parts(kept, got, first_core, i)
        tail = tail_odd + tail_joins * tail_even
        head = head_even + head_joins * head_odd
        for hop in range(hops):
            sent[2 * hop][i] = jnp.where(ups[hop], tail, head).astype(LINK)
            sent[2 * hop + 1][i] = jnp.where(ups[hop], head, tail).astype(LINK)


def join_kernel(lengths, kept, got, *rest, ndocs, rows, counts, hops):
    came, mine, theirs = rest[:2 * hops], rest[-2 * len(counts):-len(counts)], rest[-len(counts):]
    place = lax.axis_index("seq")
    first_core = lax.rem(place, 2) == 0
    even = (place - lax.rem(place, 2)) * rows
    odd = even + rows
    even_b0, _ = doc_at(lengths, ndocs, even)
    _, even_e1 = doc_at(lengths, ndocs, odd - 1)
    odd_b0, _ = doc_at(lengths, ndocs, odd)
    _, odd_e1 = doc_at(lengths, ndocs, odd + rows - 1)

    def one(flag):
        return jnp.where(flag, 1.0, 0.0)

    ups = [goes_up(place, hop) for hop in range(1, hops + 1)]
    tail_w = [one(even - hop * 2 * rows > even_b0) for hop in range(hops)]
    head_w = [one(odd + rows + hop * 2 * rows < odd_e1) for hop in range(hops)]
    state_from_tail, state_from_pair = one(odd > odd_b0), one(even > odd_b0)
    grad_from_head, grad_from_pair = one(odd < even_e1), one(odd + rows < even_e1)
    for c, count in enumerate(counts):
        for n in range(count):
            i = sum(counts[:c]) + n
            tail_even, _, _, head_odd = pair_parts(kept, got, first_core, i)
            state_even, grad_odd = 0.0, 0.0
            for hop in range(hops):
                a, b = (came[2 * hop + turn][i].astype(jnp.float32) for turn in range(2))
                state_even = state_even + tail_w[hop] * jnp.where(ups[hop], b, a)
                grad_odd = grad_odd + head_w[hop] * jnp.where(ups[hop], a, b)
            state_odd = state_from_tail * tail_even + state_from_pair * state_even
            grad_even = grad_from_head * head_odd + grad_from_pair * grad_odd
            mine[c][0, n] = jnp.where(first_core, state_even, state_odd)
            mine[c][1, n] = jnp.where(first_core, grad_even, grad_odd)
            theirs[c][0, n] = jnp.where(first_core, state_odd, state_even)
            theirs[c][1, n] = jnp.where(first_core, grad_odd, grad_even)


def split(a, axis):
    high = a.astype(jnp.bfloat16)
    return jnp.concatenate([high, (a - high.astype(jnp.float32)).astype(jnp.bfloat16)], axis=axis)


def grad_kernel(lengths, q, k, v, g, mine, got, *rest, ndocs, rows, heads, groups):
    outs, lower, upper, done = rest[-3 - groups:-3], rest[-3], rest[-2], rest[-1]
    place, column = lax.axis_index("seq"), lax.axis_index("head")
    base = place * rows

    @pl.when(pl.program_id(0) == 0)
    def _():
        line = lax.broadcasted_iota(jnp.int32, (rows, rows), 0)
        across = lax.broadcasted_iota(jnp.int32, (rows, rows), 1)
        begin_line = jnp.zeros((rows, rows), jnp.int32)
        begin_across = jnp.zeros((rows, rows), jnp.int32)
        start = jnp.int32(0) - base
        for i in range(ndocs):
            begin_line = jnp.where(line >= start, start, begin_line)
            begin_across = jnp.where(across >= start, start, begin_across)
            start = start + lengths[i]
        lower[...] = jnp.where((across <= line) & (across >= begin_line), 1, 0)
        upper[...] = jnp.where((line <= across) & (line >= begin_across), 1, 0)

    first_core = lax.rem(place, 2) == 0
    _, _, _, _, first, last = block_range(lengths, ndocs, base, rows)
    order = lax.broadcasted_iota(jnp.int32, (rows, HEAD_DIM), 0)
    first_rows, last_rows = order < first, order >= last
    in_lower, in_upper = lower[...] == 1, upper[...] == 1
    for h in range(heads):
        cols = slice(h * HEAD_DIM, (h + 1) * HEAD_DIM)
        here = first_core if h % 2 == 0 else jnp.logical_not(first_core)
        state, grad = (jnp.where(here, mine[which, h // 2], got[which, h // 2]) for which in range(2))
        qh, kh, vh, gh = (ref[:, cols] for ref in (q, k, v, g))
        k2, v2, g2 = (jnp.concatenate([a, a], axis=1) for a in (kh, vh, gh))
        weight_gv = jnp.where(in_lower, dot(gh, vh, NT), 0.0).astype(jnp.bfloat16)
        weight_vg = jnp.where(in_upper, dot(vh, gh, NT), 0.0).astype(jnp.bfloat16)
        weight_kq = jnp.where(in_upper, dot(kh, qh, NT), 0.0).astype(jnp.bfloat16)
        carry_q = jnp.where(first_rows, dot(g2, split(state, 1), NT), 0.0)
        carry_k = jnp.where(last_rows, dot(v2, split(grad, 1), NT), 0.0)
        carry_v = jnp.where(last_rows, dot(k2, split(grad, 0), NN), 0.0)
        done[0, :, cols] = (dot(weight_gv, kh, NN) + carry_q).astype(jnp.bfloat16)
        done[1, :, cols] = (dot(weight_vg, qh, NN) + carry_k).astype(jnp.bfloat16)
        done[2, :, cols] = (dot(weight_kq, gh, NN) + carry_v).astype(jnp.bfloat16)
    part = rows // groups
    for j in range(groups):
        at = pl.ds(pl.multiple_of(lax.rem(column + j, groups) * part, part), part)
        for i in range(3):
            outs[j][i] = done[i, at, :]


def place_kernel(*refs, groups, offset, cw, width):
    parts, outs, sems = refs[:groups], refs[-4:-1], refs[-1]
    column = lax.axis_index("head")
    copies = []
    for j in range(groups):
        start = pl.multiple_of(lax.rem(column + groups - j, groups) * width + offset, 128)
        for i in range(3):
            copies.append(pltpu.make_async_copy(parts[j].at[i], outs[i].at[:, pl.ds(start, cw)], sems.at[len(copies)]))
            copies[-1].start()
    for copy in copies:
        copy.wait()


def cuts_of(width):
    heads = width // HEAD_DIM
    sizes = CUTS if sum(CUTS) == heads else (2,) * (heads // 2)
    offsets = [sum(sizes[:c]) for c in range(len(sizes))]
    return [(o * HEAD_DIM, s * HEAD_DIM) for o, s in zip(offsets, sizes)]


def shards(queries, keys, values, out_grad, doc_lengths):
    rows, width = queries.shape
    ndocs = doc_lengths.shape[0]
    seq, groups = lax.axis_size("seq"), lax.axis_size("head")
    pairs = seq // 2
    hops = -(-MOST // (2 * rows))
    cuts = cuts_of(width)
    group = GROUP if width % (GROUP * HEAD_DIM) == 0 else 2
    gw, step = group * HEAD_DIM, 2 * HEAD_DIM
    count = width // HEAD_DIM // 2
    counts = [cw // HEAD_DIM // 2 for _, cw in cuts]
    part = rows // groups
    anywhere = pl.BlockSpec(memory_space=pl.ANY)
    in_vmem = pl.BlockSpec(memory_space=pltpu.VMEM)
    in_smem = pl.BlockSpec(memory_space=pltpu.SMEM)
    f32, bf16 = jnp.float32, jnp.bfloat16
    inputs = (queries, keys, values, out_grad)
    sizes = dict(ndocs=ndocs, rows=rows)
    cheap = pl.CostEstimate(flops=0, bytes_accessed=1024, transcendentals=0)

    def shape_of(*dims, dtype=f32):
        return jax.ShapeDtypeStruct(dims, dtype)

    def call(name, kernel, args, outs, scratch=(), after=()):
        return pl.pallas_call(
            kernel, in_specs=[in_smem] + [in_vmem] * len(args) + [anywhere] * len(after), out_specs=[in_vmem] * len(outs), out_shape=outs,
            scratch_shapes=list(scratch), cost_estimate=cheap,
            compiler_params=pltpu.CompilerParams(vmem_limit_bytes=VMEM_LIMIT), name=name,
        )(doc_lengths, *args, *after)

    def swap_cores(a):
        return lax.ppermute(a, "seq", [(b, b ^ 1) for b in range(seq)])

    def swap_pairs(sent):
        came = []
        for hop in range(1, hops + 1):
            for turn in range(2):
                lower = [m for m in range(pairs - hop) if (m // hop) % 2 == turn]
                perm = [(2 * m + core, 2 * (m + hop) + core) for m in lower for core in range(2)]
                came.append(lax.ppermute(sent[2 * (hop - 1) + turn], "seq", perm + [(b, a) for a, b in perm]))
        return came

    def send_rows(outs):
        arrived = list(outs[:1])
        for j in range(1, groups):
            arrived.append(lax.ppermute(outs[j], "head", [(x, (x + j) % groups) for x in range(groups)]))
        return arrived

    square = (HEAD_DIM, HEAD_DIM)
    state_block = pl.BlockSpec((2, group // 2) + square, lambda c, lengths: (0, c, 0, 0))
    kept, sent = pl.pallas_call(
        functools.partial(state_kernel, heads=group, **sizes),
        grid_spec=pltpu.PrefetchScalarGridSpec(
            num_scalar_prefetch=1, grid=(width // gw,),
            in_specs=[pl.BlockSpec((rows, gw), lambda c, lengths: (0, c))] * 4, out_specs=[state_block] * 2,
        ),
        out_shape=[shape_of(2, count, *square)] * 2, cost_estimate=cheap,
        compiler_params=pltpu.CompilerParams(vmem_limit_bytes=FIRST_LIMIT), name="states",
    )(doc_lengths, *inputs)
    got = swap_cores(sent)
    sent = call(
        "pair", functools.partial(pair_kernel, count=count, hops=hops, **sizes), (kept, got),
        [shape_of(count, *square, dtype=LINK)] * (2 * hops),
    )
    came = swap_pairs(sent)
    joined = call(
        "join", functools.partial(join_kernel, counts=counts, hops=hops, **sizes), (kept, got, *came),
        [shape_of(2, n, *square) for n in counts] * 2,
    )
    parts, last = [], joined[0]
    for c, (offset, cw) in enumerate(cuts):
        mine, theirs = joined[c], joined[len(cuts) + c]
        block = pl.BlockSpec((rows, step), lambda s, lengths, at=offset // step: (0, at + s))
        pair_block = pl.BlockSpec((2, 1) + square, lambda s, lengths: (0, s, 0, 0))
        out_block = pl.BlockSpec((3, part, step), lambda s, lengths: (0, 0, s))
        outs = pl.pallas_call(
            functools.partial(grad_kernel, heads=2, groups=groups, **sizes),
            grid_spec=pltpu.PrefetchScalarGridSpec(
                num_scalar_prefetch=1, grid=(cw // step,), in_specs=[block] * 4 + [pair_block] * 2 + [anywhere],
                out_specs=[out_block] * groups,
                scratch_shapes=[pltpu.VMEM((rows, rows), jnp.int32)] * 2 + [pltpu.VMEM((3, rows, step), bf16)],
            ),
            out_shape=[shape_of(3, part, cw, dtype=bf16)] * groups, cost_estimate=cheap,
            compiler_params=pltpu.CompilerParams(vmem_limit_bytes=GRAD_LIMIT), name="grads",
        )(doc_lengths, *inputs, mine, swap_cores(theirs), last)
        last = outs[0]
        parts += send_rows(outs)

    placed = []
    for c, (offset, cw) in enumerate(cuts):
        some = parts[c * groups:(c + 1) * groups]
        placed = pl.pallas_call(
            functools.partial(place_kernel, groups=groups, offset=offset, cw=cw, width=width),
            grid_spec=pl.GridSpec(
                grid=(1,), in_specs=[anywhere] * (groups + len(placed)), out_specs=[anywhere] * 3,
                scratch_shapes=[pltpu.SemaphoreType.DMA((3 * groups,))],
            ),
            out_shape=[shape_of(part, width * groups, dtype=bf16)] * 3,
            input_output_aliases={groups + i: i for i in range(len(placed))},
            cost_estimate=cheap,
            compiler_params=pltpu.CompilerParams(vmem_limit_bytes=VMEM_LIMIT), name="place",
        )(*some, *placed)
    return tuple(placed)


def solution(mesh):
    return jax.shard_map(
        shards,
        mesh=mesh,
        in_specs=(P("seq", "head"), P("seq", "head"), P("seq", "head"), P("seq", "head"), P()),
        out_specs=(P(("seq", "head"), None), P(("seq", "head"), None), P(("seq", "head"), None)),
        check_vma=False,
    )
```

```python
import functools

import jax
import jax.numpy as jnp
from jax import lax
from jax.experimental import pallas as pl
from jax.experimental.pallas import tpu as pltpu
from jax.sharding import PartitionSpec as P

HEAD_DIM = 128
MOST = 1024
GROUP = 4
CHUNK = 4
LINK = jnp.bfloat16
VMEM_LIMIT = 16 * 1024 * 1024
GRAD_LIMIT = 48 * 1024 * 1024
FIRST_LIMIT = 52 * 1024 * 1024
NT = (((1,), (1,)), ((), ()))
TN = (((0,), (0,)), ((), ()))
NN = (((1,), (0,)), ((), ()))


def dot(a, b, dims):
    return lax.dot_general(a, b, dims, preferred_element_type=jnp.float32)


def doc_at(meta, ndocs, position):
    start, begin, end = jnp.int32(0), jnp.int32(0), jnp.int32(0)
    for i in range(ndocs):
        stop = start + meta[i]
        begin = jnp.where(start <= position, start, begin)
        end = jnp.where(start <= position, stop, end)
        start = stop
    return begin, end


def block_range(meta, ndocs, base, rows):
    begin0, end0 = doc_at(meta, ndocs, base)
    begin1, end1 = doc_at(meta, ndocs, base + rows - 1)
    first = jnp.where(begin0 < base, end0, base) - base
    return begin0, end0, begin1, end1, first, begin1 - base


def goes_up(place, hop):
    return lax.rem(lax.div(lax.div(place, 2), hop), 2) == 0


def state_kernel(lengths, q, k, v, g, *rest, ndocs, rows, offset, heads, group):
    kept, sent, held, sems = rest[-4:]
    gw = group * HEAD_DIM
    copies = []
    for c in range(heads // group):
        for i, ref in enumerate((q, k, v, g)):
            src = ref.at[:, pl.ds(offset + c * gw, gw)]
            copies.append(pltpu.make_async_copy(src, held.at[i, :, pl.ds(c * gw, gw)], sems.at[c, i]))
            copies[-1].start()
    place = lax.axis_index("seq")
    first_core = lax.rem(place, 2) == 0
    _, _, _, _, first, last = block_range(lengths, ndocs, place * rows, rows)
    order = lax.broadcasted_iota(jnp.int32, (rows, HEAD_DIM), 0)
    first_rows, last_rows = order < first, order >= last
    zero = jnp.zeros((), held.dtype)

    def one(h):
        cols = slice(h * HEAD_DIM, (h + 1) * HEAD_DIM)
        tail = dot(jnp.where(last_rows, held[1, :, cols], zero), held[2, :, cols], TN)
        return tail, dot(jnp.where(first_rows, held[0, :, cols], zero), held[3, :, cols], TN)

    for i in range(heads // 2):
        if 2 * i % group == 0:
            for copy in copies[8 * i // group:8 * i // group + 4]:
                copy.wait()
        for which, (low, high) in enumerate(zip(one(2 * i), one(2 * i + 1))):
            kept[which, i] = jnp.where(first_core, low, high)
            sent[which, i] = jnp.where(first_core, high, low)


def pair_parts(kept, got, first_core, i):
    tail_even = jnp.where(first_core, kept[0, i], got[0, i])
    tail_odd = jnp.where(first_core, got[0, i], kept[0, i])
    head_even = jnp.where(first_core, kept[1, i], got[1, i])
    head_odd = jnp.where(first_core, got[1, i], kept[1, i])
    return tail_even, tail_odd, head_even, head_odd


def pair_kernel(lengths, kept, got, *rest, ndocs, rows, count, hops):
    sent = rest[-2 * hops:]
    place = lax.axis_index("seq")
    first_core = lax.rem(place, 2) == 0
    even = (place - lax.rem(place, 2)) * rows
    odd = even + rows
    _, even_e0 = doc_at(lengths, ndocs, even)
    odd_b1, _ = doc_at(lengths, ndocs, odd + rows - 1)
    tail_joins = jnp.where(odd_b1 < odd, 1.0, 0.0)
    head_joins = jnp.where(even_e0 > odd, 1.0, 0.0)
    ups = [goes_up(place, hop) for hop in range(1, hops + 1)]
    for i in range(count):
        tail_even, tail_odd, head_even, head_odd = pair_parts(kept, got, first_core, i)
        tail = tail_odd + tail_joins * tail_even
        head = head_even + head_joins * head_odd
        for hop in range(hops):
            sent[2 * hop][i] = jnp.where(ups[hop], tail, head).astype(LINK)
            sent[2 * hop + 1][i] = jnp.where(ups[hop], head, tail).astype(LINK)


def join_kernel(lengths, kept, got, *rest, ndocs, rows, counts, hops):
    came, mine, theirs = rest[:2 * hops], rest[-2 * len(counts):-len(counts)], rest[-len(counts):]
    place = lax.axis_index("seq")
    first_core = lax.rem(place, 2) == 0
    even = (place - lax.rem(place, 2)) * rows
    odd = even + rows
    even_b0, _ = doc_at(lengths, ndocs, even)
    _, even_e1 = doc_at(lengths, ndocs, odd - 1)
    odd_b0, _ = doc_at(lengths, ndocs, odd)
    _, odd_e1 = doc_at(lengths, ndocs, odd + rows - 1)

    def one(flag):
        return jnp.where(flag, 1.0, 0.0)

    ups = [goes_up(place, hop) for hop in range(1, hops + 1)]
    tail_w = [one(even - hop * 2 * rows > even_b0) for hop in range(hops)]
    head_w = [one(odd + rows + hop * 2 * rows < odd_e1) for hop in range(hops)]
    state_from_tail, state_from_pair = one(odd > odd_b0), one(even > odd_b0)
    grad_from_head, grad_from_pair = one(odd < even_e1), one(odd + rows < even_e1)
    for c, count in enumerate(counts):
        for n in range(count):
            i = sum(counts[:c]) + n
            tail_even, _, _, head_odd = pair_parts(kept, got, first_core, i)
            state_even, grad_odd = 0.0, 0.0
            for hop in range(hops):
                a, b = (came[2 * hop + turn][i].astype(jnp.float32) for turn in range(2))
                state_even = state_even + tail_w[hop] * jnp.where(ups[hop], b, a)
                grad_odd = grad_odd + head_w[hop] * jnp.where(ups[hop], a, b)
            state_odd = state_from_tail * tail_even + state_from_pair * state_even
            grad_even = grad_from_head * head_odd + grad_from_pair * grad_odd
            mine[c][0, n] = jnp.where(first_core, state_even, state_odd)
            mine[c][1, n] = jnp.where(first_core, grad_even, grad_odd)
            theirs[c][0, n] = jnp.where(first_core, state_odd, state_even)
            theirs[c][1, n] = jnp.where(first_core, grad_odd, grad_even)


def split(a, axis):
    high = a.astype(jnp.bfloat16)
    return jnp.concatenate([high, (a - high.astype(jnp.float32)).astype(jnp.bfloat16)], axis=axis)


def grad_kernel(lengths, q, k, v, g, mine, got, *rest, ndocs, rows, heads, groups):
    outs, lower, upper, done = rest[-3 - groups:-3], rest[-3], rest[-2], rest[-1]
    place, column = lax.axis_index("seq"), lax.axis_index("head")
    base = place * rows

    @pl.when(pl.program_id(0) == 0)
    def _():
        line = lax.broadcasted_iota(jnp.int32, (rows, rows), 0)
        across = lax.broadcasted_iota(jnp.int32, (rows, rows), 1)
        begin_line = jnp.zeros((rows, rows), jnp.int32)
        begin_across = jnp.zeros((rows, rows), jnp.int32)
        start = jnp.int32(0) - base
        for i in range(ndocs):
            begin_line = jnp.where(line >= start, start, begin_line)
            begin_across = jnp.where(across >= start, start, begin_across)
            start = start + lengths[i]
        lower[...] = jnp.where((across <= line) & (across >= begin_line), 1, 0)
        upper[...] = jnp.where((line <= across) & (line >= begin_across), 1, 0)

    first_core = lax.rem(place, 2) == 0
    _, _, _, _, first, last = block_range(lengths, ndocs, base, rows)
    order = lax.broadcasted_iota(jnp.int32, (rows, HEAD_DIM), 0)
    first_rows, last_rows = order < first, order >= last
    in_lower, in_upper = lower[...] == 1, upper[...] == 1
    for h in range(heads):
        cols = slice(h * HEAD_DIM, (h + 1) * HEAD_DIM)
        here = first_core if h % 2 == 0 else jnp.logical_not(first_core)
        state, grad = (jnp.where(here, mine[which, h // 2], got[which, h // 2]) for which in range(2))
        qh, kh, vh, gh = (ref[:, cols] for ref in (q, k, v, g))
        k2, v2, g2 = (jnp.concatenate([a, a], axis=1) for a in (kh, vh, gh))
        weight_gv = jnp.where(in_lower, dot(gh, vh, NT), 0.0).astype(jnp.bfloat16)
        weight_vg = jnp.where(in_upper, dot(vh, gh, NT), 0.0).astype(jnp.bfloat16)
        weight_kq = jnp.where(in_upper, dot(kh, qh, NT), 0.0).astype(jnp.bfloat16)
        carry_q = jnp.where(first_rows, dot(g2, split(state, 1), NT), 0.0)
        carry_k = jnp.where(last_rows, dot(v2, split(grad, 1), NT), 0.0)
        carry_v = jnp.where(last_rows, dot(k2, split(grad, 0), NN), 0.0)
        done[0, :, cols] = (dot(weight_gv, kh, NN) + carry_q).astype(jnp.bfloat16)
        done[1, :, cols] = (dot(weight_vg, qh, NN) + carry_k).astype(jnp.bfloat16)
        done[2, :, cols] = (dot(weight_kq, gh, NN) + carry_v).astype(jnp.bfloat16)
    part = rows // groups
    for j in range(groups):
        at = pl.ds(pl.multiple_of(lax.rem(column + j, groups) * part, part), part)
        for i in range(3):
            outs[j][i] = done[i, at, :]


def place_kernel(*refs, groups, offset, cw, width):
    parts, outs, sems = refs[:groups], refs[-4:-1], refs[-1]
    column = lax.axis_index("head")
    copies = []
    for j in range(groups):
        start = pl.multiple_of(lax.rem(column + groups - j, groups) * width + offset, 128)
        for i in range(3):
            copies.append(pltpu.make_async_copy(parts[j].at[i], outs[i].at[:, pl.ds(start, cw)], sems.at[len(copies)]))
            copies[-1].start()
    for copy in copies:
        copy.wait()


def cuts_of(width):
    heads = width // HEAD_DIM
    size = CHUNK if heads % (2 * CHUNK) == 0 else 2
    cw, half = size * HEAD_DIM, max(heads // 2, size) * HEAD_DIM
    return [(at, half, [(o, cw) for o in range(at, at + half, cw)]) for at in range(0, width, half)]


def shards(queries, keys, values, out_grad, doc_lengths):
    rows, width = queries.shape
    ndocs = doc_lengths.shape[0]
    seq, groups = lax.axis_size("seq"), lax.axis_size("head")
    pairs = seq // 2
    hops = -(-MOST // (2 * rows))
    halves = cuts_of(width)
    step = 2 * HEAD_DIM
    part = rows // groups
    anywhere = pl.BlockSpec(memory_space=pl.ANY)
    in_vmem = pl.BlockSpec(memory_space=pltpu.VMEM)
    in_smem = pl.BlockSpec(memory_space=pltpu.SMEM)
    f32, bf16 = jnp.float32, jnp.bfloat16
    inputs = (queries, keys, values, out_grad)
    sizes = dict(ndocs=ndocs, rows=rows)
    cheap = pl.CostEstimate(flops=0, bytes_accessed=1024, transcendentals=0)

    def shape_of(*dims, dtype=f32):
        return jax.ShapeDtypeStruct(dims, dtype)

    def call(name, kernel, args, outs, scratch=(), after=()):
        return pl.pallas_call(
            kernel, in_specs=[in_smem] + [in_vmem] * len(args) + [anywhere] * len(after), out_specs=[in_vmem] * len(outs), out_shape=outs,
            scratch_shapes=list(scratch), cost_estimate=cheap,
            compiler_params=pltpu.CompilerParams(vmem_limit_bytes=VMEM_LIMIT), name=name,
        )(doc_lengths, *args, *after)

    def swap_cores(a):
        return lax.ppermute(a, "seq", [(b, b ^ 1) for b in range(seq)])

    def swap_pairs(sent):
        came = []
        for hop in range(1, hops + 1):
            for turn in range(2):
                lower = [m for m in range(pairs - hop) if (m // hop) % 2 == turn]
                perm = [(2 * m + core, 2 * (m + hop) + core) for m in lower for core in range(2)]
                came.append(lax.ppermute(sent[2 * (hop - 1) + turn], "seq", perm + [(b, a) for a, b in perm]))
        return came

    def send_rows(outs):
        arrived = list(outs[:1])
        for j in range(1, groups):
            arrived.append(lax.ppermute(outs[j], "head", [(x, (x + j) % groups) for x in range(groups)]))
        return arrived

    square = (HEAD_DIM, HEAD_DIM)

    def states(offset, half, after):
        heads = half // HEAD_DIM
        group = GROUP if heads % GROUP == 0 else 2
        kept, sent = pl.pallas_call(
            functools.partial(state_kernel, offset=offset, heads=heads, group=group, **sizes),
            in_specs=[in_smem] + [anywhere] * (4 + len(after)), out_specs=[in_vmem] * 2,
            out_shape=[shape_of(2, heads // 2, *square)] * 2,
            scratch_shapes=[pltpu.VMEM((4, rows, half), bf16), pltpu.SemaphoreType.DMA((heads // group, 4))],
            cost_estimate=cheap, compiler_params=pltpu.CompilerParams(vmem_limit_bytes=FIRST_LIMIT), name="states",
        )(doc_lengths, *inputs, *after)
        return kept, swap_cores(sent)

    def pair_up(kept, got, after):
        sent = call(
            "pair", functools.partial(pair_kernel, count=kept.shape[1], hops=hops, **sizes), (kept, got),
            [shape_of(kept.shape[1], *square, dtype=LINK)] * (2 * hops), after=after,
        )
        return swap_pairs(sent)

    def join(kept, got, came, chunks, after):
        counts = [cw // step for _, cw in chunks]
        joined = call(
            "join", functools.partial(join_kernel, counts=counts, hops=hops, **sizes), (kept, got, *came),
            [shape_of(2, n, *square) for n in counts] * 2, after=after,
        )
        return [(mine, swap_cores(theirs)) for mine, theirs in zip(joined[:len(chunks)], joined[len(chunks):])]

    def grads(offset, cw, mine, theirs, after):
        block = pl.BlockSpec((rows, step), lambda s, lengths: (0, offset // step + s))
        pair_block = pl.BlockSpec((2, 1) + square, lambda s, lengths: (0, s, 0, 0))
        out_block = pl.BlockSpec((3, part, step), lambda s, lengths: (0, 0, s))
        return pl.pallas_call(
            functools.partial(grad_kernel, heads=2, groups=groups, **sizes),
            grid_spec=pltpu.PrefetchScalarGridSpec(
                num_scalar_prefetch=1, grid=(cw // step,),
                in_specs=[block] * 4 + [pair_block] * 2 + [anywhere] * len(after), out_specs=[out_block] * groups,
                scratch_shapes=[pltpu.VMEM((rows, rows), jnp.int32)] * 2 + [pltpu.VMEM((3, rows, step), bf16)],
            ),
            out_shape=[shape_of(3, part, cw, dtype=bf16)] * groups, cost_estimate=cheap,
            compiler_params=pltpu.CompilerParams(vmem_limit_bytes=GRAD_LIMIT), name="grads",
        )(doc_lengths, *inputs, mine, theirs, *after)

    own = []
    for offset, half, _ in halves:
        own.append(states(offset, half, [kept for kept, _ in own[-1:]]))
    cuts, parts, outs, first_outs = [], [], [], []
    for (kept, got), (_, _, chunks) in zip(own, halves):
        came = pair_up(kept, got, first_outs)
        joined = join(kept, got, came, chunks, parts[1:2] + outs)
        for (offset, cw), (mine, theirs) in zip(chunks, joined):
            outs = list(grads(offset, cw, mine, theirs, outs[:1]))
            first_outs = first_outs or outs[:1]
            parts += send_rows(outs)
            outs = outs[:1]
        cuts += chunks

    placed = []
    for c, (offset, cw) in enumerate(cuts):
        some = parts[c * groups:(c + 1) * groups]
        placed = pl.pallas_call(
            functools.partial(place_kernel, groups=groups, offset=offset, cw=cw, width=width),
            grid_spec=pl.GridSpec(
                grid=(1,), in_specs=[anywhere] * (groups + len(placed)), out_specs=[anywhere] * 3,
                scratch_shapes=[pltpu.SemaphoreType.DMA((3 * groups,))],
            ),
            out_shape=[shape_of(part, width * groups, dtype=bf16)] * 3,
            input_output_aliases={groups + i: i for i in range(len(placed))},
            cost_estimate=cheap,
            compiler_params=pltpu.CompilerParams(vmem_limit_bytes=VMEM_LIMIT), name="place",
        )(*some, *placed)
    return tuple(placed)


def solution(mesh):
    return jax.shard_map(
        shards,
        mesh=mesh,
        in_specs=(P("seq", "head"), P("seq", "head"), P("seq", "head"), P("seq", "head"), P()),
        out_specs=(P(("seq", "head"), None), P(("seq", "head"), None), P(("seq", "head"), None)),
        check_vma=False,
    )
```

```python
import functools

import jax
import jax.numpy as jnp
from jax import lax
from jax.experimental import pallas as pl
from jax.experimental.pallas import tpu as pltpu
from jax.sharding import PartitionSpec as P

HEAD_DIM = 128
MOST = 1024
GROUP = 4
CHUNK = 4
LINK = jnp.bfloat16
VMEM_LIMIT = 16 * 1024 * 1024
GRAD_LIMIT = 48 * 1024 * 1024
FIRST_LIMIT = 52 * 1024 * 1024
NT = (((1,), (1,)), ((), ()))
TN = (((0,), (0,)), ((), ()))
NN = (((1,), (0,)), ((), ()))


def dot(a, b, dims):
    return lax.dot_general(a, b, dims, preferred_element_type=jnp.float32)


def doc_at(meta, ndocs, position):
    start, begin, end = jnp.int32(0), jnp.int32(0), jnp.int32(0)
    for i in range(ndocs):
        stop = start + meta[i]
        begin = jnp.where(start <= position, start, begin)
        end = jnp.where(start <= position, stop, end)
        start = stop
    return begin, end


def block_range(meta, ndocs, base, rows):
    begin0, end0 = doc_at(meta, ndocs, base)
    begin1, end1 = doc_at(meta, ndocs, base + rows - 1)
    first = jnp.where(begin0 < base, end0, base) - base
    return begin0, end0, begin1, end1, first, begin1 - base


def state_kernel(lengths, q, k, v, g, *rest, ndocs, rows, offset, heads, group):
    kept, sent, held, sems = rest[-4:]
    gw = group * HEAD_DIM
    copies = []
    for c in range(heads // group):
        for i, ref in enumerate((q, k, v, g)):
            src = ref.at[:, pl.ds(offset + c * gw, gw)]
            copies.append(pltpu.make_async_copy(src, held.at[i, :, pl.ds(c * gw, gw)], sems.at[c, i]))
            copies[-1].start()
    place = lax.axis_index("seq")
    first_core = lax.rem(place, 2) == 0
    _, _, _, _, first, last = block_range(lengths, ndocs, place * rows, rows)
    order = lax.broadcasted_iota(jnp.int32, (rows, HEAD_DIM), 0)
    first_rows, last_rows = order < first, order >= last
    zero = jnp.zeros((), held.dtype)

    def one(h):
        cols = slice(h * HEAD_DIM, (h + 1) * HEAD_DIM)
        tail = dot(jnp.where(last_rows, held[1, :, cols], zero), held[2, :, cols], TN)
        return tail, dot(jnp.where(first_rows, held[0, :, cols], zero), held[3, :, cols], TN)

    for h in range(heads):
        if h % group == 0:
            for copy in copies[4 * h // group:4 * h // group + 4]:
                copy.wait()
        tail, head = one(h)
        kept[h] = jnp.where(first_core, tail, head)
        sent[h] = jnp.where(first_core, head, tail)


def pair_kernel(lengths, kept, got, *rest, ndocs, rows):
    sent = rest[-1]
    place = lax.axis_index("seq")
    first_core = lax.rem(place, 2) == 0
    even = (place - lax.rem(place, 2)) * rows
    odd = even + rows
    _, even_e0 = doc_at(lengths, ndocs, even)
    odd_b1, _ = doc_at(lengths, ndocs, odd + rows - 1)
    joins = jnp.where(jnp.where(first_core, odd_b1 < odd, even_e0 > odd), 1.0, 0.0)
    sent[...] = (got[...] + joins * kept[...]).astype(LINK)


def join_kernel(lengths, other, *rest, ndocs, rows, counts, hops):
    came, mine, theirs = rest[:hops], rest[-2 * len(counts):-len(counts)], rest[-len(counts):]
    place = lax.axis_index("seq")
    first_core = lax.rem(place, 2) == 0
    even = (place - lax.rem(place, 2)) * rows
    odd = even + rows
    even_b0, _ = doc_at(lengths, ndocs, even)
    _, even_e1 = doc_at(lengths, ndocs, odd - 1)
    odd_b0, _ = doc_at(lengths, ndocs, odd)
    _, odd_e1 = doc_at(lengths, ndocs, odd + rows - 1)

    def one(if_first, if_second):
        return jnp.where(jnp.where(first_core, if_first, if_second), 1.0, 0.0)

    weights = [
        one(odd + rows + hop * 2 * rows < odd_e1, even - hop * 2 * rows > even_b0) for hop in range(hops)
    ]
    from_other, from_pair = one(odd < even_e1, odd > odd_b0), one(odd + rows < even_e1, even > odd_b0)
    for c, count in enumerate(counts):
        at = slice(sum(counts[:c]), sum(counts[:c + 1]))
        total = weights[0] * came[0][at].astype(jnp.float32)
        for hop in range(1, hops):
            total = total + weights[hop] * came[hop][at].astype(jnp.float32)
        theirs[c][...] = total
        mine[c][...] = from_other * other[at] + from_pair * total


def split(a, axis):
    high = a.astype(jnp.bfloat16)
    return jnp.concatenate([high, (a - high.astype(jnp.float32)).astype(jnp.bfloat16)], axis=axis)


def grad_kernel(lengths, q, k, v, g, mine, got, *rest, ndocs, rows, heads, groups):
    outs, lower, upper, done = rest[-3 - groups:-3], rest[-3], rest[-2], rest[-1]
    place, column = lax.axis_index("seq"), lax.axis_index("head")
    base = place * rows

    @pl.when(pl.program_id(0) == 0)
    def _():
        line = lax.broadcasted_iota(jnp.int32, (rows, rows), 0)
        across = lax.broadcasted_iota(jnp.int32, (rows, rows), 1)
        begin_line = jnp.zeros((rows, rows), jnp.int32)
        begin_across = jnp.zeros((rows, rows), jnp.int32)
        start = jnp.int32(0) - base
        for i in range(ndocs):
            begin_line = jnp.where(line >= start, start, begin_line)
            begin_across = jnp.where(across >= start, start, begin_across)
            start = start + lengths[i]
        lower[...] = jnp.where((across <= line) & (across >= begin_line), 1, 0)
        upper[...] = jnp.where((line <= across) & (line >= begin_across), 1, 0)

    first_core = lax.rem(place, 2) == 0
    _, _, _, _, first, last = block_range(lengths, ndocs, base, rows)
    order = lax.broadcasted_iota(jnp.int32, (rows, HEAD_DIM), 0)
    first_rows, last_rows = order < first, order >= last
    in_lower, in_upper = lower[...] == 1, upper[...] == 1
    for h in range(heads):
        cols = slice(h * HEAD_DIM, (h + 1) * HEAD_DIM)
        state = jnp.where(first_core, got[h], mine[h])
        grad = jnp.where(first_core, mine[h], got[h])
        qh, kh, vh, gh = (ref[:, cols] for ref in (q, k, v, g))
        k2, v2, g2 = (jnp.concatenate([a, a], axis=1) for a in (kh, vh, gh))
        weight_gv = jnp.where(in_lower, dot(gh, vh, NT), 0.0).astype(jnp.bfloat16)
        weight_vg = jnp.where(in_upper, dot(vh, gh, NT), 0.0).astype(jnp.bfloat16)
        weight_kq = jnp.where(in_upper, dot(kh, qh, NT), 0.0).astype(jnp.bfloat16)
        carry_q = jnp.where(first_rows, dot(g2, split(state, 1), NT), 0.0)
        carry_k = jnp.where(last_rows, dot(v2, split(grad, 1), NT), 0.0)
        carry_v = jnp.where(last_rows, dot(k2, split(grad, 0), NN), 0.0)
        done[0, :, cols] = (dot(weight_gv, kh, NN) + carry_q).astype(jnp.bfloat16)
        done[1, :, cols] = (dot(weight_vg, qh, NN) + carry_k).astype(jnp.bfloat16)
        done[2, :, cols] = (dot(weight_kq, gh, NN) + carry_v).astype(jnp.bfloat16)
    part = rows // groups
    for j in range(groups):
        at = pl.ds(pl.multiple_of(lax.rem(column + j, groups) * part, part), part)
        for i in range(3):
            outs[j][i] = done[i, at, :]


def place_kernel(*refs, groups, offset, cw, width):
    parts, outs, sems = refs[:groups], refs[-4:-1], refs[-1]
    column = lax.axis_index("head")
    copies = []
    for j in range(groups):
        start = pl.multiple_of(lax.rem(column + groups - j, groups) * width + offset, 128)
        for i in range(3):
            copies.append(pltpu.make_async_copy(parts[j].at[i], outs[i].at[:, pl.ds(start, cw)], sems.at[len(copies)]))
            copies[-1].start()
    for copy in copies:
        copy.wait()


def cuts_of(width):
    heads = width // HEAD_DIM
    size = CHUNK if heads % (2 * CHUNK) == 0 else 2
    cw, half = size * HEAD_DIM, max(heads // 2, size) * HEAD_DIM
    return [(at, half, [(o, cw) for o in range(at, at + half, cw)]) for at in range(0, width, half)]


def shards(queries, keys, values, out_grad, doc_lengths):
    rows, width = queries.shape
    ndocs = doc_lengths.shape[0]
    seq, groups = lax.axis_size("seq"), lax.axis_size("head")
    pairs = seq // 2
    hops = -(-MOST // (2 * rows))
    halves = cuts_of(width)
    step = 2 * HEAD_DIM
    part = rows // groups
    anywhere = pl.BlockSpec(memory_space=pl.ANY)
    in_vmem = pl.BlockSpec(memory_space=pltpu.VMEM)
    in_smem = pl.BlockSpec(memory_space=pltpu.SMEM)
    f32, bf16 = jnp.float32, jnp.bfloat16
    inputs = (queries, keys, values, out_grad)
    sizes = dict(ndocs=ndocs, rows=rows)
    cheap = pl.CostEstimate(flops=0, bytes_accessed=1024, transcendentals=0)

    def shape_of(*dims, dtype=f32):
        return jax.ShapeDtypeStruct(dims, dtype)

    def call(name, kernel, args, outs, scratch=(), after=()):
        return pl.pallas_call(
            kernel, in_specs=[in_smem] + [in_vmem] * len(args) + [anywhere] * len(after), out_specs=[in_vmem] * len(outs), out_shape=outs,
            scratch_shapes=list(scratch), cost_estimate=cheap,
            compiler_params=pltpu.CompilerParams(vmem_limit_bytes=VMEM_LIMIT), name=name,
        )(doc_lengths, *args, *after)

    def swap_cores(a):
        return lax.ppermute(a, "seq", [(b, b ^ 1) for b in range(seq)])

    def swap_pairs(sent):
        came = []
        for hop in range(1, hops + 1):
            perm = [(2 * m, 2 * (m + hop) + 1) for m in range(pairs - hop)]
            came.append(lax.ppermute(sent, "seq", perm + [(b, a) for a, b in perm]))
        return came

    def send_rows(outs):
        arrived = list(outs[:1])
        for j in range(1, groups):
            arrived.append(lax.ppermute(outs[j], "head", [(x, (x + j) % groups) for x in range(groups)]))
        return arrived

    square = (HEAD_DIM, HEAD_DIM)

    def states(offset, half, after):
        heads = half // HEAD_DIM
        group = GROUP if heads % GROUP == 0 else 2
        kept, sent = pl.pallas_call(
            functools.partial(state_kernel, offset=offset, heads=heads, group=group, **sizes),
            in_specs=[in_smem] + [anywhere] * (4 + len(after)), out_specs=[in_vmem] * 2,
            out_shape=[shape_of(heads, *square)] * 2,
            scratch_shapes=[pltpu.VMEM((4, rows, half), bf16), pltpu.SemaphoreType.DMA((heads // group, 4))],
            cost_estimate=cheap, compiler_params=pltpu.CompilerParams(vmem_limit_bytes=FIRST_LIMIT), name="states",
        )(doc_lengths, *inputs, *after)
        return kept, swap_cores(sent)

    def pair_up(kept, got, after):
        out = shape_of(*kept.shape, dtype=LINK)
        return swap_pairs(call("pair", functools.partial(pair_kernel, **sizes), (kept, got), [out], after=after)[0])

    def join(kept, came, chunks, after):
        counts = [cw // HEAD_DIM for _, cw in chunks]
        joined = call(
            "join", functools.partial(join_kernel, counts=counts, hops=hops, **sizes), (swap_cores(kept), *came),
            [shape_of(n, *square) for n in counts] * 2, after=after,
        )
        return [(mine, swap_cores(theirs)) for mine, theirs in zip(joined[:len(chunks)], joined[len(chunks):])]

    def grads(offset, cw, mine, theirs, after):
        block = pl.BlockSpec((rows, step), lambda s, lengths: (0, offset // step + s))
        state_block = pl.BlockSpec((2,) + square, lambda s, lengths: (s, 0, 0))
        out_block = pl.BlockSpec((3, part, step), lambda s, lengths: (0, 0, s))
        return pl.pallas_call(
            functools.partial(grad_kernel, heads=2, groups=groups, **sizes),
            grid_spec=pltpu.PrefetchScalarGridSpec(
                num_scalar_prefetch=1, grid=(cw // step,),
                in_specs=[block] * 4 + [state_block] * 2 + [anywhere] * len(after), out_specs=[out_block] * groups,
                scratch_shapes=[pltpu.VMEM((rows, rows), jnp.int32)] * 2 + [pltpu.VMEM((3, rows, step), bf16)],
            ),
            out_shape=[shape_of(3, part, cw, dtype=bf16)] * groups, cost_estimate=cheap,
            compiler_params=pltpu.CompilerParams(vmem_limit_bytes=GRAD_LIMIT), name="grads",
        )(doc_lengths, *inputs, mine, theirs, *after)

    own = []
    for offset, half, _ in halves:
        own.append(states(offset, half, [kept for kept, _ in own[-1:]]))
    cuts, sent, arrived = [], [], []
    for (kept, got), (_, _, chunks) in zip(own, halves):
        came = pair_up(kept, got, [outs[0] for outs in sent[:1]])
        for (offset, cw), (mine, theirs) in zip(chunks, join(kept, came, chunks, [parts[1] for parts in arrived[:1]])):
            sent.append(grads(offset, cw, mine, theirs, [outs[0] for outs in sent[-1:]] + [parts[1] for parts in arrived[1:-1]][-1:]))
            arrived.append(send_rows(sent[-1]))
        cuts += chunks

    placed = []
    for c, (offset, cw) in enumerate(cuts):
        placed = pl.pallas_call(
            functools.partial(place_kernel, groups=groups, offset=offset, cw=cw, width=width),
            grid_spec=pl.GridSpec(
                grid=(1,), in_specs=[anywhere] * (groups + len(placed)), out_specs=[anywhere] * 3,
                scratch_shapes=[pltpu.SemaphoreType.DMA((3 * groups,))],
            ),
            out_shape=[shape_of(part, width * groups, dtype=bf16)] * 3,
            input_output_aliases={groups + i: i for i in range(len(placed))},
            cost_estimate=cheap,
            compiler_params=pltpu.CompilerParams(vmem_limit_bytes=VMEM_LIMIT), name="place",
        )(*arrived[c], *placed)
    return tuple(placed)


def solution(mesh):
    return jax.shard_map(
        shards,
        mesh=mesh,
        in_specs=(P("seq", "head"), P("seq", "head"), P("seq", "head"), P("seq", "head"), P()),
        out_specs=(P(("seq", "head"), None), P(("seq", "head"), None), P(("seq", "head"), None)),
        check_vma=False,
    )
```

```python
import functools

import jax
import jax.numpy as jnp
from jax import lax
from jax.experimental import pallas as pl
from jax.experimental.pallas import tpu as pltpu
from jax.sharding import PartitionSpec as P

HEAD_DIM = 128
MOST = 1024
GROUP = 4
CHUNK = 4
LINK = jnp.bfloat16
VMEM_LIMIT = 16 * 1024 * 1024
GRAD_LIMIT = 48 * 1024 * 1024
FIRST_LIMIT = 52 * 1024 * 1024
NT = (((1,), (1,)), ((), ()))
TN = (((0,), (0,)), ((), ()))
NN = (((1,), (0,)), ((), ()))


def dot(a, b, dims):
    return lax.dot_general(a, b, dims, preferred_element_type=jnp.float32)


def doc_at(meta, ndocs, position):
    start, begin, end = jnp.int32(0), jnp.int32(0), jnp.int32(0)
    for i in range(ndocs):
        stop = start + meta[i]
        begin = jnp.where(start <= position, start, begin)
        end = jnp.where(start <= position, stop, end)
        start = stop
    return begin, end


def block_range(meta, ndocs, base, rows):
    begin0, end0 = doc_at(meta, ndocs, base)
    begin1, end1 = doc_at(meta, ndocs, base + rows - 1)
    first = jnp.where(begin0 < base, end0, base) - base
    return begin0, end0, begin1, end1, first, begin1 - base


def roles(place):
    core, turned = lax.rem(place, 2), lax.rem(lax.div(place, 4), 2)
    return core == turned, turned == 0


def state_kernel(lengths, q, k, v, g, *rest, ndocs, rows, offset, heads, group):
    kept, sent, held, sems = rest[-4:]
    gw = group * HEAD_DIM
    copies = []
    for c in range(heads // group):
        for i, ref in enumerate((q, k, v, g)):
            src = ref.at[:, pl.ds(offset + c * gw, gw)]
            copies.append(pltpu.make_async_copy(src, held.at[i, :, pl.ds(c * gw, gw)], sems.at[c, i]))
            copies[-1].start()
    place = lax.axis_index("seq")
    tails_here, _ = roles(place)
    _, _, _, _, first, last = block_range(lengths, ndocs, place * rows, rows)
    order = lax.broadcasted_iota(jnp.int32, (rows, HEAD_DIM), 0)
    first_rows, last_rows = order < first, order >= last
    zero = jnp.zeros((), held.dtype)

    def one(h):
        cols = slice(h * HEAD_DIM, (h + 1) * HEAD_DIM)
        tail = dot(jnp.where(last_rows, held[1, :, cols], zero), held[2, :, cols], TN)
        return tail, dot(jnp.where(first_rows, held[0, :, cols], zero), held[3, :, cols], TN)

    for h in range(heads):
        if h % group == 0:
            for copy in copies[4 * h // group:4 * h // group + 4]:
                copy.wait()
        tail, head = one(h)
        kept[h] = jnp.where(tails_here, tail, head)
        sent[h] = jnp.where(tails_here, head, tail)


def pair_kernel(lengths, kept, got, *rest, ndocs, rows, counts):
    total, *again = rest[-1 - len(counts):]
    place = lax.axis_index("seq")
    tails_here, _ = roles(place)
    even = (place - lax.rem(place, 2)) * rows
    odd = even + rows
    _, even_e0 = doc_at(lengths, ndocs, even)
    odd_b1, _ = doc_at(lengths, ndocs, odd + rows - 1)
    joins = jnp.where(jnp.where(tails_here, odd_b1 < odd, even_e0 > odd), 1.0, 0.0)
    inner = tails_here == (lax.rem(place, 2) == 0)
    own, far = jnp.where(inner, joins, 1.0), jnp.where(inner, 1.0, joins)
    total[...] = (own * kept[...] + far * got[...]).astype(LINK)
    for c, out in enumerate(again):
        out[...] = kept[sum(counts[:c]):sum(counts[:c + 1])]


def join_kernel(lengths, sent, *rest, ndocs, rows, counts, hops):
    came, others = rest[:hops], rest[hops:hops + len(counts)]
    mine, theirs = rest[-2 * len(counts):-len(counts)], rest[-len(counts):]
    place = lax.axis_index("seq")
    tails_here, straight = roles(place)
    even = (place - lax.rem(place, 2)) * rows
    odd = even + rows
    even_b0, _ = doc_at(lengths, ndocs, even)
    _, even_e1 = doc_at(lengths, ndocs, odd - 1)
    odd_b0, _ = doc_at(lengths, ndocs, odd)
    _, odd_e1 = doc_at(lengths, ndocs, odd + rows - 1)

    def one(if_tails, if_heads):
        return jnp.where(jnp.where(tails_here, if_tails, if_heads), 1.0, 0.0)

    weights = [
        one(odd + rows + hop * 2 * rows < odd_e1, even - hop * 2 * rows > even_b0) for hop in range(hops)
    ]
    from_near, from_pair = one(odd < even_e1, odd > odd_b0), one(odd + rows < even_e1, even > odd_b0)
    for c, count in enumerate(counts):
        at = slice(sum(counts[:c]), sum(counts[:c + 1]))
        total = weights[0] * came[0][at].astype(jnp.float32)
        for hop in range(1, hops):
            total = total + weights[hop] * came[hop][at].astype(jnp.float32)
        through = from_near * jnp.where(straight, others[c][...], sent[at]) + from_pair * total
        mine[c][...] = jnp.where(straight, through, total)
        theirs[c][...] = jnp.where(straight, total, through)


def split(a, axis):
    high = a.astype(jnp.bfloat16)
    return jnp.concatenate([high, (a - high.astype(jnp.float32)).astype(jnp.bfloat16)], axis=axis)


def grad_kernel(lengths, q, k, v, g, mine, got, *rest, ndocs, rows, heads, groups):
    outs, lower, upper, done = rest[-3 - groups:-3], rest[-3], rest[-2], rest[-1]
    place, column = lax.axis_index("seq"), lax.axis_index("head")
    base = place * rows

    @pl.when(pl.program_id(0) == 0)
    def _():
        line = lax.broadcasted_iota(jnp.int32, (rows, rows), 0)
        across = lax.broadcasted_iota(jnp.int32, (rows, rows), 1)
        begin_line = jnp.zeros((rows, rows), jnp.int32)
        begin_across = jnp.zeros((rows, rows), jnp.int32)
        start = jnp.int32(0) - base
        for i in range(ndocs):
            begin_line = jnp.where(line >= start, start, begin_line)
            begin_across = jnp.where(across >= start, start, begin_across)
            start = start + lengths[i]
        lower[...] = jnp.where((across <= line) & (across >= begin_line), 1, 0)
        upper[...] = jnp.where((line <= across) & (line >= begin_across), 1, 0)

    tails_here, _ = roles(place)
    _, _, _, _, first, last = block_range(lengths, ndocs, base, rows)
    order = lax.broadcasted_iota(jnp.int32, (rows, HEAD_DIM), 0)
    first_rows, last_rows = order < first, order >= last
    in_lower, in_upper = lower[...] == 1, upper[...] == 1
    for h in range(heads):
        cols = slice(h * HEAD_DIM, (h + 1) * HEAD_DIM)
        state = jnp.where(tails_here, got[h], mine[h])
        grad = jnp.where(tails_here, mine[h], got[h])
        qh, kh, vh, gh = (ref[:, cols] for ref in (q, k, v, g))
        k2, v2, g2 = (jnp.concatenate([a, a], axis=1) for a in (kh, vh, gh))
        weight_gv = jnp.where(in_lower, dot(gh, vh, NT), 0.0).astype(jnp.bfloat16)
        weight_vg = jnp.where(in_upper, dot(vh, gh, NT), 0.0).astype(jnp.bfloat16)
        weight_kq = jnp.where(in_upper, dot(kh, qh, NT), 0.0).astype(jnp.bfloat16)
        carry_q = jnp.where(first_rows, dot(g2, split(state, 1), NT), 0.0)
        carry_k = jnp.where(last_rows, dot(v2, split(grad, 1), NT), 0.0)
        carry_v = jnp.where(last_rows, dot(k2, split(grad, 0), NN), 0.0)
        done[0, :, cols] = (dot(weight_gv, kh, NN) + carry_q).astype(jnp.bfloat16)
        done[1, :, cols] = (dot(weight_vg, qh, NN) + carry_k).astype(jnp.bfloat16)
        done[2, :, cols] = (dot(weight_kq, gh, NN) + carry_v).astype(jnp.bfloat16)
    part = rows // groups
    for j in range(groups):
        at = pl.ds(pl.multiple_of(lax.rem(column + j, groups) * part, part), part)
        for i in range(3):
            outs[j][i] = done[i, at, :]


def place_kernel(*refs, groups, offset, cw, width):
    parts, outs, sems = refs[:groups], refs[-4:-1], refs[-1]
    column = lax.axis_index("head")
    copies = []
    for j in range(groups):
        start = pl.multiple_of(lax.rem(column + groups - j, groups) * width + offset, 128)
        for i in range(3):
            copies.append(pltpu.make_async_copy(parts[j].at[i], outs[i].at[:, pl.ds(start, cw)], sems.at[len(copies)]))
            copies[-1].start()
    for copy in copies:
        copy.wait()


def cuts_of(width):
    heads = width // HEAD_DIM
    size = CHUNK if heads % (2 * CHUNK) == 0 else 2
    cw, half = size * HEAD_DIM, max(heads // 2, size) * HEAD_DIM
    return [(at, half, [(o, cw) for o in range(at, at + half, cw)]) for at in range(0, width, half)]


def shards(queries, keys, values, out_grad, doc_lengths):
    rows, width = queries.shape
    ndocs = doc_lengths.shape[0]
    seq, groups = lax.axis_size("seq"), lax.axis_size("head")
    pairs = seq // 2
    hops = -(-MOST // (2 * rows))
    halves = cuts_of(width)
    step = 2 * HEAD_DIM
    part = rows // groups
    anywhere = pl.BlockSpec(memory_space=pl.ANY)
    in_vmem = pl.BlockSpec(memory_space=pltpu.VMEM)
    in_smem = pl.BlockSpec(memory_space=pltpu.SMEM)
    f32, bf16 = jnp.float32, jnp.bfloat16
    inputs = (queries, keys, values, out_grad)
    sizes = dict(ndocs=ndocs, rows=rows)
    cheap = pl.CostEstimate(flops=0, bytes_accessed=1024, transcendentals=0)

    def shape_of(*dims, dtype=f32):
        return jax.ShapeDtypeStruct(dims, dtype)

    def call(name, kernel, args, outs, scratch=(), after=()):
        return pl.pallas_call(
            kernel, in_specs=[in_smem] + [in_vmem] * len(args) + [anywhere] * len(after), out_specs=[in_vmem] * len(outs), out_shape=outs,
            scratch_shapes=list(scratch), cost_estimate=cheap,
            compiler_params=pltpu.CompilerParams(vmem_limit_bytes=VMEM_LIMIT), name=name,
        )(doc_lengths, *args, *after)

    def swap_cores(a):
        return lax.ppermute(a, "seq", [(b, b ^ 1) for b in range(seq)])

    def swap_pairs(sent):
        came = []
        for hop in range(1, hops + 1):
            perm = [(2 * m + m // 2 % 2, 2 * (m + hop) + 1 - (m + hop) // 2 % 2) for m in range(pairs - hop)]
            came.append(lax.ppermute(sent, "seq", perm + [(b, a) for a, b in perm]))
        return came

    def send_rows(outs):
        arrived = list(outs[:1])
        for j in range(1, groups):
            arrived.append(lax.ppermute(outs[j], "head", [(x, (x + j) % groups) for x in range(groups)]))
        return arrived

    square = (HEAD_DIM, HEAD_DIM)

    def states(offset, half, after):
        heads = half // HEAD_DIM
        group = GROUP if heads % GROUP == 0 else 2
        return pl.pallas_call(
            functools.partial(state_kernel, offset=offset, heads=heads, group=group, **sizes),
            in_specs=[in_smem] + [anywhere] * (4 + len(after)), out_specs=[in_vmem] * 2,
            out_shape=[shape_of(heads, *square)] * 2,
            scratch_shapes=[pltpu.VMEM((4, rows, half), bf16), pltpu.SemaphoreType.DMA((heads // group, 4))],
            cost_estimate=cheap, compiler_params=pltpu.CompilerParams(vmem_limit_bytes=FIRST_LIMIT), name="states",
        )(doc_lengths, *inputs, *after)

    def pair_up(kept, got, counts, after):
        outs = [shape_of(*kept.shape, dtype=LINK)] + [shape_of(n, *square) for n in counts]
        total, *again = call("pair", functools.partial(pair_kernel, counts=counts, **sizes), (kept, got), outs, after=after)
        return total, swap_pairs(total), [swap_cores(a) for a in again]

    def join(sent, others, came, counts, after):
        joined = call(
            "join", functools.partial(join_kernel, counts=counts, hops=hops, **sizes), (sent, *came, *others),
            [shape_of(n, *square) for n in counts] * 2, after=after,
        )
        return [(mine, swap_cores(theirs)) for mine, theirs in zip(joined[:len(counts)], joined[len(counts):])]

    def grads(offset, cw, mine, theirs, after):
        block = pl.BlockSpec((rows, step), lambda s, lengths: (0, offset // step + s))
        state_block = pl.BlockSpec((2,) + square, lambda s, lengths: (s, 0, 0))
        out_block = pl.BlockSpec((3, part, step), lambda s, lengths: (0, 0, s))
        return pl.pallas_call(
            functools.partial(grad_kernel, heads=2, groups=groups, **sizes),
            grid_spec=pltpu.PrefetchScalarGridSpec(
                num_scalar_prefetch=1, grid=(cw // step,),
                in_specs=[block] * 4 + [state_block] * 2 + [anywhere] * len(after), out_specs=[out_block] * groups,
                scratch_shapes=[pltpu.VMEM((rows, rows), jnp.int32)] * 2 + [pltpu.VMEM((3, rows, step), bf16)],
            ),
            out_shape=[shape_of(3, part, cw, dtype=bf16)] * groups, cost_estimate=cheap,
            compiler_params=pltpu.CompilerParams(vmem_limit_bytes=GRAD_LIMIT), name="grads",
        )(doc_lengths, *inputs, mine, theirs, *after)

    cuts, outs, arrived, paired = [], [], [], []
    for offset, half, chunks in halves:
        counts = [cw // HEAD_DIM for _, cw in chunks]
        kept, sent = states(offset, half, paired[-1:])
        total, came, others = pair_up(kept, swap_cores(sent), counts, [made[0] for made in outs[:1]])
        paired.append(total)
        joined = join(sent, others, came, counts, [parts[1] for parts in arrived[:1]])
        for (offset, cw), (mine, theirs) in zip(chunks, joined):
            after = [made[0] for made in outs[-1:]] + [parts[1] for parts in arrived[1:-1]][-1:]
            outs.append(grads(offset, cw, mine, theirs, after))
            arrived.append(send_rows(outs[-1]))
        cuts += chunks

    placed = []
    for c, (offset, cw) in enumerate(cuts):
        placed = pl.pallas_call(
            functools.partial(place_kernel, groups=groups, offset=offset, cw=cw, width=width),
            grid_spec=pl.GridSpec(
                grid=(1,), in_specs=[anywhere] * (groups + len(placed)), out_specs=[anywhere] * 3,
                scratch_shapes=[pltpu.SemaphoreType.DMA((3 * groups,))],
            ),
            out_shape=[shape_of(part, width * groups, dtype=bf16)] * 3,
            input_output_aliases={groups + i: i for i in range(len(placed))},
            cost_estimate=cheap,
            compiler_params=pltpu.CompilerParams(vmem_limit_bytes=VMEM_LIMIT), name="place",
        )(*arrived[c], *placed)
    return tuple(placed)


def solution(mesh):
    return jax.shard_map(
        shards,
        mesh=mesh,
        in_specs=(P("seq", "head"), P("seq", "head"), P("seq", "head"), P("seq", "head"), P()),
        out_specs=(P(("seq", "head"), None), P(("seq", "head"), None), P(("seq", "head"), None)),
        check_vma=False,
    )
```

```python
import functools

import jax
import jax.numpy as jnp
from jax import lax
from jax.experimental import pallas as pl
from jax.experimental.pallas import tpu as pltpu
from jax.sharding import PartitionSpec as P

HEAD_DIM = 128
MOST = 1024
GROUP = 4
CHUNK = 4
LINK = jnp.bfloat16
VMEM_LIMIT = 16 * 1024 * 1024
GRAD_LIMIT = 48 * 1024 * 1024
LOCAL_LIMIT = 52 * 1024 * 1024
FIRST_LIMIT = 52 * 1024 * 1024
NT = (((1,), (1,)), ((), ()))
TN = (((0,), (0,)), ((), ()))
NN = (((1,), (0,)), ((), ()))


def dot(a, b, dims):
    return lax.dot_general(a, b, dims, preferred_element_type=jnp.float32)


def doc_at(meta, ndocs, position):
    start, begin, end = jnp.int32(0), jnp.int32(0), jnp.int32(0)
    for i in range(ndocs):
        stop = start + meta[i]
        begin = jnp.where(start <= position, start, begin)
        end = jnp.where(start <= position, stop, end)
        start = stop
    return begin, end


def block_range(meta, ndocs, base, rows):
    begin0, end0 = doc_at(meta, ndocs, base)
    begin1, end1 = doc_at(meta, ndocs, base + rows - 1)
    first = jnp.where(begin0 < base, end0, base) - base
    return begin0, end0, begin1, end1, first, begin1 - base


def state_kernel(lengths, q, k, v, g, *rest, ndocs, rows, offset, heads, group):
    kept, sent, held, sems = rest[-4:]
    gw = group * HEAD_DIM
    copies = []
    for c in range(heads // group):
        for i, ref in enumerate((q, k, v, g)):
            src = ref.at[:, pl.ds(offset + c * gw, gw)]
            copies.append(pltpu.make_async_copy(src, held.at[i, :, pl.ds(c * gw, gw)], sems.at[c, i]))
            copies[-1].start()
    place = lax.axis_index("seq")
    first_core = lax.rem(place, 2) == 0
    _, _, _, _, first, last = block_range(lengths, ndocs, place * rows, rows)
    order = lax.broadcasted_iota(jnp.int32, (rows, HEAD_DIM), 0)
    first_rows, last_rows = order < first, order >= last
    zero = jnp.zeros((), held.dtype)

    def one(h):
        cols = slice(h * HEAD_DIM, (h + 1) * HEAD_DIM)
        tail = dot(jnp.where(last_rows, held[1, :, cols], zero), held[2, :, cols], TN)
        return tail, dot(jnp.where(first_rows, held[0, :, cols], zero), held[3, :, cols], TN)

    for h in range(heads):
        if h % group == 0:
            for copy in copies[4 * h // group:4 * h // group + 4]:
                copy.wait()
        tail, head = one(h)
        kept[h] = jnp.where(first_core, tail, head)
        sent[h] = jnp.where(first_core, head, tail)


def pair_kernel(lengths, kept, got, *rest, ndocs, rows):
    sent = rest[-1]
    place = lax.axis_index("seq")
    first_core = lax.rem(place, 2) == 0
    even = (place - lax.rem(place, 2)) * rows
    odd = even + rows
    _, even_e0 = doc_at(lengths, ndocs, even)
    odd_b1, _ = doc_at(lengths, ndocs, odd + rows - 1)
    joins = jnp.where(jnp.where(first_core, odd_b1 < odd, even_e0 > odd), 1.0, 0.0)
    sent[...] = (got[...] + joins * kept[...]).astype(LINK)


def join_kernel(lengths, other, *rest, ndocs, rows, counts, hops):
    came, mine, theirs = rest[:hops], rest[-2 * len(counts):-len(counts)], rest[-len(counts):]
    place = lax.axis_index("seq")
    first_core = lax.rem(place, 2) == 0
    even = (place - lax.rem(place, 2)) * rows
    odd = even + rows
    even_b0, _ = doc_at(lengths, ndocs, even)
    _, even_e1 = doc_at(lengths, ndocs, odd - 1)
    odd_b0, _ = doc_at(lengths, ndocs, odd)
    _, odd_e1 = doc_at(lengths, ndocs, odd + rows - 1)

    def one(if_first, if_second):
        return jnp.where(jnp.where(first_core, if_first, if_second), 1.0, 0.0)

    weights = [
        one(odd + rows + hop * 2 * rows < odd_e1, even - hop * 2 * rows > even_b0) for hop in range(hops)
    ]
    from_other, from_pair = one(odd < even_e1, odd > odd_b0), one(odd + rows < even_e1, even > odd_b0)
    for c, count in enumerate(counts):
        at = slice(sum(counts[:c]), sum(counts[:c + 1]))
        total = weights[0] * came[0][at].astype(jnp.float32)
        for hop in range(1, hops):
            total = total + weights[hop] * came[hop][at].astype(jnp.float32)
        theirs[c][...] = total
        mine[c][...] = from_other * other[at] + from_pair * total


def split(a, axis):
    high = a.astype(jnp.bfloat16)
    return jnp.concatenate([high, (a - high.astype(jnp.float32)).astype(jnp.bfloat16)], axis=axis)


def masks(lengths, lower, upper, ndocs, rows):
    line = lax.broadcasted_iota(jnp.int32, (rows, rows), 0)
    across = lax.broadcasted_iota(jnp.int32, (rows, rows), 1)
    begin_line = jnp.zeros((rows, rows), jnp.int32)
    begin_across = jnp.zeros((rows, rows), jnp.int32)
    start = jnp.int32(0) - lax.axis_index("seq") * rows
    for i in range(ndocs):
        begin_line = jnp.where(line >= start, start, begin_line)
        begin_across = jnp.where(across >= start, start, begin_across)
        start = start + lengths[i]
    lower[...] = jnp.where((across <= line) & (across >= begin_line), 1, 0)
    upper[...] = jnp.where((line <= across) & (line >= begin_across), 1, 0)


def local_kernel(lengths, q, k, v, g, *rest, ndocs, rows, heads):
    near, kvg, token, lower, upper = rest[-5:]
    token[...] = jnp.zeros_like(token)
    for i, ref in enumerate((k, v, g)):
        kvg[i] = ref[...]

    @pl.when(pl.program_id(0) == 0)
    def _():
        masks(lengths, lower, upper, ndocs, rows)

    for h in range(heads):
        cols = slice(h * HEAD_DIM, (h + 1) * HEAD_DIM)
        qh, kh, vh, gh = (ref[:, cols] for ref in (q, k, v, g))
        weight_gv = jnp.where(lower[...] == 1, dot(gh, vh, NT), 0.0).astype(jnp.bfloat16)
        weight_vg = jnp.where(upper[...] == 1, dot(vh, gh, NT), 0.0).astype(jnp.bfloat16)
        weight_kq = jnp.where(upper[...] == 1, dot(kh, qh, NT), 0.0).astype(jnp.bfloat16)
        near[0, :, cols] = dot(weight_gv, kh, NN)
        near[1, :, cols] = dot(weight_vg, qh, NN)
        near[2, :, cols] = dot(weight_kq, gh, NN)


def carry_kernel(lengths, near, kvg, mine, got, *rest, ndocs, rows, heads, groups):
    outs, done = rest[-1 - groups:-1], rest[-1]
    place, column = lax.axis_index("seq"), lax.axis_index("head")
    first_core = lax.rem(place, 2) == 0
    _, _, _, _, first, last = block_range(lengths, ndocs, place * rows, rows)
    order = lax.broadcasted_iota(jnp.int32, (rows, HEAD_DIM), 0)
    first_rows, last_rows = order < first, order >= last
    for h in range(heads):
        cols = slice(h * HEAD_DIM, (h + 1) * HEAD_DIM)
        state = jnp.where(first_core, got[h], mine[h])
        grad = jnp.where(first_core, mine[h], got[h])
        k2, v2, g2 = (jnp.concatenate([kvg[i, :, cols]] * 2, axis=1) for i in range(3))
        carry_q = jnp.where(first_rows, dot(g2, split(state, 1), NT), 0.0)
        carry_k = jnp.where(last_rows, dot(v2, split(grad, 1), NT), 0.0)
        carry_v = jnp.where(last_rows, dot(k2, split(grad, 0), NN), 0.0)
        for i, carry in enumerate((carry_q, carry_k, carry_v)):
            done[i, :, cols] = (near[i, :, cols] + carry).astype(jnp.bfloat16)
    part = rows // groups
    for j in range(groups):
        at = pl.ds(pl.multiple_of(lax.rem(column + j, groups) * part, part), part)
        for i in range(3):
            outs[j][i] = done[i, at, :]


def grad_kernel(lengths, q, k, v, g, mine, got, *rest, ndocs, rows, heads, groups):
    outs, lower, upper, done = rest[-3 - groups:-3], rest[-3], rest[-2], rest[-1]
    place, column = lax.axis_index("seq"), lax.axis_index("head")
    base = place * rows

    @pl.when(pl.program_id(0) == 0)
    def _():
        masks(lengths, lower, upper, ndocs, rows)

    first_core = lax.rem(place, 2) == 0
    _, _, _, _, first, last = block_range(lengths, ndocs, base, rows)
    order = lax.broadcasted_iota(jnp.int32, (rows, HEAD_DIM), 0)
    first_rows, last_rows = order < first, order >= last
    in_lower, in_upper = lower[...] == 1, upper[...] == 1
    for h in range(heads):
        cols = slice(h * HEAD_DIM, (h + 1) * HEAD_DIM)
        state = jnp.where(first_core, got[h], mine[h])
        grad = jnp.where(first_core, mine[h], got[h])
        qh, kh, vh, gh = (ref[:, cols] for ref in (q, k, v, g))
        k2, v2, g2 = (jnp.concatenate([a, a], axis=1) for a in (kh, vh, gh))
        weight_gv = jnp.where(in_lower, dot(gh, vh, NT), 0.0).astype(jnp.bfloat16)
        weight_vg = jnp.where(in_upper, dot(vh, gh, NT), 0.0).astype(jnp.bfloat16)
        weight_kq = jnp.where(in_upper, dot(kh, qh, NT), 0.0).astype(jnp.bfloat16)
        carry_q = jnp.where(first_rows, dot(g2, split(state, 1), NT), 0.0)
        carry_k = jnp.where(last_rows, dot(v2, split(grad, 1), NT), 0.0)
        carry_v = jnp.where(last_rows, dot(k2, split(grad, 0), NN), 0.0)
        done[0, :, cols] = (dot(weight_gv, kh, NN) + carry_q).astype(jnp.bfloat16)
        done[1, :, cols] = (dot(weight_vg, qh, NN) + carry_k).astype(jnp.bfloat16)
        done[2, :, cols] = (dot(weight_kq, gh, NN) + carry_v).astype(jnp.bfloat16)
    part = rows // groups
    for j in range(groups):
        at = pl.ds(pl.multiple_of(lax.rem(column + j, groups) * part, part), part)
        for i in range(3):
            outs[j][i] = done[i, at, :]


def place_kernel(*refs, groups, offset, cw, width):
    parts, outs, sems = refs[:groups], refs[-4:-1], refs[-1]
    column = lax.axis_index("head")
    copies = []
    for j in range(groups):
        start = pl.multiple_of(lax.rem(column + groups - j, groups) * width + offset, 128)
        for i in range(3):
            copies.append(pltpu.make_async_copy(parts[j].at[i], outs[i].at[:, pl.ds(start, cw)], sems.at[len(copies)]))
            copies[-1].start()
    for copy in copies:
        copy.wait()


def cuts_of(width):
    heads = width // HEAD_DIM
    size = CHUNK if heads % (2 * CHUNK) == 0 else 2
    cw, half = size * HEAD_DIM, max(heads // 2, size) * HEAD_DIM
    return [(at, half, [(o, cw) for o in range(at, at + half, cw)]) for at in range(0, width, half)]


def shards(queries, keys, values, out_grad, doc_lengths):
    rows, width = queries.shape
    ndocs = doc_lengths.shape[0]
    seq, groups = lax.axis_size("seq"), lax.axis_size("head")
    pairs = seq // 2
    hops = -(-MOST // (2 * rows))
    halves = cuts_of(width)
    step = 2 * HEAD_DIM
    part = rows // groups
    anywhere = pl.BlockSpec(memory_space=pl.ANY)
    in_vmem = pl.BlockSpec(memory_space=pltpu.VMEM)
    in_smem = pl.BlockSpec(memory_space=pltpu.SMEM)
    f32, bf16 = jnp.float32, jnp.bfloat16
    inputs = (queries, keys, values, out_grad)
    sizes = dict(ndocs=ndocs, rows=rows)
    cheap = pl.CostEstimate(flops=0, bytes_accessed=1024, transcendentals=0)

    def shape_of(*dims, dtype=f32):
        return jax.ShapeDtypeStruct(dims, dtype)

    def call(name, kernel, args, outs, scratch=(), after=()):
        return pl.pallas_call(
            kernel, in_specs=[in_smem] + [in_vmem] * len(args) + [anywhere] * len(after), out_specs=[in_vmem] * len(outs), out_shape=outs,
            scratch_shapes=list(scratch), cost_estimate=cheap,
            compiler_params=pltpu.CompilerParams(vmem_limit_bytes=VMEM_LIMIT), name=name,
        )(doc_lengths, *args, *after)

    def swap_cores(a):
        return lax.ppermute(a, "seq", [(b, b ^ 1) for b in range(seq)])

    def swap_pairs(sent):
        came = []
        for hop in range(1, hops + 1):
            perm = [(2 * m, 2 * (m + hop) + 1) for m in range(pairs - hop)]
            came.append(lax.ppermute(sent, "seq", perm + [(b, a) for a, b in perm]))
        return came

    def send_rows(outs):
        arrived = list(outs[:1])
        for j in range(1, groups):
            arrived.append(lax.ppermute(outs[j], "head", [(x, (x + j) % groups) for x in range(groups)]))
        return arrived

    square = (HEAD_DIM, HEAD_DIM)

    def states(offset, half, after):
        heads = half // HEAD_DIM
        group = GROUP if heads % GROUP == 0 else 2
        return pl.pallas_call(
            functools.partial(state_kernel, offset=offset, heads=heads, group=group, **sizes),
            in_specs=[in_smem] + [anywhere] * (4 + len(after)), out_specs=[in_vmem] * 2,
            out_shape=[shape_of(heads, *square)] * 2,
            scratch_shapes=[pltpu.VMEM((4, rows, half), bf16), pltpu.SemaphoreType.DMA((heads // group, 4))],
            cost_estimate=cheap, compiler_params=pltpu.CompilerParams(vmem_limit_bytes=FIRST_LIMIT), name="states",
        )(doc_lengths, *inputs, *after)

    def pair_up(kept, got, after):
        out = shape_of(*kept.shape, dtype=LINK)
        total = call("pair", functools.partial(pair_kernel, **sizes), (kept, got), [out], after=after)[0]
        return total, swap_pairs(total)

    def join(kept, came, chunks, after):
        counts = [cw // HEAD_DIM for _, cw in chunks]
        joined = call(
            "join", functools.partial(join_kernel, counts=counts, hops=hops, **sizes), (swap_cores(kept), *came),
            [shape_of(n, *square) for n in counts] * 2, after=after,
        )
        return [(mine, swap_cores(theirs)) for mine, theirs in zip(joined[:len(chunks)], joined[len(chunks):])]

    def grads(offset, cw, mine, theirs, after):
        block = pl.BlockSpec((rows, step), lambda s, lengths: (0, offset // step + s))
        state_block = pl.BlockSpec((2,) + square, lambda s, lengths: (s, 0, 0))
        out_block = pl.BlockSpec((3, part, step), lambda s, lengths: (0, 0, s))
        return pl.pallas_call(
            functools.partial(grad_kernel, heads=2, groups=groups, **sizes),
            grid_spec=pltpu.PrefetchScalarGridSpec(
                num_scalar_prefetch=1, grid=(cw // step,),
                in_specs=[block] * 4 + [state_block] * 2 + [anywhere] * len(after), out_specs=[out_block] * groups,
                scratch_shapes=[pltpu.VMEM((rows, rows), jnp.int32)] * 2 + [pltpu.VMEM((3, rows, step), bf16)],
            ),
            out_shape=[shape_of(3, part, cw, dtype=bf16)] * groups, cost_estimate=cheap,
            compiler_params=pltpu.CompilerParams(vmem_limit_bytes=GRAD_LIMIT), name="grads",
        )(doc_lengths, *inputs, mine, theirs, *after)

    def local(offset, cw, after):
        block = pl.BlockSpec((rows, step), lambda s, lengths: (0, offset // step + s))
        out_block = pl.BlockSpec((3, rows, step), lambda s, lengths: (0, 0, s))
        return pl.pallas_call(
            functools.partial(local_kernel, heads=2, **sizes),
            grid_spec=pltpu.PrefetchScalarGridSpec(
                num_scalar_prefetch=1, grid=(cw // step,), in_specs=[block] * 4 + [anywhere] * len(after),
                out_specs=[out_block] * 2 + [pl.BlockSpec((8, 128), lambda s, lengths: (0, 0))],
                scratch_shapes=[pltpu.VMEM((rows, rows), jnp.int32)] * 2,
            ),
            out_shape=[shape_of(3, rows, cw), shape_of(3, rows, cw, dtype=bf16), shape_of(8, 128)], cost_estimate=cheap,
            compiler_params=pltpu.CompilerParams(vmem_limit_bytes=LOCAL_LIMIT), name="local",
        )(doc_lengths, *inputs, *after)

    def carry(near, kvg, mine, theirs, cw, after):
        kernel = functools.partial(carry_kernel, heads=cw // HEAD_DIM, groups=groups, **sizes)
        return call(
            "carry", kernel, (near, kvg, mine, theirs), [shape_of(3, part, cw, dtype=bf16)] * groups,
            [pltpu.VMEM((3, rows, cw), bf16)], after,
        )

    cuts, near, outs, arrived, total = [], [], [], [], None
    for start, half, chunks in halves:
        early = total is None
        kept, sent = states(start, half, [] if early else [total])
        if early:
            near.append(local(*chunks[0], [kept]))
        total, came = pair_up(kept, swap_cores(sent), near[0][2:] if early else [outs[0][0]])
        if early:
            for chunk in chunks[1:]:
                near.append(local(*chunk, [total]))
        joined = join(kept, came, chunks, [made[2] for made in near[1:]] if early else [arrived[0][1]])
        for c, ((offset, cw), (mine, theirs)) in enumerate(zip(chunks, joined)):
            after = [made[0] for made in outs[-1:]] + [parts[1] for parts in arrived[1:-1]][-1:]
            if early:
                outs.append(carry(*near[c][:2], mine, theirs, cw, after))
            else:
                outs.append(grads(offset, cw, mine, theirs, after))
            arrived.append(send_rows(outs[-1]))
        cuts += chunks

    placed = []
    for c, (offset, cw) in enumerate(cuts):
        placed = pl.pallas_call(
            functools.partial(place_kernel, groups=groups, offset=offset, cw=cw, width=width),
            grid_spec=pl.GridSpec(
                grid=(1,), in_specs=[anywhere] * (groups + len(placed)), out_specs=[anywhere] * 3,
                scratch_shapes=[pltpu.SemaphoreType.DMA((3 * groups,))],
            ),
            out_shape=[shape_of(part, width * groups, dtype=bf16)] * 3,
            input_output_aliases={groups + i: i for i in range(len(placed))},
            cost_estimate=cheap,
            compiler_params=pltpu.CompilerParams(vmem_limit_bytes=VMEM_LIMIT), name="place",
        )(*arrived[c], *placed)
    return tuple(placed)


def solution(mesh):
    return jax.shard_map(
        shards,
        mesh=mesh,
        in_specs=(P("seq", "head"), P("seq", "head"), P("seq", "head"), P("seq", "head"), P()),
        out_specs=(P(("seq", "head"), None), P(("seq", "head"), None), P(("seq", "head"), None)),
        check_vma=False,
    )
```

```python
import functools

import jax
import jax.numpy as jnp
from jax import lax
from jax.experimental import pallas as pl
from jax.experimental.pallas import tpu as pltpu
from jax.sharding import PartitionSpec as P

HEAD_DIM = 128
MOST = 1024
GROUP = 4
CHUNK = 4
LINK = jnp.bfloat16
VMEM_LIMIT = 16 * 1024 * 1024
GRAD_LIMIT = 40 * 1024 * 1024
FIRST_LIMIT = 52 * 1024 * 1024
NT = (((1,), (1,)), ((), ()))
TN = (((0,), (0,)), ((), ()))
NN = (((1,), (0,)), ((), ()))


def dot(a, b, dims):
    return lax.dot_general(a, b, dims, preferred_element_type=jnp.float32)


def doc_at(meta, ndocs, position):
    start, begin, end = jnp.int32(0), jnp.int32(0), jnp.int32(0)
    for i in range(ndocs):
        stop = start + meta[i]
        begin = jnp.where(start <= position, start, begin)
        end = jnp.where(start <= position, stop, end)
        start = stop
    return begin, end


def block_range(meta, ndocs, base, rows):
    begin0, end0 = doc_at(meta, ndocs, base)
    begin1, end1 = doc_at(meta, ndocs, base + rows - 1)
    first = jnp.where(begin0 < base, end0, base) - base
    return begin0, end0, begin1, end1, first, begin1 - base


def state_kernel(lengths, q, k, v, g, *rest, ndocs, rows, offset, heads, group):
    kept, sent, held, sems = rest[-4:]
    gw = group * HEAD_DIM
    copies = []
    for c in range(heads // group):
        for i, ref in enumerate((q, k, v, g)):
            src = ref.at[:, pl.ds(offset + c * gw, gw)]
            copies.append(pltpu.make_async_copy(src, held.at[i, :, pl.ds(c * gw, gw)], sems.at[c, i]))
            copies[-1].start()
    place = lax.axis_index("seq")
    first_core = lax.rem(place, 2) == 0
    _, _, _, _, first, last = block_range(lengths, ndocs, place * rows, rows)
    order = lax.broadcasted_iota(jnp.int32, (rows, HEAD_DIM), 0)
    first_rows, last_rows = order < first, order >= last
    zero = jnp.zeros((), held.dtype)

    def one(h):
        cols = slice(h * HEAD_DIM, (h + 1) * HEAD_DIM)
        tail = dot(jnp.where(last_rows, held[1, :, cols], zero), held[2, :, cols], TN)
        return tail, dot(jnp.where(first_rows, held[0, :, cols], zero), held[3, :, cols], TN)

    for h in range(heads):
        if h % group == 0:
            for copy in copies[4 * h // group:4 * h // group + 4]:
                copy.wait()
        tail, head = one(h)
        kept[h] = jnp.where(first_core, tail, head)
        sent[h] = jnp.where(first_core, head, tail)


def pair_kernel(lengths, kept, got, *rest, ndocs, rows):
    sent = rest[-1]
    place = lax.axis_index("seq")
    first_core = lax.rem(place, 2) == 0
    even = (place - lax.rem(place, 2)) * rows
    odd = even + rows
    _, even_e0 = doc_at(lengths, ndocs, even)
    odd_b1, _ = doc_at(lengths, ndocs, odd + rows - 1)
    joins = jnp.where(jnp.where(first_core, odd_b1 < odd, even_e0 > odd), 1.0, 0.0)
    sent[...] = (got[...] + joins * kept[...]).astype(LINK)


def join_kernel(lengths, other, *rest, ndocs, rows, counts, hops):
    came, mine, theirs = rest[:hops], rest[-2 * len(counts):-len(counts)], rest[-len(counts):]
    place = lax.axis_index("seq")
    first_core = lax.rem(place, 2) == 0
    even = (place - lax.rem(place, 2)) * rows
    odd = even + rows
    even_b0, _ = doc_at(lengths, ndocs, even)
    _, even_e1 = doc_at(lengths, ndocs, odd - 1)
    odd_b0, _ = doc_at(lengths, ndocs, odd)
    _, odd_e1 = doc_at(lengths, ndocs, odd + rows - 1)

    def one(if_first, if_second):
        return jnp.where(jnp.where(first_core, if_first, if_second), 1.0, 0.0)

    weights = [
        one(odd + rows + hop * 2 * rows < odd_e1, even - hop * 2 * rows > even_b0) for hop in range(hops)
    ]
    from_other, from_pair = one(odd < even_e1, odd > odd_b0), one(odd + rows < even_e1, even > odd_b0)
    for c, count in enumerate(counts):
        at = slice(sum(counts[:c]), sum(counts[:c + 1]))
        total = weights[0] * came[0][at].astype(jnp.float32)
        for hop in range(1, hops):
            total = total + weights[hop] * came[hop][at].astype(jnp.float32)
        theirs[c][...] = total
        mine[c][...] = from_other * other[at] + from_pair * total


def split(a, axis):
    high = a.astype(jnp.bfloat16)
    return jnp.concatenate([high, (a - high.astype(jnp.float32)).astype(jnp.bfloat16)], axis=axis)


def mask_kernel(lengths, *rest, ndocs, rows):
    lower, upper = rest[-2:]
    line = lax.broadcasted_iota(jnp.int32, (rows, rows), 0)
    across = lax.broadcasted_iota(jnp.int32, (rows, rows), 1)
    begin_line = jnp.zeros((rows, rows), jnp.int32)
    begin_across = jnp.zeros((rows, rows), jnp.int32)
    start = jnp.int32(0) - lax.axis_index("seq") * rows
    for i in range(ndocs):
        begin_line = jnp.where(line >= start, start, begin_line)
        begin_across = jnp.where(across >= start, start, begin_across)
        start = start + lengths[i]
    lower[...] = jnp.where((across <= line) & (across >= begin_line), 1.0, 0.0)
    upper[...] = jnp.where((line <= across) & (line >= begin_across), 1.0, 0.0)


def grad_kernel(lengths, q, k, v, g, lower, upper, mine, got, *rest, ndocs, rows, offset, heads, groups):
    outs, done = rest[-1 - groups:-1], rest[-1]
    place, column = lax.axis_index("seq"), lax.axis_index("head")
    first_core = lax.rem(place, 2) == 0
    _, _, _, _, first, last = block_range(lengths, ndocs, place * rows, rows)
    order = lax.broadcasted_iota(jnp.int32, (rows, HEAD_DIM), 0)
    first_rows, last_rows = order < first, order >= last
    for h in range(heads):
        cols = slice(h * HEAD_DIM, (h + 1) * HEAD_DIM)
        state = jnp.where(first_core, got[h], mine[h])
        grad = jnp.where(first_core, mine[h], got[h])
        qh, kh, vh, gh = (ref[:, offset + h * HEAD_DIM:offset + (h + 1) * HEAD_DIM] for ref in (q, k, v, g))
        k2, v2, g2 = (jnp.concatenate([a, a], axis=1) for a in (kh, vh, gh))
        weight_gv = (dot(gh, vh, NT) * lower[...]).astype(jnp.bfloat16)
        weight_vg = (dot(vh, gh, NT) * upper[...]).astype(jnp.bfloat16)
        weight_kq = (dot(kh, qh, NT) * upper[...]).astype(jnp.bfloat16)
        carry_q = jnp.where(first_rows, dot(g2, split(state, 1), NT), 0.0)
        carry_k = jnp.where(last_rows, dot(v2, split(grad, 1), NT), 0.0)
        carry_v = jnp.where(last_rows, dot(k2, split(grad, 0), NN), 0.0)
        done[0, :, cols] = (dot(weight_gv, kh, NN) + carry_q).astype(jnp.bfloat16)
        done[1, :, cols] = (dot(weight_vg, qh, NN) + carry_k).astype(jnp.bfloat16)
        done[2, :, cols] = (dot(weight_kq, gh, NN) + carry_v).astype(jnp.bfloat16)
    part = rows // groups
    for j in range(groups):
        at = pl.ds(pl.multiple_of(lax.rem(column + j, groups) * part, part), part)
        for i in range(3):
            outs[j][i] = done[i, at, :]


def place_kernel(*refs, groups, offset, cw, width):
    parts, outs, sems = refs[:groups], refs[-4:-1], refs[-1]
    column = lax.axis_index("head")
    copies = []
    for j in range(groups):
        start = pl.multiple_of(lax.rem(column + groups - j, groups) * width + offset, 128)
        for i in range(3):
            copies.append(pltpu.make_async_copy(parts[j].at[i], outs[i].at[:, pl.ds(start, cw)], sems.at[len(copies)]))
            copies[-1].start()
    for copy in copies:
        copy.wait()


def cuts_of(width):
    heads = width // HEAD_DIM
    size = CHUNK if heads % (2 * CHUNK) == 0 else 2
    cw, half = size * HEAD_DIM, max(heads // 2, size) * HEAD_DIM
    return [(at, half, [(o, cw) for o in range(at, at + half, cw)]) for at in range(0, width, half)]


def shards(queries, keys, values, out_grad, doc_lengths):
    rows, width = queries.shape
    ndocs = doc_lengths.shape[0]
    seq, groups = lax.axis_size("seq"), lax.axis_size("head")
    pairs = seq // 2
    hops = -(-MOST // (2 * rows))
    halves = cuts_of(width)
    part = rows // groups
    anywhere = pl.BlockSpec(memory_space=pl.ANY)
    in_vmem = pl.BlockSpec(memory_space=pltpu.VMEM)
    in_smem = pl.BlockSpec(memory_space=pltpu.SMEM)
    f32, bf16 = jnp.float32, jnp.bfloat16
    inputs = (queries, keys, values, out_grad)
    sizes = dict(ndocs=ndocs, rows=rows)
    cheap = pl.CostEstimate(flops=0, bytes_accessed=1024, transcendentals=0)

    def shape_of(*dims, dtype=f32):
        return jax.ShapeDtypeStruct(dims, dtype)

    def call(name, kernel, args, outs, scratch=(), after=(), limit=VMEM_LIMIT):
        return pl.pallas_call(
            kernel, in_specs=[in_smem] + [in_vmem] * len(args) + [anywhere] * len(after), out_specs=[in_vmem] * len(outs), out_shape=outs,
            scratch_shapes=list(scratch), cost_estimate=cheap,
            compiler_params=pltpu.CompilerParams(vmem_limit_bytes=limit), name=name,
        )(doc_lengths, *args, *after)

    def swap_cores(a):
        return lax.ppermute(a, "seq", [(b, b ^ 1) for b in range(seq)])

    def swap_pairs(sent):
        came = []
        for hop in range(1, hops + 1):
            perm = [(2 * m, 2 * (m + hop) + 1) for m in range(pairs - hop)]
            came.append(lax.ppermute(sent, "seq", perm + [(b, a) for a, b in perm]))
        return came

    def send_rows(outs):
        arrived = list(outs[:1])
        for j in range(1, groups):
            arrived.append(lax.ppermute(outs[j], "head", [(x, (x + j) % groups) for x in range(groups)]))
        return arrived

    square = (HEAD_DIM, HEAD_DIM)

    def states(offset, half, after):
        heads = half // HEAD_DIM
        group = GROUP if heads % GROUP == 0 else 2
        kept, sent = pl.pallas_call(
            functools.partial(state_kernel, offset=offset, heads=heads, group=group, **sizes),
            in_specs=[in_smem] + [anywhere] * (4 + len(after)), out_specs=[in_vmem] * 2,
            out_shape=[shape_of(heads, *square)] * 2,
            scratch_shapes=[pltpu.VMEM((4, rows, half), bf16), pltpu.SemaphoreType.DMA((heads // group, 4))],
            cost_estimate=cheap, compiler_params=pltpu.CompilerParams(vmem_limit_bytes=FIRST_LIMIT), name="states",
        )(doc_lengths, *inputs, *after)
        return kept, sent

    def pair_up(kept, got, after):
        out = shape_of(*kept.shape, dtype=LINK)
        total = call("pair", functools.partial(pair_kernel, **sizes), (kept, got), [out], after=after)[0]
        return total, swap_pairs(total)

    def join(kept, came, chunks, after):
        counts = [cw // HEAD_DIM for _, cw in chunks]
        joined = call(
            "join", functools.partial(join_kernel, counts=counts, hops=hops, **sizes), (swap_cores(kept), *came),
            [shape_of(n, *square) for n in counts] * 2, after=after,
        )
        return [(mine, swap_cores(theirs)) for mine, theirs in zip(joined[:len(chunks)], joined[len(chunks):])]

    def grads(masks, offset, cw, mine, theirs, after):
        return call(
            "grads", functools.partial(grad_kernel, offset=offset, heads=cw // HEAD_DIM, groups=groups, **sizes),
            (*inputs, *masks, mine, theirs), [shape_of(3, part, cw, dtype=bf16)] * groups,
            [pltpu.VMEM((3, rows, cw), bf16)], after, GRAD_LIMIT,
        )

    cuts, outs, arrived, totals, masks = [], [], [], [], None
    for start, half, chunks in halves:
        kept, sent = states(start, half, totals)
        total, came = pair_up(kept, swap_cores(sent), [made[0] for made in outs[-1:]])
        totals = [total]
        masks = masks or call("masks", functools.partial(mask_kernel, **sizes), (), [shape_of(rows, rows)] * 2, after=totals)
        joined = join(kept, came, chunks, [parts[1] for parts in arrived[:1]] or masks[:1])
        for (offset, cw), (mine, theirs) in zip(chunks, joined):
            after = [made[0] for made in outs[-1:]] + [parts[1] for parts in arrived[1:-1]][-1:]
            outs.append(grads(masks, offset, cw, mine, theirs, after))
            arrived.append(send_rows(outs[-1]))
        cuts += chunks

    placed = []
    for c, (offset, cw) in enumerate(cuts):
        placed = pl.pallas_call(
            functools.partial(place_kernel, groups=groups, offset=offset, cw=cw, width=width),
            grid_spec=pl.GridSpec(
                grid=(1,), in_specs=[anywhere] * (groups + len(placed)), out_specs=[anywhere] * 3,
                scratch_shapes=[pltpu.SemaphoreType.DMA((3 * groups,))],
            ),
            out_shape=[shape_of(part, width * groups, dtype=bf16)] * 3,
            input_output_aliases={groups + i: i for i in range(len(placed))},
            cost_estimate=cheap,
            compiler_params=pltpu.CompilerParams(vmem_limit_bytes=VMEM_LIMIT), name="place",
        )(*arrived[c], *placed)
    return tuple(placed)


def solution(mesh):
    return jax.shard_map(
        shards,
        mesh=mesh,
        in_specs=(P("seq", "head"), P("seq", "head"), P("seq", "head"), P("seq", "head"), P()),
        out_specs=(P(("seq", "head"), None), P(("seq", "head"), None), P(("seq", "head"), None)),
        check_vma=False,
    )
```

```python
import functools

import jax
import jax.numpy as jnp
from jax import lax
from jax.experimental import pallas as pl
from jax.experimental.pallas import tpu as pltpu
from jax.sharding import PartitionSpec as P

HEAD_DIM = 128
MOST = 1024
GROUP = 2
CHUNK = 4
LINK = jnp.bfloat16
VMEM_LIMIT = 16 * 1024 * 1024
GRAD_LIMIT = 40 * 1024 * 1024
FIRST_LIMIT = 52 * 1024 * 1024
NT = (((1,), (1,)), ((), ()))
TN = (((0,), (0,)), ((), ()))
NN = (((1,), (0,)), ((), ()))


def dot(a, b, dims):
    return lax.dot_general(a, b, dims, preferred_element_type=jnp.float32)


def doc_at(meta, ndocs, position):
    start, begin, end = jnp.int32(0), jnp.int32(0), jnp.int32(0)
    for i in range(ndocs):
        stop = start + meta[i]
        begin = jnp.where(start <= position, start, begin)
        end = jnp.where(start <= position, stop, end)
        start = stop
    return begin, end


def block_range(meta, ndocs, base, rows):
    begin0, end0 = doc_at(meta, ndocs, base)
    begin1, end1 = doc_at(meta, ndocs, base + rows - 1)
    first = jnp.where(begin0 < base, end0, base) - base
    return begin0, end0, begin1, end1, first, begin1 - base


def state_kernel(lengths, q, k, v, g, *rest, ndocs, rows, offset, heads, group):
    kept, sent, handed, held, sems = rest[-5:]
    gw = group * HEAD_DIM
    copies = []
    for c in range(heads // group):
        for i, ref in enumerate((q, k, v, g)):
            src = ref.at[:, pl.ds(offset + c * gw, gw)]
            copies.append(pltpu.make_async_copy(src, held.at[i, :, pl.ds(c * gw, gw)], sems.at[c, i]))
            copies[-1].start()
    for i in range(ndocs):
        handed[i] = lengths[i]
    place = lax.axis_index("seq")
    first_core = lax.rem(place, 2) == 0
    _, _, _, _, first, last = block_range(lengths, ndocs, place * rows, rows)
    order = lax.broadcasted_iota(jnp.int32, (rows, HEAD_DIM), 0)
    first_rows, last_rows = order < first, order >= last
    zero = jnp.zeros((), held.dtype)

    def one(h):
        cols = slice(h * HEAD_DIM, (h + 1) * HEAD_DIM)
        tail = dot(jnp.where(last_rows, held[1, :, cols], zero), held[2, :, cols], TN)
        return tail, dot(jnp.where(first_rows, held[0, :, cols], zero), held[3, :, cols], TN)

    for h in range(heads):
        if h % group == 0:
            for copy in copies[4 * h // group:4 * h // group + 4]:
                copy.wait()
        tail, head = one(h)
        kept[h] = jnp.where(first_core, tail, head)
        sent[h] = jnp.where(first_core, head, tail)


def pair_kernel(lengths, kept, got, *rest, ndocs, rows):
    sent = rest[-1]
    place = lax.axis_index("seq")
    first_core = lax.rem(place, 2) == 0
    even = (place - lax.rem(place, 2)) * rows
    odd = even + rows
    _, even_e0 = doc_at(lengths, ndocs, even)
    odd_b1, _ = doc_at(lengths, ndocs, odd + rows - 1)
    joins = jnp.where(jnp.where(first_core, odd_b1 < odd, even_e0 > odd), 1.0, 0.0)
    sent[...] = (got[...] + joins * kept[...]).astype(LINK)


def join_kernel(lengths, other, *rest, ndocs, rows, counts, hops):
    came, mine, theirs = rest[:hops], rest[-2 * len(counts):-len(counts)], rest[-len(counts):]
    place = lax.axis_index("seq")
    first_core = lax.rem(place, 2) == 0
    even = (place - lax.rem(place, 2)) * rows
    odd = even + rows
    even_b0, _ = doc_at(lengths, ndocs, even)
    _, even_e1 = doc_at(lengths, ndocs, odd - 1)
    odd_b0, _ = doc_at(lengths, ndocs, odd)
    _, odd_e1 = doc_at(lengths, ndocs, odd + rows - 1)

    def one(if_first, if_second):
        return jnp.where(jnp.where(first_core, if_first, if_second), 1.0, 0.0)

    weights = [
        one(odd + rows + hop * 2 * rows < odd_e1, even - hop * 2 * rows > even_b0) for hop in range(hops)
    ]
    from_other, from_pair = one(odd < even_e1, odd > odd_b0), one(odd + rows < even_e1, even > odd_b0)
    for c, count in enumerate(counts):
        at = slice(sum(counts[:c]), sum(counts[:c + 1]))
        total = weights[0] * came[0][at].astype(jnp.float32)
        for hop in range(1, hops):
            total = total + weights[hop] * came[hop][at].astype(jnp.float32)
        theirs[c][...] = total
        mine[c][...] = from_other * other[at] + from_pair * total


def split(a, axis):
    high = a.astype(jnp.bfloat16)
    return jnp.concatenate([high, (a - high.astype(jnp.float32)).astype(jnp.bfloat16)], axis=axis)


def mask_kernel(lengths, *rest, ndocs, rows):
    lower, upper = rest[-2:]
    line = lax.broadcasted_iota(jnp.int32, (rows, rows), 0)
    across = lax.broadcasted_iota(jnp.int32, (rows, rows), 1)
    begin_line = jnp.zeros((rows, rows), jnp.int32)
    begin_across = jnp.zeros((rows, rows), jnp.int32)
    start = jnp.int32(0) - lax.axis_index("seq") * rows
    for i in range(ndocs):
        begin_line = jnp.where(line >= start, start, begin_line)
        begin_across = jnp.where(across >= start, start, begin_across)
        start = start + lengths[i]
    lower[...] = jnp.where((across <= line) & (across >= begin_line), 1.0, 0.0)
    upper[...] = jnp.where((line <= across) & (line >= begin_across), 1.0, 0.0)


def grad_kernel(lengths, q, k, v, g, lower, upper, mine, got, *rest, ndocs, rows, offset, heads, groups):
    outs, done = rest[-1 - groups:-1], rest[-1]
    place, column = lax.axis_index("seq"), lax.axis_index("head")
    first_core = lax.rem(place, 2) == 0
    _, _, _, _, first, last = block_range(lengths, ndocs, place * rows, rows)
    order = lax.broadcasted_iota(jnp.int32, (rows, HEAD_DIM), 0)
    first_rows, last_rows = order < first, order >= last
    for h in range(heads):
        cols = slice(h * HEAD_DIM, (h + 1) * HEAD_DIM)
        state = jnp.where(first_core, got[h], mine[h])
        grad = jnp.where(first_core, mine[h], got[h])
        qh, kh, vh, gh = (ref[:, offset + h * HEAD_DIM:offset + (h + 1) * HEAD_DIM] for ref in (q, k, v, g))
        k2, v2, g2 = (jnp.concatenate([a, a], axis=1) for a in (kh, vh, gh))
        weight_gv = (dot(gh, vh, NT) * lower[...]).astype(jnp.bfloat16)
        weight_vg = (dot(vh, gh, NT) * upper[...]).astype(jnp.bfloat16)
        weight_kq = (dot(kh, qh, NT) * upper[...]).astype(jnp.bfloat16)
        carry_q = jnp.where(first_rows, dot(g2, split(state, 1), NT), 0.0)
        carry_k = jnp.where(last_rows, dot(v2, split(grad, 1), NT), 0.0)
        carry_v = jnp.where(last_rows, dot(k2, split(grad, 0), NN), 0.0)
        done[0, :, cols] = (dot(weight_gv, kh, NN) + carry_q).astype(jnp.bfloat16)
        done[1, :, cols] = (dot(weight_vg, qh, NN) + carry_k).astype(jnp.bfloat16)
        done[2, :, cols] = (dot(weight_kq, gh, NN) + carry_v).astype(jnp.bfloat16)
    part = rows // groups
    for j in range(groups):
        at = pl.ds(pl.multiple_of(lax.rem(column + j, groups) * part, part), part)
        for i in range(3):
            outs[j][i] = done[i, at, :]


def place_kernel(*refs, groups, offset, cw, width):
    parts, outs, sems = refs[:groups], refs[-4:-1], refs[-1]
    column = lax.axis_index("head")
    copies = []
    for j in range(groups):
        start = pl.multiple_of(lax.rem(column + groups - j, groups) * width + offset, 128)
        for i in range(3):
            copies.append(pltpu.make_async_copy(parts[j].at[i], outs[i].at[:, pl.ds(start, cw)], sems.at[len(copies)]))
            copies[-1].start()
    for copy in copies:
        copy.wait()


def cuts_of(width):
    heads = width // HEAD_DIM
    size = CHUNK if heads % (2 * CHUNK) == 0 else 2
    cw, half = size * HEAD_DIM, max(heads // 2, size) * HEAD_DIM
    return [(at, half, [(o, cw) for o in range(at, at + half, cw)]) for at in range(0, width, half)]


def shards(queries, keys, values, out_grad, doc_lengths):
    rows, width = queries.shape
    ndocs = doc_lengths.shape[0]
    seq, groups = lax.axis_size("seq"), lax.axis_size("head")
    pairs = seq // 2
    hops = -(-MOST // (2 * rows))
    halves = cuts_of(width)
    part = rows // groups
    anywhere = pl.BlockSpec(memory_space=pl.ANY)
    in_vmem = pl.BlockSpec(memory_space=pltpu.VMEM)
    in_smem = pl.BlockSpec(memory_space=pltpu.SMEM)
    f32, bf16 = jnp.float32, jnp.bfloat16
    inputs = (queries, keys, values, out_grad)
    sizes = dict(ndocs=ndocs, rows=rows)
    cheap = pl.CostEstimate(flops=0, bytes_accessed=1024, transcendentals=0)

    def shape_of(*dims, dtype=f32):
        return jax.ShapeDtypeStruct(dims, dtype)

    def call(name, kernel, args, outs, scratch=(), after=(), limit=VMEM_LIMIT):
        lengths, *args = args
        return pl.pallas_call(
            kernel, in_specs=[in_smem] + [in_vmem] * len(args) + [anywhere] * len(after), out_specs=[in_vmem] * len(outs), out_shape=outs,
            scratch_shapes=list(scratch), cost_estimate=cheap,
            compiler_params=pltpu.CompilerParams(vmem_limit_bytes=limit), name=name,
        )(lengths, *args, *after)

    def swap_cores(a):
        return lax.ppermute(a, "seq", [(b, b ^ 1) for b in range(seq)])

    def swap_pairs(sent):
        came = []
        for hop in range(hops, 0, -1):
            perm = [(2 * m, 2 * (m + hop) + 1) for m in range(pairs - hop)]
            came.insert(0, lax.ppermute(sent, "seq", perm + [(b, a) for a, b in perm]))
        return came

    def send_rows(outs):
        arrived = list(outs[:1])
        for j in range(1, groups):
            arrived.append(lax.ppermute(outs[j], "head", [(x, (x + j) % groups) for x in range(groups)]))
        return arrived

    square = (HEAD_DIM, HEAD_DIM)

    def states(lengths, offset, half, after):
        heads = half // HEAD_DIM
        group = GROUP if heads % GROUP == 0 else 2
        return pl.pallas_call(
            functools.partial(state_kernel, offset=offset, heads=heads, group=group, **sizes),
            in_specs=[in_smem] + [anywhere] * (4 + len(after)), out_specs=[in_vmem] * 2 + [in_smem],
            out_shape=[shape_of(heads, *square)] * 2 + [shape_of(ndocs, dtype=jnp.int32)],
            scratch_shapes=[pltpu.VMEM((4, rows, half), bf16), pltpu.SemaphoreType.DMA((heads // group, 4))],
            cost_estimate=cheap, compiler_params=pltpu.CompilerParams(vmem_limit_bytes=FIRST_LIMIT), name="states",
        )(lengths, *inputs, *after)

    def pair_up(lengths, kept, got, after):
        out = shape_of(*kept.shape, dtype=LINK)
        total = call("pair", functools.partial(pair_kernel, **sizes), (lengths, kept, got), [out], after=after)[0]
        return total, swap_pairs(total)

    def join(lengths, kept, came, chunks, after):
        counts = [cw // HEAD_DIM for _, cw in chunks]
        joined = call(
            "join", functools.partial(join_kernel, counts=counts, hops=hops, **sizes), (lengths, swap_cores(kept), *came),
            [shape_of(n, *square) for n in counts] * 2, after=after,
        )
        return [(mine, swap_cores(theirs)) for mine, theirs in zip(joined[:len(chunks)], joined[len(chunks):])]

    def grads(lengths, masks, offset, cw, mine, theirs, after):
        return call(
            "grads", functools.partial(grad_kernel, offset=offset, heads=cw // HEAD_DIM, groups=groups, **sizes),
            (lengths, *inputs, *masks, mine, theirs), [shape_of(3, part, cw, dtype=bf16)] * groups,
            [pltpu.VMEM((3, rows, cw), bf16)], after, GRAD_LIMIT,
        )

    cuts, outs, arrived, totals, masks, lengths = [], [], [], [], None, doc_lengths
    for start, half, chunks in halves:
        kept, sent, lengths = states(lengths, start, half, totals)
        total, came = pair_up(lengths, kept, swap_cores(sent), [made[0] for made in outs[:1]])
        totals = [total]
        masks = masks or call("masks", functools.partial(mask_kernel, **sizes), (lengths,), [shape_of(rows, rows)] * 2, after=totals)
        joined = join(lengths, kept, came, chunks, [parts[1] for parts in arrived[:1]] or masks[:1])
        for (offset, cw), (mine, theirs) in zip(chunks, joined):
            after = [made[0] for made in outs[-1:]] + [parts[1] for parts in arrived[1:-1]][-1:]
            outs.append(grads(lengths, masks, offset, cw, mine, theirs, after))
            arrived.append(send_rows(outs[-1]))
        cuts += chunks

    placed = []
    for c, (offset, cw) in enumerate(cuts):
        placed = pl.pallas_call(
            functools.partial(place_kernel, groups=groups, offset=offset, cw=cw, width=width),
            grid_spec=pl.GridSpec(
                grid=(1,), in_specs=[anywhere] * (groups + len(placed)), out_specs=[anywhere] * 3,
                scratch_shapes=[pltpu.SemaphoreType.DMA((3 * groups,))],
            ),
            out_shape=[shape_of(part, width * groups, dtype=bf16)] * 3,
            input_output_aliases={groups + i: i for i in range(len(placed))},
            cost_estimate=cheap,
            compiler_params=pltpu.CompilerParams(vmem_limit_bytes=VMEM_LIMIT), name="place",
        )(*arrived[c], *placed)
    return tuple(placed)


def solution(mesh):
    return jax.shard_map(
        shards,
        mesh=mesh,
        in_specs=(P("seq", "head"), P("seq", "head"), P("seq", "head"), P("seq", "head"), P()),
        out_specs=(P(("seq", "head"), None), P(("seq", "head"), None), P(("seq", "head"), None)),
        check_vma=False,
    )
```

```python
import functools

import jax
import jax.numpy as jnp
from jax import lax
from jax.experimental import pallas as pl
from jax.experimental.pallas import tpu as pltpu
from jax.sharding import PartitionSpec as P

HEAD_DIM = 128
MOST = 1024
GROUP = 4
CHUNK = 4
PAD = 16
LINK = jnp.bfloat16
VMEM_LIMIT = 16 * 1024 * 1024
GRAD_LIMIT = 40 * 1024 * 1024
FIRST_LIMIT = 52 * 1024 * 1024
NT = (((1,), (1,)), ((), ()))
TN = (((0,), (0,)), ((), ()))
NN = (((1,), (0,)), ((), ()))


def dot(a, b, dims):
    return lax.dot_general(a, b, dims, preferred_element_type=jnp.float32)


def doc_at(meta, ndocs, position):
    start, begin, end = jnp.int32(0), jnp.int32(0), jnp.int32(0)
    for i in range(ndocs):
        stop = start + meta[i]
        begin = jnp.where(start <= position, start, begin)
        end = jnp.where(start <= position, stop, end)
        start = stop
    return begin, end


def block_range(meta, ndocs, base, rows):
    begin0, end0 = doc_at(meta, ndocs, base)
    begin1, end1 = doc_at(meta, ndocs, base + rows - 1)
    first = jnp.where(begin0 < base, end0, base) - base
    return begin0, end0, begin1, end1, first, begin1 - base


def state_kernel(lengths, q, k, v, g, *rest, ndocs, rows, offset, heads, group):
    kept, sent, held, sems = rest[-4:]
    gw = group * HEAD_DIM
    copies = []
    for c in range(heads // group):
        for i, ref in enumerate((q, k, v, g)):
            src = ref.at[:, pl.ds(offset + c * gw, gw)]
            copies.append(pltpu.make_async_copy(src, held.at[i, :, pl.ds(c * gw, gw)], sems.at[c, i]))
            copies[-1].start()
    place = lax.axis_index("seq")
    first_core = lax.rem(place, 2) == 0
    _, _, _, _, first, last = block_range(lengths, ndocs, place * rows, rows)
    order = lax.broadcasted_iota(jnp.int32, (rows, HEAD_DIM), 0)
    first_rows, last_rows = order < first, order >= last
    zero = jnp.zeros((), held.dtype)

    def one(h):
        cols = slice(h * HEAD_DIM, (h + 1) * HEAD_DIM)
        tail = dot(jnp.where(last_rows, held[1, :, cols], zero), held[2, :, cols], TN)
        return tail, dot(jnp.where(first_rows, held[0, :, cols], zero), held[3, :, cols], TN)

    for h in range(heads):
        if h % group == 0:
            for copy in copies[4 * h // group:4 * h // group + 4]:
                copy.wait()
        tail, head = one(h)
        kept[h] = jnp.where(first_core, tail, head)
        sent[h] = jnp.where(first_core, head, tail)


def pair_kernel(lengths, kept, got, *rest, ndocs, rows, hops):
    sent = rest[-hops:]
    place = lax.axis_index("seq")
    first_core = lax.rem(place, 2) == 0
    even = (place - lax.rem(place, 2)) * rows
    odd = even + rows
    _, even_e0 = doc_at(lengths, ndocs, even)
    odd_b1, _ = doc_at(lengths, ndocs, odd + rows - 1)
    joins = jnp.where(jnp.where(first_core, odd_b1 < odd, even_e0 > odd), 1.0, 0.0)
    size = kept.shape[0] * HEAD_DIM
    total = (got[...] + joins * kept[...]).astype(LINK).reshape(size, HEAD_DIM)
    for out in sent:
        out[:size] = total
        if out.shape[0] > size:
            out[size:] = jnp.zeros((out.shape[0] - size, HEAD_DIM), LINK)


def join_kernel(lengths, other, *rest, ndocs, rows, counts, hops):
    came, mine, theirs = rest[:hops], rest[-2 * len(counts):-len(counts)], rest[-len(counts):]
    place = lax.axis_index("seq")
    first_core = lax.rem(place, 2) == 0
    even = (place - lax.rem(place, 2)) * rows
    odd = even + rows
    even_b0, _ = doc_at(lengths, ndocs, even)
    _, even_e1 = doc_at(lengths, ndocs, odd - 1)
    odd_b0, _ = doc_at(lengths, ndocs, odd)
    _, odd_e1 = doc_at(lengths, ndocs, odd + rows - 1)

    def one(if_first, if_second):
        return jnp.where(jnp.where(first_core, if_first, if_second), 1.0, 0.0)

    weights = [
        one(odd + rows + hop * 2 * rows < odd_e1, even - hop * 2 * rows > even_b0) for hop in range(hops)
    ]
    from_other, from_pair = one(odd < even_e1, odd > odd_b0), one(odd + rows < even_e1, even > odd_b0)
    for c, count in enumerate(counts):
        at = slice(sum(counts[:c]), sum(counts[:c + 1]))
        lines = slice(at.start * HEAD_DIM, at.stop * HEAD_DIM)
        total = weights[0] * came[0][lines].astype(jnp.float32)
        for hop in range(1, hops):
            total = total + weights[hop] * came[hop][lines].astype(jnp.float32)
        total = total.reshape(count, HEAD_DIM, HEAD_DIM)
        theirs[c][...] = total
        mine[c][...] = from_other * other[at] + from_pair * total


def split(a, axis):
    high = a.astype(jnp.bfloat16)
    return jnp.concatenate([high, (a - high.astype(jnp.float32)).astype(jnp.bfloat16)], axis=axis)


def mask_kernel(lengths, *rest, ndocs, rows):
    lower, upper = rest[-2:]
    line = lax.broadcasted_iota(jnp.int32, (rows, rows), 0)
    across = lax.broadcasted_iota(jnp.int32, (rows, rows), 1)
    begin_line = jnp.zeros((rows, rows), jnp.int32)
    begin_across = jnp.zeros((rows, rows), jnp.int32)
    start = jnp.int32(0) - lax.axis_index("seq") * rows
    for i in range(ndocs):
        begin_line = jnp.where(line >= start, start, begin_line)
        begin_across = jnp.where(across >= start, start, begin_across)
        start = start + lengths[i]
    lower[...] = jnp.where((across <= line) & (across >= begin_line), 1.0, 0.0)
    upper[...] = jnp.where((line <= across) & (line >= begin_across), 1.0, 0.0)


def grad_kernel(lengths, q, k, v, g, lower, upper, mine, got, *rest, ndocs, rows, offset, heads, groups):
    outs, done = rest[-1 - groups:-1], rest[-1]
    place, column = lax.axis_index("seq"), lax.axis_index("head")
    first_core = lax.rem(place, 2) == 0
    _, _, _, _, first, last = block_range(lengths, ndocs, place * rows, rows)
    order = lax.broadcasted_iota(jnp.int32, (rows, HEAD_DIM), 0)
    first_rows, last_rows = order < first, order >= last
    for h in range(heads):
        cols = slice(h * HEAD_DIM, (h + 1) * HEAD_DIM)
        state = jnp.where(first_core, got[h], mine[h])
        grad = jnp.where(first_core, mine[h], got[h])
        qh, kh, vh, gh = (ref[:, offset + h * HEAD_DIM:offset + (h + 1) * HEAD_DIM] for ref in (q, k, v, g))
        k2, v2, g2 = (jnp.concatenate([a, a], axis=1) for a in (kh, vh, gh))
        weight_gv = (dot(gh, vh, NT) * lower[...]).astype(jnp.bfloat16)
        weight_vg = (dot(vh, gh, NT) * upper[...]).astype(jnp.bfloat16)
        weight_kq = (dot(kh, qh, NT) * upper[...]).astype(jnp.bfloat16)
        carry_q = jnp.where(first_rows, dot(g2, split(state, 1), NT), 0.0)
        carry_k = jnp.where(last_rows, dot(v2, split(grad, 1), NT), 0.0)
        carry_v = jnp.where(last_rows, dot(k2, split(grad, 0), NN), 0.0)
        done[0, :, cols] = (dot(weight_gv, kh, NN) + carry_q).astype(jnp.bfloat16)
        done[1, :, cols] = (dot(weight_vg, qh, NN) + carry_k).astype(jnp.bfloat16)
        done[2, :, cols] = (dot(weight_kq, gh, NN) + carry_v).astype(jnp.bfloat16)
    part = rows // groups
    for j in range(groups):
        at = pl.ds(pl.multiple_of(lax.rem(column + j, groups) * part, part), part)
        for i in range(3):
            outs[j][i] = done[i, at, :]


def place_kernel(*refs, groups, offset, cw, width):
    parts, outs, sems = refs[:groups], refs[-4:-1], refs[-1]
    column = lax.axis_index("head")
    copies = []
    for j in range(groups):
        start = pl.multiple_of(lax.rem(column + groups - j, groups) * width + offset, 128)
        for i in range(3):
            copies.append(pltpu.make_async_copy(parts[j].at[i], outs[i].at[:, pl.ds(start, cw)], sems.at[len(copies)]))
            copies[-1].start()
    for copy in copies:
        copy.wait()


def cuts_of(width):
    heads = width // HEAD_DIM
    size = CHUNK if heads % (2 * CHUNK) == 0 else 2
    cw, half = size * HEAD_DIM, max(heads // 2, size) * HEAD_DIM
    return [(at, half, [(o, cw) for o in range(at, at + half, cw)]) for at in range(0, width, half)]


def shards(queries, keys, values, out_grad, doc_lengths):
    rows, width = queries.shape
    ndocs = doc_lengths.shape[0]
    seq, groups = lax.axis_size("seq"), lax.axis_size("head")
    pairs = seq // 2
    hops = -(-MOST // (2 * rows))
    halves = cuts_of(width)
    part = rows // groups
    anywhere = pl.BlockSpec(memory_space=pl.ANY)
    in_vmem = pl.BlockSpec(memory_space=pltpu.VMEM)
    in_smem = pl.BlockSpec(memory_space=pltpu.SMEM)
    f32, bf16 = jnp.float32, jnp.bfloat16
    inputs = (queries, keys, values, out_grad)
    sizes = dict(ndocs=ndocs, rows=rows)
    cheap = pl.CostEstimate(flops=0, bytes_accessed=1024, transcendentals=0)

    def shape_of(*dims, dtype=f32):
        return jax.ShapeDtypeStruct(dims, dtype)

    def call(name, kernel, args, outs, scratch=(), after=(), limit=VMEM_LIMIT):
        return pl.pallas_call(
            kernel, in_specs=[in_smem] + [in_vmem] * len(args) + [anywhere] * len(after), out_specs=[in_vmem] * len(outs), out_shape=outs,
            scratch_shapes=list(scratch), cost_estimate=cheap,
            compiler_params=pltpu.CompilerParams(vmem_limit_bytes=limit), name=name,
        )(doc_lengths, *args, *after)

    def swap_cores(a):
        return lax.ppermute(a, "seq", [(b, b ^ 1) for b in range(seq)])

    def swap_pairs(sent):
        came = []
        for hop in range(1, hops + 1):
            perm = [(2 * m, 2 * (m + hop) + 1) for m in range(pairs - hop)]
            came.append(lax.ppermute(sent[hop - 1], "seq", perm + [(b, a) for a, b in perm]))
        return came

    def send_rows(outs):
        arrived = list(outs[:1])
        for j in range(1, groups):
            arrived.append(lax.ppermute(outs[j], "head", [(x, (x + j) % groups) for x in range(groups)]))
        return arrived

    square = (HEAD_DIM, HEAD_DIM)

    def states(offset, half, after):
        heads = half // HEAD_DIM
        group = GROUP if heads % GROUP == 0 else 2
        kept, sent = pl.pallas_call(
            functools.partial(state_kernel, offset=offset, heads=heads, group=group, **sizes),
            in_specs=[in_smem] + [anywhere] * (4 + len(after)), out_specs=[in_vmem] * 2,
            out_shape=[shape_of(heads, *square)] * 2,
            scratch_shapes=[pltpu.VMEM((4, rows, half), bf16), pltpu.SemaphoreType.DMA((heads // group, 4))],
            cost_estimate=cheap, compiler_params=pltpu.CompilerParams(vmem_limit_bytes=FIRST_LIMIT), name="states",
        )(doc_lengths, *inputs, *after)
        return kept, sent

    def pair_up(kept, got, after):
        lines = kept.shape[0] * HEAD_DIM
        outs = [shape_of(lines + PAD * (hops - hop), HEAD_DIM, dtype=LINK) for hop in range(1, hops + 1)]
        totals = call("pair", functools.partial(pair_kernel, hops=hops, **sizes), (kept, got), outs, after=after)
        return totals[-1], swap_pairs(totals)

    def join(kept, came, chunks, after):
        counts = [cw // HEAD_DIM for _, cw in chunks]
        joined = call(
            "join", functools.partial(join_kernel, counts=counts, hops=hops, **sizes), (swap_cores(kept), *came),
            [shape_of(n, *square) for n in counts] * 2, after=after,
        )
        return [(mine, swap_cores(theirs)) for mine, theirs in zip(joined[:len(chunks)], joined[len(chunks):])]

    def grads(masks, offset, cw, mine, theirs, after):
        return call(
            "grads", functools.partial(grad_kernel, offset=offset, heads=cw // HEAD_DIM, groups=groups, **sizes),
            (*inputs, *masks, mine, theirs), [shape_of(3, part, cw, dtype=bf16)] * groups,
            [pltpu.VMEM((3, rows, cw), bf16)], after, GRAD_LIMIT,
        )

    cuts, outs, arrived, totals, masks = [], [], [], [], None
    for start, half, chunks in halves:
        kept, sent = states(start, half, totals)
        total, came = pair_up(kept, swap_cores(sent), [made[0] for made in outs[:1]])
        totals = [total]
        masks = masks or call("masks", functools.partial(mask_kernel, **sizes), (), [shape_of(rows, rows)] * 2, after=totals)
        joined = join(kept, came, chunks, [parts[1] for parts in arrived[:1]] or masks[:1])
        for (offset, cw), (mine, theirs) in zip(chunks, joined):
            after = [made[0] for made in outs[-1:]] + [parts[1] for parts in arrived[1:-1]][-1:]
            outs.append(grads(masks, offset, cw, mine, theirs, after))
            arrived.append(send_rows(outs[-1]))
        cuts += chunks

    placed = []
    for c, (offset, cw) in enumerate(cuts):
        placed = pl.pallas_call(
            functools.partial(place_kernel, groups=groups, offset=offset, cw=cw, width=width),
            grid_spec=pl.GridSpec(
                grid=(1,), in_specs=[anywhere] * (groups + len(placed)), out_specs=[anywhere] * 3,
                scratch_shapes=[pltpu.SemaphoreType.DMA((3 * groups,))],
            ),
            out_shape=[shape_of(part, width * groups, dtype=bf16)] * 3,
            input_output_aliases={groups + i: i for i in range(len(placed))},
            cost_estimate=cheap,
            compiler_params=pltpu.CompilerParams(vmem_limit_bytes=VMEM_LIMIT), name="place",
        )(*arrived[c], *placed)
    return tuple(placed)


def solution(mesh):
    return jax.shard_map(
        shards,
        mesh=mesh,
        in_specs=(P("seq", "head"), P("seq", "head"), P("seq", "head"), P("seq", "head"), P()),
        out_specs=(P(("seq", "head"), None), P(("seq", "head"), None), P(("seq", "head"), None)),
        check_vma=False,
    )
```

```python
import functools

import jax
import jax.numpy as jnp
from jax import lax
from jax.experimental import pallas as pl
from jax.experimental.pallas import tpu as pltpu
from jax.sharding import PartitionSpec as P

HEAD_DIM = 128
MOST = 1024
GROUP = 4
CHUNK = 4
PAD = 16
LINK = jnp.bfloat16
VMEM_LIMIT = 16 * 1024 * 1024
GRAD_LIMIT = 40 * 1024 * 1024
FIRST_LIMIT = 53 * 1024 * 1024
SECOND_LIMIT = 52 * 1024 * 1024
NT = (((1,), (1,)), ((), ()))
TN = (((0,), (0,)), ((), ()))
NN = (((1,), (0,)), ((), ()))


def dot(a, b, dims):
    return lax.dot_general(a, b, dims, preferred_element_type=jnp.float32)


def doc_at(meta, ndocs, position):
    start, begin, end = jnp.int32(0), jnp.int32(0), jnp.int32(0)
    for i in range(ndocs):
        stop = start + meta[i]
        begin = jnp.where(start <= position, start, begin)
        end = jnp.where(start <= position, stop, end)
        start = stop
    return begin, end


def block_range(meta, ndocs, base, rows):
    begin0, end0 = doc_at(meta, ndocs, base)
    begin1, end1 = doc_at(meta, ndocs, base + rows - 1)
    first = jnp.where(begin0 < base, end0, base) - base
    return begin0, end0, begin1, end1, first, begin1 - base


def state_kernel(lengths, q, k, v, g, *rest, ndocs, rows, offset, heads, group, kinds):
    outs, held, sems, known, got = rest[-4 - len(kinds):-4], rest[-4], rest[-3], rest[-2], rest[-1]
    gw = group * HEAD_DIM
    place = lax.axis_index("seq")
    first_core = lax.rem(place, 2) == 0

    def copy(n, c, i, ref):
        src = ref.at[:, pl.ds(offset + c * gw, gw)]
        return pltpu.make_async_copy(src, held.at[n, i, :, pl.ds(c * gw, gw)], sems.at[n, c, i])

    fetch = pltpu.make_async_copy(lengths, known, got)
    fetch.start()
    for n, kind in enumerate(kinds):
        tails = first_core if kind == "kept" else jnp.logical_not(first_core)
        for c in range(heads // group):

            @pl.when(tails)
            def _():
                copy(n, c, 0, k).start()
                copy(n, c, 1, v).start()

            @pl.when(jnp.logical_not(tails))
            def _():
                copy(n, c, 0, q).start()
                copy(n, c, 1, g).start()

    fetch.wait()
    _, _, _, _, first, last = block_range(known, ndocs, place * rows, rows)
    order = lax.broadcasted_iota(jnp.int32, (rows, HEAD_DIM), 0)
    zero = jnp.zeros((), held.dtype)
    for n, (kind, out) in enumerate(zip(kinds, outs)):
        tails = first_core if kind == "kept" else jnp.logical_not(first_core)
        low, high = jnp.where(tails, last, 0), jnp.where(tails, rows, first)
        here = (order >= low) & (order < high)
        for h in range(heads):
            if h % group == 0:
                copy(n, h // group, 0, k).wait()
                copy(n, h // group, 1, v).wait()
            cols = slice(h * HEAD_DIM, (h + 1) * HEAD_DIM)
            out[h] = dot(jnp.where(here, held[n, 0, :, cols], zero), held[n, 1, :, cols], TN)


def pair_kernel(lengths, kept, got, *rest, ndocs, rows, hops):
    sent = rest[-hops:]
    place = lax.axis_index("seq")
    first_core = lax.rem(place, 2) == 0
    even = (place - lax.rem(place, 2)) * rows
    odd = even + rows
    _, even_e0 = doc_at(lengths, ndocs, even)
    odd_b1, _ = doc_at(lengths, ndocs, odd + rows - 1)
    joins = jnp.where(jnp.where(first_core, odd_b1 < odd, even_e0 > odd), 1.0, 0.0)
    size = kept.shape[0] * HEAD_DIM
    total = (got[...] + joins * kept[...]).astype(LINK).reshape(size, HEAD_DIM)
    for out in sent:
        out[:size] = total
        if out.shape[0] > size:
            out[size:] = jnp.zeros((out.shape[0] - size, HEAD_DIM), LINK)


def join_kernel(lengths, other, *rest, ndocs, rows, counts, hops):
    came, mine, theirs = rest[:hops], rest[-2 * len(counts):-len(counts)], rest[-len(counts):]
    place = lax.axis_index("seq")
    first_core = lax.rem(place, 2) == 0
    even = (place - lax.rem(place, 2)) * rows
    odd = even + rows
    even_b0, _ = doc_at(lengths, ndocs, even)
    _, even_e1 = doc_at(lengths, ndocs, odd - 1)
    odd_b0, _ = doc_at(lengths, ndocs, odd)
    _, odd_e1 = doc_at(lengths, ndocs, odd + rows - 1)

    def one(if_first, if_second):
        return jnp.where(jnp.where(first_core, if_first, if_second), 1.0, 0.0)

    weights = [
        one(odd + rows + hop * 2 * rows < odd_e1, even - hop * 2 * rows > even_b0) for hop in range(hops)
    ]
    from_other, from_pair = one(odd < even_e1, odd > odd_b0), one(odd + rows < even_e1, even > odd_b0)
    for c, count in enumerate(counts):
        at = slice(sum(counts[:c]), sum(counts[:c + 1]))
        lines = slice(at.start * HEAD_DIM, at.stop * HEAD_DIM)
        total = weights[0] * came[0][lines].astype(jnp.float32)
        for hop in range(1, hops):
            total = total + weights[hop] * came[hop][lines].astype(jnp.float32)
        total = total.reshape(count, HEAD_DIM, HEAD_DIM)
        theirs[c][...] = total
        mine[c][...] = from_other * other[at] + from_pair * total


def split(a, axis):
    high = a.astype(jnp.bfloat16)
    return jnp.concatenate([high, (a - high.astype(jnp.float32)).astype(jnp.bfloat16)], axis=axis)


def mask_kernel(lengths, *rest, ndocs, rows):
    lower, upper = rest[-2:]
    line = lax.broadcasted_iota(jnp.int32, (rows, rows), 0)
    across = lax.broadcasted_iota(jnp.int32, (rows, rows), 1)
    begin_line = jnp.zeros((rows, rows), jnp.int32)
    begin_across = jnp.zeros((rows, rows), jnp.int32)
    start = jnp.int32(0) - lax.axis_index("seq") * rows
    for i in range(ndocs):
        begin_line = jnp.where(line >= start, start, begin_line)
        begin_across = jnp.where(across >= start, start, begin_across)
        start = start + lengths[i]
    lower[...] = jnp.where((across <= line) & (across >= begin_line), 1.0, 0.0)
    upper[...] = jnp.where((line <= across) & (line >= begin_across), 1.0, 0.0)


def own_range(lengths, ndocs, rows):
    place = lax.axis_index("seq")
    _, _, _, _, first, last = block_range(lengths, ndocs, place * rows, rows)
    order = lax.broadcasted_iota(jnp.int32, (rows, HEAD_DIM), 0)
    return lax.rem(place, 2) == 0, order < first, order >= last


def local_part(q, k, v, g, lower, upper, at):
    qh, kh, vh, gh = (ref[:, at] for ref in (q, k, v, g))
    weight_gv = (dot(gh, vh, NT) * lower[...]).astype(jnp.bfloat16)
    weight_vg = (dot(vh, gh, NT) * upper[...]).astype(jnp.bfloat16)
    weight_kq = (dot(kh, qh, NT) * upper[...]).astype(jnp.bfloat16)
    return dot(weight_gv, kh, NN), dot(weight_vg, qh, NN), dot(weight_kq, gh, NN)


def twice(ref, at):
    return jnp.concatenate([ref[:, at]] * 2, axis=1)


def carry_of_state(g, state, first_rows, at):
    return jnp.where(first_rows, dot(twice(g, at), split(state, 1), NT), 0.0)


def carries_of_grad(k, v, grad, last_rows, at):
    carry_k = jnp.where(last_rows, dot(twice(v, at), split(grad, 1), NT), 0.0)
    return carry_k, jnp.where(last_rows, dot(twice(k, at), split(grad, 0), NN), 0.0)


def deal(done, outs, rows, groups):
    part, column = rows // groups, lax.axis_index("head")
    for j in range(groups):
        at = pl.ds(pl.multiple_of(lax.rem(column + j, groups) * part, part), part)
        for i in range(3):
            outs[j][i] = done[i, at, :]


def grad_kernel(lengths, q, k, v, g, lower, upper, mine, got, *rest, ndocs, rows, offset, heads, groups):
    outs, done = rest[-1 - groups:-1], rest[-1]
    first_core, first_rows, last_rows = own_range(lengths, ndocs, rows)
    for h in range(heads):
        cols = slice(h * HEAD_DIM, (h + 1) * HEAD_DIM)
        at = slice(offset + h * HEAD_DIM, offset + (h + 1) * HEAD_DIM)
        state = jnp.where(first_core, got[h], mine[h])
        grad = jnp.where(first_core, mine[h], got[h])
        near = local_part(q, k, v, g, lower, upper, at)
        carries = (carry_of_state(g, state, first_rows, at), *carries_of_grad(k, v, grad, last_rows, at))
        for i in range(3):
            done[i, :, cols] = (near[i] + carries[i]).astype(jnp.bfloat16)
    deal(done, outs, rows, groups)


def begin_kernel(lengths, q, k, v, g, lower, upper, mine, *rest, ndocs, rows, offset, heads):
    near = rest[-1]
    first_core, first_rows, last_rows = own_range(lengths, ndocs, rows)
    for h in range(heads):
        cols = slice(h * HEAD_DIM, (h + 1) * HEAD_DIM)
        at = slice(offset + h * HEAD_DIM, offset + (h + 1) * HEAD_DIM)
        for i, value in enumerate(local_part(q, k, v, g, lower, upper, at)):
            near[i, :, cols] = value

    @pl.when(first_core)
    def _():
        for h in range(heads):
            cols = slice(h * HEAD_DIM, (h + 1) * HEAD_DIM)
            at = slice(offset + h * HEAD_DIM, offset + (h + 1) * HEAD_DIM)
            carry_k, carry_v = carries_of_grad(k, v, mine[h], last_rows, at)
            near[1, :, cols] += carry_k
            near[2, :, cols] += carry_v

    @pl.when(jnp.logical_not(first_core))
    def _():
        for h in range(heads):
            cols = slice(h * HEAD_DIM, (h + 1) * HEAD_DIM)
            at = slice(offset + h * HEAD_DIM, offset + (h + 1) * HEAD_DIM)
            near[0, :, cols] += carry_of_state(g, mine[h], first_rows, at)


def end_kernel(lengths, k, v, g, near, got, *rest, ndocs, rows, offset, heads, groups):
    outs, done = rest[-1 - groups:-1], rest[-1]
    first_core, first_rows, last_rows = own_range(lengths, ndocs, rows)

    @pl.when(first_core)
    def _():
        for h in range(heads):
            cols = slice(h * HEAD_DIM, (h + 1) * HEAD_DIM)
            at = slice(offset + h * HEAD_DIM, offset + (h + 1) * HEAD_DIM)
            done[0, :, cols] = (near[0, :, cols] + carry_of_state(g, got[h], first_rows, at)).astype(jnp.bfloat16)
            done[1, :, cols] = near[1, :, cols].astype(jnp.bfloat16)
            done[2, :, cols] = near[2, :, cols].astype(jnp.bfloat16)

    @pl.when(jnp.logical_not(first_core))
    def _():
        for h in range(heads):
            cols = slice(h * HEAD_DIM, (h + 1) * HEAD_DIM)
            at = slice(offset + h * HEAD_DIM, offset + (h + 1) * HEAD_DIM)
            carry_k, carry_v = carries_of_grad(k, v, got[h], last_rows, at)
            done[0, :, cols] = near[0, :, cols].astype(jnp.bfloat16)
            done[1, :, cols] = (near[1, :, cols] + carry_k).astype(jnp.bfloat16)
            done[2, :, cols] = (near[2, :, cols] + carry_v).astype(jnp.bfloat16)

    deal(done, outs, rows, groups)


def place_kernel(*refs, groups, offset, cw, width):
    parts, outs, sems = refs[:groups], refs[-4:-1], refs[-1]
    column = lax.axis_index("head")
    copies = []
    for j in range(groups):
        start = pl.multiple_of(lax.rem(column + groups - j, groups) * width + offset, 128)
        for i in range(3):
            copies.append(pltpu.make_async_copy(parts[j].at[i], outs[i].at[:, pl.ds(start, cw)], sems.at[len(copies)]))
            copies[-1].start()
    for copy in copies:
        copy.wait()


def cuts_of(width):
    heads = width // HEAD_DIM
    size = CHUNK if heads % (2 * CHUNK) == 0 else 2
    cw, half = size * HEAD_DIM, max(heads // 2, size) * HEAD_DIM
    return [(at, half, [(o, cw) for o in range(at, at + half, cw)]) for at in range(0, width, half)]


def shards(queries, keys, values, out_grad, doc_lengths):
    rows, width = queries.shape
    ndocs = doc_lengths.shape[0]
    seq, groups = lax.axis_size("seq"), lax.axis_size("head")
    pairs = seq // 2
    hops = -(-MOST // (2 * rows))
    halves = cuts_of(width)
    part = rows // groups
    anywhere = pl.BlockSpec(memory_space=pl.ANY)
    in_vmem = pl.BlockSpec(memory_space=pltpu.VMEM)
    in_smem = pl.BlockSpec(memory_space=pltpu.SMEM)
    f32, bf16 = jnp.float32, jnp.bfloat16
    inputs = (queries, keys, values, out_grad)
    sizes = dict(ndocs=ndocs, rows=rows)
    cheap = pl.CostEstimate(flops=0, bytes_accessed=1024, transcendentals=0)

    def shape_of(*dims, dtype=f32):
        return jax.ShapeDtypeStruct(dims, dtype)

    def call(name, kernel, args, outs, scratch=(), after=(), limit=VMEM_LIMIT):
        return pl.pallas_call(
            kernel, in_specs=[in_smem] + [in_vmem] * len(args) + [anywhere] * len(after), out_specs=[in_vmem] * len(outs), out_shape=outs,
            scratch_shapes=list(scratch), cost_estimate=cheap,
            compiler_params=pltpu.CompilerParams(vmem_limit_bytes=limit), name=name,
        )(doc_lengths, *args, *after)

    def swap_cores(a):
        return lax.ppermute(a, "seq", [(b, b ^ 1) for b in range(seq)])

    def swap_pairs(sent):
        came = []
        for hop in range(1, hops + 1):
            perm = [(2 * m, 2 * (m + hop) + 1) for m in range(pairs - hop)]
            came.append(lax.ppermute(sent[hop - 1], "seq", perm + [(b, a) for a, b in perm]))
        return came

    def send_rows(outs):
        arrived = list(outs[:1])
        for j in range(1, groups):
            arrived.append(lax.ppermute(outs[j], "head", [(x, (x + j) % groups) for x in range(groups)]))
        return arrived

    square = (HEAD_DIM, HEAD_DIM)

    def states(kinds, offset, half, after):
        heads = half // HEAD_DIM
        group = GROUP if heads % GROUP == 0 else 2
        return pl.pallas_call(
            functools.partial(state_kernel, offset=offset, heads=heads, group=group, kinds=kinds, **sizes),
            in_specs=[anywhere] * (5 + len(after)), out_specs=[in_vmem] * len(kinds),
            out_shape=[shape_of(heads, *square)] * len(kinds),
            scratch_shapes=[
                pltpu.VMEM((len(kinds), 2, rows, half), bf16), pltpu.SemaphoreType.DMA((len(kinds), heads // group, 2)),
                pltpu.SMEM((ndocs,), jnp.int32), pltpu.SemaphoreType.DMA,
            ],
            cost_estimate=cheap, compiler_params=pltpu.CompilerParams(vmem_limit_bytes=SECOND_LIMIT if after else FIRST_LIMIT), name="states",
        )(doc_lengths, *inputs, *after)

    def pair_up(kept, got, after):
        lines = kept.shape[0] * HEAD_DIM
        outs = [shape_of(lines + PAD * (hops - hop), HEAD_DIM, dtype=LINK) for hop in range(1, hops + 1)]
        totals = call("pair", functools.partial(pair_kernel, hops=hops, **sizes), (kept, got), outs, after=after)
        return totals[-1], swap_pairs(totals)

    def join(kept, came, chunks, after):
        counts = [cw // HEAD_DIM for _, cw in chunks]
        joined = call(
            "join", functools.partial(join_kernel, counts=counts, hops=hops, **sizes), (swap_cores(kept), *came),
            [shape_of(n, *square) for n in counts] * 2, after=after,
        )
        return [(mine, swap_cores(theirs)) for mine, theirs in zip(joined[:len(chunks)], joined[len(chunks):])]

    def grads(masks, offset, cw, mine, theirs, after):
        return call(
            "grads", functools.partial(grad_kernel, offset=offset, heads=cw // HEAD_DIM, groups=groups, **sizes),
            (*inputs, *masks, mine, theirs), [shape_of(3, part, cw, dtype=bf16)] * groups,
            [pltpu.VMEM((3, rows, cw), bf16)], after, GRAD_LIMIT,
        )

    def grads_early(masks, offset, cw, mine, theirs):
        more = dict(offset=offset, heads=cw // HEAD_DIM, **sizes)
        near = call(
            "begin", functools.partial(begin_kernel, **more), (*inputs, *masks, mine), [shape_of(3, rows, cw)],
            limit=GRAD_LIMIT,
        )[0]
        return call(
            "end", functools.partial(end_kernel, groups=groups, **more), (*inputs[1:], near, theirs),
            [shape_of(3, part, cw, dtype=bf16)] * groups, [pltpu.VMEM((3, rows, cw), bf16)], limit=GRAD_LIMIT,
        )

    cuts, outs, arrived, totals, masks = [], [], [], [], None
    for start, half, chunks in halves:
        if not totals:
            (sent,) = states(("sent",), start, half, [])
            (kept,) = states(("kept",), start, half, [])
        else:
            kept, sent = states(("kept", "sent"), start, half, totals)
        total, came = pair_up(kept, swap_cores(sent), [made[0] for made in outs[:1]])
        totals = [total]
        masks = masks or call("masks", functools.partial(mask_kernel, **sizes), (), [shape_of(rows, rows)] * 2, after=totals)
        joined = join(kept, came, chunks, [parts[1] for parts in arrived[:1]] or masks[:1])
        for (offset, cw), (mine, theirs) in zip(chunks, joined):
            after = [made[0] for made in outs[-1:]] + [parts[1] for parts in arrived[1:-1]][-1:]
            if outs:
                outs.append(grads(masks, offset, cw, mine, theirs, after))
            else:
                outs.append(grads_early(masks, offset, cw, mine, theirs))
            arrived.append(send_rows(outs[-1]))
        cuts += chunks

    placed = []
    for c, (offset, cw) in enumerate(cuts):
        placed = pl.pallas_call(
            functools.partial(place_kernel, groups=groups, offset=offset, cw=cw, width=width),
            grid_spec=pl.GridSpec(
                grid=(1,), in_specs=[anywhere] * (groups + len(placed)), out_specs=[anywhere] * 3,
                scratch_shapes=[pltpu.SemaphoreType.DMA((3 * groups,))],
            ),
            out_shape=[shape_of(part, width * groups, dtype=bf16)] * 3,
            input_output_aliases={groups + i: i for i in range(len(placed))},
            cost_estimate=cheap,
            compiler_params=pltpu.CompilerParams(vmem_limit_bytes=VMEM_LIMIT), name="place",
        )(*arrived[c], *placed)
    return tuple(placed)


def solution(mesh):
    return jax.shard_map(
        shards,
        mesh=mesh,
        in_specs=(P("seq", "head"), P("seq", "head"), P("seq", "head"), P("seq", "head"), P()),
        out_specs=(P(("seq", "head"), None), P(("seq", "head"), None), P(("seq", "head"), None)),
        check_vma=False,
    )
```

```python
import functools

import jax
import jax.numpy as jnp
from jax import lax
from jax.experimental import pallas as pl
from jax.experimental.pallas import tpu as pltpu
from jax.sharding import PartitionSpec as P

HEAD_DIM = 128
MOST = 1024
GROUP = 4
CHUNK = 4
PAD = 16
LINK = jnp.bfloat16
VMEM_LIMIT = 16 * 1024 * 1024
GRAD_LIMIT = 40 * 1024 * 1024
FIRST_LIMIT = 53 * 1024 * 1024
SECOND_LIMIT = 52 * 1024 * 1024
NT = (((1,), (1,)), ((), ()))
TN = (((0,), (0,)), ((), ()))
NN = (((1,), (0,)), ((), ()))


def dot(a, b, dims):
    return lax.dot_general(a, b, dims, preferred_element_type=jnp.float32)


def doc_at(meta, ndocs, position):
    start, begin, end = jnp.int32(0), jnp.int32(0), jnp.int32(0)
    for i in range(ndocs):
        stop = start + meta[i]
        begin = jnp.where(start <= position, start, begin)
        end = jnp.where(start <= position, stop, end)
        start = stop
    return begin, end


def block_range(meta, ndocs, base, rows):
    begin0, end0 = doc_at(meta, ndocs, base)
    begin1, end1 = doc_at(meta, ndocs, base + rows - 1)
    first = jnp.where(begin0 < base, end0, base) - base
    return begin0, end0, begin1, end1, first, begin1 - base


def state_kernel(lengths, q, k, v, g, *rest, ndocs, rows, offset, heads, group, kinds):
    outs, held, sems, known, got = rest[-4 - len(kinds):-4], rest[-4], rest[-3], rest[-2], rest[-1]
    gw = group * HEAD_DIM
    place = lax.axis_index("seq")
    first_core = lax.rem(place, 2) == 0

    def copy(n, c, i, ref):
        src = ref.at[:, pl.ds(offset + c * gw, gw)]
        return pltpu.make_async_copy(src, held.at[n, i, :, pl.ds(c * gw, gw)], sems.at[n, c, i])

    fetch = pltpu.make_async_copy(lengths, known, got)
    fetch.start()
    for n, kind in enumerate(kinds):
        tails = first_core if kind == "kept" else jnp.logical_not(first_core)
        for c in range(heads // group):

            @pl.when(tails)
            def _():
                copy(n, c, 0, k).start()
                copy(n, c, 1, v).start()

            @pl.when(jnp.logical_not(tails))
            def _():
                copy(n, c, 0, q).start()
                copy(n, c, 1, g).start()

    fetch.wait()
    _, _, _, _, first, last = block_range(known, ndocs, place * rows, rows)
    order = lax.broadcasted_iota(jnp.int32, (rows, HEAD_DIM), 0)
    zero = jnp.zeros((), held.dtype)
    for n, (kind, out) in enumerate(zip(kinds, outs)):
        tails = first_core if kind == "kept" else jnp.logical_not(first_core)
        low, high = jnp.where(tails, last, 0), jnp.where(tails, rows, first)
        here = (order >= low) & (order < high)
        for h in range(heads):
            if h % group == 0:
                copy(n, h // group, 0, k).wait()
                copy(n, h // group, 1, v).wait()
            cols = slice(h * HEAD_DIM, (h + 1) * HEAD_DIM)
            out[h] = dot(jnp.where(here, held[n, 0, :, cols], zero), held[n, 1, :, cols], TN)


def pair_kernel(lengths, kept, got, *rest, ndocs, rows, hops, copies):
    sent, again = rest[-hops - copies:len(rest) - copies], rest[len(rest) - copies:]
    place = lax.axis_index("seq")
    first_core = lax.rem(place, 2) == 0
    even = (place - lax.rem(place, 2)) * rows
    odd = even + rows
    _, even_e0 = doc_at(lengths, ndocs, even)
    odd_b1, _ = doc_at(lengths, ndocs, odd + rows - 1)
    joins = jnp.where(jnp.where(first_core, odd_b1 < odd, even_e0 > odd), 1.0, 0.0)
    size = kept.shape[0] * HEAD_DIM
    total = (got[...] + joins * kept[...]).astype(LINK).reshape(size, HEAD_DIM)
    for out in sent:
        out[:size] = total
        if out.shape[0] > size:
            out[size:] = jnp.zeros((out.shape[0] - size, HEAD_DIM), LINK)
    for i, out in enumerate(again):
        count = out.shape[0]
        out[...] = kept[i * count:(i + 1) * count]


def join_kernel(lengths, *rest, ndocs, rows, counts, hops, pieces):
    others, came = rest[:len(counts)], rest[len(counts):len(counts) + hops]
    mine, theirs = rest[-pieces - len(counts):-pieces], rest[-pieces:]
    place = lax.axis_index("seq")
    first_core = lax.rem(place, 2) == 0
    even = (place - lax.rem(place, 2)) * rows
    odd = even + rows
    even_b0, _ = doc_at(lengths, ndocs, even)
    _, even_e1 = doc_at(lengths, ndocs, odd - 1)
    odd_b0, _ = doc_at(lengths, ndocs, odd)
    _, odd_e1 = doc_at(lengths, ndocs, odd + rows - 1)

    def one(if_first, if_second):
        return jnp.where(jnp.where(first_core, if_first, if_second), 1.0, 0.0)

    weights = [
        one(odd + rows + hop * 2 * rows < odd_e1, even - hop * 2 * rows > even_b0) for hop in range(hops)
    ]
    from_other, from_pair = one(odd < even_e1, odd > odd_b0), one(odd + rows < even_e1, even > odd_b0)
    for c, count in enumerate(counts):
        at = slice(sum(counts[:c]), sum(counts[:c + 1]))
        lines = slice(at.start * HEAD_DIM, at.stop * HEAD_DIM)
        total = weights[0] * came[0][lines].astype(jnp.float32)
        for hop in range(1, hops):
            total = total + weights[hop] * came[hop][lines].astype(jnp.float32)
        total = total.reshape(count, HEAD_DIM, HEAD_DIM)
        if pieces == 1:
            theirs[0][at] = total
        else:
            theirs[c][...] = total
        mine[c][...] = from_other * others[c][...] + from_pair * total


def split(a, axis):
    high = a.astype(jnp.bfloat16)
    return jnp.concatenate([high, (a - high.astype(jnp.float32)).astype(jnp.bfloat16)], axis=axis)


def mask_kernel(lengths, *rest, ndocs, rows):
    lower, upper = rest[-2:]
    line = lax.broadcasted_iota(jnp.int32, (rows, rows), 0)
    across = lax.broadcasted_iota(jnp.int32, (rows, rows), 1)
    begin_line = jnp.zeros((rows, rows), jnp.int32)
    begin_across = jnp.zeros((rows, rows), jnp.int32)
    start = jnp.int32(0) - lax.axis_index("seq") * rows
    for i in range(ndocs):
        begin_line = jnp.where(line >= start, start, begin_line)
        begin_across = jnp.where(across >= start, start, begin_across)
        start = start + lengths[i]
    lower[...] = jnp.where((across <= line) & (across >= begin_line), 1.0, 0.0)
    upper[...] = jnp.where((line <= across) & (line >= begin_across), 1.0, 0.0)


def own_range(lengths, ndocs, rows):
    place = lax.axis_index("seq")
    _, _, _, _, first, last = block_range(lengths, ndocs, place * rows, rows)
    order = lax.broadcasted_iota(jnp.int32, (rows, HEAD_DIM), 0)
    return lax.rem(place, 2) == 0, order < first, order >= last


def local_part(q, k, v, g, lower, upper, at):
    qh, kh, vh, gh = (ref[:, at] for ref in (q, k, v, g))
    weight_gv = (dot(gh, vh, NT) * lower[...]).astype(jnp.bfloat16)
    weight_vg = (dot(vh, gh, NT) * upper[...]).astype(jnp.bfloat16)
    weight_kq = (dot(kh, qh, NT) * upper[...]).astype(jnp.bfloat16)
    return dot(weight_gv, kh, NN), dot(weight_vg, qh, NN), dot(weight_kq, gh, NN)


def twice(ref, at):
    return jnp.concatenate([ref[:, at]] * 2, axis=1)


def carry_of_state(g, state, first_rows, at):
    return jnp.where(first_rows, dot(twice(g, at), split(state, 1), NT), 0.0)


def carries_of_grad(k, v, grad, last_rows, at):
    carry_k = jnp.where(last_rows, dot(twice(v, at), split(grad, 1), NT), 0.0)
    return carry_k, jnp.where(last_rows, dot(twice(k, at), split(grad, 0), NN), 0.0)


def deal(done, outs, rows, groups):
    part, column = rows // groups, lax.axis_index("head")
    for j in range(groups):
        at = pl.ds(pl.multiple_of(lax.rem(column + j, groups) * part, part), part)
        for i in range(3):
            outs[j][i] = done[i, at, :]


def grad_kernel(lengths, q, k, v, g, lower, upper, mine, got, *rest, ndocs, rows, offset, base, heads, groups):
    outs, done = rest[-1 - groups:-1], rest[-1]
    first_core, first_rows, last_rows = own_range(lengths, ndocs, rows)
    for h in range(heads):
        cols = slice(h * HEAD_DIM, (h + 1) * HEAD_DIM)
        at = slice(offset + h * HEAD_DIM, offset + (h + 1) * HEAD_DIM)
        state = jnp.where(first_core, got[base + h], mine[h])
        grad = jnp.where(first_core, mine[h], got[base + h])
        near = local_part(q, k, v, g, lower, upper, at)
        carries = (carry_of_state(g, state, first_rows, at), *carries_of_grad(k, v, grad, last_rows, at))
        for i in range(3):
            done[i, :, cols] = (near[i] + carries[i]).astype(jnp.bfloat16)
    deal(done, outs, rows, groups)


def begin_kernel(lengths, q, k, v, g, lower, upper, mine, *rest, ndocs, rows, offset, heads):
    near = rest[-1]
    first_core, first_rows, last_rows = own_range(lengths, ndocs, rows)
    for h in range(heads):
        cols = slice(h * HEAD_DIM, (h + 1) * HEAD_DIM)
        at = slice(offset + h * HEAD_DIM, offset + (h + 1) * HEAD_DIM)
        for i, value in enumerate(local_part(q, k, v, g, lower, upper, at)):
            near[i, :, cols] = value

    @pl.when(first_core)
    def _():
        for h in range(heads):
            cols = slice(h * HEAD_DIM, (h + 1) * HEAD_DIM)
            at = slice(offset + h * HEAD_DIM, offset + (h + 1) * HEAD_DIM)
            carry_k, carry_v = carries_of_grad(k, v, mine[h], last_rows, at)
            near[1, :, cols] += carry_k
            near[2, :, cols] += carry_v

    @pl.when(jnp.logical_not(first_core))
    def _():
        for h in range(heads):
            cols = slice(h * HEAD_DIM, (h + 1) * HEAD_DIM)
            at = slice(offset + h * HEAD_DIM, offset + (h + 1) * HEAD_DIM)
            near[0, :, cols] += carry_of_state(g, mine[h], first_rows, at)


def end_kernel(lengths, k, v, g, near, got, *rest, ndocs, rows, offset, heads, groups):
    outs, done = rest[-1 - groups:-1], rest[-1]
    first_core, first_rows, last_rows = own_range(lengths, ndocs, rows)

    @pl.when(first_core)
    def _():
        for h in range(heads):
            cols = slice(h * HEAD_DIM, (h + 1) * HEAD_DIM)
            at = slice(offset + h * HEAD_DIM, offset + (h + 1) * HEAD_DIM)
            done[0, :, cols] = (near[0, :, cols] + carry_of_state(g, got[h], first_rows, at)).astype(jnp.bfloat16)
            done[1, :, cols] = near[1, :, cols].astype(jnp.bfloat16)
            done[2, :, cols] = near[2, :, cols].astype(jnp.bfloat16)

    @pl.when(jnp.logical_not(first_core))
    def _():
        for h in range(heads):
            cols = slice(h * HEAD_DIM, (h + 1) * HEAD_DIM)
            at = slice(offset + h * HEAD_DIM, offset + (h + 1) * HEAD_DIM)
            carry_k, carry_v = carries_of_grad(k, v, got[h], last_rows, at)
            done[0, :, cols] = near[0, :, cols].astype(jnp.bfloat16)
            done[1, :, cols] = (near[1, :, cols] + carry_k).astype(jnp.bfloat16)
            done[2, :, cols] = (near[2, :, cols] + carry_v).astype(jnp.bfloat16)

    deal(done, outs, rows, groups)


def place_kernel(*refs, groups, offset, cw, width):
    parts, outs, sems = refs[:groups], refs[-4:-1], refs[-1]
    column = lax.axis_index("head")
    copies = []
    for j in range(groups):
        start = pl.multiple_of(lax.rem(column + groups - j, groups) * width + offset, 128)
        for i in range(3):
            copies.append(pltpu.make_async_copy(parts[j].at[i], outs[i].at[:, pl.ds(start, cw)], sems.at[len(copies)]))
            copies[-1].start()
    for copy in copies:
        copy.wait()


def cuts_of(width):
    heads = width // HEAD_DIM
    size = CHUNK if heads % (2 * CHUNK) == 0 else 2
    cw, half = size * HEAD_DIM, max(heads // 2, size) * HEAD_DIM
    return [(at, half, [(o, cw) for o in range(at, at + half, cw)]) for at in range(0, width, half)]


def shards(queries, keys, values, out_grad, doc_lengths):
    rows, width = queries.shape
    ndocs = doc_lengths.shape[0]
    seq, groups = lax.axis_size("seq"), lax.axis_size("head")
    pairs = seq // 2
    hops = -(-MOST // (2 * rows))
    halves = cuts_of(width)
    part = rows // groups
    anywhere = pl.BlockSpec(memory_space=pl.ANY)
    in_vmem = pl.BlockSpec(memory_space=pltpu.VMEM)
    in_smem = pl.BlockSpec(memory_space=pltpu.SMEM)
    f32, bf16 = jnp.float32, jnp.bfloat16
    inputs = (queries, keys, values, out_grad)
    sizes = dict(ndocs=ndocs, rows=rows)
    cheap = pl.CostEstimate(flops=0, bytes_accessed=1024, transcendentals=0)

    def shape_of(*dims, dtype=f32):
        return jax.ShapeDtypeStruct(dims, dtype)

    def call(name, kernel, args, outs, scratch=(), after=(), limit=VMEM_LIMIT):
        return pl.pallas_call(
            kernel, in_specs=[in_smem] + [in_vmem] * len(args) + [anywhere] * len(after), out_specs=[in_vmem] * len(outs), out_shape=outs,
            scratch_shapes=list(scratch), cost_estimate=cheap,
            compiler_params=pltpu.CompilerParams(vmem_limit_bytes=limit), name=name,
        )(doc_lengths, *args, *after)

    def swap_cores(a):
        return lax.ppermute(a, "seq", [(b, b ^ 1) for b in range(seq)])

    def swap_pairs(sent):
        came = []
        for hop in range(1, hops + 1):
            perm = [(2 * m, 2 * (m + hop) + 1) for m in range(pairs - hop)]
            came.append(lax.ppermute(sent[hop - 1], "seq", perm + [(b, a) for a, b in perm]))
        return came

    def send_rows(outs):
        arrived = list(outs[:1])
        for j in range(1, groups):
            arrived.append(lax.ppermute(outs[j], "head", [(x, (x + j) % groups) for x in range(groups)]))
        return arrived

    square = (HEAD_DIM, HEAD_DIM)

    def states(kinds, offset, half, after):
        heads = half // HEAD_DIM
        group = GROUP if heads % GROUP == 0 else 2
        return pl.pallas_call(
            functools.partial(state_kernel, offset=offset, heads=heads, group=group, kinds=kinds, **sizes),
            in_specs=[anywhere] * (5 + len(after)), out_specs=[in_vmem] * len(kinds),
            out_shape=[shape_of(heads, *square)] * len(kinds),
            scratch_shapes=[
                pltpu.VMEM((len(kinds), 2, rows, half), bf16), pltpu.SemaphoreType.DMA((len(kinds), heads // group, 2)),
                pltpu.SMEM((ndocs,), jnp.int32), pltpu.SemaphoreType.DMA,
            ],
            cost_estimate=cheap, compiler_params=pltpu.CompilerParams(vmem_limit_bytes=SECOND_LIMIT if after else FIRST_LIMIT), name="states",
        )(doc_lengths, *inputs, *after)

    def pair_up(kept, got, counts, after):
        lines = kept.shape[0] * HEAD_DIM
        outs = [shape_of(lines + PAD * (hops - hop + 1), HEAD_DIM, dtype=LINK) for hop in range(1, hops + 1)]
        outs += [shape_of(n, *square) for n in counts]
        kernel = functools.partial(pair_kernel, hops=hops, copies=len(counts), **sizes)
        made = call("pair", kernel, (kept, got), outs, after=after)
        return made[hops - 1], swap_pairs(made[:hops]), [swap_cores(a) for a in made[hops:]]

    def join(others, came, chunks, after, at_once):
        counts = [cw // HEAD_DIM for _, cw in chunks]
        pieces = [sum(counts)] if at_once else counts
        kernel = functools.partial(join_kernel, counts=counts, hops=hops, pieces=len(pieces), **sizes)
        made = call("join", kernel, (*others, *came), [shape_of(n, *square) for n in (*counts, *pieces)], after=after)
        return made[:len(counts)], [swap_cores(a) for a in made[len(counts):]]

    def grads(masks, offset, base, cw, mine, theirs, after):
        return call(
            "grads", functools.partial(grad_kernel, offset=offset, base=base, heads=cw // HEAD_DIM, groups=groups, **sizes),
            (*inputs, *masks, mine, theirs), [shape_of(3, part, cw, dtype=bf16)] * groups,
            [pltpu.VMEM((3, rows, cw), bf16)], after, GRAD_LIMIT,
        )

    def grads_early(masks, offset, cw, mine, theirs):
        more = dict(offset=offset, heads=cw // HEAD_DIM, **sizes)
        near = call(
            "begin", functools.partial(begin_kernel, **more), (*inputs, *masks, mine), [shape_of(3, rows, cw)],
            limit=GRAD_LIMIT,
        )[0]
        return call(
            "end", functools.partial(end_kernel, groups=groups, **more), (*inputs[1:], near, theirs),
            [shape_of(3, part, cw, dtype=bf16)] * groups, [pltpu.VMEM((3, rows, cw), bf16)], limit=GRAD_LIMIT,
        )

    outs, arrived = [], []

    def half_grads(chunks, joined):
        mine, theirs = joined
        base = 0
        for c, (offset, cw) in enumerate(chunks):
            after = [made[0] for made in outs[-1:]] + [parts[1] for parts in arrived[1:-1]][-1:]
            if outs:
                at = base if len(theirs) == 1 else 0
                outs.append(grads(masks, offset, at, cw, mine[c], theirs[c % len(theirs)], after))
            else:
                outs.append(grads_early(masks, offset, cw, mine[c], theirs[0]))
            arrived.append(send_rows(outs[-1]))
            base += cw // HEAD_DIM

    (start, half, chunks), (second, _, second_chunks) = halves
    counts = [cw // HEAD_DIM for _, cw in chunks]
    (sent,) = states(("sent",), start, half, [])
    (kept,) = states(("kept",), start, half, [])
    total, came, others = pair_up(kept, swap_cores(sent), counts, [])
    masks = call("masks", functools.partial(mask_kernel, **sizes), (), [shape_of(rows, rows)] * 2, after=[total])
    kept, sent = states(("kept", "sent"), second, half, [total])
    got = swap_cores(sent)
    half_grads(chunks, join(others, came, chunks, [masks[0], sent], True))
    _, came, others = pair_up(kept, got, counts, [outs[0][0]])
    half_grads(second_chunks, join(others, came, second_chunks, [outs[-1][0], arrived[0][1]], False))
    cuts = chunks + second_chunks

    placed = []
    for c, (offset, cw) in enumerate(cuts):
        placed = pl.pallas_call(
            functools.partial(place_kernel, groups=groups, offset=offset, cw=cw, width=width),
            grid_spec=pl.GridSpec(
                grid=(1,), in_specs=[anywhere] * (groups + len(placed)), out_specs=[anywhere] * 3,
                scratch_shapes=[pltpu.SemaphoreType.DMA((3 * groups,))],
            ),
            out_shape=[shape_of(part, width * groups, dtype=bf16)] * 3,
            input_output_aliases={groups + i: i for i in range(len(placed))},
            cost_estimate=cheap,
            compiler_params=pltpu.CompilerParams(vmem_limit_bytes=VMEM_LIMIT), name="place",
        )(*arrived[c], *placed)
    return tuple(placed)


def solution(mesh):
    return jax.shard_map(
        shards,
        mesh=mesh,
        in_specs=(P("seq", "head"), P("seq", "head"), P("seq", "head"), P("seq", "head"), P()),
        out_specs=(P(("seq", "head"), None), P(("seq", "head"), None), P(("seq", "head"), None)),
        check_vma=False,
    )
```

```python
import functools

import jax
import jax.numpy as jnp
from jax import lax
from jax.experimental import pallas as pl
from jax.experimental.pallas import tpu as pltpu
from jax.sharding import PartitionSpec as P

HEAD_DIM = 128
MOST = 1024
GROUP = 4
CHUNK = 4
PAD = 16
LINK = jnp.bfloat16
VMEM_LIMIT = 16 * 1024 * 1024
GRAD_LIMIT = 32 * 1024 * 1024
FIRST_LIMIT = 53 * 1024 * 1024
SECOND_LIMIT = 40 * 1024 * 1024
NT = (((1,), (1,)), ((), ()))
TN = (((0,), (0,)), ((), ()))
NN = (((1,), (0,)), ((), ()))


def dot(a, b, dims):
    return lax.dot_general(a, b, dims, preferred_element_type=jnp.float32)


def doc_at(meta, ndocs, position):
    start, begin, end = jnp.int32(0), jnp.int32(0), jnp.int32(0)
    for i in range(ndocs):
        stop = start + meta[i]
        begin = jnp.where(start <= position, start, begin)
        end = jnp.where(start <= position, stop, end)
        start = stop
    return begin, end


def block_range(meta, ndocs, base, rows):
    begin0, end0 = doc_at(meta, ndocs, base)
    begin1, end1 = doc_at(meta, ndocs, base + rows - 1)
    first = jnp.where(begin0 < base, end0, base) - base
    return begin0, end0, begin1, end1, first, begin1 - base


def state_kernel(lengths, q, k, v, g, *rest, ndocs, rows, offset, heads, group, kinds):
    outs, held, sems, known, got = rest[-4 - len(kinds):-4], rest[-4], rest[-3], rest[-2], rest[-1]
    gw = group * HEAD_DIM
    place = lax.axis_index("seq")
    first_core = lax.rem(place, 2) == 0

    def copy(n, c, i, ref):
        src = ref.at[:, pl.ds(offset + c * gw, gw)]
        return pltpu.make_async_copy(src, held.at[n, i, :, pl.ds(c * gw, gw)], sems.at[n, c, i])

    fetch = pltpu.make_async_copy(lengths, known, got)
    fetch.start()
    for n, kind in enumerate(kinds):
        tails = first_core if kind == "kept" else jnp.logical_not(first_core)
        for c in range(heads // group):

            @pl.when(tails)
            def _():
                copy(n, c, 0, k).start()
                copy(n, c, 1, v).start()

            @pl.when(jnp.logical_not(tails))
            def _():
                copy(n, c, 0, q).start()
                copy(n, c, 1, g).start()

    fetch.wait()
    _, _, _, _, first, last = block_range(known, ndocs, place * rows, rows)
    order = lax.broadcasted_iota(jnp.int32, (rows, HEAD_DIM), 0)
    zero = jnp.zeros((), held.dtype)
    for n, (kind, out) in enumerate(zip(kinds, outs)):
        tails = first_core if kind == "kept" else jnp.logical_not(first_core)
        low, high = jnp.where(tails, last, 0), jnp.where(tails, rows, first)
        here = (order >= low) & (order < high)
        for h in range(heads):
            if h % group == 0:
                copy(n, h // group, 0, k).wait()
                copy(n, h // group, 1, v).wait()
            cols = slice(h * HEAD_DIM, (h + 1) * HEAD_DIM)
            out[h] = dot(jnp.where(here, held[n, 0, :, cols], zero), held[n, 1, :, cols], TN)


def pair_kernel(lengths, kept, got, *rest, ndocs, rows, hops):
    sent = rest[-hops:]
    place = lax.axis_index("seq")
    first_core = lax.rem(place, 2) == 0
    even = (place - lax.rem(place, 2)) * rows
    odd = even + rows
    _, even_e0 = doc_at(lengths, ndocs, even)
    odd_b1, _ = doc_at(lengths, ndocs, odd + rows - 1)
    joins = jnp.where(jnp.where(first_core, odd_b1 < odd, even_e0 > odd), 1.0, 0.0)
    size = kept.shape[0] * HEAD_DIM
    total = (got[...] + joins * kept[...]).astype(LINK).reshape(size, HEAD_DIM)
    for out in sent:
        out[:size] = total
        if out.shape[0] > size:
            out[size:] = jnp.zeros((out.shape[0] - size, HEAD_DIM), LINK)


def join_kernel(lengths, other, *rest, ndocs, rows, counts, hops):
    came, mine, theirs = rest[:hops], rest[-2 * len(counts):-len(counts)], rest[-len(counts):]
    place = lax.axis_index("seq")
    first_core = lax.rem(place, 2) == 0
    even = (place - lax.rem(place, 2)) * rows
    odd = even + rows
    even_b0, _ = doc_at(lengths, ndocs, even)
    _, even_e1 = doc_at(lengths, ndocs, odd - 1)
    odd_b0, _ = doc_at(lengths, ndocs, odd)
    _, odd_e1 = doc_at(lengths, ndocs, odd + rows - 1)

    def one(if_first, if_second):
        return jnp.where(jnp.where(first_core, if_first, if_second), 1.0, 0.0)

    weights = [
        one(odd + rows + hop * 2 * rows < odd_e1, even - hop * 2 * rows > even_b0) for hop in range(hops)
    ]
    from_other, from_pair = one(odd < even_e1, odd > odd_b0), one(odd + rows < even_e1, even > odd_b0)
    for c, count in enumerate(counts):
        at = slice(sum(counts[:c]), sum(counts[:c + 1]))
        lines = slice(at.start * HEAD_DIM, at.stop * HEAD_DIM)
        total = weights[0] * came[0][lines].astype(jnp.float32)
        for hop in range(1, hops):
            total = total + weights[hop] * came[hop][lines].astype(jnp.float32)
        total = total.reshape(count, HEAD_DIM, HEAD_DIM)
        theirs[c][...] = total
        mine[c][...] = from_other * other[at] + from_pair * total


def split(a, axis):
    high = a.astype(jnp.bfloat16)
    return jnp.concatenate([high, (a - high.astype(jnp.float32)).astype(jnp.bfloat16)], axis=axis)


def mask_kernel(lengths, *rest, ndocs, rows):
    lower, upper = rest[-2:]
    line = lax.broadcasted_iota(jnp.int32, (rows, rows), 0)
    across = lax.broadcasted_iota(jnp.int32, (rows, rows), 1)
    begin_line = jnp.zeros((rows, rows), jnp.int32)
    begin_across = jnp.zeros((rows, rows), jnp.int32)
    start = jnp.int32(0) - lax.axis_index("seq") * rows
    for i in range(ndocs):
        begin_line = jnp.where(line >= start, start, begin_line)
        begin_across = jnp.where(across >= start, start, begin_across)
        start = start + lengths[i]
    lower[...] = jnp.where((across <= line) & (across >= begin_line), 1.0, 0.0)
    upper[...] = jnp.where((line <= across) & (line >= begin_across), 1.0, 0.0)


def own_range(lengths, ndocs, rows):
    place = lax.axis_index("seq")
    _, _, _, _, first, last = block_range(lengths, ndocs, place * rows, rows)
    order = lax.broadcasted_iota(jnp.int32, (rows, HEAD_DIM), 0)
    return lax.rem(place, 2) == 0, order < first, order >= last


def local_part(q, k, v, g, lower, upper, at):
    qh, kh, vh, gh = (ref[:, at] for ref in (q, k, v, g))
    weight_gv = (dot(gh, vh, NT) * lower[...]).astype(jnp.bfloat16)
    weight_vg = (dot(vh, gh, NT) * upper[...]).astype(jnp.bfloat16)
    weight_kq = (dot(kh, qh, NT) * upper[...]).astype(jnp.bfloat16)
    return dot(weight_gv, kh, NN), dot(weight_vg, qh, NN), dot(weight_kq, gh, NN)


def twice(ref, at):
    return jnp.concatenate([ref[:, at]] * 2, axis=1)


def carry_of_state(g, state, first_rows, at):
    return jnp.where(first_rows, dot(twice(g, at), split(state, 1), NT), 0.0)


def carries_of_grad(k, v, grad, last_rows, at):
    carry_k = jnp.where(last_rows, dot(twice(v, at), split(grad, 1), NT), 0.0)
    return carry_k, jnp.where(last_rows, dot(twice(k, at), split(grad, 0), NN), 0.0)


def deal(done, outs, rows, groups):
    part, column = rows // groups, lax.axis_index("head")
    for j in range(groups):
        at = pl.ds(pl.multiple_of(lax.rem(column + j, groups) * part, part), part)
        for i in range(3):
            outs[j][i] = done[i, at, :]


def grad_kernel(lengths, q, k, v, g, lower, upper, mine, got, *rest, ndocs, rows, offset, heads, groups):
    outs, done = rest[-1 - groups:-1], rest[-1]
    first_core, first_rows, last_rows = own_range(lengths, ndocs, rows)
    for h in range(heads):
        cols = slice(h * HEAD_DIM, (h + 1) * HEAD_DIM)
        at = slice(offset + h * HEAD_DIM, offset + (h + 1) * HEAD_DIM)
        state = jnp.where(first_core, got[h], mine[h])
        grad = jnp.where(first_core, mine[h], got[h])
        near = local_part(q, k, v, g, lower, upper, at)
        carries = (carry_of_state(g, state, first_rows, at), *carries_of_grad(k, v, grad, last_rows, at))
        for i in range(3):
            done[i, :, cols] = (near[i] + carries[i]).astype(jnp.bfloat16)
    deal(done, outs, rows, groups)


def local_kernel(lengths, q, k, v, g, lower, upper, near, token, *, offset, heads):
    token[...] = jnp.zeros_like(token)
    for h in range(heads):
        cols = slice(h * HEAD_DIM, (h + 1) * HEAD_DIM)
        at = slice(offset + h * HEAD_DIM, offset + (h + 1) * HEAD_DIM)
        for i, value in enumerate(local_part(q, k, v, g, lower, upper, at)):
            near[i, :, cols] = value


def carry_kernel(lengths, k, v, g, near, mine, got, *rest, ndocs, rows, offset, heads, groups):
    outs, done = rest[-1 - groups:-1], rest[-1]
    first_core, first_rows, last_rows = own_range(lengths, ndocs, rows)
    for h in range(heads):
        cols = slice(h * HEAD_DIM, (h + 1) * HEAD_DIM)
        at = slice(offset + h * HEAD_DIM, offset + (h + 1) * HEAD_DIM)
        state = jnp.where(first_core, got[h], mine[h])
        grad = jnp.where(first_core, mine[h], got[h])
        carries = (carry_of_state(g, state, first_rows, at), *carries_of_grad(k, v, grad, last_rows, at))
        for i in range(3):
            done[i, :, cols] = (near[i, :, cols] + carries[i]).astype(jnp.bfloat16)
    deal(done, outs, rows, groups)


def place_kernel(*refs, groups, offset, cw, width):
    parts, outs, sems = refs[:groups], refs[-4:-1], refs[-1]
    column = lax.axis_index("head")
    copies = []
    for j in range(groups):
        start = pl.multiple_of(lax.rem(column + groups - j, groups) * width + offset, 128)
        for i in range(3):
            copies.append(pltpu.make_async_copy(parts[j].at[i], outs[i].at[:, pl.ds(start, cw)], sems.at[len(copies)]))
            copies[-1].start()
    for copy in copies:
        copy.wait()


def cuts_of(width):
    heads = width // HEAD_DIM
    size = CHUNK if heads % (2 * CHUNK) == 0 else 2
    cw, half = size * HEAD_DIM, max(heads // 2, size) * HEAD_DIM
    return [(at, half, [(o, cw) for o in range(at, at + half, cw)]) for at in range(0, width, half)]


def shards(queries, keys, values, out_grad, doc_lengths):
    rows, width = queries.shape
    ndocs = doc_lengths.shape[0]
    seq, groups = lax.axis_size("seq"), lax.axis_size("head")
    pairs = seq // 2
    hops = -(-MOST // (2 * rows))
    halves = cuts_of(width)
    part = rows // groups
    anywhere = pl.BlockSpec(memory_space=pl.ANY)
    in_vmem = pl.BlockSpec(memory_space=pltpu.VMEM)
    in_smem = pl.BlockSpec(memory_space=pltpu.SMEM)
    f32, bf16 = jnp.float32, jnp.bfloat16
    inputs = (queries, keys, values, out_grad)
    sizes = dict(ndocs=ndocs, rows=rows)
    cheap = pl.CostEstimate(flops=0, bytes_accessed=1024, transcendentals=0)

    def shape_of(*dims, dtype=f32):
        return jax.ShapeDtypeStruct(dims, dtype)

    def call(name, kernel, args, outs, scratch=(), after=(), limit=VMEM_LIMIT):
        return pl.pallas_call(
            kernel, in_specs=[in_smem] + [in_vmem] * len(args) + [anywhere] * len(after), out_specs=[in_vmem] * len(outs), out_shape=outs,
            scratch_shapes=list(scratch), cost_estimate=cheap,
            compiler_params=pltpu.CompilerParams(vmem_limit_bytes=limit), name=name,
        )(doc_lengths, *args, *after)

    def swap_cores(a):
        return lax.ppermute(a, "seq", [(b, b ^ 1) for b in range(seq)])

    def swap_pairs(sent):
        came = []
        for hop in range(1, hops + 1):
            perm = [(2 * m, 2 * (m + hop) + 1) for m in range(pairs - hop)]
            came.append(lax.ppermute(sent[hop - 1], "seq", perm + [(b, a) for a, b in perm]))
        return came

    def send_rows(outs):
        arrived = list(outs[:1])
        for j in range(1, groups):
            arrived.append(lax.ppermute(outs[j], "head", [(x, (x + j) % groups) for x in range(groups)]))
        return arrived

    square = (HEAD_DIM, HEAD_DIM)

    def states(kinds, offset, half, after):
        heads = half // HEAD_DIM
        group = GROUP if heads % GROUP == 0 else 2
        return pl.pallas_call(
            functools.partial(state_kernel, offset=offset, heads=heads, group=group, kinds=kinds, **sizes),
            in_specs=[anywhere] * (5 + len(after)), out_specs=[in_vmem] * len(kinds),
            out_shape=[shape_of(heads, *square)] * len(kinds),
            scratch_shapes=[
                pltpu.VMEM((len(kinds), 2, rows, half), bf16), pltpu.SemaphoreType.DMA((len(kinds), heads // group, 2)),
                pltpu.SMEM((ndocs,), jnp.int32), pltpu.SemaphoreType.DMA,
            ],
            cost_estimate=cheap, compiler_params=pltpu.CompilerParams(vmem_limit_bytes=SECOND_LIMIT if after else FIRST_LIMIT), name="states",
        )(doc_lengths, *inputs, *after)

    def pair_up(kept, got, after):
        lines = kept.shape[0] * HEAD_DIM
        outs = [shape_of(lines + PAD * (hops - hop), HEAD_DIM, dtype=LINK) for hop in range(1, hops + 1)]
        totals = call("pair", functools.partial(pair_kernel, hops=hops, **sizes), (kept, got), outs, after=after)
        return totals[-1], swap_pairs(totals)

    def join(kept, came, chunks, after):
        counts = [cw // HEAD_DIM for _, cw in chunks]
        joined = call(
            "join", functools.partial(join_kernel, counts=counts, hops=hops, **sizes), (swap_cores(kept), *came),
            [shape_of(n, *square) for n in counts] * 2, after=after,
        )
        return [(mine, swap_cores(theirs)) for mine, theirs in zip(joined[:len(chunks)], joined[len(chunks):])]

    def grads(masks, offset, cw, mine, theirs, after):
        return call(
            "grads", functools.partial(grad_kernel, offset=offset, heads=cw // HEAD_DIM, groups=groups, **sizes),
            (*inputs, *masks, mine, theirs), [shape_of(3, part, cw, dtype=bf16)] * groups,
            [pltpu.VMEM((3, rows, cw), bf16)], after, GRAD_LIMIT,
        )

    def local(masks, offset, cw):
        kernel = functools.partial(local_kernel, offset=offset, heads=cw // HEAD_DIM)
        return call(
            "local", kernel, (*inputs, *masks), [shape_of(3, rows, cw), shape_of(8, HEAD_DIM)], limit=GRAD_LIMIT,
        )

    def carry(near, offset, cw, mine, theirs, after):
        kernel = functools.partial(carry_kernel, offset=offset, heads=cw // HEAD_DIM, groups=groups, **sizes)
        return call(
            "carry", kernel, (*inputs[1:], near, mine, theirs), [shape_of(3, part, cw, dtype=bf16)] * groups,
            [pltpu.VMEM((3, rows, cw), bf16)], after, GRAD_LIMIT,
        )

    cuts, outs, arrived, totals, masks = [], [], [], [], None
    for start, half, chunks in halves:
        if not totals:
            (sent,) = states(("sent",), start, half, [])
            (kept,) = states(("kept",), start, half, [])
        else:
            kept, sent = states(("kept", "sent"), start, half, [token])
        total, came = pair_up(kept, swap_cores(sent), [made[0] for made in outs[:1]])
        if not totals:
            masks = call("masks", functools.partial(mask_kernel, **sizes), (), [shape_of(rows, rows)] * 2, after=[total])
            near = [local(masks, *chunk) for chunk in chunks]
            token = near[0][1]
        joined = join(kept, came, chunks, [parts[1] for parts in arrived[:1]] or [made[1] for made in near])
        for c, ((offset, cw), (mine, theirs)) in enumerate(zip(chunks, joined)):
            after = [made[0] for made in outs[-1:]] + [parts[1] for parts in arrived[1:-1]][-1:]
            if totals:
                outs.append(grads(masks, offset, cw, mine, theirs, after))
            else:
                outs.append(carry(near[c][0], offset, cw, mine, theirs, after))
            arrived.append(send_rows(outs[-1]))
        totals = [total]
        cuts += chunks

    placed = []
    for c, (offset, cw) in enumerate(cuts):
        placed = pl.pallas_call(
            functools.partial(place_kernel, groups=groups, offset=offset, cw=cw, width=width),
            grid_spec=pl.GridSpec(
                grid=(1,), in_specs=[anywhere] * (groups + len(placed)), out_specs=[anywhere] * 3,
                scratch_shapes=[pltpu.SemaphoreType.DMA((3 * groups,))],
            ),
            out_shape=[shape_of(part, width * groups, dtype=bf16)] * 3,
            input_output_aliases={groups + i: i for i in range(len(placed))},
            cost_estimate=cheap,
            compiler_params=pltpu.CompilerParams(vmem_limit_bytes=VMEM_LIMIT), name="place",
        )(*arrived[c], *placed)
    return tuple(placed)


def solution(mesh):
    return jax.shard_map(
        shards,
        mesh=mesh,
        in_specs=(P("seq", "head"), P("seq", "head"), P("seq", "head"), P("seq", "head"), P()),
        out_specs=(P(("seq", "head"), None), P(("seq", "head"), None), P(("seq", "head"), None)),
        check_vma=False,
    )
```

```python
import functools

import jax
import jax.numpy as jnp
from jax import lax
from jax.experimental import pallas as pl
from jax.experimental.pallas import tpu as pltpu
from jax.sharding import PartitionSpec as P

HEAD_DIM = 128
MOST = 1024
GROUP = 4
CHUNK = 4
PAD = 16
LINK = jnp.bfloat16
VMEM_LIMIT = 16 * 1024 * 1024
GRAD_LIMIT = 32 * 1024 * 1024
FIRST_LIMIT = 53 * 1024 * 1024
KEPT_LIMIT = 53 * 1024 * 1024
NT = (((1,), (1,)), ((), ()))
TN = (((0,), (0,)), ((), ()))
NN = (((1,), (0,)), ((), ()))


def dot(a, b, dims):
    return lax.dot_general(a, b, dims, preferred_element_type=jnp.float32)


def doc_at(meta, ndocs, position):
    start, begin, end = jnp.int32(0), jnp.int32(0), jnp.int32(0)
    for i in range(ndocs):
        stop = start + meta[i]
        begin = jnp.where(start <= position, start, begin)
        end = jnp.where(start <= position, stop, end)
        start = stop
    return begin, end


def block_range(meta, ndocs, base, rows):
    begin0, end0 = doc_at(meta, ndocs, base)
    begin1, end1 = doc_at(meta, ndocs, base + rows - 1)
    first = jnp.where(begin0 < base, end0, base) - base
    return begin0, end0, begin1, end1, first, begin1 - base


def make_masks(lengths, lower, upper, ndocs, rows):
    line = lax.broadcasted_iota(jnp.int32, (rows, rows), 0)
    across = lax.broadcasted_iota(jnp.int32, (rows, rows), 1)
    begin_line = jnp.zeros((rows, rows), jnp.int32)
    begin_across = jnp.zeros((rows, rows), jnp.int32)
    start = jnp.int32(0) - lax.axis_index("seq") * rows
    for i in range(ndocs):
        begin_line = jnp.where(line >= start, start, begin_line)
        begin_across = jnp.where(across >= start, start, begin_across)
        start = start + lengths[i]
    lower[...] = jnp.where((across <= line) & (across >= begin_line), 1.0, 0.0).astype(lower.dtype)
    upper[...] = jnp.where((line <= across) & (line >= begin_across), 1.0, 0.0).astype(upper.dtype)


def state_kernel(lengths, q, k, v, g, out, *rest, ndocs, rows, offset, heads, group, kept):
    *masks, held, sems, known, got = rest
    gw = group * HEAD_DIM
    place = lax.axis_index("seq")
    first_core = lax.rem(place, 2) == 0

    tails = first_core if kept else jnp.logical_not(first_core)

    def copy(c, i, ref):
        src = ref.at[:, pl.ds(offset + c * gw, gw)]
        return pltpu.make_async_copy(src, held.at[i, :, pl.ds(c * gw, gw)], sems.at[c, i])

    fetch = pltpu.make_async_copy(lengths, known, got)
    fetch.start()
    for c in range(heads // group):

        @pl.when(tails)
        def _():
            copy(c, 0, k).start()
            copy(c, 1, v).start()

        @pl.when(jnp.logical_not(tails))
        def _():
            copy(c, 0, q).start()
            copy(c, 1, g).start()

    fetch.wait()
    if masks:
        make_masks(known, *masks, ndocs, rows)
    _, _, _, _, first, last = block_range(known, ndocs, place * rows, rows)
    order = lax.broadcasted_iota(jnp.int32, (rows, HEAD_DIM), 0)
    zero = jnp.zeros((), held.dtype)
    low, high = jnp.where(tails, last, 0), jnp.where(tails, rows, first)
    here = (order >= low) & (order < high)
    for h in range(heads):
        if h % group == 0:
            copy(h // group, 0, k).wait()
            copy(h // group, 1, v).wait()
        cols = slice(h * HEAD_DIM, (h + 1) * HEAD_DIM)
        out[h] = dot(jnp.where(here, held[0, :, cols], zero), held[1, :, cols], TN)


def late_state_kernel(lengths, q, k, v, g, *rest, ndocs, rows, offset, heads):
    kept, sent = rest[-2:]
    first_core, first_rows, last_rows = own_range(lengths, ndocs, rows)
    zero = jnp.zeros((), q.dtype)
    for h in range(heads):
        at = slice(offset + h * HEAD_DIM, offset + (h + 1) * HEAD_DIM)
        tail = dot(jnp.where(last_rows, k[:, at], zero), v[:, at], TN)
        head = dot(jnp.where(first_rows, q[:, at], zero), g[:, at], TN)
        kept[h] = jnp.where(first_core, tail, head)
        sent[h] = jnp.where(first_core, head, tail)


def pair_kernel(lengths, kept, got, *rest, ndocs, rows, hops):
    sent = rest[-hops:]
    place = lax.axis_index("seq")
    first_core = lax.rem(place, 2) == 0
    even = (place - lax.rem(place, 2)) * rows
    odd = even + rows
    _, even_e0 = doc_at(lengths, ndocs, even)
    odd_b1, _ = doc_at(lengths, ndocs, odd + rows - 1)
    joins = jnp.where(jnp.where(first_core, odd_b1 < odd, even_e0 > odd), 1.0, 0.0)
    size = kept.shape[0] * HEAD_DIM
    total = (got[...] + joins * kept[...]).astype(LINK).reshape(size, HEAD_DIM)
    for out in sent:
        out[:size] = total
        if out.shape[0] > size:
            out[size:] = jnp.zeros((out.shape[0] - size, HEAD_DIM), LINK)


def join_kernel(lengths, other, *rest, ndocs, rows, counts, hops):
    came, mine, theirs = rest[:hops], rest[-2 * len(counts):-len(counts)], rest[-len(counts):]
    place = lax.axis_index("seq")
    first_core = lax.rem(place, 2) == 0
    even = (place - lax.rem(place, 2)) * rows
    odd = even + rows
    even_b0, _ = doc_at(lengths, ndocs, even)
    _, even_e1 = doc_at(lengths, ndocs, odd - 1)
    odd_b0, _ = doc_at(lengths, ndocs, odd)
    _, odd_e1 = doc_at(lengths, ndocs, odd + rows - 1)

    def one(if_first, if_second):
        return jnp.where(jnp.where(first_core, if_first, if_second), 1.0, 0.0)

    weights = [
        one(odd + rows + hop * 2 * rows < odd_e1, even - hop * 2 * rows > even_b0) for hop in range(hops)
    ]
    from_other, from_pair = one(odd < even_e1, odd > odd_b0), one(odd + rows < even_e1, even > odd_b0)
    for c, count in enumerate(counts):
        at = slice(sum(counts[:c]), sum(counts[:c + 1]))
        lines = slice(at.start * HEAD_DIM, at.stop * HEAD_DIM)
        total = weights[0] * came[0][lines].astype(jnp.float32)
        for hop in range(1, hops):
            total = total + weights[hop] * came[hop][lines].astype(jnp.float32)
        total = total.reshape(count, HEAD_DIM, HEAD_DIM)
        theirs[c][...] = total
        mine[c][...] = from_other * other[at] + from_pair * total


def split(a, axis):
    high = a.astype(jnp.bfloat16)
    return jnp.concatenate([high, (a - high.astype(jnp.float32)).astype(jnp.bfloat16)], axis=axis)


def own_range(lengths, ndocs, rows):
    place = lax.axis_index("seq")
    _, _, _, _, first, last = block_range(lengths, ndocs, place * rows, rows)
    order = lax.broadcasted_iota(jnp.int32, (rows, HEAD_DIM), 0)
    return lax.rem(place, 2) == 0, order < first, order >= last


def local_part(q, k, v, g, lower, upper, at):
    qh, kh, vh, gh = (ref[:, at] for ref in (q, k, v, g))
    weight_gv = dot(gh, vh, NT).astype(jnp.bfloat16) * lower[...]
    weight_vg = dot(vh, gh, NT).astype(jnp.bfloat16) * upper[...]
    weight_kq = dot(kh, qh, NT).astype(jnp.bfloat16) * upper[...]
    return dot(weight_gv, kh, NN), dot(weight_vg, qh, NN), dot(weight_kq, gh, NN)


def twice(ref, at):
    return jnp.concatenate([ref[:, at]] * 2, axis=1)


def carry_of_state(g, state, first_rows, at):
    return jnp.where(first_rows, dot(twice(g, at), split(state, 1), NT), 0.0)


def carries_of_grad(k, v, grad, last_rows, at):
    carry_k = jnp.where(last_rows, dot(twice(v, at), split(grad, 1), NT), 0.0)
    return carry_k, jnp.where(last_rows, dot(twice(k, at), split(grad, 0), NN), 0.0)


def deal(done, outs, rows, groups):
    part, column = rows // groups, lax.axis_index("head")
    for j in range(groups):
        at = pl.ds(pl.multiple_of(lax.rem(column + j, groups) * part, part), part)
        for i in range(3):
            outs[j][i] = done[i, at, :]


def grad_kernel(lengths, q, k, v, g, lower, upper, mine, got, *rest, ndocs, rows, offset, heads, groups):
    outs, done = rest[-1 - groups:-1], rest[-1]
    first_core, first_rows, last_rows = own_range(lengths, ndocs, rows)
    for h in range(heads):
        cols = slice(h * HEAD_DIM, (h + 1) * HEAD_DIM)
        at = slice(offset + h * HEAD_DIM, offset + (h + 1) * HEAD_DIM)
        state = jnp.where(first_core, got[h], mine[h])
        grad = jnp.where(first_core, mine[h], got[h])
        near = local_part(q, k, v, g, lower, upper, at)
        carries = (carry_of_state(g, state, first_rows, at), *carries_of_grad(k, v, grad, last_rows, at))
        for i in range(3):
            done[i, :, cols] = (near[i] + carries[i]).astype(jnp.bfloat16)
    deal(done, outs, rows, groups)


def local_kernel(lengths, q, k, v, g, lower, upper, near, token, *, offset, heads):
    token[...] = jnp.zeros_like(token)
    for h in range(heads):
        cols = slice(h * HEAD_DIM, (h + 1) * HEAD_DIM)
        at = slice(offset + h * HEAD_DIM, offset + (h + 1) * HEAD_DIM)
        for i, value in enumerate(local_part(q, k, v, g, lower, upper, at)):
            near[i, :, cols] = value


def carry_kernel(lengths, k, v, g, near, mine, got, *rest, ndocs, rows, offset, heads, groups):
    outs, done = rest[-1 - groups:-1], rest[-1]
    first_core, first_rows, last_rows = own_range(lengths, ndocs, rows)
    for h in range(heads):
        cols = slice(h * HEAD_DIM, (h + 1) * HEAD_DIM)
        at = slice(offset + h * HEAD_DIM, offset + (h + 1) * HEAD_DIM)
        state = jnp.where(first_core, got[h], mine[h])
        grad = jnp.where(first_core, mine[h], got[h])
        carries = (carry_of_state(g, state, first_rows, at), *carries_of_grad(k, v, grad, last_rows, at))
        for i in range(3):
            done[i, :, cols] = (near[i, :, cols] + carries[i]).astype(jnp.bfloat16)
    deal(done, outs, rows, groups)


def place_kernel(*refs, groups, offset, cw, width):
    parts, outs, sems = refs[:groups], refs[-4:-1], refs[-1]
    column = lax.axis_index("head")
    copies = []
    for j in range(groups):
        start = pl.multiple_of(lax.rem(column + groups - j, groups) * width + offset, 128)
        for i in range(3):
            copies.append(pltpu.make_async_copy(parts[j].at[i], outs[i].at[:, pl.ds(start, cw)], sems.at[len(copies)]))
            copies[-1].start()
    for copy in copies:
        copy.wait()


def cuts_of(width):
    heads = width // HEAD_DIM
    size = CHUNK if heads % (2 * CHUNK) == 0 else 2
    cw, half = size * HEAD_DIM, max(heads // 2, size) * HEAD_DIM
    return [(at, half, [(o, cw) for o in range(at, at + half, cw)]) for at in range(0, width, half)]


def shards(queries, keys, values, out_grad, doc_lengths):
    rows, width = queries.shape
    ndocs = doc_lengths.shape[0]
    seq, groups = lax.axis_size("seq"), lax.axis_size("head")
    pairs = seq // 2
    hops = -(-MOST // (2 * rows))
    halves = cuts_of(width)
    part = rows // groups
    anywhere = pl.BlockSpec(memory_space=pl.ANY)
    in_vmem = pl.BlockSpec(memory_space=pltpu.VMEM)
    in_smem = pl.BlockSpec(memory_space=pltpu.SMEM)
    f32, bf16 = jnp.float32, jnp.bfloat16
    inputs = (queries, keys, values, out_grad)
    sizes = dict(ndocs=ndocs, rows=rows)
    cheap = pl.CostEstimate(flops=0, bytes_accessed=1024, transcendentals=0)

    def shape_of(*dims, dtype=f32):
        return jax.ShapeDtypeStruct(dims, dtype)

    def call(name, kernel, args, outs, scratch=(), after=(), limit=VMEM_LIMIT):
        return pl.pallas_call(
            kernel, in_specs=[in_smem] + [in_vmem] * len(args) + [anywhere] * len(after), out_specs=[in_vmem] * len(outs), out_shape=outs,
            scratch_shapes=list(scratch), cost_estimate=cheap,
            compiler_params=pltpu.CompilerParams(vmem_limit_bytes=limit), name=name,
        )(doc_lengths, *args, *after)

    def swap_cores(a):
        return lax.ppermute(a, "seq", [(b, b ^ 1) for b in range(seq)])

    def swap_pairs(sent):
        came = []
        for hop in range(1, hops + 1):
            perm = [(2 * m, 2 * (m + hop) + 1) for m in range(pairs - hop)]
            came.append(lax.ppermute(sent[hop - 1], "seq", perm + [(b, a) for a, b in perm]))
        return came

    def send_rows(outs):
        arrived = list(outs[:1])
        for j in range(1, groups):
            arrived.append(lax.ppermute(outs[j], "head", [(x, (x + j) % groups) for x in range(groups)]))
        return arrived

    square = (HEAD_DIM, HEAD_DIM)

    def states(kept, offset, half):
        heads = half // HEAD_DIM
        group = GROUP if heads % GROUP == 0 else 2
        outs = [shape_of(heads, *square)] + [shape_of(rows, rows, dtype=bf16)] * (2 * kept)
        return pl.pallas_call(
            functools.partial(state_kernel, offset=offset, heads=heads, group=group, kept=kept, **sizes),
            in_specs=[anywhere] * 5, out_specs=[in_vmem] * len(outs), out_shape=outs,
            scratch_shapes=[
                pltpu.VMEM((2, rows, half), bf16), pltpu.SemaphoreType.DMA((heads // group, 2)),
                pltpu.SMEM((ndocs,), jnp.int32), pltpu.SemaphoreType.DMA,
            ],
            cost_estimate=cheap, compiler_params=pltpu.CompilerParams(vmem_limit_bytes=KEPT_LIMIT if kept else FIRST_LIMIT), name="states",
        )(doc_lengths, *inputs)

    def late_states(offset, half, after):
        heads = half // HEAD_DIM
        return call(
            "states", functools.partial(late_state_kernel, offset=offset, heads=heads, **sizes), inputs,
            [shape_of(heads, *square)] * 2, after=after, limit=GRAD_LIMIT,
        )

    def pair_up(kept, got, after):
        lines = kept.shape[0] * HEAD_DIM
        outs = [shape_of(lines + PAD * (hops - hop), HEAD_DIM, dtype=LINK) for hop in range(1, hops + 1)]
        totals = call("pair", functools.partial(pair_kernel, hops=hops, **sizes), (kept, got), outs, after=after)
        return totals[-1], swap_pairs(totals)

    def join(kept, came, chunks, after):
        counts = [cw // HEAD_DIM for _, cw in chunks]
        joined = call(
            "join", functools.partial(join_kernel, counts=counts, hops=hops, **sizes), (swap_cores(kept), *came),
            [shape_of(n, *square) for n in counts] * 2, after=after,
        )
        return [(mine, swap_cores(theirs)) for mine, theirs in zip(joined[:len(chunks)], joined[len(chunks):])]

    def grads(masks, offset, cw, mine, theirs, after):
        return call(
            "grads", functools.partial(grad_kernel, offset=offset, heads=cw // HEAD_DIM, groups=groups, **sizes),
            (*inputs, *masks, mine, theirs), [shape_of(3, part, cw, dtype=bf16)] * groups,
            [pltpu.VMEM((3, rows, cw), bf16)], after, GRAD_LIMIT,
        )

    def local(masks, offset, cw):
        kernel = functools.partial(local_kernel, offset=offset, heads=cw // HEAD_DIM)
        return call(
            "local", kernel, (*inputs, *masks), [shape_of(3, rows, cw), shape_of(8, HEAD_DIM)], limit=GRAD_LIMIT,
        )

    def carry(near, offset, cw, mine, theirs, after):
        kernel = functools.partial(carry_kernel, offset=offset, heads=cw // HEAD_DIM, groups=groups, **sizes)
        return call(
            "carry", kernel, (*inputs[1:], near, mine, theirs), [shape_of(3, part, cw, dtype=bf16)] * groups,
            [pltpu.VMEM((3, rows, cw), bf16)], after, GRAD_LIMIT,
        )

    cuts, outs, arrived, totals, masks = [], [], [], [], None
    for start, half, chunks in halves:
        if not totals:
            (sent,) = states(False, start, half)
            kept, *masks = states(True, start, half)
        else:
            kept, sent = late_states(start, half, [token])
        total, came = pair_up(kept, swap_cores(sent), [made[0] for made in outs[:1]])
        if not totals:
            near = [local(masks, *chunk) for chunk in chunks]
            token = near[0][1]
        joined = join(kept, came, chunks, [parts[1] for parts in arrived[:1]] or [made[1] for made in near])
        for c, ((offset, cw), (mine, theirs)) in enumerate(zip(chunks, joined)):
            after = [made[0] for made in outs[-1:]] + [parts[1] for parts in arrived[1:-1]][-1:]
            if totals:
                outs.append(grads(masks, offset, cw, mine, theirs, after))
            else:
                outs.append(carry(near[c][0], offset, cw, mine, theirs, after))
            arrived.append(send_rows(outs[-1]))
        totals = [total]
        cuts += chunks

    placed = []
    for c, (offset, cw) in enumerate(cuts):
        placed = pl.pallas_call(
            functools.partial(place_kernel, groups=groups, offset=offset, cw=cw, width=width),
            grid_spec=pl.GridSpec(
                grid=(1,), in_specs=[anywhere] * (groups + len(placed)), out_specs=[anywhere] * 3,
                scratch_shapes=[pltpu.SemaphoreType.DMA((3 * groups,))],
            ),
            out_shape=[shape_of(part, width * groups, dtype=bf16)] * 3,
            input_output_aliases={groups + i: i for i in range(len(placed))},
            cost_estimate=cheap,
            compiler_params=pltpu.CompilerParams(vmem_limit_bytes=VMEM_LIMIT), name="place",
        )(*arrived[c], *placed)
    return tuple(placed)


def solution(mesh):
    return jax.shard_map(
        shards,
        mesh=mesh,
        in_specs=(P("seq", "head"), P("seq", "head"), P("seq", "head"), P("seq", "head"), P()),
        out_specs=(P(("seq", "head"), None), P(("seq", "head"), None), P(("seq", "head"), None)),
        check_vma=False,
    )
```

```python
import functools

import jax
import jax.numpy as jnp
from jax import lax
from jax.experimental import pallas as pl
from jax.experimental.pallas import tpu as pltpu
from jax.sharding import PartitionSpec as P

HEAD_DIM = 128
MOST = 1024
GROUP = 4
CHUNK = 4
PAD = 16
LINK = jnp.bfloat16
VMEM_LIMIT = 16 * 1024 * 1024
GRAD_LIMIT = 32 * 1024 * 1024
FIRST_LIMIT = 53 * 1024 * 1024
KEPT_LIMIT = 53 * 1024 * 1024
NT = (((1,), (1,)), ((), ()))
TN = (((0,), (0,)), ((), ()))
NN = (((1,), (0,)), ((), ()))


def dot(a, b, dims):
    return lax.dot_general(a, b, dims, preferred_element_type=jnp.float32)


def doc_at(meta, ndocs, position):
    start, begin, end = jnp.int32(0), jnp.int32(0), jnp.int32(0)
    for i in range(ndocs):
        stop = start + meta[i]
        begin = jnp.where(start <= position, start, begin)
        end = jnp.where(start <= position, stop, end)
        start = stop
    return begin, end


def block_range(meta, ndocs, base, rows):
    begin0, end0 = doc_at(meta, ndocs, base)
    begin1, end1 = doc_at(meta, ndocs, base + rows - 1)
    first = jnp.where(begin0 < base, end0, base) - base
    return begin0, end0, begin1, end1, first, begin1 - base


def make_masks(lengths, lower, upper, ndocs, rows):
    line = lax.broadcasted_iota(jnp.int32, (rows, rows), 0)
    across = lax.broadcasted_iota(jnp.int32, (rows, rows), 1)
    begin_line = jnp.zeros((rows, rows), jnp.int32)
    begin_across = jnp.zeros((rows, rows), jnp.int32)
    start = jnp.int32(0) - lax.axis_index("seq") * rows
    for i in range(ndocs):
        begin_line = jnp.where(line >= start, start, begin_line)
        begin_across = jnp.where(across >= start, start, begin_across)
        start = start + lengths[i]
    lower[...] = jnp.where((across <= line) & (across >= begin_line), 1.0, 0.0).astype(lower.dtype)
    upper[...] = jnp.where((line <= across) & (line >= begin_across), 1.0, 0.0).astype(upper.dtype)


def state_kernel(lengths, q, k, v, g, out, *rest, ndocs, rows, offset, heads, group, kept):
    *masks, held, sems, known, got = rest
    gw = group * HEAD_DIM
    place = lax.axis_index("seq")
    first_core = lax.rem(place, 2) == 0

    tails = first_core if kept else jnp.logical_not(first_core)

    def copy(c, i, ref):
        src = ref.at[:, pl.ds(offset + c * gw, gw)]
        return pltpu.make_async_copy(src, held.at[i, :, pl.ds(c * gw, gw)], sems.at[c, i])

    fetch = pltpu.make_async_copy(lengths, known, got)
    fetch.start()
    for c in range(heads // group):

        @pl.when(tails)
        def _():
            copy(c, 0, k).start()
            copy(c, 1, v).start()

        @pl.when(jnp.logical_not(tails))
        def _():
            copy(c, 0, q).start()
            copy(c, 1, g).start()

    fetch.wait()
    if masks:
        make_masks(known, *masks, ndocs, rows)
    _, _, _, _, first, last = block_range(known, ndocs, place * rows, rows)
    order = lax.broadcasted_iota(jnp.int32, (rows, HEAD_DIM), 0)
    zero = jnp.zeros((), held.dtype)
    low, high = jnp.where(tails, last, 0), jnp.where(tails, rows, first)
    here = (order >= low) & (order < high)
    for h in range(heads):
        if h % group == 0:
            copy(h // group, 0, k).wait()
            copy(h // group, 1, v).wait()
        cols = slice(h * HEAD_DIM, (h + 1) * HEAD_DIM)
        out[h] = dot(jnp.where(here, held[0, :, cols], zero), held[1, :, cols], TN)


def late_state_kernel(lengths, q, k, v, g, *rest, ndocs, rows, offset, heads):
    kept, sent = rest[-2:]
    first_core, first_rows, last_rows = own_range(lengths, ndocs, rows)
    zero = jnp.zeros((), q.dtype)
    for h in range(heads):
        at = slice(offset + h * HEAD_DIM, offset + (h + 1) * HEAD_DIM)
        tail = dot(jnp.where(last_rows, k[:, at], zero), v[:, at], TN)
        head = dot(jnp.where(first_rows, q[:, at], zero), g[:, at], TN)
        kept[h] = jnp.where(first_core, tail, head)
        sent[h] = jnp.where(first_core, head, tail)


def pair_kernel(lengths, kept, got, *rest, ndocs, rows, hops, copies):
    sent, again = rest[-hops - copies:len(rest) - copies], rest[len(rest) - copies:]
    place = lax.axis_index("seq")
    first_core = lax.rem(place, 2) == 0
    even = (place - lax.rem(place, 2)) * rows
    odd = even + rows
    _, even_e0 = doc_at(lengths, ndocs, even)
    odd_b1, _ = doc_at(lengths, ndocs, odd + rows - 1)
    joins = jnp.where(jnp.where(first_core, odd_b1 < odd, even_e0 > odd), 1.0, 0.0)
    size = kept.shape[0] * HEAD_DIM
    total = (got[...] + joins * kept[...]).astype(LINK).reshape(size, HEAD_DIM)
    for out in sent:
        out[:size] = total
        if out.shape[0] > size:
            out[size:] = jnp.zeros((out.shape[0] - size, HEAD_DIM), LINK)
    for i, out in enumerate(again):
        count = out.shape[0]
        out[...] = kept[i * count:(i + 1) * count]


def join_kernel(lengths, *rest, ndocs, rows, spans, hops):
    others, came = rest[:len(spans)], rest[len(spans):len(spans) + hops]
    mine, theirs = rest[-2 * len(spans):-len(spans)], rest[-len(spans):]
    place = lax.axis_index("seq")
    first_core = lax.rem(place, 2) == 0
    even = (place - lax.rem(place, 2)) * rows
    odd = even + rows
    even_b0, _ = doc_at(lengths, ndocs, even)
    _, even_e1 = doc_at(lengths, ndocs, odd - 1)
    odd_b0, _ = doc_at(lengths, ndocs, odd)
    _, odd_e1 = doc_at(lengths, ndocs, odd + rows - 1)

    def one(if_first, if_second):
        return jnp.where(jnp.where(first_core, if_first, if_second), 1.0, 0.0)

    weights = [
        one(odd + rows + hop * 2 * rows < odd_e1, even - hop * 2 * rows > even_b0) for hop in range(hops)
    ]
    from_other, from_pair = one(odd < even_e1, odd > odd_b0), one(odd + rows < even_e1, even > odd_b0)
    for c, (other_at, came_at, count) in enumerate(spans):
        lines = slice(came_at * HEAD_DIM, (came_at + count) * HEAD_DIM)
        total = weights[0] * came[0][lines].astype(jnp.float32)
        for hop in range(1, hops):
            total = total + weights[hop] * came[hop][lines].astype(jnp.float32)
        total = total.reshape(count, HEAD_DIM, HEAD_DIM)
        theirs[c][...] = total
        mine[c][...] = from_other * others[c][other_at:other_at + count] + from_pair * total


def split(a, axis):
    high = a.astype(jnp.bfloat16)
    return jnp.concatenate([high, (a - high.astype(jnp.float32)).astype(jnp.bfloat16)], axis=axis)


def own_range(lengths, ndocs, rows):
    place = lax.axis_index("seq")
    _, _, _, _, first, last = block_range(lengths, ndocs, place * rows, rows)
    order = lax.broadcasted_iota(jnp.int32, (rows, HEAD_DIM), 0)
    return lax.rem(place, 2) == 0, order < first, order >= last


def local_part(q, k, v, g, lower, upper, at):
    qh, kh, vh, gh = (ref[:, at] for ref in (q, k, v, g))
    weight_gv = dot(gh, vh, NT).astype(jnp.bfloat16) * lower[...]
    weight_vg = dot(vh, gh, NT).astype(jnp.bfloat16) * upper[...]
    weight_kq = dot(kh, qh, NT).astype(jnp.bfloat16) * upper[...]
    return dot(weight_gv, kh, NN), dot(weight_vg, qh, NN), dot(weight_kq, gh, NN)


def twice(ref, at):
    return jnp.concatenate([ref[:, at]] * 2, axis=1)


def carry_of_state(g, state, first_rows, at):
    return jnp.where(first_rows, dot(twice(g, at), split(state, 1), NT), 0.0)


def carries_of_grad(k, v, grad, last_rows, at):
    carry_k = jnp.where(last_rows, dot(twice(v, at), split(grad, 1), NT), 0.0)
    return carry_k, jnp.where(last_rows, dot(twice(k, at), split(grad, 0), NN), 0.0)


def deal(done, outs, rows, groups):
    part, column = rows // groups, lax.axis_index("head")
    for j in range(groups):
        at = pl.ds(pl.multiple_of(lax.rem(column + j, groups) * part, part), part)
        for i in range(3):
            outs[j][i] = done[i, at, :]


def grad_kernel(lengths, q, k, v, g, lower, upper, mine, got, *rest, ndocs, rows, offset, heads, groups):
    outs, done = rest[-1 - groups:-1], rest[-1]
    first_core, first_rows, last_rows = own_range(lengths, ndocs, rows)
    for h in range(heads):
        cols = slice(h * HEAD_DIM, (h + 1) * HEAD_DIM)
        at = slice(offset + h * HEAD_DIM, offset + (h + 1) * HEAD_DIM)
        state = jnp.where(first_core, got[h], mine[h])
        grad = jnp.where(first_core, mine[h], got[h])
        near = local_part(q, k, v, g, lower, upper, at)
        carries = (carry_of_state(g, state, first_rows, at), *carries_of_grad(k, v, grad, last_rows, at))
        for i in range(3):
            done[i, :, cols] = (near[i] + carries[i]).astype(jnp.bfloat16)
    deal(done, outs, rows, groups)


def local_kernel(lengths, q, k, v, g, lower, upper, near, token, *, offset, heads):
    token[...] = jnp.zeros_like(token)
    for h in range(heads):
        cols = slice(h * HEAD_DIM, (h + 1) * HEAD_DIM)
        at = slice(offset + h * HEAD_DIM, offset + (h + 1) * HEAD_DIM)
        for i, value in enumerate(local_part(q, k, v, g, lower, upper, at)):
            near[i, :, cols] = value


def carry_kernel(lengths, k, v, g, near, mine, got, *rest, ndocs, rows, offset, heads, groups):
    outs, done = rest[-1 - groups:-1], rest[-1]
    first_core, first_rows, last_rows = own_range(lengths, ndocs, rows)
    for h in range(heads):
        cols = slice(h * HEAD_DIM, (h + 1) * HEAD_DIM)
        at = slice(offset + h * HEAD_DIM, offset + (h + 1) * HEAD_DIM)
        state = jnp.where(first_core, got[h], mine[h])
        grad = jnp.where(first_core, mine[h], got[h])
        carries = (carry_of_state(g, state, first_rows, at), *carries_of_grad(k, v, grad, last_rows, at))
        for i in range(3):
            done[i, :, cols] = (near[i, :, cols] + carries[i]).astype(jnp.bfloat16)
    deal(done, outs, rows, groups)


def place_kernel(*refs, groups, plan, width):
    parts, outs, sems = refs[:len(plan)], refs[-4:-1], refs[-1]
    column = lax.axis_index("head")
    copies = []
    for ref, (j, offset, cw) in zip(parts, plan):
        start = pl.multiple_of(lax.rem(column + groups - j, groups) * width + offset, 128)
        for i in range(3):
            copies.append(pltpu.make_async_copy(ref.at[i], outs[i].at[:, pl.ds(start, cw)], sems.at[len(copies)]))
            copies[-1].start()
    for copy in copies:
        copy.wait()


def cuts_of(width):
    heads = width // HEAD_DIM
    size = CHUNK if heads % (2 * CHUNK) == 0 else 2
    cw, half = size * HEAD_DIM, max(heads // 2, size) * HEAD_DIM
    return [(at, half, [(o, cw) for o in range(at, at + half, cw)]) for at in range(0, width, half)]


def shards(queries, keys, values, out_grad, doc_lengths):
    rows, width = queries.shape
    ndocs = doc_lengths.shape[0]
    seq, groups = lax.axis_size("seq"), lax.axis_size("head")
    pairs = seq // 2
    hops = -(-MOST // (2 * rows))
    halves = cuts_of(width)
    part = rows // groups
    anywhere = pl.BlockSpec(memory_space=pl.ANY)
    in_vmem = pl.BlockSpec(memory_space=pltpu.VMEM)
    in_smem = pl.BlockSpec(memory_space=pltpu.SMEM)
    f32, bf16 = jnp.float32, jnp.bfloat16
    inputs = (queries, keys, values, out_grad)
    sizes = dict(ndocs=ndocs, rows=rows)
    cheap = pl.CostEstimate(flops=0, bytes_accessed=1024, transcendentals=0)

    def shape_of(*dims, dtype=f32):
        return jax.ShapeDtypeStruct(dims, dtype)

    def call(name, kernel, args, outs, scratch=(), after=(), limit=VMEM_LIMIT):
        return pl.pallas_call(
            kernel, in_specs=[in_smem] + [in_vmem] * len(args) + [anywhere] * len(after), out_specs=[in_vmem] * len(outs), out_shape=outs,
            scratch_shapes=list(scratch), cost_estimate=cheap,
            compiler_params=pltpu.CompilerParams(vmem_limit_bytes=limit), name=name,
        )(doc_lengths, *args, *after)

    def swap_cores(a):
        return lax.ppermute(a, "seq", [(b, b ^ 1) for b in range(seq)])

    def swap_pairs(sent):
        came = []
        for hop in range(1, hops + 1):
            perm = [(2 * m, 2 * (m + hop) + 1) for m in range(pairs - hop)]
            came.append(lax.ppermute(sent[hop - 1], "seq", perm + [(b, a) for a, b in perm]))
        return came

    def send_rows(outs):
        arrived = list(outs[:1])
        for j in range(1, groups):
            arrived.append(lax.ppermute(outs[j], "head", [(x, (x + j) % groups) for x in range(groups)]))
        return arrived

    square = (HEAD_DIM, HEAD_DIM)

    def states(kept, offset, half):
        heads = half // HEAD_DIM
        group = GROUP if heads % GROUP == 0 else 2
        outs = [shape_of(heads, *square)] + [shape_of(rows, rows, dtype=bf16)] * (2 * kept)
        return pl.pallas_call(
            functools.partial(state_kernel, offset=offset, heads=heads, group=group, kept=kept, **sizes),
            in_specs=[anywhere] * 5, out_specs=[in_vmem] * len(outs), out_shape=outs,
            scratch_shapes=[
                pltpu.VMEM((2, rows, half), bf16), pltpu.SemaphoreType.DMA((heads // group, 2)),
                pltpu.SMEM((ndocs,), jnp.int32), pltpu.SemaphoreType.DMA,
            ],
            cost_estimate=cheap, compiler_params=pltpu.CompilerParams(vmem_limit_bytes=KEPT_LIMIT if kept else FIRST_LIMIT), name="states",
        )(doc_lengths, *inputs)

    def late_states(offset, half, after):
        heads = half // HEAD_DIM
        return call(
            "states", functools.partial(late_state_kernel, offset=offset, heads=heads, **sizes), inputs,
            [shape_of(heads, *square)] * 2, after=after, limit=GRAD_LIMIT,
        )

    def pair_up(kept, got, copies, after):
        lines = kept.shape[0] * HEAD_DIM
        outs = [shape_of(lines + PAD * (hops - hop + 1), HEAD_DIM, dtype=LINK) for hop in range(1, hops + 1)]
        outs += [shape_of(kept.shape[0] // max(copies, 1), *square)] * copies
        made = call(
            "pair", functools.partial(pair_kernel, hops=hops, copies=copies, **sizes), (kept, got), outs, after=after
        )
        return made[hops - 1], swap_pairs(made[:hops]), [swap_cores(a) for a in made[hops:]]

    def join(spans, others, came, after):
        made = call(
            "join", functools.partial(join_kernel, spans=spans, hops=hops, **sizes), (*others, *came),
            [shape_of(count, *square) for _, _, count in spans] * 2, after=after,
        )
        return [(mine, swap_cores(theirs)) for mine, theirs in zip(made[:len(spans)], made[len(spans):])]

    def grads(masks, offset, cw, mine, theirs, after):
        return call(
            "grads", functools.partial(grad_kernel, offset=offset, heads=cw // HEAD_DIM, groups=groups, **sizes),
            (*inputs, *masks, mine, theirs), [shape_of(3, part, cw, dtype=bf16)] * groups,
            [pltpu.VMEM((3, rows, cw), bf16)], after, GRAD_LIMIT,
        )

    def local(masks, offset, cw):
        kernel = functools.partial(local_kernel, offset=offset, heads=cw // HEAD_DIM)
        return call(
            "local", kernel, (*inputs, *masks), [shape_of(3, rows, cw), shape_of(8, HEAD_DIM)], limit=GRAD_LIMIT,
        )

    def carry(near, offset, cw, mine, theirs, after):
        kernel = functools.partial(carry_kernel, offset=offset, heads=cw // HEAD_DIM, groups=groups, **sizes)
        return call(
            "carry", kernel, (*inputs[1:], near, mine, theirs), [shape_of(3, part, cw, dtype=bf16)] * groups,
            [pltpu.VMEM((3, rows, cw), bf16)], after, GRAD_LIMIT,
        )

    cuts, outs, arrived, totals, masks = [], [], [], [], None
    for start, half, chunks in halves:
        if not totals:
            (sent,) = states(False, start, half)
            kept, *masks = states(True, start, half)
        else:
            kept, sent = late_states(start, half, [token])
        total, came, others = pair_up(
            kept, swap_cores(sent), 0 if totals else len(chunks), [made[0] for made in outs[:1]]
        )
        if not totals:
            near = [local(masks, *chunk) for chunk in chunks]
            token = near[0][1]
        count = chunks[0][1] // HEAD_DIM
        if totals:
            spans = [(c * count, c * count, count) for c in range(len(chunks))]
            joined = join(spans, [swap_cores(kept)] * len(chunks), came, [arrived[0][1]])
        else:
            joined, after = [], [made[1] for made in near]
            for c in range(len(chunks)):
                joined += join([(0, c * count, count)], others[c:c + 1], came, after)
                after = [joined[-1][0]]
        for c, ((offset, cw), (mine, theirs)) in enumerate(zip(chunks, joined)):
            after = [made[0] for made in outs[-1:]] + [parts[1] for parts in arrived[1:-1]][-1:]
            if totals:
                outs.append(grads(masks, offset, cw, mine, theirs, after))
            else:
                outs.append(carry(near[c][0], offset, cw, mine, theirs, after))
            arrived.append(send_rows(outs[-1]))
        totals = [total]
        cuts += chunks

    placed = []
    for c in range(len(cuts)):
        own = [0, 1] if c == 0 else [c + 1]
        plan = [(arrived[n][0], (0, *cuts[n])) for n in own if n < len(cuts)]
        plan += [(arrived[c][j], (j, *cuts[c])) for j in range(1, groups)]
        some = [array for array, _ in plan]
        placed = pl.pallas_call(
            functools.partial(place_kernel, groups=groups, plan=[where for _, where in plan], width=width),
            grid_spec=pl.GridSpec(
                grid=(1,), in_specs=[anywhere] * (len(some) + len(placed)), out_specs=[anywhere] * 3,
                scratch_shapes=[pltpu.SemaphoreType.DMA((3 * len(some),))],
            ),
            out_shape=[shape_of(part, width * groups, dtype=bf16)] * 3,
            input_output_aliases={len(some) + i: i for i in range(len(placed))},
            cost_estimate=cheap,
            compiler_params=pltpu.CompilerParams(vmem_limit_bytes=VMEM_LIMIT), name="place",
        )(*some, *placed)
    return tuple(placed)


def solution(mesh):
    return jax.shard_map(
        shards,
        mesh=mesh,
        in_specs=(P("seq", "head"), P("seq", "head"), P("seq", "head"), P("seq", "head"), P()),
        out_specs=(P(("seq", "head"), None), P(("seq", "head"), None), P(("seq", "head"), None)),
        check_vma=False,
    )
```

```python
import functools

import jax
import jax.numpy as jnp
from jax import lax
from jax.experimental import pallas as pl
from jax.experimental.pallas import tpu as pltpu
from jax.sharding import PartitionSpec as P

HEAD_DIM = 128
MOST = 1024
GROUP = 4
CHUNK = 4
PAD = 16
LINK = jnp.bfloat16
VMEM_LIMIT = 16 * 1024 * 1024
GRAD_LIMIT = 32 * 1024 * 1024
FIRST_LIMIT = 56 * 1024 * 1024
KEPT_LIMIT = 53 * 1024 * 1024
NT = (((1,), (1,)), ((), ()))
TN = (((0,), (0,)), ((), ()))
NN = (((1,), (0,)), ((), ()))


def dot(a, b, dims):
    return lax.dot_general(a, b, dims, preferred_element_type=jnp.float32)


def doc_at(meta, ndocs, position):
    start, begin, end = jnp.int32(0), jnp.int32(0), jnp.int32(0)
    for i in range(ndocs):
        stop = start + meta[i]
        begin = jnp.where(start <= position, start, begin)
        end = jnp.where(start <= position, stop, end)
        start = stop
    return begin, end


def block_range(meta, ndocs, base, rows):
    begin0, end0 = doc_at(meta, ndocs, base)
    begin1, end1 = doc_at(meta, ndocs, base + rows - 1)
    first = jnp.where(begin0 < base, end0, base) - base
    return begin0, end0, begin1, end1, first, begin1 - base


def make_masks(lengths, lower, upper, ndocs, rows):
    line = lax.broadcasted_iota(jnp.int32, (rows, rows), 0)
    across = lax.broadcasted_iota(jnp.int32, (rows, rows), 1)
    begin_line = jnp.zeros((rows, rows), jnp.int32)
    begin_across = jnp.zeros((rows, rows), jnp.int32)
    start = jnp.int32(0) - lax.axis_index("seq") * rows
    for i in range(ndocs):
        begin_line = jnp.where(line >= start, start, begin_line)
        begin_across = jnp.where(across >= start, start, begin_across)
        start = start + lengths[i]
    lower[...] = jnp.where((across <= line) & (across >= begin_line), 1.0, 0.0).astype(lower.dtype)
    upper[...] = jnp.where((line <= across) & (line >= begin_across), 1.0, 0.0).astype(upper.dtype)


def state_kernel(lengths, q, k, v, g, out, *rest, ndocs, rows, offset, heads, group, kept):
    *masks, held, sems, known, got, made, leave = rest
    gw = group * HEAD_DIM
    place = lax.axis_index("seq")
    first_core = lax.rem(place, 2) == 0

    tails = first_core if kept else jnp.logical_not(first_core)
    made = out if kept else made

    def copy(c, i, ref):
        src = ref.at[:, pl.ds(offset + c * gw, gw)]
        return pltpu.make_async_copy(src, held.at[i, :, pl.ds(c * gw, gw)], sems.at[c, i])

    fetch = pltpu.make_async_copy(lengths, known, got)
    fetch.start()
    for c in range(heads // group):

        @pl.when(tails)
        def _():
            copy(c, 0, k).start()
            copy(c, 1, v).start()

        @pl.when(jnp.logical_not(tails))
        def _():
            copy(c, 0, q).start()
            copy(c, 1, g).start()

    fetch.wait()
    if masks:
        make_masks(known, *masks, ndocs, rows)
    _, _, _, _, first, last = block_range(known, ndocs, place * rows, rows)
    order = lax.broadcasted_iota(jnp.int32, (rows, HEAD_DIM), 0)
    zero = jnp.zeros((), held.dtype)
    low, high = jnp.where(tails, last, 0), jnp.where(tails, rows, first)
    here = (order >= low) & (order < high)
    for h in range(heads):
        if h % group == 0:
            copy(h // group, 0, k).wait()
            copy(h // group, 1, v).wait()
        cols = slice(h * HEAD_DIM, (h + 1) * HEAD_DIM)
        made[h] = dot(jnp.where(here, held[0, :, cols], zero), held[1, :, cols], TN)
        if not kept and h % group == group - 1:
            some = pl.ds(h + 1 - group, group)
            pltpu.make_async_copy(made.at[some], out.at[some], leave.at[h // group]).start()
    for c in range(0 if kept else heads // group):
        some = pl.ds(c * group, group)
        pltpu.make_async_copy(made.at[some], out.at[some], leave.at[c]).wait()


def late_state_kernel(lengths, q, k, v, g, *rest, ndocs, rows, offset, heads):
    kept, sent = rest[-2:]
    first_core, first_rows, last_rows = own_range(lengths, ndocs, rows)
    zero = jnp.zeros((), q.dtype)
    for h in range(heads):
        at = slice(offset + h * HEAD_DIM, offset + (h + 1) * HEAD_DIM)
        tail = dot(jnp.where(last_rows, k[:, at], zero), v[:, at], TN)
        head = dot(jnp.where(first_rows, q[:, at], zero), g[:, at], TN)
        kept[h] = jnp.where(first_core, tail, head)
        sent[h] = jnp.where(first_core, head, tail)


def pair_kernel(lengths, kept, got, *rest, ndocs, rows, hops, copies):
    sent, again = rest[-hops - copies:len(rest) - copies], rest[len(rest) - copies:]
    place = lax.axis_index("seq")
    first_core = lax.rem(place, 2) == 0
    even = (place - lax.rem(place, 2)) * rows
    odd = even + rows
    _, even_e0 = doc_at(lengths, ndocs, even)
    odd_b1, _ = doc_at(lengths, ndocs, odd + rows - 1)
    joins = jnp.where(jnp.where(first_core, odd_b1 < odd, even_e0 > odd), 1.0, 0.0)
    size = kept.shape[0] * HEAD_DIM
    total = (got[...] + joins * kept[...]).astype(LINK).reshape(size, HEAD_DIM)
    for out in sent:
        out[:size] = total
        if out.shape[0] > size:
            out[size:] = jnp.zeros((out.shape[0] - size, HEAD_DIM), LINK)
    for i, out in enumerate(again):
        count = out.shape[0]
        out[...] = kept[i * count:(i + 1) * count]


def join_kernel(lengths, *rest, ndocs, rows, spans, hops):
    others, came = rest[:len(spans)], rest[len(spans):len(spans) + hops]
    mine, theirs = rest[-2 * len(spans):-len(spans)], rest[-len(spans):]
    place = lax.axis_index("seq")
    first_core = lax.rem(place, 2) == 0
    even = (place - lax.rem(place, 2)) * rows
    odd = even + rows
    even_b0, _ = doc_at(lengths, ndocs, even)
    _, even_e1 = doc_at(lengths, ndocs, odd - 1)
    odd_b0, _ = doc_at(lengths, ndocs, odd)
    _, odd_e1 = doc_at(lengths, ndocs, odd + rows - 1)

    def one(if_first, if_second):
        return jnp.where(jnp.where(first_core, if_first, if_second), 1.0, 0.0)

    weights = [
        one(odd + rows + hop * 2 * rows < odd_e1, even - hop * 2 * rows > even_b0) for hop in range(hops)
    ]
    from_other, from_pair = one(odd < even_e1, odd > odd_b0), one(odd + rows < even_e1, even > odd_b0)
    for c, (other_at, came_at, count) in enumerate(spans):
        lines = slice(came_at * HEAD_DIM, (came_at + count) * HEAD_DIM)
        total = weights[0] * came[0][lines].astype(jnp.float32)
        for hop in range(1, hops):
            total = total + weights[hop] * came[hop][lines].astype(jnp.float32)
        total = total.reshape(count, HEAD_DIM, HEAD_DIM)
        theirs[c][...] = total
        mine[c][...] = from_other * others[c][other_at:other_at + count] + from_pair * total


def split(a, axis):
    high = a.astype(jnp.bfloat16)
    return jnp.concatenate([high, (a - high.astype(jnp.float32)).astype(jnp.bfloat16)], axis=axis)


def own_range(lengths, ndocs, rows):
    place = lax.axis_index("seq")
    _, _, _, _, first, last = block_range(lengths, ndocs, place * rows, rows)
    order = lax.broadcasted_iota(jnp.int32, (rows, HEAD_DIM), 0)
    return lax.rem(place, 2) == 0, order < first, order >= last


def local_part(q, k, v, g, lower, upper, at):
    qh, kh, vh, gh = (ref[:, at] for ref in (q, k, v, g))
    weight_gv = dot(gh, vh, NT).astype(jnp.bfloat16) * lower[...]
    weight_vg = dot(vh, gh, NT).astype(jnp.bfloat16) * upper[...]
    weight_kq = dot(kh, qh, NT).astype(jnp.bfloat16) * upper[...]
    return dot(weight_gv, kh, NN), dot(weight_vg, qh, NN), dot(weight_kq, gh, NN)


def twice(ref, at):
    return jnp.concatenate([ref[:, at]] * 2, axis=1)


def carry_of_state(g, state, first_rows, at):
    return jnp.where(first_rows, dot(twice(g, at), split(state, 1), NT), 0.0)


def carries_of_grad(k, v, grad, last_rows, at):
    carry_k = jnp.where(last_rows, dot(twice(v, at), split(grad, 1), NT), 0.0)
    return carry_k, jnp.where(last_rows, dot(twice(k, at), split(grad, 0), NN), 0.0)


def deal(done, outs, rows, groups):
    part, column = rows // groups, lax.axis_index("head")
    for j in range(groups):
        at = pl.ds(pl.multiple_of(lax.rem(column + j, groups) * part, part), part)
        for i in range(3):
            outs[j][i] = done[i, at, :]


def grad_kernel(lengths, q, k, v, g, lower, upper, mine, got, *rest, ndocs, rows, offset, heads, groups):
    outs, done = rest[-1 - groups:-1], rest[-1]
    first_core, first_rows, last_rows = own_range(lengths, ndocs, rows)
    for h in range(heads):
        cols = slice(h * HEAD_DIM, (h + 1) * HEAD_DIM)
        at = slice(offset + h * HEAD_DIM, offset + (h + 1) * HEAD_DIM)
        state = jnp.where(first_core, got[h], mine[h])
        grad = jnp.where(first_core, mine[h], got[h])
        near = local_part(q, k, v, g, lower, upper, at)
        carries = (carry_of_state(g, state, first_rows, at), *carries_of_grad(k, v, grad, last_rows, at))
        for i in range(3):
            done[i, :, cols] = (near[i] + carries[i]).astype(jnp.bfloat16)
    deal(done, outs, rows, groups)


def local_kernel(lengths, q, k, v, g, lower, upper, near, token, *, offset, heads):
    token[...] = jnp.zeros_like(token)
    for h in range(heads):
        cols = slice(h * HEAD_DIM, (h + 1) * HEAD_DIM)
        at = slice(offset + h * HEAD_DIM, offset + (h + 1) * HEAD_DIM)
        for i, value in enumerate(local_part(q, k, v, g, lower, upper, at)):
            near[i, :, cols] = value


def carry_kernel(lengths, k, v, g, near, mine, got, *rest, ndocs, rows, offset, heads, groups):
    outs, done = rest[-1 - groups:-1], rest[-1]
    first_core, first_rows, last_rows = own_range(lengths, ndocs, rows)
    for h in range(heads):
        cols = slice(h * HEAD_DIM, (h + 1) * HEAD_DIM)
        at = slice(offset + h * HEAD_DIM, offset + (h + 1) * HEAD_DIM)
        state = jnp.where(first_core, got[h], mine[h])
        grad = jnp.where(first_core, mine[h], got[h])
        carries = (carry_of_state(g, state, first_rows, at), *carries_of_grad(k, v, grad, last_rows, at))
        for i in range(3):
            done[i, :, cols] = (near[i, :, cols] + carries[i]).astype(jnp.bfloat16)
    deal(done, outs, rows, groups)


def place_kernel(*refs, groups, plan, width):
    parts, outs, sems = refs[:len(plan)], refs[-4:-1], refs[-1]
    column = lax.axis_index("head")
    copies = []
    for ref, (j, offset, cw) in zip(parts, plan):
        start = pl.multiple_of(lax.rem(column + groups - j, groups) * width + offset, 128)
        for i in range(3):
            copies.append(pltpu.make_async_copy(ref.at[i], outs[i].at[:, pl.ds(start, cw)], sems.at[len(copies)]))
            copies[-1].start()
    for copy in copies:
        copy.wait()


def cuts_of(width):
    heads = width // HEAD_DIM
    size = CHUNK if heads % (2 * CHUNK) == 0 else 2
    cw, half = size * HEAD_DIM, max(heads // 2, size) * HEAD_DIM
    return [(at, half, [(o, cw) for o in range(at, at + half, cw)]) for at in range(0, width, half)]


def shards(queries, keys, values, out_grad, doc_lengths):
    rows, width = queries.shape
    ndocs = doc_lengths.shape[0]
    seq, groups = lax.axis_size("seq"), lax.axis_size("head")
    pairs = seq // 2
    hops = -(-MOST // (2 * rows))
    halves = cuts_of(width)
    part = rows // groups
    anywhere = pl.BlockSpec(memory_space=pl.ANY)
    in_vmem = pl.BlockSpec(memory_space=pltpu.VMEM)
    in_smem = pl.BlockSpec(memory_space=pltpu.SMEM)
    f32, bf16 = jnp.float32, jnp.bfloat16
    inputs = (queries, keys, values, out_grad)
    sizes = dict(ndocs=ndocs, rows=rows)
    cheap = pl.CostEstimate(flops=0, bytes_accessed=1024, transcendentals=0)

    def shape_of(*dims, dtype=f32):
        return jax.ShapeDtypeStruct(dims, dtype)

    def call(name, kernel, args, outs, scratch=(), after=(), limit=VMEM_LIMIT):
        return pl.pallas_call(
            kernel, in_specs=[in_smem] + [in_vmem] * len(args) + [anywhere] * len(after), out_specs=[in_vmem] * len(outs), out_shape=outs,
            scratch_shapes=list(scratch), cost_estimate=cheap,
            compiler_params=pltpu.CompilerParams(vmem_limit_bytes=limit), name=name,
        )(doc_lengths, *args, *after)

    def swap_cores(a):
        return lax.ppermute(a, "seq", [(b, b ^ 1) for b in range(seq)])

    def swap_pairs(sent):
        came = []
        for hop in range(1, hops + 1):
            perm = [(2 * m, 2 * (m + hop) + 1) for m in range(pairs - hop)]
            came.append(lax.ppermute(sent[hop - 1], "seq", perm + [(b, a) for a, b in perm]))
        return came

    def send_rows(outs):
        arrived = list(outs[:1])
        for j in range(1, groups):
            arrived.append(lax.ppermute(outs[j], "head", [(x, (x + j) % groups) for x in range(groups)]))
        return arrived

    square = (HEAD_DIM, HEAD_DIM)

    def states(kept, offset, half):
        heads = half // HEAD_DIM
        group = GROUP if heads % GROUP == 0 else 2
        outs = [shape_of(heads, *square)] + [shape_of(rows, rows, dtype=bf16)] * (2 * kept)
        return pl.pallas_call(
            functools.partial(state_kernel, offset=offset, heads=heads, group=group, kept=kept, **sizes),
            in_specs=[anywhere] * 5, out_specs=[in_vmem] * len(outs) if kept else [anywhere], out_shape=outs,
            scratch_shapes=[
                pltpu.VMEM((2, rows, half), bf16), pltpu.SemaphoreType.DMA((heads // group, 2)),
                pltpu.SMEM((ndocs,), jnp.int32), pltpu.SemaphoreType.DMA,
                pltpu.VMEM((heads if not kept else 1, *square), f32), pltpu.SemaphoreType.DMA((heads // group,)),
            ],
            cost_estimate=cheap, compiler_params=pltpu.CompilerParams(vmem_limit_bytes=KEPT_LIMIT if kept else FIRST_LIMIT), name="states",
        )(doc_lengths, *inputs)

    def late_states(offset, half, after):
        heads = half // HEAD_DIM
        return call(
            "states", functools.partial(late_state_kernel, offset=offset, heads=heads, **sizes), inputs,
            [shape_of(heads, *square)] * 2, after=after, limit=GRAD_LIMIT,
        )

    def pair_up(kept, got, copies, after):
        lines = kept.shape[0] * HEAD_DIM
        outs = [shape_of(lines + PAD * (hops - hop + 1), HEAD_DIM, dtype=LINK) for hop in range(1, hops + 1)]
        outs += [shape_of(kept.shape[0] // max(copies, 1), *square)] * copies
        made = call(
            "pair", functools.partial(pair_kernel, hops=hops, copies=copies, **sizes), (kept, got), outs, after=after
        )
        return made[hops - 1], swap_pairs(made[:hops]), [swap_cores(a) for a in made[hops:]]

    def join(spans, others, came, after):
        made = call(
            "join", functools.partial(join_kernel, spans=spans, hops=hops, **sizes), (*others, *came),
            [shape_of(count, *square) for _, _, count in spans] * 2, after=after,
        )
        return [(mine, swap_cores(theirs)) for mine, theirs in zip(made[:len(spans)], made[len(spans):])]

    def grads(masks, offset, cw, mine, theirs, after):
        return call(
            "grads", functools.partial(grad_kernel, offset=offset, heads=cw // HEAD_DIM, groups=groups, **sizes),
            (*inputs, *masks, mine, theirs), [shape_of(3, part, cw, dtype=bf16)] * groups,
            [pltpu.VMEM((3, rows, cw), bf16)], after, GRAD_LIMIT,
        )

    def local(masks, offset, cw):
        kernel = functools.partial(local_kernel, offset=offset, heads=cw // HEAD_DIM)
        return call(
            "local", kernel, (*inputs, *masks), [shape_of(3, rows, cw), shape_of(8, HEAD_DIM)], limit=GRAD_LIMIT,
        )

    def carry(near, offset, cw, mine, theirs, after):
        kernel = functools.partial(carry_kernel, offset=offset, heads=cw // HEAD_DIM, groups=groups, **sizes)
        return call(
            "carry", kernel, (*inputs[1:], near, mine, theirs), [shape_of(3, part, cw, dtype=bf16)] * groups,
            [pltpu.VMEM((3, rows, cw), bf16)], after, GRAD_LIMIT,
        )

    cuts, outs, arrived, totals, masks = [], [], [], [], None
    for start, half, chunks in halves:
        if not totals:
            (sent,) = states(False, start, half)
            kept, *masks = states(True, start, half)
        else:
            kept, sent = late_states(start, half, [token])
        total, came, others = pair_up(
            kept, swap_cores(sent), 0 if totals else len(chunks), [made[0] for made in outs[:1]]
        )
        if not totals:
            near = [local(masks, *chunk) for chunk in chunks]
            token = near[0][1]
        count = chunks[0][1] // HEAD_DIM
        if totals:
            spans = [(c * count, c * count, count) for c in range(len(chunks))]
            joined = join(spans, [swap_cores(kept)] * len(chunks), came, [arrived[0][1]])
        else:
            spans = [(0, c * count, count) for c in range(len(chunks))]
            joined = join(spans, others, came, [made[1] for made in near])
        for c, ((offset, cw), (mine, theirs)) in enumerate(zip(chunks, joined)):
            after = [made[0] for made in outs[-1:]] + [parts[1] for parts in arrived[1:-1]][-1:]
            if totals:
                outs.append(grads(masks, offset, cw, mine, theirs, after))
            else:
                outs.append(carry(near[c][0], offset, cw, mine, theirs, after))
            arrived.append(send_rows(outs[-1]))
        totals = [total]
        cuts += chunks

    placed = []
    for c in range(len(cuts)):
        own = [0, 1] if c == 0 else [c + 1]
        plan = [(arrived[n][0], (0, *cuts[n])) for n in own if n < len(cuts)]
        plan += [(arrived[c][j], (j, *cuts[c])) for j in range(1, groups)]
        some = [array for array, _ in plan]
        placed = pl.pallas_call(
            functools.partial(place_kernel, groups=groups, plan=[where for _, where in plan], width=width),
            grid_spec=pl.GridSpec(
                grid=(1,), in_specs=[anywhere] * (len(some) + len(placed)), out_specs=[anywhere] * 3,
                scratch_shapes=[pltpu.SemaphoreType.DMA((3 * len(some),))],
            ),
            out_shape=[shape_of(part, width * groups, dtype=bf16)] * 3,
            input_output_aliases={len(some) + i: i for i in range(len(placed))},
            cost_estimate=cheap,
            compiler_params=pltpu.CompilerParams(vmem_limit_bytes=VMEM_LIMIT), name="place",
        )(*some, *placed)
    return tuple(placed)


def solution(mesh):
    return jax.shard_map(
        shards,
        mesh=mesh,
        in_specs=(P("seq", "head"), P("seq", "head"), P("seq", "head"), P("seq", "head"), P()),
        out_specs=(P(("seq", "head"), None), P(("seq", "head"), None), P(("seq", "head"), None)),
        check_vma=False,
    )
```

```python
import functools

import jax
import jax.numpy as jnp
from jax import lax
from jax.experimental import pallas as pl
from jax.experimental.pallas import tpu as pltpu
from jax.sharding import PartitionSpec as P

HEAD_DIM = 128
MOST = 1024
GROUP = 4
CHUNK = 4
PAD = 16
LINK = jnp.bfloat16
VMEM_LIMIT = 16 * 1024 * 1024
GRAD_LIMIT = 32 * 1024 * 1024
FIRST_LIMIT = 56 * 1024 * 1024
KEPT_LIMIT = 53 * 1024 * 1024
NT = (((1,), (1,)), ((), ()))
TN = (((0,), (0,)), ((), ()))
NN = (((1,), (0,)), ((), ()))


def dot(a, b, dims):
    return lax.dot_general(a, b, dims, preferred_element_type=jnp.float32)


def doc_at(meta, ndocs, position):
    start, begin, end = jnp.int32(0), jnp.int32(0), jnp.int32(0)
    for i in range(ndocs):
        stop = start + meta[i]
        begin = jnp.where(start <= position, start, begin)
        end = jnp.where(start <= position, stop, end)
        start = stop
    return begin, end


def block_range(meta, ndocs, base, rows):
    begin0, end0 = doc_at(meta, ndocs, base)
    begin1, end1 = doc_at(meta, ndocs, base + rows - 1)
    first = jnp.where(begin0 < base, end0, base) - base
    return begin0, end0, begin1, end1, first, begin1 - base


def make_masks(lengths, lower, upper, ndocs, rows):
    line = lax.broadcasted_iota(jnp.int32, (rows, rows), 0)
    across = lax.broadcasted_iota(jnp.int32, (rows, rows), 1)
    begin_line = jnp.zeros((rows, rows), jnp.int32)
    begin_across = jnp.zeros((rows, rows), jnp.int32)
    start = jnp.int32(0) - lax.axis_index("seq") * rows
    for i in range(ndocs):
        begin_line = jnp.where(line >= start, start, begin_line)
        begin_across = jnp.where(across >= start, start, begin_across)
        start = start + lengths[i]
    lower[...] = jnp.where((across <= line) & (across >= begin_line), 1.0, 0.0).astype(lower.dtype)
    upper[...] = jnp.where((line <= across) & (line >= begin_across), 1.0, 0.0).astype(upper.dtype)


def state_kernel(lengths, q, k, v, g, out, *rest, ndocs, rows, offset, heads, group, kept):
    *masks, held, sems, known, got, made, leave = rest
    gw = group * HEAD_DIM
    place = lax.axis_index("seq")
    first_core = lax.rem(place, 2) == 0

    tails = first_core if kept else jnp.logical_not(first_core)
    made = out if kept else made

    def copy(c, i, ref):
        src = ref.at[:, pl.ds(offset + c * gw, gw)]
        return pltpu.make_async_copy(src, held.at[i, :, pl.ds(c * gw, gw)], sems.at[c, i])

    fetch = pltpu.make_async_copy(lengths, known, got)
    fetch.start()
    for c in range(heads // group):

        @pl.when(tails)
        def _():
            copy(c, 0, k).start()
            copy(c, 1, v).start()

        @pl.when(jnp.logical_not(tails))
        def _():
            copy(c, 0, q).start()
            copy(c, 1, g).start()

    fetch.wait()
    if masks:
        make_masks(known, *masks, ndocs, rows)
    _, _, _, _, first, last = block_range(known, ndocs, place * rows, rows)
    order = lax.broadcasted_iota(jnp.int32, (rows, HEAD_DIM), 0)
    zero = jnp.zeros((), held.dtype)
    low, high = jnp.where(tails, last, 0), jnp.where(tails, rows, first)
    here = (order >= low) & (order < high)
    for h in range(heads):
        if h % group == 0:
            copy(h // group, 0, k).wait()
            copy(h // group, 1, v).wait()
        cols = slice(h * HEAD_DIM, (h + 1) * HEAD_DIM)
        made[h] = dot(jnp.where(here, held[0, :, cols], zero), held[1, :, cols], TN)
        if not kept and h % 2 == 1:
            some = pl.ds(h - 1, 2)
            pltpu.make_async_copy(made.at[some], out.at[some], leave.at[h // 2]).start()
    for c in range(0 if kept else heads // 2):
        some = pl.ds(2 * c, 2)
        pltpu.make_async_copy(made.at[some], out.at[some], leave.at[c]).wait()


def late_state_kernel(lengths, q, k, v, g, *rest, ndocs, rows, offset, heads):
    kept, sent = rest[-2:]
    first_core, first_rows, last_rows = own_range(lengths, ndocs, rows)
    zero = jnp.zeros((), q.dtype)
    for h in range(heads):
        at = slice(offset + h * HEAD_DIM, offset + (h + 1) * HEAD_DIM)
        tail = dot(jnp.where(last_rows, k[:, at], zero), v[:, at], TN)
        head = dot(jnp.where(first_rows, q[:, at], zero), g[:, at], TN)
        kept[h] = jnp.where(first_core, tail, head)
        sent[h] = jnp.where(first_core, head, tail)


def pair_kernel(lengths, kept, got, *rest, ndocs, rows, hops, copies):
    sent, again = rest[-hops - copies:len(rest) - copies], rest[len(rest) - copies:]
    place = lax.axis_index("seq")
    first_core = lax.rem(place, 2) == 0
    even = (place - lax.rem(place, 2)) * rows
    odd = even + rows
    _, even_e0 = doc_at(lengths, ndocs, even)
    odd_b1, _ = doc_at(lengths, ndocs, odd + rows - 1)
    joins = jnp.where(jnp.where(first_core, odd_b1 < odd, even_e0 > odd), 1.0, 0.0)
    size = kept.shape[0] * HEAD_DIM
    total = (got[...] + joins * kept[...]).astype(LINK).reshape(size, HEAD_DIM)
    for out in sent:
        out[:size] = total
        if out.shape[0] > size:
            out[size:] = jnp.zeros((out.shape[0] - size, HEAD_DIM), LINK)
    for i, out in enumerate(again):
        count = out.shape[0]
        out[...] = kept[i * count:(i + 1) * count]


def join_kernel(lengths, *rest, ndocs, rows, spans, hops):
    others, came = rest[:len(spans)], rest[len(spans):len(spans) + hops]
    mine, theirs = rest[-2 * len(spans):-len(spans)], rest[-len(spans):]
    place = lax.axis_index("seq")
    first_core = lax.rem(place, 2) == 0
    even = (place - lax.rem(place, 2)) * rows
    odd = even + rows
    even_b0, _ = doc_at(lengths, ndocs, even)
    _, even_e1 = doc_at(lengths, ndocs, odd - 1)
    odd_b0, _ = doc_at(lengths, ndocs, odd)
    _, odd_e1 = doc_at(lengths, ndocs, odd + rows - 1)

    def one(if_first, if_second):
        return jnp.where(jnp.where(first_core, if_first, if_second), 1.0, 0.0)

    weights = [
        one(odd + rows + hop * 2 * rows < odd_e1, even - hop * 2 * rows > even_b0) for hop in range(hops)
    ]
    from_other, from_pair = one(odd < even_e1, odd > odd_b0), one(odd + rows < even_e1, even > odd_b0)
    for c, (other_at, came_at, count) in enumerate(spans):
        lines = slice(came_at * HEAD_DIM, (came_at + count) * HEAD_DIM)
        total = weights[0] * came[0][lines].astype(jnp.float32)
        for hop in range(1, hops):
            total = total + weights[hop] * came[hop][lines].astype(jnp.float32)
        total = total.reshape(count, HEAD_DIM, HEAD_DIM)
        theirs[c][...] = total
        mine[c][...] = from_other * others[c][other_at:other_at + count] + from_pair * total


def split(a, axis):
    high = a.astype(jnp.bfloat16)
    return jnp.concatenate([high, (a - high.astype(jnp.float32)).astype(jnp.bfloat16)], axis=axis)


def own_range(lengths, ndocs, rows):
    place = lax.axis_index("seq")
    _, _, _, _, first, last = block_range(lengths, ndocs, place * rows, rows)
    order = lax.broadcasted_iota(jnp.int32, (rows, HEAD_DIM), 0)
    return lax.rem(place, 2) == 0, order < first, order >= last


def local_part(q, k, v, g, lower, upper, at):
    qh, kh, vh, gh = (ref[:, at] for ref in (q, k, v, g))
    weight_gv = dot(gh, vh, NT).astype(jnp.bfloat16) * lower[...]
    weight_vg = dot(vh, gh, NT).astype(jnp.bfloat16) * upper[...]
    weight_kq = dot(kh, qh, NT).astype(jnp.bfloat16) * upper[...]
    return dot(weight_gv, kh, NN), dot(weight_vg, qh, NN), dot(weight_kq, gh, NN)


def twice(ref, at):
    return jnp.concatenate([ref[:, at]] * 2, axis=1)


def carry_of_state(g, state, first_rows, at):
    return jnp.where(first_rows, dot(twice(g, at), split(state, 1), NT), 0.0)


def carries_of_grad(k, v, grad, last_rows, at):
    carry_k = jnp.where(last_rows, dot(twice(v, at), split(grad, 1), NT), 0.0)
    return carry_k, jnp.where(last_rows, dot(twice(k, at), split(grad, 0), NN), 0.0)


def deal(done, outs, rows, groups):
    part, column = rows // groups, lax.axis_index("head")
    for j in range(groups):
        at = pl.ds(pl.multiple_of(lax.rem(column + j, groups) * part, part), part)
        for i in range(3):
            outs[j][i] = done[i, at, :]


def grad_kernel(lengths, q, k, v, g, lower, upper, mine, got, *rest, ndocs, rows, offset, heads, groups):
    outs, done = rest[-1 - groups:-1], rest[-1]
    first_core, first_rows, last_rows = own_range(lengths, ndocs, rows)
    for h in range(heads):
        cols = slice(h * HEAD_DIM, (h + 1) * HEAD_DIM)
        at = slice(offset + h * HEAD_DIM, offset + (h + 1) * HEAD_DIM)
        state = jnp.where(first_core, got[h], mine[h])
        grad = jnp.where(first_core, mine[h], got[h])
        near = local_part(q, k, v, g, lower, upper, at)
        carries = (carry_of_state(g, state, first_rows, at), *carries_of_grad(k, v, grad, last_rows, at))
        for i in range(3):
            done[i, :, cols] = (near[i] + carries[i]).astype(jnp.bfloat16)
    deal(done, outs, rows, groups)


def local_kernel(lengths, q, k, v, g, lower, upper, near, token, *, offset, heads):
    token[...] = jnp.zeros_like(token)
    for h in range(heads):
        cols = slice(h * HEAD_DIM, (h + 1) * HEAD_DIM)
        at = slice(offset + h * HEAD_DIM, offset + (h + 1) * HEAD_DIM)
        for i, value in enumerate(local_part(q, k, v, g, lower, upper, at)):
            near[i, :, cols] = value


def carry_kernel(lengths, k, v, g, near, mine, got, *rest, ndocs, rows, offset, heads, groups):
    outs, done = rest[-1 - groups:-1], rest[-1]
    first_core, first_rows, last_rows = own_range(lengths, ndocs, rows)
    for h in range(heads):
        cols = slice(h * HEAD_DIM, (h + 1) * HEAD_DIM)
        at = slice(offset + h * HEAD_DIM, offset + (h + 1) * HEAD_DIM)
        state = jnp.where(first_core, got[h], mine[h])
        grad = jnp.where(first_core, mine[h], got[h])
        carries = (carry_of_state(g, state, first_rows, at), *carries_of_grad(k, v, grad, last_rows, at))
        for i in range(3):
            done[i, :, cols] = (near[i, :, cols] + carries[i]).astype(jnp.bfloat16)
    deal(done, outs, rows, groups)


def add_mine_kernel(lengths, k, v, g, near, mine, *rest, ndocs, rows, offset, heads):
    out = rest[-1]
    first_core, first_rows, last_rows = own_range(lengths, ndocs, rows)

    @pl.when(first_core)
    def _():
        for h in range(heads):
            cols = slice(h * HEAD_DIM, (h + 1) * HEAD_DIM)
            at = slice(offset + h * HEAD_DIM, offset + (h + 1) * HEAD_DIM)
            out[0, :, cols] = near[0, :, cols]
            for i, value in enumerate(carries_of_grad(k, v, mine[h], last_rows, at)):
                out[1 + i, :, cols] = near[1 + i, :, cols] + value

    @pl.when(jnp.logical_not(first_core))
    def _():
        for h in range(heads):
            cols = slice(h * HEAD_DIM, (h + 1) * HEAD_DIM)
            at = slice(offset + h * HEAD_DIM, offset + (h + 1) * HEAD_DIM)
            out[0, :, cols] = near[0, :, cols] + carry_of_state(g, mine[h], first_rows, at)
            for i in range(1, 3):
                out[i, :, cols] = near[i, :, cols]


def add_got_kernel(lengths, k, v, g, near, got, *rest, ndocs, rows, offset, heads, groups):
    outs, done = rest[-1 - groups:-1], rest[-1]
    first_core, first_rows, last_rows = own_range(lengths, ndocs, rows)

    @pl.when(first_core)
    def _():
        for h in range(heads):
            cols = slice(h * HEAD_DIM, (h + 1) * HEAD_DIM)
            at = slice(offset + h * HEAD_DIM, offset + (h + 1) * HEAD_DIM)
            done[0, :, cols] = (near[0, :, cols] + carry_of_state(g, got[h], first_rows, at)).astype(jnp.bfloat16)
            for i in range(1, 3):
                done[i, :, cols] = near[i, :, cols].astype(jnp.bfloat16)

    @pl.when(jnp.logical_not(first_core))
    def _():
        for h in range(heads):
            cols = slice(h * HEAD_DIM, (h + 1) * HEAD_DIM)
            at = slice(offset + h * HEAD_DIM, offset + (h + 1) * HEAD_DIM)
            done[0, :, cols] = near[0, :, cols].astype(jnp.bfloat16)
            for i, value in enumerate(carries_of_grad(k, v, got[h], last_rows, at)):
                done[1 + i, :, cols] = (near[1 + i, :, cols] + value).astype(jnp.bfloat16)

    deal(done, outs, rows, groups)


def place_kernel(*refs, groups, plan, width):
    parts, outs, sems = refs[:len(plan)], refs[-4:-1], refs[-1]
    column = lax.axis_index("head")
    copies = []
    for ref, (j, offset, cw) in zip(parts, plan):
        start = pl.multiple_of(lax.rem(column + groups - j, groups) * width + offset, 128)
        for i in range(3):
            copies.append(pltpu.make_async_copy(ref.at[i], outs[i].at[:, pl.ds(start, cw)], sems.at[len(copies)]))
            copies[-1].start()
    for copy in copies:
        copy.wait()


def cuts_of(width):
    heads = width // HEAD_DIM
    size = CHUNK if heads % (2 * CHUNK) == 0 else 2
    cw, half = size * HEAD_DIM, max(heads // 2, size) * HEAD_DIM
    return [(at, half, [(o, cw) for o in range(at, at + half, cw)]) for at in range(0, width, half)]


def shards(queries, keys, values, out_grad, doc_lengths):
    rows, width = queries.shape
    ndocs = doc_lengths.shape[0]
    seq, groups = lax.axis_size("seq"), lax.axis_size("head")
    pairs = seq // 2
    hops = -(-MOST // (2 * rows))
    halves = cuts_of(width)
    part = rows // groups
    anywhere = pl.BlockSpec(memory_space=pl.ANY)
    in_vmem = pl.BlockSpec(memory_space=pltpu.VMEM)
    in_smem = pl.BlockSpec(memory_space=pltpu.SMEM)
    f32, bf16 = jnp.float32, jnp.bfloat16
    inputs = (queries, keys, values, out_grad)
    sizes = dict(ndocs=ndocs, rows=rows)
    cheap = pl.CostEstimate(flops=0, bytes_accessed=1024, transcendentals=0)

    def shape_of(*dims, dtype=f32):
        return jax.ShapeDtypeStruct(dims, dtype)

    def call(name, kernel, args, outs, scratch=(), after=(), limit=VMEM_LIMIT, same={}):
        return pl.pallas_call(
            kernel, in_specs=[in_smem] + [in_vmem] * len(args) + [anywhere] * len(after), out_specs=[in_vmem] * len(outs), out_shape=outs,
            scratch_shapes=list(scratch), cost_estimate=cheap,
            compiler_params=pltpu.CompilerParams(vmem_limit_bytes=limit), name=name, input_output_aliases=same,
        )(doc_lengths, *args, *after)

    def swap_cores(a):
        return lax.ppermute(a, "seq", [(b, b ^ 1) for b in range(seq)])

    def swap_pairs(sent):
        came = []
        for hop in range(1, hops + 1):
            perm = [(2 * m, 2 * (m + hop) + 1) for m in range(pairs - hop)]
            came.append(lax.ppermute(sent[hop - 1], "seq", perm + [(b, a) for a, b in perm]))
        return came

    def send_rows(outs):
        arrived = list(outs[:1])
        for j in range(1, groups):
            arrived.append(lax.ppermute(outs[j], "head", [(x, (x + j) % groups) for x in range(groups)]))
        return arrived

    square = (HEAD_DIM, HEAD_DIM)

    def states(kept, offset, half):
        heads = half // HEAD_DIM
        group = GROUP if heads % GROUP == 0 else 2
        outs = [shape_of(heads, *square)] + [shape_of(rows, rows, dtype=bf16)] * (2 * kept)
        return pl.pallas_call(
            functools.partial(state_kernel, offset=offset, heads=heads, group=group, kept=kept, **sizes),
            in_specs=[anywhere] * 5, out_specs=[in_vmem] * len(outs) if kept else [anywhere], out_shape=outs,
            scratch_shapes=[
                pltpu.VMEM((2, rows, half), bf16), pltpu.SemaphoreType.DMA((heads // group, 2)),
                pltpu.SMEM((ndocs,), jnp.int32), pltpu.SemaphoreType.DMA,
                pltpu.VMEM((heads if not kept else 1, *square), f32), pltpu.SemaphoreType.DMA((heads // 2,)),
            ],
            cost_estimate=cheap, compiler_params=pltpu.CompilerParams(vmem_limit_bytes=KEPT_LIMIT if kept else FIRST_LIMIT), name="states",
        )(doc_lengths, *inputs)

    def late_states(offset, half, after):
        heads = half // HEAD_DIM
        return call(
            "states", functools.partial(late_state_kernel, offset=offset, heads=heads, **sizes), inputs,
            [shape_of(heads, *square)] * 2, after=after, limit=GRAD_LIMIT,
        )

    def pair_up(kept, got, copies, after):
        lines = kept.shape[0] * HEAD_DIM
        outs = [shape_of(lines + PAD * (hops - hop + 1), HEAD_DIM, dtype=LINK) for hop in range(1, hops + 1)]
        outs += [shape_of(kept.shape[0] // max(copies, 1), *square)] * copies
        made = call(
            "pair", functools.partial(pair_kernel, hops=hops, copies=copies, **sizes), (kept, got), outs, after=after
        )
        return made[hops - 1], swap_pairs(made[:hops]), [swap_cores(a) for a in made[hops:]]

    def join(spans, others, came, after):
        made = call(
            "join", functools.partial(join_kernel, spans=spans, hops=hops, **sizes), (*others, *came),
            [shape_of(count, *square) for _, _, count in spans] * 2, after=after,
        )
        return [(mine, swap_cores(theirs)) for mine, theirs in zip(made[:len(spans)], made[len(spans):])]

    def grads(masks, offset, cw, mine, theirs, after):
        return call(
            "grads", functools.partial(grad_kernel, offset=offset, heads=cw // HEAD_DIM, groups=groups, **sizes),
            (*inputs, *masks, mine, theirs), [shape_of(3, part, cw, dtype=bf16)] * groups,
            [pltpu.VMEM((3, rows, cw), bf16)], after, GRAD_LIMIT,
        )

    def local(masks, offset, cw):
        kernel = functools.partial(local_kernel, offset=offset, heads=cw // HEAD_DIM)
        return call(
            "local", kernel, (*inputs, *masks), [shape_of(3, rows, cw), shape_of(8, HEAD_DIM)], limit=GRAD_LIMIT,
        )

    def first_carry(near, offset, cw, mine, theirs):
        more = dict(offset=offset, heads=cw // HEAD_DIM, **sizes)
        near = call(
            "add_mine", functools.partial(add_mine_kernel, **more), (*inputs[1:], near, mine), [shape_of(3, rows, cw)],
            limit=GRAD_LIMIT, same={4: 0},
        )[0]
        return call(
            "add_got", functools.partial(add_got_kernel, groups=groups, **more), (*inputs[1:], near, theirs),
            [shape_of(3, part, cw, dtype=bf16)] * groups, [pltpu.VMEM((3, rows, cw), bf16)], limit=GRAD_LIMIT,
        )

    def carry(near, offset, cw, mine, theirs, after):
        kernel = functools.partial(carry_kernel, offset=offset, heads=cw // HEAD_DIM, groups=groups, **sizes)
        return call(
            "carry", kernel, (*inputs[1:], near, mine, theirs), [shape_of(3, part, cw, dtype=bf16)] * groups,
            [pltpu.VMEM((3, rows, cw), bf16)], after, GRAD_LIMIT,
        )

    cuts, outs, arrived, totals, masks = [], [], [], [], None
    for start, half, chunks in halves:
        if not totals:
            (sent,) = states(False, start, half)
            kept, *masks = states(True, start, half)
        else:
            kept, sent = late_states(start, half, [token])
        total, came, others = pair_up(
            kept, swap_cores(sent), 0 if totals else len(chunks), [made[0] for made in outs[:1]]
        )
        if not totals:
            near = [local(masks, *chunk) for chunk in chunks]
            token = near[0][1]
        count = chunks[0][1] // HEAD_DIM
        if totals:
            spans = [(c * count, c * count, count) for c in range(len(chunks))]
            joined = join(spans, [swap_cores(kept)] * len(chunks), came, [arrived[0][1]])
        else:
            spans = [(0, c * count, count) for c in range(len(chunks))]
            joined = join(spans, others, came, [made[1] for made in near])
        for c, ((offset, cw), (mine, theirs)) in enumerate(zip(chunks, joined)):
            after = [made[0] for made in outs[-1:]] + [parts[1] for parts in arrived[1:-1]][-1:]
            if totals:
                outs.append(grads(masks, offset, cw, mine, theirs, after))
            elif c == 0:
                outs.append(first_carry(near[c][0], offset, cw, mine, theirs))
            else:
                outs.append(carry(near[c][0], offset, cw, mine, theirs, after))
            arrived.append(send_rows(outs[-1]))
        totals = [total]
        cuts += chunks

    placed = []
    for c in range(len(cuts)):
        own = [0, 1] if c == 0 else [c + 1]
        plan = [(arrived[n][0], (0, *cuts[n])) for n in own if n < len(cuts)]
        plan += [(arrived[c][j], (j, *cuts[c])) for j in range(1, groups)]
        some = [array for array, _ in plan]
        placed = pl.pallas_call(
            functools.partial(place_kernel, groups=groups, plan=[where for _, where in plan], width=width),
            grid_spec=pl.GridSpec(
                grid=(1,), in_specs=[anywhere] * (len(some) + len(placed)), out_specs=[anywhere] * 3,
                scratch_shapes=[pltpu.SemaphoreType.DMA((3 * len(some),))],
            ),
            out_shape=[shape_of(part, width * groups, dtype=bf16)] * 3,
            input_output_aliases={len(some) + i: i for i in range(len(placed))},
            cost_estimate=cheap,
            compiler_params=pltpu.CompilerParams(vmem_limit_bytes=VMEM_LIMIT), name="place",
        )(*some, *placed)
    return tuple(placed)


def solution(mesh):
    return jax.shard_map(
        shards,
        mesh=mesh,
        in_specs=(P("seq", "head"), P("seq", "head"), P("seq", "head"), P("seq", "head"), P()),
        out_specs=(P(("seq", "head"), None), P(("seq", "head"), None), P(("seq", "head"), None)),
        check_vma=False,
    )
```

```python
import functools

import jax
import jax.numpy as jnp
from jax import lax
from jax.experimental import pallas as pl
from jax.experimental.pallas import tpu as pltpu
from jax.sharding import PartitionSpec as P

HEAD_DIM = 128
MOST = 1024
GROUP = 4
CHUNK = 4
PAD = 16
LINK = jnp.bfloat16
VMEM_LIMIT = 16 * 1024 * 1024
GRAD_LIMIT = 32 * 1024 * 1024
FIRST_LIMIT = 53 * 1024 * 1024
KEPT_LIMIT = 53 * 1024 * 1024
NT = (((1,), (1,)), ((), ()))
TN = (((0,), (0,)), ((), ()))
NN = (((1,), (0,)), ((), ()))


def dot(a, b, dims):
    return lax.dot_general(a, b, dims, preferred_element_type=jnp.float32)


def doc_at(meta, ndocs, position):
    start, begin, end = jnp.int32(0), jnp.int32(0), jnp.int32(0)
    for i in range(ndocs):
        stop = start + meta[i]
        begin = jnp.where(start <= position, start, begin)
        end = jnp.where(start <= position, stop, end)
        start = stop
    return begin, end


def block_range(meta, ndocs, base, rows):
    begin0, end0 = doc_at(meta, ndocs, base)
    begin1, end1 = doc_at(meta, ndocs, base + rows - 1)
    first = jnp.where(begin0 < base, end0, base) - base
    return begin0, end0, begin1, end1, first, begin1 - base


def make_masks(lengths, lower, upper, ndocs, rows):
    line = lax.broadcasted_iota(jnp.int32, (rows, rows), 0)
    across = lax.broadcasted_iota(jnp.int32, (rows, rows), 1)
    begin_line = jnp.zeros((rows, rows), jnp.int32)
    begin_across = jnp.zeros((rows, rows), jnp.int32)
    start = jnp.int32(0) - lax.axis_index("seq") * rows
    for i in range(ndocs):
        begin_line = jnp.where(line >= start, start, begin_line)
        begin_across = jnp.where(across >= start, start, begin_across)
        start = start + lengths[i]
    lower[...] = jnp.where((across <= line) & (across >= begin_line), 1.0, 0.0).astype(lower.dtype)
    upper[...] = jnp.where((line <= across) & (line >= begin_across), 1.0, 0.0).astype(upper.dtype)


def state_kernel(lengths, q, k, v, g, out, *rest, ndocs, rows, offset, heads, group, kept):
    *masks, held, sems, known, got = rest
    gw = group * HEAD_DIM
    place = lax.axis_index("seq")
    first_core = lax.rem(place, 2) == 0

    tails = first_core if kept else jnp.logical_not(first_core)

    def copy(c, i, ref):
        src = ref.at[:, pl.ds(offset + c * gw, gw)]
        return pltpu.make_async_copy(src, held.at[i, :, pl.ds(c * gw, gw)], sems.at[c, i])

    fetch = pltpu.make_async_copy(lengths, known, got)
    fetch.start()
    for c in range(heads // group):

        @pl.when(tails)
        def _():
            copy(c, 0, k).start()
            copy(c, 1, v).start()

        @pl.when(jnp.logical_not(tails))
        def _():
            copy(c, 0, q).start()
            copy(c, 1, g).start()

    fetch.wait()
    if masks:
        make_masks(known, *masks, ndocs, rows)
    _, _, _, _, first, last = block_range(known, ndocs, place * rows, rows)
    order = lax.broadcasted_iota(jnp.int32, (rows, HEAD_DIM), 0)
    zero = jnp.zeros((), held.dtype)
    low, high = jnp.where(tails, last, 0), jnp.where(tails, rows, first)
    here = (order >= low) & (order < high)
    for h in range(heads):
        if h % group == 0:
            copy(h // group, 0, k).wait()
            copy(h // group, 1, v).wait()
        cols = slice(h * HEAD_DIM, (h + 1) * HEAD_DIM)
        out[h] = dot(jnp.where(here, held[0, :, cols], zero), held[1, :, cols], TN)


def late_state_kernel(lengths, q, k, v, g, *rest, ndocs, rows, offset, heads):
    kept, sent = rest[-2:]
    first_core, first_rows, last_rows = own_range(lengths, ndocs, rows)
    zero = jnp.zeros((), q.dtype)
    for h in range(heads):
        at = slice(offset + h * HEAD_DIM, offset + (h + 1) * HEAD_DIM)
        tail = dot(jnp.where(last_rows, k[:, at], zero), v[:, at], TN)
        head = dot(jnp.where(first_rows, q[:, at], zero), g[:, at], TN)
        kept[h] = jnp.where(first_core, tail, head)
        sent[h] = jnp.where(first_core, head, tail)


def pair_kernel(lengths, kept, got, *rest, ndocs, rows, hops, copies):
    sent, again = rest[-hops - copies:len(rest) - copies], rest[len(rest) - copies:]
    place = lax.axis_index("seq")
    first_core = lax.rem(place, 2) == 0
    even = (place - lax.rem(place, 2)) * rows
    odd = even + rows
    _, even_e0 = doc_at(lengths, ndocs, even)
    odd_b1, _ = doc_at(lengths, ndocs, odd + rows - 1)
    joins = jnp.where(jnp.where(first_core, odd_b1 < odd, even_e0 > odd), 1.0, 0.0)
    size = kept.shape[0] * HEAD_DIM
    total = (got[...] + joins * kept[...]).astype(LINK).reshape(size, HEAD_DIM)
    for out in sent:
        out[:size] = total
        if out.shape[0] > size:
            out[size:] = jnp.zeros((out.shape[0] - size, HEAD_DIM), LINK)
    for i, out in enumerate(again):
        count = out.shape[0]
        out[...] = kept[i * count:(i + 1) * count]


def join_kernel(lengths, *rest, ndocs, rows, spans, hops):
    others, came = rest[:len(spans)], rest[len(spans):len(spans) + hops]
    mine, theirs = rest[-2 * len(spans):-len(spans)], rest[-len(spans):]
    place = lax.axis_index("seq")
    first_core = lax.rem(place, 2) == 0
    even = (place - lax.rem(place, 2)) * rows
    odd = even + rows
    even_b0, _ = doc_at(lengths, ndocs, even)
    _, even_e1 = doc_at(lengths, ndocs, odd - 1)
    odd_b0, _ = doc_at(lengths, ndocs, odd)
    _, odd_e1 = doc_at(lengths, ndocs, odd + rows - 1)

    def one(if_first, if_second):
        return jnp.where(jnp.where(first_core, if_first, if_second), 1.0, 0.0)

    weights = [
        one(odd + rows + hop * 2 * rows < odd_e1, even - hop * 2 * rows > even_b0) for hop in range(hops)
    ]
    from_other, from_pair = one(odd < even_e1, odd > odd_b0), one(odd + rows < even_e1, even > odd_b0)
    for c, (other_at, came_at, count) in enumerate(spans):
        lines = slice(came_at * HEAD_DIM, (came_at + count) * HEAD_DIM)
        total = weights[0] * came[0][lines].astype(jnp.float32)
        for hop in range(1, hops):
            total = total + weights[hop] * came[hop][lines].astype(jnp.float32)
        total = total.reshape(count, HEAD_DIM, HEAD_DIM)
        theirs[c][...] = total
        mine[c][...] = from_other * others[c][other_at:other_at + count] + from_pair * total


def split(a, axis):
    high = a.astype(jnp.bfloat16)
    return jnp.concatenate([high, (a - high.astype(jnp.float32)).astype(jnp.bfloat16)], axis=axis)


def own_range(lengths, ndocs, rows):
    place = lax.axis_index("seq")
    _, _, _, _, first, last = block_range(lengths, ndocs, place * rows, rows)
    order = lax.broadcasted_iota(jnp.int32, (rows, HEAD_DIM), 0)
    return lax.rem(place, 2) == 0, order < first, order >= last


def local_part(q, k, v, g, lower, upper, at):
    qh, kh, vh, gh = (ref[:, at] for ref in (q, k, v, g))
    weight_gv = dot(gh, vh, NT).astype(jnp.bfloat16) * lower[...]
    weight_vg = dot(vh, gh, NT).astype(jnp.bfloat16) * upper[...]
    weight_kq = dot(kh, qh, NT).astype(jnp.bfloat16) * upper[...]
    return dot(weight_gv, kh, NN), dot(weight_vg, qh, NN), dot(weight_kq, gh, NN)


def twice(ref, at):
    return jnp.concatenate([ref[:, at]] * 2, axis=1)


def carry_of_state(g, state, first_rows, at):
    return jnp.where(first_rows, dot(twice(g, at), split(state, 1), NT), 0.0)


def carries_of_grad(k, v, grad, last_rows, at):
    carry_k = jnp.where(last_rows, dot(twice(v, at), split(grad, 1), NT), 0.0)
    return carry_k, jnp.where(last_rows, dot(twice(k, at), split(grad, 0), NN), 0.0)


def deal(done, outs, rows, groups):
    part, column = rows // groups, lax.axis_index("head")
    for j in range(groups):
        at = pl.ds(pl.multiple_of(lax.rem(column + j, groups) * part, part), part)
        for i in range(3):
            outs[j][i] = done[i, at, :]


def grad_kernel(lengths, q, k, v, g, lower, upper, mine, got, *rest, ndocs, rows, offset, heads, groups):
    outs, done = rest[-1 - groups:-1], rest[-1]
    first_core, first_rows, last_rows = own_range(lengths, ndocs, rows)
    for h in range(heads):
        cols = slice(h * HEAD_DIM, (h + 1) * HEAD_DIM)
        at = slice(offset + h * HEAD_DIM, offset + (h + 1) * HEAD_DIM)
        state = jnp.where(first_core, got[h], mine[h])
        grad = jnp.where(first_core, mine[h], got[h])
        near = local_part(q, k, v, g, lower, upper, at)
        carries = (carry_of_state(g, state, first_rows, at), *carries_of_grad(k, v, grad, last_rows, at))
        for i in range(3):
            done[i, :, cols] = (near[i] + carries[i]).astype(jnp.bfloat16)
    deal(done, outs, rows, groups)


def local_kernel(lengths, q, k, v, g, lower, upper, near, token, *, offset, heads):
    token[...] = jnp.zeros_like(token)
    for h in range(heads):
        cols = slice(h * HEAD_DIM, (h + 1) * HEAD_DIM)
        at = slice(offset + h * HEAD_DIM, offset + (h + 1) * HEAD_DIM)
        for i, value in enumerate(local_part(q, k, v, g, lower, upper, at)):
            near[i, :, cols] = value


def carry_kernel(lengths, k, v, g, near, mine, got, *rest, ndocs, rows, offset, heads, groups):
    outs, done = rest[-1 - groups:-1], rest[-1]
    first_core, first_rows, last_rows = own_range(lengths, ndocs, rows)
    for h in range(heads):
        cols = slice(h * HEAD_DIM, (h + 1) * HEAD_DIM)
        at = slice(offset + h * HEAD_DIM, offset + (h + 1) * HEAD_DIM)
        state = jnp.where(first_core, got[h], mine[h])
        grad = jnp.where(first_core, mine[h], got[h])
        carries = (carry_of_state(g, state, first_rows, at), *carries_of_grad(k, v, grad, last_rows, at))
        for i in range(3):
            done[i, :, cols] = (near[i, :, cols] + carries[i]).astype(jnp.bfloat16)
    deal(done, outs, rows, groups)


def place_kernel(*refs, groups, plan, width):
    parts, outs, sems = refs[:len(plan)], refs[-4:-1], refs[-1]
    column = lax.axis_index("head")
    copies = []
    for ref, (j, offset, cw) in zip(parts, plan):
        start = pl.multiple_of(lax.rem(column + groups - j, groups) * width + offset, 128)
        for i in range(3):
            copies.append(pltpu.make_async_copy(ref.at[i], outs[i].at[:, pl.ds(start, cw)], sems.at[len(copies)]))
            copies[-1].start()
    for copy in copies:
        copy.wait()


def cuts_of(width):
    heads = width // HEAD_DIM
    size = CHUNK if heads % (2 * CHUNK) == 0 else 2
    cw, half = size * HEAD_DIM, max(heads // 2, size) * HEAD_DIM
    return [(at, half, [(o, cw) for o in range(at, at + half, cw)]) for at in range(0, width, half)]


def shards(queries, keys, values, out_grad, doc_lengths):
    rows, width = queries.shape
    ndocs = doc_lengths.shape[0]
    seq, groups = lax.axis_size("seq"), lax.axis_size("head")
    pairs = seq // 2
    hops = -(-MOST // (2 * rows))
    halves = cuts_of(width)
    part = rows // groups
    anywhere = pl.BlockSpec(memory_space=pl.ANY)
    in_vmem = pl.BlockSpec(memory_space=pltpu.VMEM)
    in_smem = pl.BlockSpec(memory_space=pltpu.SMEM)
    f32, bf16 = jnp.float32, jnp.bfloat16
    inputs = (queries, keys, values, out_grad)
    sizes = dict(ndocs=ndocs, rows=rows)
    cheap = pl.CostEstimate(flops=0, bytes_accessed=1024, transcendentals=0)

    def shape_of(*dims, dtype=f32):
        return jax.ShapeDtypeStruct(dims, dtype)

    def call(name, kernel, args, outs, scratch=(), after=(), limit=VMEM_LIMIT):
        return pl.pallas_call(
            kernel, in_specs=[in_smem] + [in_vmem] * len(args) + [anywhere] * len(after), out_specs=[in_vmem] * len(outs), out_shape=outs,
            scratch_shapes=list(scratch), cost_estimate=cheap,
            compiler_params=pltpu.CompilerParams(vmem_limit_bytes=limit), name=name,
        )(doc_lengths, *args, *after)

    def swap_cores(a):
        return lax.ppermute(a, "seq", [(b, b ^ 1) for b in range(seq)])

    def swap_pairs(sent):
        came = []
        for hop in range(1, hops + 1):
            perm = [(2 * m, 2 * (m + hop) + 1) for m in range(pairs - hop)]
            came.append(lax.ppermute(sent[hop - 1], "seq", perm + [(b, a) for a, b in perm]))
        return came

    def send_rows(outs):
        arrived = list(outs[:1])
        for j in range(1, groups):
            arrived.append(lax.ppermute(outs[j], "head", [(x, (x + j) % groups) for x in range(groups)]))
        return arrived

    square = (HEAD_DIM, HEAD_DIM)

    def states(kept, offset, half):
        heads = half // HEAD_DIM
        group = GROUP if heads % GROUP == 0 else 2
        outs = [shape_of(heads, *square)] + [shape_of(rows, rows, dtype=bf16)] * (2 * kept)
        return pl.pallas_call(
            functools.partial(state_kernel, offset=offset, heads=heads, group=group, kept=kept, **sizes),
            in_specs=[anywhere] * 5, out_specs=[in_vmem] * len(outs), out_shape=outs,
            scratch_shapes=[
                pltpu.VMEM((2, rows, half), bf16), pltpu.SemaphoreType.DMA((heads // group, 2)),
                pltpu.SMEM((ndocs,), jnp.int32), pltpu.SemaphoreType.DMA,
            ],
            cost_estimate=cheap, compiler_params=pltpu.CompilerParams(vmem_limit_bytes=KEPT_LIMIT if kept else FIRST_LIMIT), name="states",
        )(doc_lengths, *inputs)

    def late_states(offset, half, after):
        heads = half // HEAD_DIM
        return call(
            "states", functools.partial(late_state_kernel, offset=offset, heads=heads, **sizes), inputs,
            [shape_of(heads, *square)] * 2, after=after, limit=GRAD_LIMIT,
        )

    def pair_up(kept, got, copies, after):
        lines = kept.shape[0] * HEAD_DIM
        outs = [shape_of(lines + PAD * (hops - hop + 1), HEAD_DIM, dtype=LINK) for hop in range(1, hops + 1)]
        outs += [shape_of(kept.shape[0] // max(copies, 1), *square)] * copies
        made = call(
            "pair", functools.partial(pair_kernel, hops=hops, copies=copies, **sizes), (kept, got), outs, after=after
        )
        return made[hops - 1], swap_pairs(made[:hops]), [swap_cores(a) for a in made[hops:]]

    def join(spans, others, came, after):
        made = call(
            "join", functools.partial(join_kernel, spans=spans, hops=hops, **sizes), (*others, *came),
            [shape_of(count, *square) for _, _, count in spans] * 2, after=after,
        )
        return [(mine, swap_cores(theirs)) for mine, theirs in zip(made[:len(spans)], made[len(spans):])]

    def grads(masks, offset, cw, mine, theirs, after):
        return call(
            "grads", functools.partial(grad_kernel, offset=offset, heads=cw // HEAD_DIM, groups=groups, **sizes),
            (*inputs, *masks, mine, theirs), [shape_of(3, part, cw, dtype=bf16)] * groups,
            [pltpu.VMEM((3, rows, cw), bf16)], after, GRAD_LIMIT,
        )

    def local(masks, offset, cw):
        kernel = functools.partial(local_kernel, offset=offset, heads=cw // HEAD_DIM)
        return call(
            "local", kernel, (*inputs, *masks), [shape_of(3, rows, cw), shape_of(8, HEAD_DIM)], limit=GRAD_LIMIT,
        )

    def carry(near, offset, cw, mine, theirs, after):
        kernel = functools.partial(carry_kernel, offset=offset, heads=cw // HEAD_DIM, groups=groups, **sizes)
        return call(
            "carry", kernel, (*inputs[1:], near, mine, theirs), [shape_of(3, part, cw, dtype=bf16)] * groups,
            [pltpu.VMEM((3, rows, cw), bf16)], after, GRAD_LIMIT,
        )

    cuts, outs, arrived, totals, masks = [], [], [], [], None
    for start, half, chunks in halves:
        if not totals:
            (sent,) = states(False, start, half)
            kept, *masks = states(True, start, half)
        else:
            kept, sent = late_states(start, half, [token])
        total, came, others = pair_up(
            kept, swap_cores(sent), 0 if totals else len(chunks), [made[0] for made in outs[:1]]
        )
        if not totals:
            near = [local(masks, *chunk) for chunk in chunks]
            token = near[0][1]
        count = chunks[0][1] // HEAD_DIM
        if totals:
            spans = [(c * count, c * count, count) for c in range(len(chunks))]
            joined = join(spans, [swap_cores(kept)] * len(chunks), came, [arrived[0][1]])
        else:
            joined, after = [], [made[1] for made in near]
            for c in range(len(chunks)):
                joined += join([(0, c * count, count)], others[c:c + 1], came, after)
                after = [joined[-1][0]]
        for c, ((offset, cw), (mine, theirs)) in enumerate(zip(chunks, joined)):
            after = [made[0] for made in outs[-1:]] + [parts[1] for parts in arrived[1:-1]][-1:]
            if totals:
                outs.append(grads(masks, offset, cw, mine, theirs, after))
            else:
                outs.append(carry(near[c][0], offset, cw, mine, theirs, after or [made for made, _ in joined[1:]]))
            arrived.append(send_rows(outs[-1]))
        totals = [total]
        cuts += chunks

    placed = []
    for c in range(len(cuts)):
        own = [0, 1] if c == 0 else [c + 1]
        plan = [(arrived[n][0], (0, *cuts[n])) for n in own if n < len(cuts)]
        plan += [(arrived[c][j], (j, *cuts[c])) for j in range(1, groups)]
        some = [array for array, _ in plan]
        placed = pl.pallas_call(
            functools.partial(place_kernel, groups=groups, plan=[where for _, where in plan], width=width),
            grid_spec=pl.GridSpec(
                grid=(1,), in_specs=[anywhere] * (len(some) + len(placed)), out_specs=[anywhere] * 3,
                scratch_shapes=[pltpu.SemaphoreType.DMA((3 * len(some),))],
            ),
            out_shape=[shape_of(part, width * groups, dtype=bf16)] * 3,
            input_output_aliases={len(some) + i: i for i in range(len(placed))},
            cost_estimate=cheap,
            compiler_params=pltpu.CompilerParams(vmem_limit_bytes=VMEM_LIMIT), name="place",
        )(*some, *placed)
    return tuple(placed)


def solution(mesh):
    return jax.shard_map(
        shards,
        mesh=mesh,
        in_specs=(P("seq", "head"), P("seq", "head"), P("seq", "head"), P("seq", "head"), P()),
        out_specs=(P(("seq", "head"), None), P(("seq", "head"), None), P(("seq", "head"), None)),
        check_vma=False,
    )
```

```python
import functools

import jax
import jax.numpy as jnp
from jax import lax
from jax.experimental import pallas as pl
from jax.experimental.pallas import tpu as pltpu
from jax.sharding import PartitionSpec as P

HEAD_DIM = 128
MOST = 1024
GROUP = 4
CHUNK = 4
PAD = 16
LINK = jnp.bfloat16
VMEM_LIMIT = 16 * 1024 * 1024
GRAD_LIMIT = 32 * 1024 * 1024
FIRST_LIMIT = 53 * 1024 * 1024
KEPT_LIMIT = 53 * 1024 * 1024
NT = (((1,), (1,)), ((), ()))
TN = (((0,), (0,)), ((), ()))
NN = (((1,), (0,)), ((), ()))


def dot(a, b, dims):
    return lax.dot_general(a, b, dims, preferred_element_type=jnp.float32)


def doc_at(meta, ndocs, position):
    start, begin, end = jnp.int32(0), jnp.int32(0), jnp.int32(0)
    for i in range(ndocs):
        stop = start + meta[i]
        begin = jnp.where(start <= position, start, begin)
        end = jnp.where(start <= position, stop, end)
        start = stop
    return begin, end


def block_range(meta, ndocs, base, rows):
    begin0, end0 = doc_at(meta, ndocs, base)
    begin1, end1 = doc_at(meta, ndocs, base + rows - 1)
    first = jnp.where(begin0 < base, end0, base) - base
    return begin0, end0, begin1, end1, first, begin1 - base


def make_masks(lengths, lower, upper, ndocs, rows):
    line = lax.broadcasted_iota(jnp.int32, (rows, rows), 0)
    across = lax.broadcasted_iota(jnp.int32, (rows, rows), 1)
    begin_line = jnp.zeros((rows, rows), jnp.int32)
    begin_across = jnp.zeros((rows, rows), jnp.int32)
    start = jnp.int32(0) - lax.axis_index("seq") * rows
    for i in range(ndocs):
        begin_line = jnp.where(line >= start, start, begin_line)
        begin_across = jnp.where(across >= start, start, begin_across)
        start = start + lengths[i]
    lower[...] = jnp.where((across <= line) & (across >= begin_line), 1.0, 0.0).astype(lower.dtype)
    upper[...] = jnp.where((line <= across) & (line >= begin_across), 1.0, 0.0).astype(upper.dtype)


def state_kernel(lengths, q, k, v, g, out, *rest, ndocs, rows, offset, heads, group, kept):
    *masks, held, sems, known, got = rest
    gw = group * HEAD_DIM
    place = lax.axis_index("seq")
    first_core = lax.rem(place, 2) == 0

    tails = first_core if kept else jnp.logical_not(first_core)

    def copy(c, i, ref):
        src = ref.at[:, pl.ds(offset + c * gw, gw)]
        return pltpu.make_async_copy(src, held.at[i, :, pl.ds(c * gw, gw)], sems.at[c, i])

    fetch = pltpu.make_async_copy(lengths, known, got)
    fetch.start()
    for c in range(heads // group):

        @pl.when(tails)
        def _():
            copy(c, 0, k).start()
            copy(c, 1, v).start()

        @pl.when(jnp.logical_not(tails))
        def _():
            copy(c, 0, q).start()
            copy(c, 1, g).start()

    fetch.wait()
    if masks:
        make_masks(known, *masks, ndocs, rows)
    _, _, _, _, first, last = block_range(known, ndocs, place * rows, rows)
    order = lax.broadcasted_iota(jnp.int32, (rows, HEAD_DIM), 0)
    zero = jnp.zeros((), held.dtype)
    low, high = jnp.where(tails, last, 0), jnp.where(tails, rows, first)
    here = (order >= low) & (order < high)
    for h in range(heads):
        if h % group == 0:
            copy(h // group, 0, k).wait()
            copy(h // group, 1, v).wait()
        cols = slice(h * HEAD_DIM, (h + 1) * HEAD_DIM)
        out[h] = dot(jnp.where(here, held[0, :, cols], zero), held[1, :, cols], TN)


def late_state_kernel(lengths, q, k, v, g, *rest, ndocs, rows, offset, heads):
    kept, sent = rest[-2:]
    first_core, first_rows, last_rows = own_range(lengths, ndocs, rows)
    zero = jnp.zeros((), q.dtype)
    for h in range(heads):
        at = slice(offset + h * HEAD_DIM, offset + (h + 1) * HEAD_DIM)
        tail = dot(jnp.where(last_rows, k[:, at], zero), v[:, at], TN)
        head = dot(jnp.where(first_rows, q[:, at], zero), g[:, at], TN)
        kept[h] = jnp.where(first_core, tail, head)
        sent[h] = jnp.where(first_core, head, tail)


def pair_kernel(lengths, kept, got, *rest, ndocs, rows, hops, copies):
    sent, again = rest[-hops - copies:len(rest) - copies], rest[len(rest) - copies:]
    place = lax.axis_index("seq")
    first_core = lax.rem(place, 2) == 0
    even = (place - lax.rem(place, 2)) * rows
    odd = even + rows
    _, even_e0 = doc_at(lengths, ndocs, even)
    odd_b1, _ = doc_at(lengths, ndocs, odd + rows - 1)
    joins = jnp.where(jnp.where(first_core, odd_b1 < odd, even_e0 > odd), 1.0, 0.0)
    size = kept.shape[0] * HEAD_DIM
    total = (got[...] + joins * kept[...]).astype(LINK).reshape(size, HEAD_DIM)
    for out in sent:
        out[:size] = total
        if out.shape[0] > size:
            out[size:] = jnp.zeros((out.shape[0] - size, HEAD_DIM), LINK)
    for i, out in enumerate(again):
        count = out.shape[0]
        out[...] = kept[i * count:(i + 1) * count]


def join_kernel(lengths, *rest, ndocs, rows, spans, hops):
    others, came = rest[:len(spans)], rest[len(spans):len(spans) + hops]
    mine, theirs = rest[-2 * len(spans):-len(spans)], rest[-len(spans):]
    place = lax.axis_index("seq")
    first_core = lax.rem(place, 2) == 0
    even = (place - lax.rem(place, 2)) * rows
    odd = even + rows
    even_b0, _ = doc_at(lengths, ndocs, even)
    _, even_e1 = doc_at(lengths, ndocs, odd - 1)
    odd_b0, _ = doc_at(lengths, ndocs, odd)
    _, odd_e1 = doc_at(lengths, ndocs, odd + rows - 1)

    def one(if_first, if_second):
        return jnp.where(jnp.where(first_core, if_first, if_second), 1.0, 0.0)

    weights = [
        one(odd + rows + hop * 2 * rows < odd_e1, even - hop * 2 * rows > even_b0) for hop in range(hops)
    ]
    from_other, from_pair = one(odd < even_e1, odd > odd_b0), one(odd + rows < even_e1, even > odd_b0)
    for c, (other_at, came_at, count) in enumerate(spans):
        lines = slice(came_at * HEAD_DIM, (came_at + count) * HEAD_DIM)
        total = weights[0] * came[0][lines].astype(jnp.float32)
        for hop in range(1, hops):
            total = total + weights[hop] * came[hop][lines].astype(jnp.float32)
        total = total.reshape(count, HEAD_DIM, HEAD_DIM)
        theirs[c][...] = total
        mine[c][...] = from_other * others[c][other_at:other_at + count] + from_pair * total


def split(a, axis):
    high = a.astype(jnp.bfloat16)
    return jnp.concatenate([high, (a - high.astype(jnp.float32)).astype(jnp.bfloat16)], axis=axis)


def own_range(lengths, ndocs, rows):
    place = lax.axis_index("seq")
    _, _, _, _, first, last = block_range(lengths, ndocs, place * rows, rows)
    order = lax.broadcasted_iota(jnp.int32, (rows, HEAD_DIM), 0)
    return lax.rem(place, 2) == 0, order < first, order >= last


def local_part(q, k, v, g, lower, upper, at):
    qh, kh, vh, gh = (ref[:, at] for ref in (q, k, v, g))
    weight_gv = dot(gh, vh, NT).astype(jnp.bfloat16) * lower[...]
    weight_vg = dot(vh, gh, NT).astype(jnp.bfloat16) * upper[...]
    weight_kq = dot(kh, qh, NT).astype(jnp.bfloat16) * upper[...]
    return dot(weight_gv, kh, NN), dot(weight_vg, qh, NN), dot(weight_kq, gh, NN)


def twice(ref, at):
    return jnp.concatenate([ref[:, at]] * 2, axis=1)


def carry_of_state(g, state, first_rows, at):
    return jnp.where(first_rows, dot(twice(g, at), split(state, 1), NT), 0.0)


def carries_of_grad(k, v, grad, last_rows, at):
    carry_k = jnp.where(last_rows, dot(twice(v, at), split(grad, 1), NT), 0.0)
    return carry_k, jnp.where(last_rows, dot(twice(k, at), split(grad, 0), NN), 0.0)


def deal(done, outs, rows, groups):
    part, column = rows // groups, lax.axis_index("head")
    for j in range(groups):
        at = pl.ds(pl.multiple_of(lax.rem(column + j, groups) * part, part), part)
        for i in range(3):
            outs[j][i] = done[i, at, :]


def grad_kernel(lengths, q, k, v, g, lower, upper, mine, got, *rest, ndocs, rows, offset, heads, groups):
    outs, done = rest[-1 - groups:-1], rest[-1]
    first_core, first_rows, last_rows = own_range(lengths, ndocs, rows)
    for h in range(heads):
        cols = slice(h * HEAD_DIM, (h + 1) * HEAD_DIM)
        at = slice(offset + h * HEAD_DIM, offset + (h + 1) * HEAD_DIM)
        state = jnp.where(first_core, got[h], mine[h])
        grad = jnp.where(first_core, mine[h], got[h])
        near = local_part(q, k, v, g, lower, upper, at)
        carries = (carry_of_state(g, state, first_rows, at), *carries_of_grad(k, v, grad, last_rows, at))
        for i in range(3):
            done[i, :, cols] = (near[i] + carries[i]).astype(jnp.bfloat16)
    deal(done, outs, rows, groups)


def local_kernel(lengths, q, k, v, g, lower, upper, near, token, *, offset, heads):
    token[...] = jnp.zeros_like(token)
    for h in range(heads):
        cols = slice(h * HEAD_DIM, (h + 1) * HEAD_DIM)
        at = slice(offset + h * HEAD_DIM, offset + (h + 1) * HEAD_DIM)
        for i, value in enumerate(local_part(q, k, v, g, lower, upper, at)):
            near[i, :, cols] = value


def carry_kernel(lengths, k, v, g, near, mine, got, *rest, ndocs, rows, offset, heads, groups):
    outs, done = rest[-1 - groups:-1], rest[-1]
    first_core, first_rows, last_rows = own_range(lengths, ndocs, rows)
    for h in range(heads):
        cols = slice(h * HEAD_DIM, (h + 1) * HEAD_DIM)
        at = slice(offset + h * HEAD_DIM, offset + (h + 1) * HEAD_DIM)
        state = jnp.where(first_core, got[h], mine[h])
        grad = jnp.where(first_core, mine[h], got[h])
        carries = (carry_of_state(g, state, first_rows, at), *carries_of_grad(k, v, grad, last_rows, at))
        for i in range(3):
            done[i, :, cols] = (near[i, :, cols] + carries[i]).astype(jnp.bfloat16)
    deal(done, outs, rows, groups)


def carry_rows_kernel(lengths, k, v, g, near, mine, got, *rest, ndocs, rows, offset, heads, groups, shifts):
    outs = rest[-len(shifts):]
    place, column, part = lax.axis_index("seq"), lax.axis_index("head"), rows // groups
    first_core = lax.rem(place, 2) == 0
    _, _, _, _, first, last = block_range(lengths, ndocs, place * rows, rows)
    order = lax.broadcasted_iota(jnp.int32, (part, HEAD_DIM), 0)
    for j, out in zip(shifts, outs):
        start = pl.multiple_of(lax.rem(column + j, groups) * part, part)
        lines = pl.ds(start, part)
        first_rows, last_rows = order + start < first, order + start >= last
        for h in range(heads):
            cols = slice(h * HEAD_DIM, (h + 1) * HEAD_DIM)
            at = slice(offset + h * HEAD_DIM, offset + (h + 1) * HEAD_DIM)
            state = split(jnp.where(first_core, got[h], mine[h]), 1)
            grad = jnp.where(first_core, mine[h], got[h])
            k2, v2, g2 = (jnp.concatenate([ref[lines, at]] * 2, axis=1) for ref in (k, v, g))
            carry_q = jnp.where(first_rows, dot(g2, state, NT), 0.0)
            carry_k = jnp.where(last_rows, dot(v2, split(grad, 1), NT), 0.0)
            carry_v = jnp.where(last_rows, dot(k2, split(grad, 0), NN), 0.0)
            for i, value in enumerate((carry_q, carry_k, carry_v)):
                out[i, :, cols] = (near[i, lines, cols] + value).astype(jnp.bfloat16)


def place_kernel(*refs, groups, plan, width):
    parts, outs, sems = refs[:len(plan)], refs[-4:-1], refs[-1]
    column = lax.axis_index("head")
    copies = []
    for ref, (j, offset, cw) in zip(parts, plan):
        start = pl.multiple_of(lax.rem(column + groups - j, groups) * width + offset, 128)
        for i in range(3):
            copies.append(pltpu.make_async_copy(ref.at[i], outs[i].at[:, pl.ds(start, cw)], sems.at[len(copies)]))
            copies[-1].start()
    for copy in copies:
        copy.wait()


def cuts_of(width):
    heads = width // HEAD_DIM
    size = CHUNK if heads % (2 * CHUNK) == 0 else 2
    cw, half = size * HEAD_DIM, max(heads // 2, size) * HEAD_DIM
    return [(at, half, [(o, cw) for o in range(at, at + half, cw)]) for at in range(0, width, half)]


def shards(queries, keys, values, out_grad, doc_lengths):
    rows, width = queries.shape
    ndocs = doc_lengths.shape[0]
    seq, groups = lax.axis_size("seq"), lax.axis_size("head")
    pairs = seq // 2
    hops = -(-MOST // (2 * rows))
    halves = cuts_of(width)
    part = rows // groups
    anywhere = pl.BlockSpec(memory_space=pl.ANY)
    in_vmem = pl.BlockSpec(memory_space=pltpu.VMEM)
    in_smem = pl.BlockSpec(memory_space=pltpu.SMEM)
    f32, bf16 = jnp.float32, jnp.bfloat16
    inputs = (queries, keys, values, out_grad)
    sizes = dict(ndocs=ndocs, rows=rows)
    cheap = pl.CostEstimate(flops=0, bytes_accessed=1024, transcendentals=0)

    def shape_of(*dims, dtype=f32):
        return jax.ShapeDtypeStruct(dims, dtype)

    def call(name, kernel, args, outs, scratch=(), after=(), limit=VMEM_LIMIT):
        return pl.pallas_call(
            kernel, in_specs=[in_smem] + [in_vmem] * len(args) + [anywhere] * len(after), out_specs=[in_vmem] * len(outs), out_shape=outs,
            scratch_shapes=list(scratch), cost_estimate=cheap,
            compiler_params=pltpu.CompilerParams(vmem_limit_bytes=limit), name=name,
        )(doc_lengths, *args, *after)

    def swap_cores(a):
        return lax.ppermute(a, "seq", [(b, b ^ 1) for b in range(seq)])

    def swap_pairs(sent):
        came = []
        for hop in range(1, hops + 1):
            perm = [(2 * m, 2 * (m + hop) + 1) for m in range(pairs - hop)]
            came.append(lax.ppermute(sent[hop - 1], "seq", perm + [(b, a) for a, b in perm]))
        return came

    def send_rows(outs):
        arrived = list(outs[:1])
        for j in range(1, groups):
            arrived.append(lax.ppermute(outs[j], "head", [(x, (x + j) % groups) for x in range(groups)]))
        return arrived

    square = (HEAD_DIM, HEAD_DIM)

    def states(kept, offset, half):
        heads = half // HEAD_DIM
        group = GROUP if heads % GROUP == 0 else 2
        outs = [shape_of(heads, *square)] + [shape_of(rows, rows, dtype=bf16)] * (2 * kept)
        return pl.pallas_call(
            functools.partial(state_kernel, offset=offset, heads=heads, group=group, kept=kept, **sizes),
            in_specs=[anywhere] * 5, out_specs=[in_vmem] * len(outs), out_shape=outs,
            scratch_shapes=[
                pltpu.VMEM((2, rows, half), bf16), pltpu.SemaphoreType.DMA((heads // group, 2)),
                pltpu.SMEM((ndocs,), jnp.int32), pltpu.SemaphoreType.DMA,
            ],
            cost_estimate=cheap, compiler_params=pltpu.CompilerParams(vmem_limit_bytes=KEPT_LIMIT if kept else FIRST_LIMIT), name="states",
        )(doc_lengths, *inputs)

    def late_states(offset, half, after):
        heads = half // HEAD_DIM
        return call(
            "states", functools.partial(late_state_kernel, offset=offset, heads=heads, **sizes), inputs,
            [shape_of(heads, *square)] * 2, after=after, limit=GRAD_LIMIT,
        )

    def pair_up(kept, got, copies, after):
        lines = kept.shape[0] * HEAD_DIM
        outs = [shape_of(lines + PAD * (hops - hop + 1), HEAD_DIM, dtype=LINK) for hop in range(1, hops + 1)]
        outs += [shape_of(kept.shape[0] // max(copies, 1), *square)] * copies
        made = call(
            "pair", functools.partial(pair_kernel, hops=hops, copies=copies, **sizes), (kept, got), outs, after=after
        )
        return made[hops - 1], swap_pairs(made[:hops]), [swap_cores(a) for a in made[hops:]]

    def join(spans, others, came, after):
        made = call(
            "join", functools.partial(join_kernel, spans=spans, hops=hops, **sizes), (*others, *came),
            [shape_of(count, *square) for _, _, count in spans] * 2, after=after,
        )
        return [(mine, swap_cores(theirs)) for mine, theirs in zip(made[:len(spans)], made[len(spans):])]

    def grads(masks, offset, cw, mine, theirs, after):
        return call(
            "grads", functools.partial(grad_kernel, offset=offset, heads=cw // HEAD_DIM, groups=groups, **sizes),
            (*inputs, *masks, mine, theirs), [shape_of(3, part, cw, dtype=bf16)] * groups,
            [pltpu.VMEM((3, rows, cw), bf16)], after, GRAD_LIMIT,
        )

    def local(masks, offset, cw):
        kernel = functools.partial(local_kernel, offset=offset, heads=cw // HEAD_DIM)
        return call(
            "local", kernel, (*inputs, *masks), [shape_of(3, rows, cw), shape_of(8, HEAD_DIM)], limit=GRAD_LIMIT,
        )

    def carry(near, offset, cw, mine, theirs, after):
        kernel = functools.partial(carry_kernel, offset=offset, heads=cw // HEAD_DIM, groups=groups, **sizes)
        return call(
            "carry", kernel, (*inputs[1:], near, mine, theirs), [shape_of(3, part, cw, dtype=bf16)] * groups,
            [pltpu.VMEM((3, rows, cw), bf16)], after, GRAD_LIMIT,
        )

    def carry_rows(shifts, near, offset, cw, mine, theirs, after):
        kernel = functools.partial(
            carry_rows_kernel, offset=offset, heads=cw // HEAD_DIM, groups=groups, shifts=shifts, **sizes
        )
        outs = [shape_of(3, part, cw, dtype=bf16)] * len(shifts)
        return call("carry", kernel, (*inputs[1:], near, mine, theirs), outs, after=after, limit=GRAD_LIMIT)

    cuts, outs, arrived, totals, masks = [], [], [], [], None
    for start, half, chunks in halves:
        if not totals:
            (sent,) = states(False, start, half)
            kept, *masks = states(True, start, half)
        else:
            kept, sent = late_states(start, half, [token])
        total, came, others = pair_up(
            kept, swap_cores(sent), 0 if totals else len(chunks), [made[-1] for made in outs[:1]]
        )
        if not totals:
            near = [local(masks, *chunk) for chunk in chunks]
            token = near[0][1]
        count = chunks[0][1] // HEAD_DIM
        if totals:
            spans = [(c * count, c * count, count) for c in range(len(chunks))]
            joined = join(spans, [swap_cores(kept)] * len(chunks), came, [arrived[0][1]])
        else:
            joined, after = [], [made[1] for made in near]
            for c in range(len(chunks)):
                joined += join([(0, c * count, count)], others[c:c + 1], came, after)
                after = [joined[-1][0]]
        for c, ((offset, cw), (mine, theirs)) in enumerate(zip(chunks, joined)):
            after = [made[-1] for made in outs[-1:]] + [parts[1] for parts in arrived[1:-1]][-1:]
            if totals:
                outs.append(grads(masks, offset, cw, mine, theirs, after))
            elif c == 0:
                first = (near[0][0], offset, cw, mine, theirs)
                outs.append([None, *carry_rows(range(1, groups), *first, [made for made, _ in joined[1:]])])
            else:
                outs.append(carry(near[c][0], offset, cw, mine, theirs, after))
            arrived.append(send_rows(outs[-1]))
        if not totals:
            arrived[0][0] = carry_rows([0], *first, [outs[-1][-1]])[0]
        totals = [total]
        cuts += chunks

    placed = []
    for c in range(len(cuts)):
        own = [0, 1] if c == 0 else [c + 1]
        plan = [(arrived[n][0], (0, *cuts[n])) for n in own if n < len(cuts)]
        plan += [(arrived[c][j], (j, *cuts[c])) for j in range(1, groups)]
        some = [array for array, _ in plan]
        placed = pl.pallas_call(
            functools.partial(place_kernel, groups=groups, plan=[where for _, where in plan], width=width),
            grid_spec=pl.GridSpec(
                grid=(1,), in_specs=[anywhere] * (len(some) + len(placed)), out_specs=[anywhere] * 3,
                scratch_shapes=[pltpu.SemaphoreType.DMA((3 * len(some),))],
            ),
            out_shape=[shape_of(part, width * groups, dtype=bf16)] * 3,
            input_output_aliases={len(some) + i: i for i in range(len(placed))},
            cost_estimate=cheap,
            compiler_params=pltpu.CompilerParams(vmem_limit_bytes=VMEM_LIMIT), name="place",
        )(*some, *placed)
    return tuple(placed)


def solution(mesh):
    return jax.shard_map(
        shards,
        mesh=mesh,
        in_specs=(P("seq", "head"), P("seq", "head"), P("seq", "head"), P("seq", "head"), P()),
        out_specs=(P(("seq", "head"), None), P(("seq", "head"), None), P(("seq", "head"), None)),
        check_vma=False,
    )
```

```python
import functools

import jax
import jax.numpy as jnp
from jax import lax
from jax.experimental import pallas as pl
from jax.experimental.pallas import tpu as pltpu
from jax.sharding import PartitionSpec as P

HEAD_DIM = 128
MOST = 1024
GROUP = 4
CHUNK = 4
PAD = 16
LINK = jnp.bfloat16
VMEM_LIMIT = 16 * 1024 * 1024
GRAD_LIMIT = 32 * 1024 * 1024
FIRST_LIMIT = 53 * 1024 * 1024
KEPT_LIMIT = 53 * 1024 * 1024
NT = (((1,), (1,)), ((), ()))
TN = (((0,), (0,)), ((), ()))
NN = (((1,), (0,)), ((), ()))


def dot(a, b, dims):
    return lax.dot_general(a, b, dims, preferred_element_type=jnp.float32)


def doc_at(meta, ndocs, position):
    start, begin, end = jnp.int32(0), jnp.int32(0), jnp.int32(0)
    for i in range(ndocs):
        stop = start + meta[i]
        begin = jnp.where(start <= position, start, begin)
        end = jnp.where(start <= position, stop, end)
        start = stop
    return begin, end


def block_range(meta, ndocs, base, rows):
    begin0, end0 = doc_at(meta, ndocs, base)
    begin1, end1 = doc_at(meta, ndocs, base + rows - 1)
    first = jnp.where(begin0 < base, end0, base) - base
    return begin0, end0, begin1, end1, first, begin1 - base


def make_masks(lengths, lower, upper, ndocs, rows):
    line = lax.broadcasted_iota(jnp.int32, (rows, rows), 0)
    across = lax.broadcasted_iota(jnp.int32, (rows, rows), 1)
    begin_line = jnp.zeros((rows, rows), jnp.int32)
    begin_across = jnp.zeros((rows, rows), jnp.int32)
    start = jnp.int32(0) - lax.axis_index("seq") * rows
    for i in range(ndocs):
        begin_line = jnp.where(line >= start, start, begin_line)
        begin_across = jnp.where(across >= start, start, begin_across)
        start = start + lengths[i]
    lower[...] = jnp.where((across <= line) & (across >= begin_line), 1.0, 0.0).astype(lower.dtype)
    upper[...] = jnp.where((line <= across) & (line >= begin_across), 1.0, 0.0).astype(upper.dtype)


def state_kernel(lengths, q, k, v, g, out, *rest, ndocs, rows, offset, heads, group, kept):
    *masks, held, sems, known, got = rest
    gw = group * HEAD_DIM
    place = lax.axis_index("seq")
    first_core = lax.rem(place, 2) == 0

    tails = first_core if kept else jnp.logical_not(first_core)

    def copy(c, i, ref):
        src = ref.at[:, pl.ds(offset + c * gw, gw)]
        return pltpu.make_async_copy(src, held.at[i, :, pl.ds(c * gw, gw)], sems.at[c, i])

    fetch = pltpu.make_async_copy(lengths, known, got)
    fetch.start()
    for c in range(heads // group):

        @pl.when(tails)
        def _():
            copy(c, 0, k).start()
            copy(c, 1, v).start()

        @pl.when(jnp.logical_not(tails))
        def _():
            copy(c, 0, q).start()
            copy(c, 1, g).start()

    fetch.wait()
    if masks:
        make_masks(known, *masks, ndocs, rows)
    _, _, _, _, first, last = block_range(known, ndocs, place * rows, rows)
    order = lax.broadcasted_iota(jnp.int32, (rows, HEAD_DIM), 0)
    zero = jnp.zeros((), held.dtype)
    low, high = jnp.where(tails, last, 0), jnp.where(tails, rows, first)
    here = (order >= low) & (order < high)
    for h in range(heads):
        if h % group == 0:
            copy(h // group, 0, k).wait()
            copy(h // group, 1, v).wait()
        cols = slice(h * HEAD_DIM, (h + 1) * HEAD_DIM)
        out[h] = dot(jnp.where(here, held[0, :, cols], zero), held[1, :, cols], TN)


def late_state_kernel(lengths, q, k, v, g, *rest, ndocs, rows, offset, heads):
    kept, sent = rest[-2:]
    first_core, first_rows, last_rows = own_range(lengths, ndocs, rows)
    zero = jnp.zeros((), q.dtype)
    for h in range(heads):
        at = slice(offset + h * HEAD_DIM, offset + (h + 1) * HEAD_DIM)
        tail = dot(jnp.where(last_rows, k[:, at], zero), v[:, at], TN)
        head = dot(jnp.where(first_rows, q[:, at], zero), g[:, at], TN)
        kept[h] = jnp.where(first_core, tail, head)
        sent[h] = jnp.where(first_core, head, tail)


def pair_kernel(lengths, kept, got, *rest, ndocs, rows, hops, copies):
    sent, again = rest[-hops - copies:len(rest) - copies], rest[len(rest) - copies:]
    place = lax.axis_index("seq")
    first_core = lax.rem(place, 2) == 0
    even = (place - lax.rem(place, 2)) * rows
    odd = even + rows
    _, even_e0 = doc_at(lengths, ndocs, even)
    odd_b1, _ = doc_at(lengths, ndocs, odd + rows - 1)
    joins = jnp.where(jnp.where(first_core, odd_b1 < odd, even_e0 > odd), 1.0, 0.0)
    size = kept.shape[0] * HEAD_DIM
    total = (got[...] + joins * kept[...]).astype(LINK).reshape(size, HEAD_DIM)
    for out in sent:
        out[:size] = total
        if out.shape[0] > size:
            out[size:] = jnp.zeros((out.shape[0] - size, HEAD_DIM), LINK)
    for i, out in enumerate(again):
        count = out.shape[0]
        out[...] = kept[i * count:(i + 1) * count]


def join_kernel(lengths, *rest, ndocs, rows, spans, hops):
    others, came = rest[:len(spans)], rest[len(spans):len(spans) + hops]
    mine, theirs = rest[-2 * len(spans):-len(spans)], rest[-len(spans):]
    place = lax.axis_index("seq")
    first_core = lax.rem(place, 2) == 0
    even = (place - lax.rem(place, 2)) * rows
    odd = even + rows
    even_b0, _ = doc_at(lengths, ndocs, even)
    _, even_e1 = doc_at(lengths, ndocs, odd - 1)
    odd_b0, _ = doc_at(lengths, ndocs, odd)
    _, odd_e1 = doc_at(lengths, ndocs, odd + rows - 1)

    def one(if_first, if_second):
        return jnp.where(jnp.where(first_core, if_first, if_second), 1.0, 0.0)

    weights = [
        one(odd + rows + hop * 2 * rows < odd_e1, even - hop * 2 * rows > even_b0) for hop in range(hops)
    ]
    from_other, from_pair = one(odd < even_e1, odd > odd_b0), one(odd + rows < even_e1, even > odd_b0)
    for c, (other_at, came_at, count) in enumerate(spans):
        lines = slice(came_at * HEAD_DIM, (came_at + count) * HEAD_DIM)
        total = weights[0] * came[0][lines].astype(jnp.float32)
        for hop in range(1, hops):
            total = total + weights[hop] * came[hop][lines].astype(jnp.float32)
        total = total.reshape(count, HEAD_DIM, HEAD_DIM)
        theirs[c][...] = total
        mine[c][...] = from_other * others[c][other_at:other_at + count] + from_pair * total


def split(a, axis):
    high = a.astype(jnp.bfloat16)
    return jnp.concatenate([high, (a - high.astype(jnp.float32)).astype(jnp.bfloat16)], axis=axis)


def own_range(lengths, ndocs, rows):
    place = lax.axis_index("seq")
    _, _, _, _, first, last = block_range(lengths, ndocs, place * rows, rows)
    order = lax.broadcasted_iota(jnp.int32, (rows, HEAD_DIM), 0)
    return lax.rem(place, 2) == 0, order < first, order >= last


def local_part(q, k, v, g, lower, upper, at):
    qh, kh, vh, gh = (ref[:, at] for ref in (q, k, v, g))
    weight_gv = dot(gh, vh, NT).astype(jnp.bfloat16) * lower[...]
    weight_vg = dot(vh, gh, NT).astype(jnp.bfloat16) * upper[...]
    weight_kq = dot(kh, qh, NT).astype(jnp.bfloat16) * upper[...]
    return dot(weight_gv, kh, NN), dot(weight_vg, qh, NN), dot(weight_kq, gh, NN)


def twice(ref, at):
    return jnp.concatenate([ref[:, at]] * 2, axis=1)


def carry_of_state(g, state, first_rows, at):
    return jnp.where(first_rows, dot(twice(g, at), split(state, 1), NT), 0.0)


def carries_of_grad(k, v, grad, last_rows, at):
    carry_k = jnp.where(last_rows, dot(twice(v, at), split(grad, 1), NT), 0.0)
    return carry_k, jnp.where(last_rows, dot(twice(k, at), split(grad, 0), NN), 0.0)


def deal(done, outs, rows, groups):
    part, column = rows // groups, lax.axis_index("head")
    for j in range(groups):
        at = pl.ds(pl.multiple_of(lax.rem(column + j, groups) * part, part), part)
        for i in range(3):
            outs[j][i] = done[i, at, :]


def grad_kernel(lengths, q, k, v, g, lower, upper, mine, got, *rest, ndocs, rows, offset, heads, groups):
    outs, done = rest[-1 - groups:-1], rest[-1]
    first_core, first_rows, last_rows = own_range(lengths, ndocs, rows)
    for h in range(heads):
        cols = slice(h * HEAD_DIM, (h + 1) * HEAD_DIM)
        at = slice(offset + h * HEAD_DIM, offset + (h + 1) * HEAD_DIM)
        state = jnp.where(first_core, got[h], mine[h])
        grad = jnp.where(first_core, mine[h], got[h])
        near = local_part(q, k, v, g, lower, upper, at)
        carries = (carry_of_state(g, state, first_rows, at), *carries_of_grad(k, v, grad, last_rows, at))
        for i in range(3):
            done[i, :, cols] = (near[i] + carries[i]).astype(jnp.bfloat16)
    deal(done, outs, rows, groups)


def local_kernel(lengths, q, k, v, g, lower, upper, near, token, *, offset, heads):
    token[...] = jnp.zeros_like(token)
    for h in range(heads):
        cols = slice(h * HEAD_DIM, (h + 1) * HEAD_DIM)
        at = slice(offset + h * HEAD_DIM, offset + (h + 1) * HEAD_DIM)
        for i, value in enumerate(local_part(q, k, v, g, lower, upper, at)):
            near[i, :, cols] = value


def carry_rows_kernel(lengths, k, v, g, near, mine, got, *rest, ndocs, rows, offset, heads, groups, shifts):
    outs = rest[-len(shifts):]
    place, column, part = lax.axis_index("seq"), lax.axis_index("head"), rows // groups
    first_core = lax.rem(place, 2) == 0
    _, _, _, _, first, last = block_range(lengths, ndocs, place * rows, rows)
    order = lax.broadcasted_iota(jnp.int32, (part, HEAD_DIM), 0)
    for j, out in zip(shifts, outs):
        start = pl.multiple_of(lax.rem(column + j, groups) * part, part)
        lines = pl.ds(start, part)
        first_rows, last_rows = order + start < first, order + start >= last
        for h in range(heads):
            cols = slice(h * HEAD_DIM, (h + 1) * HEAD_DIM)
            at = slice(offset + h * HEAD_DIM, offset + (h + 1) * HEAD_DIM)
            state = split(jnp.where(first_core, got[h], mine[h]), 1)
            grad = jnp.where(first_core, mine[h], got[h])
            k2, v2, g2 = (jnp.concatenate([ref[lines, at]] * 2, axis=1) for ref in (k, v, g))
            carry_q = jnp.where(first_rows, dot(g2, state, NT), 0.0)
            carry_k = jnp.where(last_rows, dot(v2, split(grad, 1), NT), 0.0)
            carry_v = jnp.where(last_rows, dot(k2, split(grad, 0), NN), 0.0)
            for i, value in enumerate((carry_q, carry_k, carry_v)):
                out[i, :, cols] = (near[i, lines, cols] + value).astype(jnp.bfloat16)


def place_kernel(*refs, groups, plan, width):
    parts, outs, sems = refs[:len(plan)], refs[-4:-1], refs[-1]
    column = lax.axis_index("head")
    copies = []
    for ref, (j, offset, cw) in zip(parts, plan):
        start = pl.multiple_of(lax.rem(column + groups - j, groups) * width + offset, 128)
        for i in range(3):
            copies.append(pltpu.make_async_copy(ref.at[i], outs[i].at[:, pl.ds(start, cw)], sems.at[len(copies)]))
            copies[-1].start()
    for copy in copies:
        copy.wait()


def cuts_of(width):
    heads = width // HEAD_DIM
    size = CHUNK if heads % (2 * CHUNK) == 0 else 2
    cw, half = size * HEAD_DIM, max(heads // 2, size) * HEAD_DIM
    return [(at, half, [(o, cw) for o in range(at, at + half, cw)]) for at in range(0, width, half)]


def shards(queries, keys, values, out_grad, doc_lengths):
    rows, width = queries.shape
    ndocs = doc_lengths.shape[0]
    seq, groups = lax.axis_size("seq"), lax.axis_size("head")
    pairs = seq // 2
    hops = -(-MOST // (2 * rows))
    halves = cuts_of(width)
    part = rows // groups
    anywhere = pl.BlockSpec(memory_space=pl.ANY)
    in_vmem = pl.BlockSpec(memory_space=pltpu.VMEM)
    in_smem = pl.BlockSpec(memory_space=pltpu.SMEM)
    f32, bf16 = jnp.float32, jnp.bfloat16
    inputs = (queries, keys, values, out_grad)
    sizes = dict(ndocs=ndocs, rows=rows)
    cheap = pl.CostEstimate(flops=0, bytes_accessed=1024, transcendentals=0)

    def shape_of(*dims, dtype=f32):
        return jax.ShapeDtypeStruct(dims, dtype)

    def call(name, kernel, args, outs, scratch=(), after=(), limit=VMEM_LIMIT):
        return pl.pallas_call(
            kernel, in_specs=[in_smem] + [in_vmem] * len(args) + [anywhere] * len(after), out_specs=[in_vmem] * len(outs), out_shape=outs,
            scratch_shapes=list(scratch), cost_estimate=cheap,
            compiler_params=pltpu.CompilerParams(vmem_limit_bytes=limit), name=name,
        )(doc_lengths, *args, *after)

    def swap_cores(a):
        return lax.ppermute(a, "seq", [(b, b ^ 1) for b in range(seq)])

    def swap_pairs(sent):
        came = []
        for hop in range(1, hops + 1):
            perm = [(2 * m, 2 * (m + hop) + 1) for m in range(pairs - hop)]
            came.append(lax.ppermute(sent[hop - 1], "seq", perm + [(b, a) for a, b in perm]))
        return came

    def send_rows(outs):
        arrived = list(outs[:1])
        for j in range(1, groups):
            arrived.append(lax.ppermute(outs[j], "head", [(x, (x + j) % groups) for x in range(groups)]))
        return arrived

    square = (HEAD_DIM, HEAD_DIM)

    def states(kept, offset, half):
        heads = half // HEAD_DIM
        group = GROUP if heads % GROUP == 0 else 2
        outs = [shape_of(heads, *square)] + [shape_of(rows, rows, dtype=bf16)] * (2 * kept)
        return pl.pallas_call(
            functools.partial(state_kernel, offset=offset, heads=heads, group=group, kept=kept, **sizes),
            in_specs=[anywhere] * 5, out_specs=[in_vmem] * len(outs), out_shape=outs,
            scratch_shapes=[
                pltpu.VMEM((2, rows, half), bf16), pltpu.SemaphoreType.DMA((heads // group, 2)),
                pltpu.SMEM((ndocs,), jnp.int32), pltpu.SemaphoreType.DMA,
            ],
            cost_estimate=cheap, compiler_params=pltpu.CompilerParams(vmem_limit_bytes=KEPT_LIMIT if kept else FIRST_LIMIT), name="states",
        )(doc_lengths, *inputs)

    def late_states(offset, half, after):
        heads = half // HEAD_DIM
        return call(
            "states", functools.partial(late_state_kernel, offset=offset, heads=heads, **sizes), inputs,
            [shape_of(heads, *square)] * 2, after=after, limit=GRAD_LIMIT,
        )

    def pair_up(kept, got, copies, after):
        lines = kept.shape[0] * HEAD_DIM
        outs = [shape_of(lines + PAD * (hops - hop + 1), HEAD_DIM, dtype=LINK) for hop in range(1, hops + 1)]
        outs += [shape_of(kept.shape[0] // max(copies, 1), *square)] * copies
        made = call(
            "pair", functools.partial(pair_kernel, hops=hops, copies=copies, **sizes), (kept, got), outs, after=after
        )
        return made[hops - 1], swap_pairs(made[:hops]), [swap_cores(a) for a in made[hops:]]

    def join(spans, others, came, after):
        made = call(
            "join", functools.partial(join_kernel, spans=spans, hops=hops, **sizes), (*others, *came),
            [shape_of(count, *square) for _, _, count in spans] * 2, after=after,
        )
        return [(mine, swap_cores(theirs)) for mine, theirs in zip(made[:len(spans)], made[len(spans):])]

    def grads(masks, offset, cw, mine, theirs, after):
        return call(
            "grads", functools.partial(grad_kernel, offset=offset, heads=cw // HEAD_DIM, groups=groups, **sizes),
            (*inputs, *masks, mine, theirs), [shape_of(3, part, cw, dtype=bf16)] * groups,
            [pltpu.VMEM((3, rows, cw), bf16)], after, GRAD_LIMIT,
        )

    def local(masks, offset, cw):
        kernel = functools.partial(local_kernel, offset=offset, heads=cw // HEAD_DIM)
        return call(
            "local", kernel, (*inputs, *masks), [shape_of(3, rows, cw), shape_of(8, HEAD_DIM)], limit=GRAD_LIMIT,
        )

    def carry_rows(shifts, near, offset, cw, mine, theirs, after):
        kernel = functools.partial(
            carry_rows_kernel, offset=offset, heads=cw // HEAD_DIM, groups=groups, shifts=shifts, **sizes
        )
        outs = [shape_of(3, part, cw, dtype=bf16)] * len(shifts)
        return call("carry", kernel, (*inputs[1:], near, mine, theirs), outs, after=after, limit=GRAD_LIMIT)

    cuts, outs, arrived, totals, masks, early = [], [], [], [], None, []
    for start, half, chunks in halves:
        if not totals:
            (sent,) = states(False, start, half)
            kept, *masks = states(True, start, half)
        else:
            kept, sent = late_states(start, half, [token])
        total, came, others = pair_up(
            kept, swap_cores(sent), 0 if totals else len(chunks), [made[-1] for made in outs[:1]]
        )
        if not totals:
            near = [local(masks, *chunk) for chunk in chunks]
            token = near[0][1]
        count = chunks[0][1] // HEAD_DIM
        if totals:
            spans = [(c * count, c * count, count) for c in range(len(chunks))]
            joined = join(spans, [swap_cores(kept)] * len(chunks), came, [arrived[0][1]])
        else:
            joined, after = [], [made[1] for made in near]
            for c in range(len(chunks)):
                joined += join([(0, c * count, count)], others[c:c + 1], came, after)
                after = [joined[-1][0]]
        for c, ((offset, cw), (mine, theirs)) in enumerate(zip(chunks, joined)):
            after = [made[-1] for made in outs[-1:]] + [parts[1] for parts in arrived[1:-1]][-1:]
            if totals:
                outs.append(grads(masks, offset, cw, mine, theirs, after))
            else:
                after = after or [made for made, _ in joined[1:]]
                early.append((near[c][0], offset, cw, mine, theirs))
                outs.append([None, *carry_rows(range(1, groups), *early[-1], after)])
            arrived.append(send_rows(outs[-1]))
        if not totals:
            for c, parts in enumerate(early):
                arrived[c][0] = carry_rows([0], *parts, [outs[-1][-1]])[0]
        totals = [total]
        cuts += chunks

    placed = []
    for c in range(len(cuts)):
        own = [0, 1] if c == 0 else [c + 1]
        plan = [(arrived[n][0], (0, *cuts[n])) for n in own if n < len(cuts)]
        plan += [(arrived[c][j], (j, *cuts[c])) for j in range(1, groups)]
        some = [array for array, _ in plan]
        placed = pl.pallas_call(
            functools.partial(place_kernel, groups=groups, plan=[where for _, where in plan], width=width),
            grid_spec=pl.GridSpec(
                grid=(1,), in_specs=[anywhere] * (len(some) + len(placed)), out_specs=[anywhere] * 3,
                scratch_shapes=[pltpu.SemaphoreType.DMA((3 * len(some),))],
            ),
            out_shape=[shape_of(part, width * groups, dtype=bf16)] * 3,
            input_output_aliases={len(some) + i: i for i in range(len(placed))},
            cost_estimate=cheap,
            compiler_params=pltpu.CompilerParams(vmem_limit_bytes=VMEM_LIMIT), name="place",
        )(*some, *placed)
    return tuple(placed)


def solution(mesh):
    return jax.shard_map(
        shards,
        mesh=mesh,
        in_specs=(P("seq", "head"), P("seq", "head"), P("seq", "head"), P("seq", "head"), P()),
        out_specs=(P(("seq", "head"), None), P(("seq", "head"), None), P(("seq", "head"), None)),
        check_vma=False,
    )
```

```python
import functools

import jax
import jax.numpy as jnp
from jax import lax
from jax.experimental import pallas as pl
from jax.experimental.pallas import tpu as pltpu
from jax.sharding import PartitionSpec as P

HEAD_DIM = 128
MOST = 1024
GROUP = 4
CHUNK = 4
PAD = 16
LINK = jnp.bfloat16
VMEM_LIMIT = 16 * 1024 * 1024
GRAD_LIMIT = 32 * 1024 * 1024
FIRST_LIMIT = 53 * 1024 * 1024
KEPT_LIMIT = 53 * 1024 * 1024
NT = (((1,), (1,)), ((), ()))
TN = (((0,), (0,)), ((), ()))
NN = (((1,), (0,)), ((), ()))


def dot(a, b, dims):
    return lax.dot_general(a, b, dims, preferred_element_type=jnp.float32)


def doc_at(meta, ndocs, position):
    start, begin, end = jnp.int32(0), jnp.int32(0), jnp.int32(0)
    for i in range(ndocs):
        stop = start + meta[i]
        begin = jnp.where(start <= position, start, begin)
        end = jnp.where(start <= position, stop, end)
        start = stop
    return begin, end


def block_range(meta, ndocs, base, rows):
    begin0, end0 = doc_at(meta, ndocs, base)
    begin1, end1 = doc_at(meta, ndocs, base + rows - 1)
    first = jnp.where(begin0 < base, end0, base) - base
    return begin0, end0, begin1, end1, first, begin1 - base


def make_masks(lengths, lower, upper, ndocs, rows):
    line = lax.broadcasted_iota(jnp.int32, (rows, rows), 0)
    across = lax.broadcasted_iota(jnp.int32, (rows, rows), 1)
    begin_line = jnp.zeros((rows, rows), jnp.int32)
    begin_across = jnp.zeros((rows, rows), jnp.int32)
    start = jnp.int32(0) - lax.axis_index("seq") * rows
    for i in range(ndocs):
        begin_line = jnp.where(line >= start, start, begin_line)
        begin_across = jnp.where(across >= start, start, begin_across)
        start = start + lengths[i]
    lower[...] = jnp.where((across <= line) & (across >= begin_line), 1.0, 0.0).astype(lower.dtype)
    upper[...] = jnp.where((line <= across) & (line >= begin_across), 1.0, 0.0).astype(upper.dtype)


def state_kernel(lengths, q, k, v, g, out, *rest, ndocs, rows, offset, heads, group, kept):
    *masks, held, sems, known, got = rest
    gw = group * HEAD_DIM
    place = lax.axis_index("seq")
    first_core = lax.rem(place, 2) == 0

    tails = first_core if kept else jnp.logical_not(first_core)

    def copy(c, i, ref):
        src = ref.at[:, pl.ds(offset + c * gw, gw)]
        return pltpu.make_async_copy(src, held.at[i, :, pl.ds(c * gw, gw)], sems.at[c, i])

    fetch = pltpu.make_async_copy(lengths, known, got)
    fetch.start()
    for c in range(heads // group):

        @pl.when(tails)
        def _():
            copy(c, 0, k).start()
            copy(c, 1, v).start()

        @pl.when(jnp.logical_not(tails))
        def _():
            copy(c, 0, q).start()
            copy(c, 1, g).start()

    fetch.wait()
    if masks:
        make_masks(known, *masks, ndocs, rows)
    _, _, _, _, first, last = block_range(known, ndocs, place * rows, rows)
    order = lax.broadcasted_iota(jnp.int32, (rows, HEAD_DIM), 0)
    zero = jnp.zeros((), held.dtype)
    low, high = jnp.where(tails, last, 0), jnp.where(tails, rows, first)
    here = (order >= low) & (order < high)
    for h in range(heads):
        if h % group == 0:
            copy(h // group, 0, k).wait()
            copy(h // group, 1, v).wait()
        cols = slice(h * HEAD_DIM, (h + 1) * HEAD_DIM)
        out[h] = dot(jnp.where(here, held[0, :, cols], zero), held[1, :, cols], TN)


def late_state_kernel(lengths, q, k, v, g, *rest, ndocs, rows, offset, heads):
    kept, sent = rest[-2:]
    first_core, first_rows, last_rows = own_range(lengths, ndocs, rows)
    zero = jnp.zeros((), q.dtype)
    for h in range(heads):
        at = slice(offset + h * HEAD_DIM, offset + (h + 1) * HEAD_DIM)
        tail = dot(jnp.where(last_rows, k[:, at], zero), v[:, at], TN)
        head = dot(jnp.where(first_rows, q[:, at], zero), g[:, at], TN)
        kept[h] = jnp.where(first_core, tail, head)
        sent[h] = jnp.where(first_core, head, tail)


def pair_kernel(lengths, kept, got, *rest, ndocs, rows, hops, copies):
    sent, again = rest[-hops - copies:len(rest) - copies], rest[len(rest) - copies:]
    place = lax.axis_index("seq")
    first_core = lax.rem(place, 2) == 0
    even = (place - lax.rem(place, 2)) * rows
    odd = even + rows
    _, even_e0 = doc_at(lengths, ndocs, even)
    odd_b1, _ = doc_at(lengths, ndocs, odd + rows - 1)
    joins = jnp.where(jnp.where(first_core, odd_b1 < odd, even_e0 > odd), 1.0, 0.0)
    size = kept.shape[0] * HEAD_DIM
    total = (got[...] + joins * kept[...]).astype(LINK).reshape(size, HEAD_DIM)
    for out in sent:
        out[:size] = total
        if out.shape[0] > size:
            out[size:] = jnp.zeros((out.shape[0] - size, HEAD_DIM), LINK)
    for i, out in enumerate(again):
        count = out.shape[0]
        out[...] = kept[i * count:(i + 1) * count]


def join_kernel(lengths, *rest, ndocs, rows, spans, hops):
    others, came = rest[:len(spans)], rest[len(spans):len(spans) + hops]
    mine, theirs = rest[-2 * len(spans):-len(spans)], rest[-len(spans):]
    place = lax.axis_index("seq")
    first_core = lax.rem(place, 2) == 0
    even = (place - lax.rem(place, 2)) * rows
    odd = even + rows
    even_b0, _ = doc_at(lengths, ndocs, even)
    _, even_e1 = doc_at(lengths, ndocs, odd - 1)
    odd_b0, _ = doc_at(lengths, ndocs, odd)
    _, odd_e1 = doc_at(lengths, ndocs, odd + rows - 1)

    def one(if_first, if_second):
        return jnp.where(jnp.where(first_core, if_first, if_second), 1.0, 0.0)

    weights = [
        one(odd + rows + hop * 2 * rows < odd_e1, even - hop * 2 * rows > even_b0) for hop in range(hops)
    ]
    from_other, from_pair = one(odd < even_e1, odd > odd_b0), one(odd + rows < even_e1, even > odd_b0)
    for c, (other_at, came_at, count) in enumerate(spans):
        lines = slice(came_at * HEAD_DIM, (came_at + count) * HEAD_DIM)
        total = weights[0] * came[0][lines].astype(jnp.float32)
        for hop in range(1, hops):
            total = total + weights[hop] * came[hop][lines].astype(jnp.float32)
        total = total.reshape(count, HEAD_DIM, HEAD_DIM)
        theirs[c][...] = total
        mine[c][...] = from_other * others[c][other_at:other_at + count] + from_pair * total


def split(a, axis):
    high = a.astype(jnp.bfloat16)
    return jnp.concatenate([high, (a - high.astype(jnp.float32)).astype(jnp.bfloat16)], axis=axis)


def own_range(lengths, ndocs, rows):
    place = lax.axis_index("seq")
    _, _, _, _, first, last = block_range(lengths, ndocs, place * rows, rows)
    order = lax.broadcasted_iota(jnp.int32, (rows, HEAD_DIM), 0)
    return lax.rem(place, 2) == 0, order < first, order >= last


def local_part(q, k, v, g, lower, upper, at):
    qh, kh, vh, gh = (ref[:, at] for ref in (q, k, v, g))
    weight_gv = dot(gh, vh, NT).astype(jnp.bfloat16) * lower[...]
    weight_vg = dot(vh, gh, NT).astype(jnp.bfloat16) * upper[...]
    weight_kq = dot(kh, qh, NT).astype(jnp.bfloat16) * upper[...]
    return dot(weight_gv, kh, NN), dot(weight_vg, qh, NN), dot(weight_kq, gh, NN)


def twice(ref, at):
    return jnp.concatenate([ref[:, at]] * 2, axis=1)


def carry_of_state(g, state, first_rows, at):
    return jnp.where(first_rows, dot(twice(g, at), split(state, 1), NT), 0.0)


def carries_of_grad(k, v, grad, last_rows, at):
    carry_k = jnp.where(last_rows, dot(twice(v, at), split(grad, 1), NT), 0.0)
    return carry_k, jnp.where(last_rows, dot(twice(k, at), split(grad, 0), NN), 0.0)


def deal(done, outs, rows, groups):
    part, column = rows // groups, lax.axis_index("head")
    for j in range(groups):
        at = pl.ds(pl.multiple_of(lax.rem(column + j, groups) * part, part), part)
        for i in range(3):
            outs[j][i] = done[i, at, :]


def grad_kernel(lengths, q, k, v, g, lower, upper, mine, got, *rest, ndocs, rows, offset, heads, groups):
    outs, done = rest[-1 - groups:-1], rest[-1]
    first_core, first_rows, last_rows = own_range(lengths, ndocs, rows)
    for h in range(heads):
        cols = slice(h * HEAD_DIM, (h + 1) * HEAD_DIM)
        at = slice(offset + h * HEAD_DIM, offset + (h + 1) * HEAD_DIM)
        state = jnp.where(first_core, got[h], mine[h])
        grad = jnp.where(first_core, mine[h], got[h])
        near = local_part(q, k, v, g, lower, upper, at)
        carries = (carry_of_state(g, state, first_rows, at), *carries_of_grad(k, v, grad, last_rows, at))
        for i in range(3):
            done[i, :, cols] = (near[i] + carries[i]).astype(jnp.bfloat16)
    deal(done, outs, rows, groups)


def local_kernel(lengths, q, k, v, g, lower, upper, near, token, *, offset, heads):
    token[...] = jnp.zeros_like(token)
    for h in range(heads):
        cols = slice(h * HEAD_DIM, (h + 1) * HEAD_DIM)
        at = slice(offset + h * HEAD_DIM, offset + (h + 1) * HEAD_DIM)
        for i, value in enumerate(local_part(q, k, v, g, lower, upper, at)):
            near[i, :, cols] = value


def carry_rows_kernel(lengths, k, v, g, near, mine, got, *rest, ndocs, rows, offset, heads, groups, shifts):
    outs = rest[-len(shifts):]
    place, column, part = lax.axis_index("seq"), lax.axis_index("head"), rows // groups
    first_core = lax.rem(place, 2) == 0
    _, _, _, _, first, last = block_range(lengths, ndocs, place * rows, rows)
    order = lax.broadcasted_iota(jnp.int32, (part, HEAD_DIM), 0)
    for j, out in zip(shifts, outs):
        start = pl.multiple_of(lax.rem(column + j, groups) * part, part)
        lines = pl.ds(start, part)
        first_rows, last_rows = order + start < first, order + start >= last
        for h in range(heads):
            cols = slice(h * HEAD_DIM, (h + 1) * HEAD_DIM)
            at = slice(offset + h * HEAD_DIM, offset + (h + 1) * HEAD_DIM)
            state = split(jnp.where(first_core, got[h], mine[h]), 1)
            grad = jnp.where(first_core, mine[h], got[h])
            k2, v2, g2 = (jnp.concatenate([ref[lines, at]] * 2, axis=1) for ref in (k, v, g))
            carry_q = jnp.where(first_rows, dot(g2, state, NT), 0.0)
            carry_k = jnp.where(last_rows, dot(v2, split(grad, 1), NT), 0.0)
            carry_v = jnp.where(last_rows, dot(k2, split(grad, 0), NN), 0.0)
            for i, value in enumerate((carry_q, carry_k, carry_v)):
                out[i, :, cols] = (near[i, lines, cols] + value).astype(jnp.bfloat16)


def place_kernel(*refs, groups, plan, width):
    parts, outs, sems = refs[:len(plan)], refs[-4:-1], refs[-1]
    column = lax.axis_index("head")
    copies = []
    for ref, (j, offset, cw) in zip(parts, plan):
        start = pl.multiple_of(lax.rem(column + groups - j, groups) * width + offset, 128)
        for i in range(3):
            copies.append(pltpu.make_async_copy(ref.at[i], outs[i].at[:, pl.ds(start, cw)], sems.at[len(copies)]))
            copies[-1].start()
    for copy in copies:
        copy.wait()


def cuts_of(width):
    heads = width // HEAD_DIM
    size = CHUNK if heads % (2 * CHUNK) == 0 else 2
    cw, half = size * HEAD_DIM, max(heads // 2, size) * HEAD_DIM
    return [(at, half, [(o, cw) for o in range(at, at + half, cw)]) for at in range(0, width, half)]


def shards(queries, keys, values, out_grad, doc_lengths):
    rows, width = queries.shape
    ndocs = doc_lengths.shape[0]
    seq, groups = lax.axis_size("seq"), lax.axis_size("head")
    pairs = seq // 2
    hops = -(-MOST // (2 * rows))
    halves = cuts_of(width)
    part = rows // groups
    anywhere = pl.BlockSpec(memory_space=pl.ANY)
    in_vmem = pl.BlockSpec(memory_space=pltpu.VMEM)
    in_smem = pl.BlockSpec(memory_space=pltpu.SMEM)
    f32, bf16 = jnp.float32, jnp.bfloat16
    inputs = (queries, keys, values, out_grad)
    sizes = dict(ndocs=ndocs, rows=rows)
    cheap = pl.CostEstimate(flops=0, bytes_accessed=1024, transcendentals=0)

    def shape_of(*dims, dtype=f32):
        return jax.ShapeDtypeStruct(dims, dtype)

    def call(name, kernel, args, outs, scratch=(), after=(), limit=VMEM_LIMIT):
        return pl.pallas_call(
            kernel, in_specs=[in_smem] + [in_vmem] * len(args) + [anywhere] * len(after), out_specs=[in_vmem] * len(outs), out_shape=outs,
            scratch_shapes=list(scratch), cost_estimate=cheap,
            compiler_params=pltpu.CompilerParams(vmem_limit_bytes=limit), name=name,
        )(doc_lengths, *args, *after)

    def swap_cores(a):
        return lax.ppermute(a, "seq", [(b, b ^ 1) for b in range(seq)])

    def swap_pairs(sent):
        came = []
        for hop in range(1, hops + 1):
            perm = [(2 * m, 2 * (m + hop) + 1) for m in range(pairs - hop)]
            came.append(lax.ppermute(sent[hop - 1], "seq", perm + [(b, a) for a, b in perm]))
        return came

    def send_rows(outs):
        arrived = list(outs[:1])
        for j in range(1, groups):
            arrived.append(lax.ppermute(outs[j], "head", [(x, (x + j) % groups) for x in range(groups)]))
        return arrived

    square = (HEAD_DIM, HEAD_DIM)

    def states(kept, offset, half):
        heads = half // HEAD_DIM
        group = GROUP if heads % GROUP == 0 else 2
        outs = [shape_of(heads, *square)] + [shape_of(rows, rows, dtype=bf16)] * (2 * kept)
        return pl.pallas_call(
            functools.partial(state_kernel, offset=offset, heads=heads, group=group, kept=kept, **sizes),
            in_specs=[anywhere] * 5, out_specs=[in_vmem] * len(outs), out_shape=outs,
            scratch_shapes=[
                pltpu.VMEM((2, rows, half), bf16), pltpu.SemaphoreType.DMA((heads // group, 2)),
                pltpu.SMEM((ndocs,), jnp.int32), pltpu.SemaphoreType.DMA,
            ],
            cost_estimate=cheap, compiler_params=pltpu.CompilerParams(vmem_limit_bytes=KEPT_LIMIT if kept else FIRST_LIMIT), name="states",
        )(doc_lengths, *inputs)

    def late_states(offset, half, after):
        heads = half // HEAD_DIM
        return call(
            "states", functools.partial(late_state_kernel, offset=offset, heads=heads, **sizes), inputs,
            [shape_of(heads, *square)] * 2, after=after, limit=GRAD_LIMIT,
        )

    def pair_up(kept, got, copies, after):
        lines = kept.shape[0] * HEAD_DIM
        outs = [shape_of(lines + PAD * (hops - hop + 1), HEAD_DIM, dtype=LINK) for hop in range(1, hops + 1)]
        outs += [shape_of(kept.shape[0] // max(copies, 1), *square)] * copies
        made = call(
            "pair", functools.partial(pair_kernel, hops=hops, copies=copies, **sizes), (kept, got), outs, after=after
        )
        return made[hops - 1], swap_pairs(made[:hops]), [swap_cores(a) for a in made[hops:]]

    def join(spans, others, came, after):
        made = call(
            "join", functools.partial(join_kernel, spans=spans, hops=hops, **sizes), (*others, *came),
            [shape_of(count, *square) for _, _, count in spans] * 2, after=after,
        )
        return [(mine, swap_cores(theirs)) for mine, theirs in zip(made[:len(spans)], made[len(spans):])]

    def grads(masks, offset, cw, mine, theirs, after):
        return call(
            "grads", functools.partial(grad_kernel, offset=offset, heads=cw // HEAD_DIM, groups=groups, **sizes),
            (*inputs, *masks, mine, theirs), [shape_of(3, part, cw, dtype=bf16)] * groups,
            [pltpu.VMEM((3, rows, cw), bf16)], after, GRAD_LIMIT,
        )

    def local(masks, offset, cw):
        kernel = functools.partial(local_kernel, offset=offset, heads=cw // HEAD_DIM)
        return call(
            "local", kernel, (*inputs, *masks), [shape_of(3, rows, cw), shape_of(8, HEAD_DIM)], limit=GRAD_LIMIT,
        )

    def carry_rows(shifts, near, offset, cw, mine, theirs, after):
        kernel = functools.partial(
            carry_rows_kernel, offset=offset, heads=cw // HEAD_DIM, groups=groups, shifts=shifts, **sizes
        )
        outs = [shape_of(3, part, cw, dtype=bf16)] * len(shifts)
        return call("carry", kernel, (*inputs[1:], near, mine, theirs), outs, after=after, limit=GRAD_LIMIT)

    cuts, outs, arrived, totals, masks, early = [], [], [], [], None, []
    for start, half, chunks in halves:
        if not totals:
            (sent,) = states(False, start, half)
            kept, *masks = states(True, start, half)
        else:
            kept, sent = late_states(start, half, [token])
        total, came, others = pair_up(
            kept, swap_cores(sent), len(chunks), [made[-1] for made in outs[:1]]
        )
        if not totals:
            near = [local(masks, *chunk) for chunk in chunks]
            token = near[0][1]
        count = chunks[0][1] // HEAD_DIM
        if totals:
            spans = [(0, c * count, count) for c in range(len(chunks))]
            joined = join(spans, others, came, [arrived[0][1]])
        else:
            joined, after = [], [made[1] for made in near]
            for c in range(len(chunks)):
                joined += join([(0, c * count, count)], others[c:c + 1], came, after)
                after = [joined[-1][0]]
        for c, ((offset, cw), (mine, theirs)) in enumerate(zip(chunks, joined)):
            after = [made[-1] for made in outs[-1:]] + [parts[1] for parts in arrived[1:-1]][-1:]
            if totals:
                outs.append(grads(masks, offset, cw, mine, theirs, after))
            else:
                after = after or [made for made, _ in joined[1:]]
                early.append((near[c][0], offset, cw, mine, theirs))
                outs.append([None, *carry_rows(range(1, groups), *early[-1], after)])
            arrived.append(send_rows(outs[-1]))
        if not totals:
            for c, parts in enumerate(early):
                arrived[c][0] = carry_rows([0], *parts, [outs[-1][-1]])[0]
        totals = [total]
        cuts += chunks

    placed = []
    for c in range(len(cuts)):
        own = [0, 1] if c == 0 else [c + 1]
        plan = [(arrived[n][0], (0, *cuts[n])) for n in own if n < len(cuts)]
        plan += [(arrived[c][j], (j, *cuts[c])) for j in range(1, groups)]
        some = [array for array, _ in plan]
        placed = pl.pallas_call(
            functools.partial(place_kernel, groups=groups, plan=[where for _, where in plan], width=width),
            grid_spec=pl.GridSpec(
                grid=(1,), in_specs=[anywhere] * (len(some) + len(placed)), out_specs=[anywhere] * 3,
                scratch_shapes=[pltpu.SemaphoreType.DMA((3 * len(some),))],
            ),
            out_shape=[shape_of(part, width * groups, dtype=bf16)] * 3,
            input_output_aliases={len(some) + i: i for i in range(len(placed))},
            cost_estimate=cheap,
            compiler_params=pltpu.CompilerParams(vmem_limit_bytes=VMEM_LIMIT), name="place",
        )(*some, *placed)
    return tuple(placed)


def solution(mesh):
    return jax.shard_map(
        shards,
        mesh=mesh,
        in_specs=(P("seq", "head"), P("seq", "head"), P("seq", "head"), P("seq", "head"), P()),
        out_specs=(P(("seq", "head"), None), P(("seq", "head"), None), P(("seq", "head"), None)),
        check_vma=False,
    )
```

```python
import functools

import jax
import jax.numpy as jnp
from jax import lax
from jax.experimental import pallas as pl
from jax.experimental.pallas import tpu as pltpu
from jax.sharding import PartitionSpec as P

HEAD_DIM = 128
MOST = 1024
GROUP = 4
CHUNK = 4
PAD = 16
LINK = jnp.bfloat16
VMEM_LIMIT = 16 * 1024 * 1024
GRAD_LIMIT = 32 * 1024 * 1024
FIRST_LIMIT = 53 * 1024 * 1024
KEPT_LIMIT = 53 * 1024 * 1024
NT = (((1,), (1,)), ((), ()))
TN = (((0,), (0,)), ((), ()))
NN = (((1,), (0,)), ((), ()))


def dot(a, b, dims):
    return lax.dot_general(a, b, dims, preferred_element_type=jnp.float32)


def doc_at(meta, ndocs, position):
    start, begin, end = jnp.int32(0), jnp.int32(0), jnp.int32(0)
    for i in range(ndocs):
        stop = start + meta[i]
        begin = jnp.where(start <= position, start, begin)
        end = jnp.where(start <= position, stop, end)
        start = stop
    return begin, end


def block_range(meta, ndocs, base, rows):
    begin0, end0 = doc_at(meta, ndocs, base)
    begin1, end1 = doc_at(meta, ndocs, base + rows - 1)
    first = jnp.where(begin0 < base, end0, base) - base
    return begin0, end0, begin1, end1, first, begin1 - base


def make_masks(lengths, lower, upper, ndocs, rows):
    line = lax.broadcasted_iota(jnp.int32, (rows, rows), 0)
    across = lax.broadcasted_iota(jnp.int32, (rows, rows), 1)
    begin_line = jnp.zeros((rows, rows), jnp.int32)
    begin_across = jnp.zeros((rows, rows), jnp.int32)
    start = jnp.int32(0) - lax.axis_index("seq") * rows
    for i in range(ndocs):
        begin_line = jnp.where(line >= start, start, begin_line)
        begin_across = jnp.where(across >= start, start, begin_across)
        start = start + lengths[i]
    lower[...] = jnp.where((across <= line) & (across >= begin_line), 1.0, 0.0).astype(lower.dtype)
    upper[...] = jnp.where((line <= across) & (line >= begin_across), 1.0, 0.0).astype(upper.dtype)


def fill_table(lengths, table, ndocs, rows, hops):
    place = lax.axis_index("seq")
    first_core = lax.rem(place, 2) == 0
    even = (place - lax.rem(place, 2)) * rows
    odd = even + rows
    even_b0, even_e0 = doc_at(lengths, ndocs, even)
    _, even_e1 = doc_at(lengths, ndocs, odd - 1)
    odd_b0, _ = doc_at(lengths, ndocs, odd)
    odd_b1, odd_e1 = doc_at(lengths, ndocs, odd + rows - 1)
    flags = [(odd_b1 < odd, even_e0 > odd)]
    flags += [(odd + rows + hop * 2 * rows < odd_e1, even - hop * 2 * rows > even_b0) for hop in range(hops)]
    flags += [(odd < even_e1, odd > odd_b0), (odd + rows < even_e1, even > odd_b0)]
    for row, (if_first, if_second) in enumerate(flags):
        value = jnp.where(jnp.where(first_core, if_first, if_second), 1.0, 0.0)
        table[row:row + 1] = jnp.full((1, HEAD_DIM), value, jnp.float32)


def state_kernel(lengths, q, k, v, g, out, *rest, ndocs, rows, offset, heads, group, kept, hops):
    *masks, held, sems, known, got = rest
    gw = group * HEAD_DIM
    place = lax.axis_index("seq")
    first_core = lax.rem(place, 2) == 0

    tails = first_core if kept else jnp.logical_not(first_core)

    def copy(c, i, ref):
        src = ref.at[:, pl.ds(offset + c * gw, gw)]
        return pltpu.make_async_copy(src, held.at[i, :, pl.ds(c * gw, gw)], sems.at[c, i])

    fetch = pltpu.make_async_copy(lengths, known, got)
    fetch.start()
    for c in range(heads // group):

        @pl.when(tails)
        def _():
            copy(c, 0, k).start()
            copy(c, 1, v).start()

        @pl.when(jnp.logical_not(tails))
        def _():
            copy(c, 0, q).start()
            copy(c, 1, g).start()

    fetch.wait()
    if masks:
        make_masks(known, *masks[:2], ndocs, rows)
        fill_table(known, masks[2], ndocs, rows, hops)
    _, _, _, _, first, last = block_range(known, ndocs, place * rows, rows)
    order = lax.broadcasted_iota(jnp.int32, (rows, HEAD_DIM), 0)
    zero = jnp.zeros((), held.dtype)
    low, high = jnp.where(tails, last, 0), jnp.where(tails, rows, first)
    here = (order >= low) & (order < high)
    for h in range(heads):
        if h % group == 0:
            copy(h // group, 0, k).wait()
            copy(h // group, 1, v).wait()
        cols = slice(h * HEAD_DIM, (h + 1) * HEAD_DIM)
        out[h] = dot(jnp.where(here, held[0, :, cols], zero), held[1, :, cols], TN)


def late_state_kernel(lengths, q, k, v, g, *rest, ndocs, rows, offset, heads):
    kept, sent = rest[-2:]
    first_core, first_rows, last_rows = own_range(lengths, ndocs, rows)
    zero = jnp.zeros((), q.dtype)
    for h in range(heads):
        at = slice(offset + h * HEAD_DIM, offset + (h + 1) * HEAD_DIM)
        tail = dot(jnp.where(last_rows, k[:, at], zero), v[:, at], TN)
        head = dot(jnp.where(first_rows, q[:, at], zero), g[:, at], TN)
        kept[h] = jnp.where(first_core, tail, head)
        sent[h] = jnp.where(first_core, head, tail)


def pair_kernel(table, kept, got, *rest, hops, copies):
    sent, again = rest[-hops - copies:len(rest) - copies], rest[len(rest) - copies:]
    joins = table[0:1]
    size = kept.shape[0] * HEAD_DIM
    total = (got[...] + joins * kept[...]).astype(LINK).reshape(size, HEAD_DIM)
    for out in sent:
        out[:size] = total
        if out.shape[0] > size:
            out[size:] = jnp.zeros((out.shape[0] - size, HEAD_DIM), LINK)
    for i, out in enumerate(again):
        count = out.shape[0]
        out[...] = kept[i * count:(i + 1) * count]


def join_kernel(table, *rest, spans, hops):
    others, came = rest[:len(spans)], rest[len(spans):len(spans) + hops]
    mine, theirs = rest[-2 * len(spans):-len(spans)], rest[-len(spans):]
    weights = [table[1 + hop:2 + hop] for hop in range(hops)]
    from_other, from_pair = table[1 + hops:2 + hops], table[2 + hops:3 + hops]
    for c, (other_at, came_at, count) in enumerate(spans):
        lines = slice(came_at * HEAD_DIM, (came_at + count) * HEAD_DIM)
        total = weights[0] * came[0][lines].astype(jnp.float32)
        for hop in range(1, hops):
            total = total + weights[hop] * came[hop][lines].astype(jnp.float32)
        total = total.reshape(count, HEAD_DIM, HEAD_DIM)
        theirs[c][...] = total
        mine[c][...] = from_other * others[c][other_at:other_at + count] + from_pair * total


def split(a, axis):
    high = a.astype(jnp.bfloat16)
    return jnp.concatenate([high, (a - high.astype(jnp.float32)).astype(jnp.bfloat16)], axis=axis)


def own_range(lengths, ndocs, rows):
    place = lax.axis_index("seq")
    _, _, _, _, first, last = block_range(lengths, ndocs, place * rows, rows)
    order = lax.broadcasted_iota(jnp.int32, (rows, HEAD_DIM), 0)
    return lax.rem(place, 2) == 0, order < first, order >= last


def local_part(q, k, v, g, lower, upper, at):
    qh, kh, vh, gh = (ref[:, at] for ref in (q, k, v, g))
    weight_gv = dot(gh, vh, NT).astype(jnp.bfloat16) * lower[...]
    weight_vg = dot(vh, gh, NT).astype(jnp.bfloat16) * upper[...]
    weight_kq = dot(kh, qh, NT).astype(jnp.bfloat16) * upper[...]
    return dot(weight_gv, kh, NN), dot(weight_vg, qh, NN), dot(weight_kq, gh, NN)


def twice(ref, at):
    return jnp.concatenate([ref[:, at]] * 2, axis=1)


def carry_of_state(g, state, first_rows, at):
    return jnp.where(first_rows, dot(twice(g, at), split(state, 1), NT), 0.0)


def carries_of_grad(k, v, grad, last_rows, at):
    carry_k = jnp.where(last_rows, dot(twice(v, at), split(grad, 1), NT), 0.0)
    return carry_k, jnp.where(last_rows, dot(twice(k, at), split(grad, 0), NN), 0.0)


def deal(done, outs, rows, groups):
    part, column = rows // groups, lax.axis_index("head")
    for j in range(groups):
        at = pl.ds(pl.multiple_of(lax.rem(column + j, groups) * part, part), part)
        for i in range(3):
            outs[j][i] = done[i, at, :]


def grad_kernel(lengths, q, k, v, g, lower, upper, mine, got, *rest, ndocs, rows, offset, heads, groups):
    outs, done = rest[-1 - groups:-1], rest[-1]
    first_core, first_rows, last_rows = own_range(lengths, ndocs, rows)
    for h in range(heads):
        cols = slice(h * HEAD_DIM, (h + 1) * HEAD_DIM)
        at = slice(offset + h * HEAD_DIM, offset + (h + 1) * HEAD_DIM)
        state = jnp.where(first_core, got[h], mine[h])
        grad = jnp.where(first_core, mine[h], got[h])
        near = local_part(q, k, v, g, lower, upper, at)
        carries = (carry_of_state(g, state, first_rows, at), *carries_of_grad(k, v, grad, last_rows, at))
        for i in range(3):
            done[i, :, cols] = (near[i] + carries[i]).astype(jnp.bfloat16)
    deal(done, outs, rows, groups)


def local_kernel(lengths, q, k, v, g, lower, upper, near, token, *, offset, heads):
    token[...] = jnp.zeros_like(token)
    for h in range(heads):
        cols = slice(h * HEAD_DIM, (h + 1) * HEAD_DIM)
        at = slice(offset + h * HEAD_DIM, offset + (h + 1) * HEAD_DIM)
        for i, value in enumerate(local_part(q, k, v, g, lower, upper, at)):
            near[i, :, cols] = value


def carry_kernel(lengths, k, v, g, near, mine, got, *rest, ndocs, rows, offset, heads, groups):
    outs, done = rest[-1 - groups:-1], rest[-1]
    first_core, first_rows, last_rows = own_range(lengths, ndocs, rows)
    for h in range(heads):
        cols = slice(h * HEAD_DIM, (h + 1) * HEAD_DIM)
        at = slice(offset + h * HEAD_DIM, offset + (h + 1) * HEAD_DIM)
        state = jnp.where(first_core, got[h], mine[h])
        grad = jnp.where(first_core, mine[h], got[h])
        carries = (carry_of_state(g, state, first_rows, at), *carries_of_grad(k, v, grad, last_rows, at))
        for i in range(3):
            done[i, :, cols] = (near[i, :, cols] + carries[i]).astype(jnp.bfloat16)
    deal(done, outs, rows, groups)


def carry_rows_kernel(lengths, k, v, g, near, mine, got, *rest, ndocs, rows, offset, heads, groups, shifts):
    outs = rest[-len(shifts):]
    place, column, part = lax.axis_index("seq"), lax.axis_index("head"), rows // groups
    first_core = lax.rem(place, 2) == 0
    _, _, _, _, first, last = block_range(lengths, ndocs, place * rows, rows)
    order = lax.broadcasted_iota(jnp.int32, (part, HEAD_DIM), 0)
    for j, out in zip(shifts, outs):
        start = pl.multiple_of(lax.rem(column + j, groups) * part, part)
        lines = pl.ds(start, part)
        first_rows, last_rows = order + start < first, order + start >= last
        for h in range(heads):
            cols = slice(h * HEAD_DIM, (h + 1) * HEAD_DIM)
            at = slice(offset + h * HEAD_DIM, offset + (h + 1) * HEAD_DIM)
            state = split(jnp.where(first_core, got[h], mine[h]), 1)
            grad = jnp.where(first_core, mine[h], got[h])
            k2, v2, g2 = (jnp.concatenate([ref[lines, at]] * 2, axis=1) for ref in (k, v, g))
            carry_q = jnp.where(first_rows, dot(g2, state, NT), 0.0)
            carry_k = jnp.where(last_rows, dot(v2, split(grad, 1), NT), 0.0)
            carry_v = jnp.where(last_rows, dot(k2, split(grad, 0), NN), 0.0)
            for i, value in enumerate((carry_q, carry_k, carry_v)):
                out[i, :, cols] = (near[i, lines, cols] + value).astype(jnp.bfloat16)


def place_kernel(*refs, groups, plan, width):
    parts, outs, sems = refs[:len(plan)], refs[-4:-1], refs[-1]
    column = lax.axis_index("head")
    copies = []
    for ref, (j, offset, cw) in zip(parts, plan):
        start = pl.multiple_of(lax.rem(column + groups - j, groups) * width + offset, 128)
        for i in range(3):
            copies.append(pltpu.make_async_copy(ref.at[i], outs[i].at[:, pl.ds(start, cw)], sems.at[len(copies)]))
            copies[-1].start()
    for copy in copies:
        copy.wait()


def cuts_of(width):
    heads = width // HEAD_DIM
    size = CHUNK if heads % (2 * CHUNK) == 0 else 2
    cw, half = size * HEAD_DIM, max(heads // 2, size) * HEAD_DIM
    return [(at, half, [(o, cw) for o in range(at, at + half, cw)]) for at in range(0, width, half)]


def shards(queries, keys, values, out_grad, doc_lengths):
    rows, width = queries.shape
    ndocs = doc_lengths.shape[0]
    seq, groups = lax.axis_size("seq"), lax.axis_size("head")
    pairs = seq // 2
    hops = -(-MOST // (2 * rows))
    halves = cuts_of(width)
    part = rows // groups
    anywhere = pl.BlockSpec(memory_space=pl.ANY)
    in_vmem = pl.BlockSpec(memory_space=pltpu.VMEM)
    in_smem = pl.BlockSpec(memory_space=pltpu.SMEM)
    f32, bf16 = jnp.float32, jnp.bfloat16
    inputs = (queries, keys, values, out_grad)
    sizes = dict(ndocs=ndocs, rows=rows)
    cheap = pl.CostEstimate(flops=0, bytes_accessed=1024, transcendentals=0)

    def shape_of(*dims, dtype=f32):
        return jax.ShapeDtypeStruct(dims, dtype)

    def call(name, kernel, args, outs, scratch=(), after=(), limit=VMEM_LIMIT, known=None):
        known = doc_lengths if known is None else known
        return pl.pallas_call(
            kernel, in_specs=[in_smem if known is doc_lengths else in_vmem] + [in_vmem] * len(args) + [anywhere] * len(after), out_specs=[in_vmem] * len(outs), out_shape=outs,
            scratch_shapes=list(scratch), cost_estimate=cheap,
            compiler_params=pltpu.CompilerParams(vmem_limit_bytes=limit), name=name,
        )(known, *args, *after)

    def swap_cores(a):
        return lax.ppermute(a, "seq", [(b, b ^ 1) for b in range(seq)])

    def swap_pairs(sent):
        came = []
        for hop in range(1, hops + 1):
            perm = [(2 * m, 2 * (m + hop) + 1) for m in range(pairs - hop)]
            came.append(lax.ppermute(sent[hop - 1], "seq", perm + [(b, a) for a, b in perm]))
        return came

    def send_rows(outs):
        arrived = list(outs[:1])
        for j in range(1, groups):
            arrived.append(lax.ppermute(outs[j], "head", [(x, (x + j) % groups) for x in range(groups)]))
        return arrived

    square = (HEAD_DIM, HEAD_DIM)

    def states(kept, offset, half):
        heads = half // HEAD_DIM
        group = GROUP if heads % GROUP == 0 else 2
        outs = [shape_of(heads, *square)] + ([shape_of(rows, rows, dtype=bf16)] * 2 + [shape_of(16, HEAD_DIM)]) * kept
        return pl.pallas_call(
            functools.partial(state_kernel, offset=offset, heads=heads, group=group, kept=kept, hops=hops, **sizes),
            in_specs=[anywhere] * 5, out_specs=[in_vmem] * len(outs), out_shape=outs,
            scratch_shapes=[
                pltpu.VMEM((2, rows, half), bf16), pltpu.SemaphoreType.DMA((heads // group, 2)),
                pltpu.SMEM((ndocs,), jnp.int32), pltpu.SemaphoreType.DMA,
            ],
            cost_estimate=cheap, compiler_params=pltpu.CompilerParams(vmem_limit_bytes=KEPT_LIMIT if kept else FIRST_LIMIT), name="states",
        )(doc_lengths, *inputs)

    def late_states(offset, half, after):
        heads = half // HEAD_DIM
        return call(
            "states", functools.partial(late_state_kernel, offset=offset, heads=heads, **sizes), inputs,
            [shape_of(heads, *square)] * 2, after=after, limit=GRAD_LIMIT,
        )

    def pair_up(table, kept, got, copies, after):
        lines = kept.shape[0] * HEAD_DIM
        outs = [shape_of(lines + PAD * (hops - hop + 1), HEAD_DIM, dtype=LINK) for hop in range(1, hops + 1)]
        outs += [shape_of(kept.shape[0] // max(copies, 1), *square)] * copies
        made = call(
            "pair", functools.partial(pair_kernel, hops=hops, copies=copies), (kept, got), outs, after=after, known=table
        )
        return made[hops - 1], swap_pairs(made[:hops]), [swap_cores(a) for a in made[hops:]]

    def join(table, spans, others, came, after):
        made = call(
            "join", functools.partial(join_kernel, spans=spans, hops=hops), (*others, *came),
            [shape_of(count, *square) for _, _, count in spans] * 2, after=after, known=table,
        )
        return [(mine, swap_cores(theirs)) for mine, theirs in zip(made[:len(spans)], made[len(spans):])]

    def grads(masks, offset, cw, mine, theirs, after):
        return call(
            "grads", functools.partial(grad_kernel, offset=offset, heads=cw // HEAD_DIM, groups=groups, **sizes),
            (*inputs, *masks, mine, theirs), [shape_of(3, part, cw, dtype=bf16)] * groups,
            [pltpu.VMEM((3, rows, cw), bf16)], after, GRAD_LIMIT,
        )

    def local(masks, offset, cw):
        kernel = functools.partial(local_kernel, offset=offset, heads=cw // HEAD_DIM)
        return call(
            "local", kernel, (*inputs, *masks), [shape_of(3, rows, cw), shape_of(8, HEAD_DIM)], limit=GRAD_LIMIT,
        )

    def carry(near, offset, cw, mine, theirs, after):
        kernel = functools.partial(carry_kernel, offset=offset, heads=cw // HEAD_DIM, groups=groups, **sizes)
        return call(
            "carry", kernel, (*inputs[1:], near, mine, theirs), [shape_of(3, part, cw, dtype=bf16)] * groups,
            [pltpu.VMEM((3, rows, cw), bf16)], after, GRAD_LIMIT,
        )

    def carry_rows(shifts, near, offset, cw, mine, theirs, after):
        kernel = functools.partial(
            carry_rows_kernel, offset=offset, heads=cw // HEAD_DIM, groups=groups, shifts=shifts, **sizes
        )
        outs = [shape_of(3, part, cw, dtype=bf16)] * len(shifts)
        return call("carry", kernel, (*inputs[1:], near, mine, theirs), outs, after=after, limit=GRAD_LIMIT)

    cuts, outs, arrived, totals, masks = [], [], [], [], None
    for start, half, chunks in halves:
        if not totals:
            (sent,) = states(False, start, half)
            kept, *masks, table = states(True, start, half)
        else:
            kept, sent = late_states(start, half, [token])
        total, came, others = pair_up(
            table, kept, swap_cores(sent), 0 if totals else len(chunks), [made[-1] for made in outs[:1]]
        )
        if not totals:
            near = [local(masks, *chunk) for chunk in chunks]
            token = near[0][1]
        count = chunks[0][1] // HEAD_DIM
        if totals:
            spans = [(c * count, c * count, count) for c in range(len(chunks))]
            joined = join(table, spans, [swap_cores(kept)] * len(chunks), came, [arrived[0][1]])
        else:
            joined, after = [], [made[1] for made in near]
            for c in range(len(chunks)):
                joined += join(table, [(0, c * count, count)], others[c:c + 1], came, after)
                after = [joined[-1][0]]
        for c, ((offset, cw), (mine, theirs)) in enumerate(zip(chunks, joined)):
            after = [made[-1] for made in outs[-1:]] + [parts[1] for parts in arrived[1:-1]][-1:]
            if totals:
                outs.append(grads(masks, offset, cw, mine, theirs, after))
            elif c == 0:
                first = (near[0][0], offset, cw, mine, theirs)
                outs.append([None, *carry_rows(range(1, groups), *first, [made for made, _ in joined[1:]])])
            else:
                outs.append(carry(near[c][0], offset, cw, mine, theirs, after))
            arrived.append(send_rows(outs[-1]))
        if not totals:
            arrived[0][0] = carry_rows([0], *first, [outs[-1][-1]])[0]
        totals = [total]
        cuts += chunks

    placed = []
    for c in range(len(cuts)):
        own = [0, 1] if c == 0 else [c + 1]
        plan = [(arrived[n][0], (0, *cuts[n])) for n in own if n < len(cuts)]
        plan += [(arrived[c][j], (j, *cuts[c])) for j in range(1, groups)]
        some = [array for array, _ in plan]
        placed = pl.pallas_call(
            functools.partial(place_kernel, groups=groups, plan=[where for _, where in plan], width=width),
            grid_spec=pl.GridSpec(
                grid=(1,), in_specs=[anywhere] * (len(some) + len(placed)), out_specs=[anywhere] * 3,
                scratch_shapes=[pltpu.SemaphoreType.DMA((3 * len(some),))],
            ),
            out_shape=[shape_of(part, width * groups, dtype=bf16)] * 3,
            input_output_aliases={len(some) + i: i for i in range(len(placed))},
            cost_estimate=cheap,
            compiler_params=pltpu.CompilerParams(vmem_limit_bytes=VMEM_LIMIT), name="place",
        )(*some, *placed)
    return tuple(placed)


def solution(mesh):
    return jax.shard_map(
        shards,
        mesh=mesh,
        in_specs=(P("seq", "head"), P("seq", "head"), P("seq", "head"), P("seq", "head"), P()),
        out_specs=(P(("seq", "head"), None), P(("seq", "head"), None), P(("seq", "head"), None)),
        check_vma=False,
    )
```

```python
import functools

import jax
import jax.numpy as jnp
from jax import lax
from jax.experimental import pallas as pl
from jax.experimental.pallas import tpu as pltpu
from jax.sharding import PartitionSpec as P

HEAD_DIM = 128
MOST = 1024
GROUP = 4
CHUNK = 4
PAD = 16
FIRST, LAST = 14, 15
LINK = jnp.bfloat16
VMEM_LIMIT = 16 * 1024 * 1024
GRAD_LIMIT = 32 * 1024 * 1024
FIRST_LIMIT = 53 * 1024 * 1024
KEPT_LIMIT = 53 * 1024 * 1024
NT = (((1,), (1,)), ((), ()))
TN = (((0,), (0,)), ((), ()))
NN = (((1,), (0,)), ((), ()))


def dot(a, b, dims):
    return lax.dot_general(a, b, dims, preferred_element_type=jnp.float32)


def doc_at(meta, ndocs, position):
    start, begin, end = jnp.int32(0), jnp.int32(0), jnp.int32(0)
    for i in range(ndocs):
        stop = start + meta[i]
        begin = jnp.where(start <= position, start, begin)
        end = jnp.where(start <= position, stop, end)
        start = stop
    return begin, end


def block_range(meta, ndocs, base, rows):
    begin0, end0 = doc_at(meta, ndocs, base)
    begin1, end1 = doc_at(meta, ndocs, base + rows - 1)
    first = jnp.where(begin0 < base, end0, base) - base
    return begin0, end0, begin1, end1, first, begin1 - base


def make_masks(lengths, lower, upper, ndocs, rows):
    line = lax.broadcasted_iota(jnp.int32, (rows, rows), 0)
    across = lax.broadcasted_iota(jnp.int32, (rows, rows), 1)
    begin_line = jnp.zeros((rows, rows), jnp.int32)
    begin_across = jnp.zeros((rows, rows), jnp.int32)
    start = jnp.int32(0) - lax.axis_index("seq") * rows
    for i in range(ndocs):
        begin_line = jnp.where(line >= start, start, begin_line)
        begin_across = jnp.where(across >= start, start, begin_across)
        start = start + lengths[i]
    lower[...] = jnp.where((across <= line) & (across >= begin_line), 1.0, 0.0).astype(lower.dtype)
    upper[...] = jnp.where((line <= across) & (line >= begin_across), 1.0, 0.0).astype(upper.dtype)


def fill_table(lengths, table, ndocs, rows, hops):
    place = lax.axis_index("seq")
    first_core = lax.rem(place, 2) == 0
    even = (place - lax.rem(place, 2)) * rows
    odd = even + rows
    even_b0, even_e0 = doc_at(lengths, ndocs, even)
    _, even_e1 = doc_at(lengths, ndocs, odd - 1)
    odd_b0, _ = doc_at(lengths, ndocs, odd)
    odd_b1, odd_e1 = doc_at(lengths, ndocs, odd + rows - 1)
    flags = [(odd_b1 < odd, even_e0 > odd)]
    flags += [(odd + rows + hop * 2 * rows < odd_e1, even - hop * 2 * rows > even_b0) for hop in range(hops)]
    flags += [(odd < even_e1, odd > odd_b0), (odd + rows < even_e1, even > odd_b0)]
    for row, (if_first, if_second) in enumerate(flags):
        value = jnp.where(jnp.where(first_core, if_first, if_second), 1.0, 0.0)
        table[row:row + 1] = jnp.full((1, HEAD_DIM), value, jnp.float32)
    _, _, _, _, first, last = block_range(lengths, ndocs, place * rows, rows)
    for row, value in ((FIRST, first), (LAST, last)):
        table[row:row + 1] = jnp.full((1, HEAD_DIM), value, jnp.int32).astype(jnp.float32)


def state_kernel(lengths, q, k, v, g, out, *rest, ndocs, rows, offset, heads, group, kept, hops):
    *masks, held, sems, known, got = rest
    gw = group * HEAD_DIM
    place = lax.axis_index("seq")
    first_core = lax.rem(place, 2) == 0

    tails = first_core if kept else jnp.logical_not(first_core)

    def copy(c, i, ref):
        src = ref.at[:, pl.ds(offset + c * gw, gw)]
        return pltpu.make_async_copy(src, held.at[i, :, pl.ds(c * gw, gw)], sems.at[c, i])

    fetch = pltpu.make_async_copy(lengths, known, got)
    fetch.start()
    for c in range(heads // group):

        @pl.when(tails)
        def _():
            copy(c, 0, k).start()
            copy(c, 1, v).start()

        @pl.when(jnp.logical_not(tails))
        def _():
            copy(c, 0, q).start()
            copy(c, 1, g).start()

    fetch.wait()
    if masks:
        make_masks(known, *masks[:2], ndocs, rows)
        fill_table(known, masks[2], ndocs, rows, hops)
    _, _, _, _, first, last = block_range(known, ndocs, place * rows, rows)
    order = lax.broadcasted_iota(jnp.int32, (rows, HEAD_DIM), 0)
    zero = jnp.zeros((), held.dtype)
    low, high = jnp.where(tails, last, 0), jnp.where(tails, rows, first)
    here = (order >= low) & (order < high)
    for h in range(heads):
        if h % group == 0:
            copy(h // group, 0, k).wait()
            copy(h // group, 1, v).wait()
        cols = slice(h * HEAD_DIM, (h + 1) * HEAD_DIM)
        out[h] = dot(jnp.where(here, held[0, :, cols], zero), held[1, :, cols], TN)


def late_state_kernel(table, q, k, v, g, *rest, ndocs, rows, offset, heads):
    kept, sent = rest[-2:]
    first_core, first_rows, last_rows = own_range(table, rows)
    zero = jnp.zeros((), q.dtype)
    for h in range(heads):
        at = slice(offset + h * HEAD_DIM, offset + (h + 1) * HEAD_DIM)
        tail = dot(jnp.where(last_rows, k[:, at], zero), v[:, at], TN)
        head = dot(jnp.where(first_rows, q[:, at], zero), g[:, at], TN)
        kept[h] = jnp.where(first_core, tail, head)
        sent[h] = jnp.where(first_core, head, tail)


def pair_kernel(table, kept, got, *rest, hops, copies):
    sent, again = rest[-hops - copies:len(rest) - copies], rest[len(rest) - copies:]
    joins = table[0:1]
    size = kept.shape[0] * HEAD_DIM
    total = (got[...] + joins * kept[...]).astype(LINK).reshape(size, HEAD_DIM)
    for out in sent:
        out[:size] = total
        if out.shape[0] > size:
            out[size:] = jnp.zeros((out.shape[0] - size, HEAD_DIM), LINK)
    for i, out in enumerate(again):
        count = out.shape[0]
        out[...] = kept[i * count:(i + 1) * count]


def join_kernel(table, *rest, spans, hops):
    others, came = rest[:len(spans)], rest[len(spans):len(spans) + hops]
    mine, theirs = rest[-2 * len(spans):-len(spans)], rest[-len(spans):]
    weights = [table[1 + hop:2 + hop] for hop in range(hops)]
    from_other, from_pair = table[1 + hops:2 + hops], table[2 + hops:3 + hops]
    for c, (other_at, came_at, count) in enumerate(spans):
        lines = slice(came_at * HEAD_DIM, (came_at + count) * HEAD_DIM)
        total = weights[0] * came[0][lines].astype(jnp.float32)
        for hop in range(1, hops):
            total = total + weights[hop] * came[hop][lines].astype(jnp.float32)
        total = total.reshape(count, HEAD_DIM, HEAD_DIM)
        theirs[c][...] = total
        mine[c][...] = from_other * others[c][other_at:other_at + count] + from_pair * total


def split(a, axis):
    high = a.astype(jnp.bfloat16)
    return jnp.concatenate([high, (a - high.astype(jnp.float32)).astype(jnp.bfloat16)], axis=axis)


def own_range(table, rows, start=0):
    order = (lax.broadcasted_iota(jnp.int32, (rows, HEAD_DIM), 0) + start).astype(jnp.float32)
    return lax.rem(lax.axis_index("seq"), 2) == 0, order < table[FIRST:FIRST + 1], order >= table[LAST:LAST + 1]


def local_part(q, k, v, g, lower, upper, at):
    qh, kh, vh, gh = (ref[:, at] for ref in (q, k, v, g))
    weight_gv = dot(gh, vh, NT).astype(jnp.bfloat16) * lower[...]
    weight_vg = dot(vh, gh, NT).astype(jnp.bfloat16) * upper[...]
    weight_kq = dot(kh, qh, NT).astype(jnp.bfloat16) * upper[...]
    return dot(weight_gv, kh, NN), dot(weight_vg, qh, NN), dot(weight_kq, gh, NN)


def twice(ref, at):
    return jnp.concatenate([ref[:, at]] * 2, axis=1)


def carry_of_state(g, state, first_rows, at):
    return jnp.where(first_rows, dot(twice(g, at), split(state, 1), NT), 0.0)


def carries_of_grad(k, v, grad, last_rows, at):
    carry_k = jnp.where(last_rows, dot(twice(v, at), split(grad, 1), NT), 0.0)
    return carry_k, jnp.where(last_rows, dot(twice(k, at), split(grad, 0), NN), 0.0)


def deal(done, outs, rows, groups):
    part, column = rows // groups, lax.axis_index("head")
    for j in range(groups):
        at = pl.ds(pl.multiple_of(lax.rem(column + j, groups) * part, part), part)
        for i in range(3):
            outs[j][i] = done[i, at, :]


def grad_kernel(table, q, k, v, g, lower, upper, mine, got, *rest, ndocs, rows, offset, heads, groups):
    outs, done = rest[-1 - groups:-1], rest[-1]
    first_core, first_rows, last_rows = own_range(table, rows)
    for h in range(heads):
        cols = slice(h * HEAD_DIM, (h + 1) * HEAD_DIM)
        at = slice(offset + h * HEAD_DIM, offset + (h + 1) * HEAD_DIM)
        state = jnp.where(first_core, got[h], mine[h])
        grad = jnp.where(first_core, mine[h], got[h])
        near = local_part(q, k, v, g, lower, upper, at)
        carries = (carry_of_state(g, state, first_rows, at), *carries_of_grad(k, v, grad, last_rows, at))
        for i in range(3):
            done[i, :, cols] = (near[i] + carries[i]).astype(jnp.bfloat16)
    deal(done, outs, rows, groups)


def local_kernel(table, q, k, v, g, lower, upper, near, token, *, offset, heads):
    token[...] = jnp.zeros_like(token)
    for h in range(heads):
        cols = slice(h * HEAD_DIM, (h + 1) * HEAD_DIM)
        at = slice(offset + h * HEAD_DIM, offset + (h + 1) * HEAD_DIM)
        for i, value in enumerate(local_part(q, k, v, g, lower, upper, at)):
            near[i, :, cols] = value


def carry_kernel(table, k, v, g, near, mine, got, *rest, ndocs, rows, offset, heads, groups):
    outs, done = rest[-1 - groups:-1], rest[-1]
    first_core, first_rows, last_rows = own_range(table, rows)
    for h in range(heads):
        cols = slice(h * HEAD_DIM, (h + 1) * HEAD_DIM)
        at = slice(offset + h * HEAD_DIM, offset + (h + 1) * HEAD_DIM)
        state = jnp.where(first_core, got[h], mine[h])
        grad = jnp.where(first_core, mine[h], got[h])
        carries = (carry_of_state(g, state, first_rows, at), *carries_of_grad(k, v, grad, last_rows, at))
        for i in range(3):
            done[i, :, cols] = (near[i, :, cols] + carries[i]).astype(jnp.bfloat16)
    deal(done, outs, rows, groups)


def carry_rows_kernel(table, k, v, g, near, mine, got, *rest, ndocs, rows, offset, heads, groups, shifts):
    outs = rest[-len(shifts):]
    column, part = lax.axis_index("head"), rows // groups
    for j, out in zip(shifts, outs):
        start = pl.multiple_of(lax.rem(column + j, groups) * part, part)
        lines = pl.ds(start, part)
        first_core, first_rows, last_rows = own_range(table, part, start)
        for h in range(heads):
            cols = slice(h * HEAD_DIM, (h + 1) * HEAD_DIM)
            at = slice(offset + h * HEAD_DIM, offset + (h + 1) * HEAD_DIM)
            state = split(jnp.where(first_core, got[h], mine[h]), 1)
            grad = jnp.where(first_core, mine[h], got[h])
            k2, v2, g2 = (jnp.concatenate([ref[lines, at]] * 2, axis=1) for ref in (k, v, g))
            carry_q = jnp.where(first_rows, dot(g2, state, NT), 0.0)
            carry_k = jnp.where(last_rows, dot(v2, split(grad, 1), NT), 0.0)
            carry_v = jnp.where(last_rows, dot(k2, split(grad, 0), NN), 0.0)
            for i, value in enumerate((carry_q, carry_k, carry_v)):
                out[i, :, cols] = (near[i, lines, cols] + value).astype(jnp.bfloat16)


def place_kernel(*refs, groups, plan, width):
    parts, outs, sems = refs[:len(plan)], refs[-4:-1], refs[-1]
    column = lax.axis_index("head")
    copies = []
    for ref, (j, offset, cw) in zip(parts, plan):
        start = pl.multiple_of(lax.rem(column + groups - j, groups) * width + offset, 128)
        for i in range(3):
            copies.append(pltpu.make_async_copy(ref.at[i], outs[i].at[:, pl.ds(start, cw)], sems.at[len(copies)]))
            copies[-1].start()
    for copy in copies:
        copy.wait()


def cuts_of(width):
    heads = width // HEAD_DIM
    size = CHUNK if heads % (2 * CHUNK) == 0 else 2
    cw, half = size * HEAD_DIM, max(heads // 2, size) * HEAD_DIM
    return [(at, half, [(o, cw) for o in range(at, at + half, cw)]) for at in range(0, width, half)]


def shards(queries, keys, values, out_grad, doc_lengths):
    rows, width = queries.shape
    ndocs = doc_lengths.shape[0]
    seq, groups = lax.axis_size("seq"), lax.axis_size("head")
    pairs = seq // 2
    hops = -(-MOST // (2 * rows))
    halves = cuts_of(width)
    part = rows // groups
    anywhere = pl.BlockSpec(memory_space=pl.ANY)
    in_vmem = pl.BlockSpec(memory_space=pltpu.VMEM)
    in_smem = pl.BlockSpec(memory_space=pltpu.SMEM)
    f32, bf16 = jnp.float32, jnp.bfloat16
    inputs = (queries, keys, values, out_grad)
    sizes = dict(ndocs=ndocs, rows=rows)
    cheap = pl.CostEstimate(flops=0, bytes_accessed=1024, transcendentals=0)

    def shape_of(*dims, dtype=f32):
        return jax.ShapeDtypeStruct(dims, dtype)

    def call(name, kernel, args, outs, scratch=(), after=(), limit=VMEM_LIMIT, known=None):
        known = doc_lengths if known is None else known
        return pl.pallas_call(
            kernel, in_specs=[in_smem if known is doc_lengths else in_vmem] + [in_vmem] * len(args) + [anywhere] * len(after), out_specs=[in_vmem] * len(outs), out_shape=outs,
            scratch_shapes=list(scratch), cost_estimate=cheap,
            compiler_params=pltpu.CompilerParams(vmem_limit_bytes=limit), name=name,
        )(known, *args, *after)

    def swap_cores(a):
        return lax.ppermute(a, "seq", [(b, b ^ 1) for b in range(seq)])

    def swap_pairs(sent):
        came = []
        for hop in range(1, hops + 1):
            perm = [(2 * m, 2 * (m + hop) + 1) for m in range(pairs - hop)]
            came.append(lax.ppermute(sent[hop - 1], "seq", perm + [(b, a) for a, b in perm]))
        return came

    def send_rows(outs):
        arrived = list(outs[:1])
        for j in range(1, groups):
            arrived.append(lax.ppermute(outs[j], "head", [(x, (x + j) % groups) for x in range(groups)]))
        return arrived

    square = (HEAD_DIM, HEAD_DIM)

    def states(kept, offset, half):
        heads = half // HEAD_DIM
        group = GROUP if heads % GROUP == 0 else 2
        outs = [shape_of(heads, *square)] + ([shape_of(rows, rows, dtype=bf16)] * 2 + [shape_of(16, HEAD_DIM)]) * kept
        return pl.pallas_call(
            functools.partial(state_kernel, offset=offset, heads=heads, group=group, kept=kept, hops=hops, **sizes),
            in_specs=[anywhere] * 5, out_specs=[in_vmem] * len(outs), out_shape=outs,
            scratch_shapes=[
                pltpu.VMEM((2, rows, half), bf16), pltpu.SemaphoreType.DMA((heads // group, 2)),
                pltpu.SMEM((ndocs,), jnp.int32), pltpu.SemaphoreType.DMA,
            ],
            cost_estimate=cheap, compiler_params=pltpu.CompilerParams(vmem_limit_bytes=KEPT_LIMIT if kept else FIRST_LIMIT), name="states",
        )(doc_lengths, *inputs)

    def late_states(offset, half, after):
        heads = half // HEAD_DIM
        return call(
            "states", functools.partial(late_state_kernel, offset=offset, heads=heads, **sizes), inputs,
            [shape_of(heads, *square)] * 2, after=after, limit=GRAD_LIMIT, known=table,
        )

    def pair_up(table, kept, got, copies, after):
        lines = kept.shape[0] * HEAD_DIM
        outs = [shape_of(lines + PAD * (hops - hop + 1), HEAD_DIM, dtype=LINK) for hop in range(1, hops + 1)]
        outs += [shape_of(kept.shape[0] // max(copies, 1), *square)] * copies
        made = call(
            "pair", functools.partial(pair_kernel, hops=hops, copies=copies), (kept, got), outs, after=after, known=table
        )
        return made[hops - 1], swap_pairs(made[:hops]), [swap_cores(a) for a in made[hops:]]

    def join(table, spans, others, came, after):
        made = call(
            "join", functools.partial(join_kernel, spans=spans, hops=hops), (*others, *came),
            [shape_of(count, *square) for _, _, count in spans] * 2, after=after, known=table,
        )
        return [(mine, swap_cores(theirs)) for mine, theirs in zip(made[:len(spans)], made[len(spans):])]

    def grads(masks, offset, cw, mine, theirs, after):
        return call(
            "grads", functools.partial(grad_kernel, offset=offset, heads=cw // HEAD_DIM, groups=groups, **sizes),
            (*inputs, *masks, mine, theirs), [shape_of(3, part, cw, dtype=bf16)] * groups,
            [pltpu.VMEM((3, rows, cw), bf16)], after, GRAD_LIMIT, table,
        )

    def local(masks, offset, cw):
        kernel = functools.partial(local_kernel, offset=offset, heads=cw // HEAD_DIM)
        return call(
            "local", kernel, (*inputs, *masks), [shape_of(3, rows, cw), shape_of(8, HEAD_DIM)], limit=GRAD_LIMIT, known=table,
        )

    def carry(near, offset, cw, mine, theirs, after):
        kernel = functools.partial(carry_kernel, offset=offset, heads=cw // HEAD_DIM, groups=groups, **sizes)
        return call(
            "carry", kernel, (*inputs[1:], near, mine, theirs), [shape_of(3, part, cw, dtype=bf16)] * groups,
            [pltpu.VMEM((3, rows, cw), bf16)], after, GRAD_LIMIT, table,
        )

    def carry_rows(shifts, near, offset, cw, mine, theirs, after):
        kernel = functools.partial(
            carry_rows_kernel, offset=offset, heads=cw // HEAD_DIM, groups=groups, shifts=shifts, **sizes
        )
        outs = [shape_of(3, part, cw, dtype=bf16)] * len(shifts)
        return call("carry", kernel, (*inputs[1:], near, mine, theirs), outs, after=after, limit=GRAD_LIMIT, known=table)

    cuts, outs, arrived, totals, masks, table = [], [], [], [], None, None
    for start, half, chunks in halves:
        if not totals:
            (sent,) = states(False, start, half)
            kept, *masks, table = states(True, start, half)
        else:
            kept, sent = late_states(start, half, [token])
        total, came, others = pair_up(
            table, kept, swap_cores(sent), 0 if totals else len(chunks), [made[-1] for made in outs[:1]]
        )
        if not totals:
            near = [local(masks, *chunk) for chunk in chunks]
            token = near[0][1]
        count = chunks[0][1] // HEAD_DIM
        if totals:
            spans = [(c * count, c * count, count) for c in range(len(chunks))]
            joined = join(table, spans, [swap_cores(kept)] * len(chunks), came, [arrived[0][1]])
        else:
            joined, after = [], [made[1] for made in near]
            for c in range(len(chunks)):
                joined += join(table, [(0, c * count, count)], others[c:c + 1], came, after)
                after = [joined[-1][0]]
        for c, ((offset, cw), (mine, theirs)) in enumerate(zip(chunks, joined)):
            after = [made[-1] for made in outs[-1:]] + [parts[1] for parts in arrived[1:-1]][-1:]
            if totals:
                outs.append(grads(masks, offset, cw, mine, theirs, after))
            elif c == 0:
                first = (near[0][0], offset, cw, mine, theirs)
                outs.append([None, *carry_rows(range(1, groups), *first, [made for made, _ in joined[1:]])])
            else:
                outs.append(carry(near[c][0], offset, cw, mine, theirs, after))
            arrived.append(send_rows(outs[-1]))
        if not totals:
            arrived[0][0] = carry_rows([0], *first, [outs[-1][-1]])[0]
        totals = [total]
        cuts += chunks

    placed = []
    for c in range(len(cuts)):
        own = [0, 1] if c == 0 else [c + 1]
        plan = [(arrived[n][0], (0, *cuts[n])) for n in own if n < len(cuts)]
        plan += [(arrived[c][j], (j, *cuts[c])) for j in range(1, groups)]
        some = [array for array, _ in plan]
        placed = pl.pallas_call(
            functools.partial(place_kernel, groups=groups, plan=[where for _, where in plan], width=width),
            grid_spec=pl.GridSpec(
                grid=(1,), in_specs=[anywhere] * (len(some) + len(placed)), out_specs=[anywhere] * 3,
                scratch_shapes=[pltpu.SemaphoreType.DMA((3 * len(some),))],
            ),
            out_shape=[shape_of(part, width * groups, dtype=bf16)] * 3,
            input_output_aliases={len(some) + i: i for i in range(len(placed))},
            cost_estimate=cheap,
            compiler_params=pltpu.CompilerParams(vmem_limit_bytes=VMEM_LIMIT), name="place",
        )(*some, *placed)
    return tuple(placed)


def solution(mesh):
    return jax.shard_map(
        shards,
        mesh=mesh,
        in_specs=(P("seq", "head"), P("seq", "head"), P("seq", "head"), P("seq", "head"), P()),
        out_specs=(P(("seq", "head"), None), P(("seq", "head"), None), P(("seq", "head"), None)),
        check_vma=False,
    )
```

```python
import functools

import jax
import jax.numpy as jnp
from jax import lax
from jax.experimental import pallas as pl
from jax.experimental.pallas import tpu as pltpu
from jax.sharding import PartitionSpec as P

HEAD_DIM = 128
MOST = 1024
GROUP = 4
CHUNK = 4
PAD = 16
FIRST, LAST = 14, 15
LINK = jnp.bfloat16
VMEM_LIMIT = 16 * 1024 * 1024
GRAD_LIMIT = 32 * 1024 * 1024
FIRST_LIMIT = 53 * 1024 * 1024
KEPT_LIMIT = 53 * 1024 * 1024
NT = (((1,), (1,)), ((), ()))
TN = (((0,), (0,)), ((), ()))
NN = (((1,), (0,)), ((), ()))


def dot(a, b, dims):
    return lax.dot_general(a, b, dims, preferred_element_type=jnp.float32)


def doc_at(meta, ndocs, position):
    start, begin, end = jnp.int32(0), jnp.int32(0), jnp.int32(0)
    for i in range(ndocs):
        stop = start + meta[i]
        begin = jnp.where(start <= position, start, begin)
        end = jnp.where(start <= position, stop, end)
        start = stop
    return begin, end


def block_range(meta, ndocs, base, rows):
    begin0, end0 = doc_at(meta, ndocs, base)
    begin1, end1 = doc_at(meta, ndocs, base + rows - 1)
    first = jnp.where(begin0 < base, end0, base) - base
    return begin0, end0, begin1, end1, first, begin1 - base


def make_masks(lengths, lower, upper, ndocs, rows):
    line = lax.broadcasted_iota(jnp.int32, (rows, rows), 0)
    across = lax.broadcasted_iota(jnp.int32, (rows, rows), 1)
    begin_line = jnp.zeros((rows, rows), jnp.int32)
    begin_across = jnp.zeros((rows, rows), jnp.int32)
    start = jnp.int32(0) - lax.axis_index("seq") * rows
    for i in range(ndocs):
        begin_line = jnp.where(line >= start, start, begin_line)
        begin_across = jnp.where(across >= start, start, begin_across)
        start = start + lengths[i]
    lower[...] = jnp.where((across <= line) & (across >= begin_line), 1.0, 0.0).astype(lower.dtype)
    upper[...] = jnp.where((line <= across) & (line >= begin_across), 1.0, 0.0).astype(upper.dtype)


def fill_table(lengths, table, ndocs, rows, hops):
    place = lax.axis_index("seq")
    first_core = lax.rem(place, 2) == 0
    even = (place - lax.rem(place, 2)) * rows
    odd = even + rows
    even_b0, even_e0 = doc_at(lengths, ndocs, even)
    _, even_e1 = doc_at(lengths, ndocs, odd - 1)
    odd_b0, _ = doc_at(lengths, ndocs, odd)
    odd_b1, odd_e1 = doc_at(lengths, ndocs, odd + rows - 1)
    flags = [(odd_b1 < odd, even_e0 > odd)]
    flags += [(odd + rows + hop * 2 * rows < odd_e1, even - hop * 2 * rows > even_b0) for hop in range(hops)]
    flags += [(odd < even_e1, odd > odd_b0), (odd + rows < even_e1, even > odd_b0)]
    for row, (if_first, if_second) in enumerate(flags):
        value = jnp.where(jnp.where(first_core, if_first, if_second), 1.0, 0.0)
        table[row:row + 1] = jnp.full((1, HEAD_DIM), value, jnp.float32)
    _, _, _, _, first, last = block_range(lengths, ndocs, place * rows, rows)
    for row, value in ((FIRST, first), (LAST, last)):
        table[row:row + 1] = jnp.full((1, HEAD_DIM), value, jnp.int32).astype(jnp.float32)


def state_kernel(lengths, q, k, v, g, out, *rest, ndocs, rows, offset, heads, group, kept, hops):
    *masks, held, sems, known, got = rest
    gw = group * HEAD_DIM
    place = lax.axis_index("seq")
    first_core = lax.rem(place, 2) == 0

    tails = first_core if kept else jnp.logical_not(first_core)

    def copy(c, i, ref):
        src = ref.at[:, pl.ds(offset + c * gw, gw)]
        return pltpu.make_async_copy(src, held.at[i, :, pl.ds(c * gw, gw)], sems.at[c, i])

    fetch = pltpu.make_async_copy(lengths, known, got)
    fetch.start()
    for c in range(heads // group):

        @pl.when(tails)
        def _():
            copy(c, 0, k).start()
            copy(c, 1, v).start()

        @pl.when(jnp.logical_not(tails))
        def _():
            copy(c, 0, q).start()
            copy(c, 1, g).start()

    fetch.wait()
    if masks:
        make_masks(known, *masks[:2], ndocs, rows)
        fill_table(known, masks[2], ndocs, rows, hops)
    _, _, _, _, first, last = block_range(known, ndocs, place * rows, rows)
    order = lax.broadcasted_iota(jnp.int32, (rows, HEAD_DIM), 0)
    zero = jnp.zeros((), held.dtype)
    low, high = jnp.where(tails, last, 0), jnp.where(tails, rows, first)
    here = (order >= low) & (order < high)
    for h in range(heads):
        if h % group == 0:
            copy(h // group, 0, k).wait()
            copy(h // group, 1, v).wait()
        cols = slice(h * HEAD_DIM, (h + 1) * HEAD_DIM)
        out[h] = dot(jnp.where(here, held[0, :, cols], zero), held[1, :, cols], TN)


def late_state_kernel(table, q, k, v, g, *rest, ndocs, rows, offset, heads):
    kept, sent = rest[-2:]
    first_core, first_rows, last_rows = own_range(table, rows)
    zero = jnp.zeros((), q.dtype)
    for h in range(heads):
        at = slice(offset + h * HEAD_DIM, offset + (h + 1) * HEAD_DIM)
        tail = dot(jnp.where(last_rows, k[:, at], zero), v[:, at], TN)
        head = dot(jnp.where(first_rows, q[:, at], zero), g[:, at], TN)
        kept[h] = jnp.where(first_core, tail, head)
        sent[h] = jnp.where(first_core, head, tail)


def pair_kernel(table, kept, got, *rest, hops, copies):
    sent, again = rest[-hops - copies:len(rest) - copies], rest[len(rest) - copies:]
    joins = table[0:1]
    size = kept.shape[0] * HEAD_DIM
    total = (got[...] + joins * kept[...]).astype(LINK).reshape(size, HEAD_DIM)
    for out in sent:
        out[:size] = total
        if out.shape[0] > size:
            out[size:] = jnp.zeros((out.shape[0] - size, HEAD_DIM), LINK)
    for i, out in enumerate(again):
        count = out.shape[0]
        out[...] = kept[i * count:(i + 1) * count]


def join_kernel(table, *rest, spans, hops):
    others, came = rest[:len(spans)], rest[len(spans):len(spans) + hops]
    mine, theirs = rest[-2 * len(spans):-len(spans)], rest[-len(spans):]
    weights = [table[1 + hop:2 + hop] for hop in range(hops)]
    from_other, from_pair = table[1 + hops:2 + hops], table[2 + hops:3 + hops]
    for c, (other_at, came_at, count) in enumerate(spans):
        lines = slice(came_at * HEAD_DIM, (came_at + count) * HEAD_DIM)
        total = weights[0] * came[0][lines].astype(jnp.float32)
        for hop in range(1, hops):
            total = total + weights[hop] * came[hop][lines].astype(jnp.float32)
        total = total.reshape(count, HEAD_DIM, HEAD_DIM)
        theirs[c][...] = total
        mine[c][...] = from_other * others[c][other_at:other_at + count] + from_pair * total


def split(a, axis):
    high = a.astype(jnp.bfloat16)
    return jnp.concatenate([high, (a - high.astype(jnp.float32)).astype(jnp.bfloat16)], axis=axis)


def own_range(table, rows, start=0):
    order = (lax.broadcasted_iota(jnp.int32, (rows, HEAD_DIM), 0) + start).astype(jnp.float32)
    return lax.rem(lax.axis_index("seq"), 2) == 0, order < table[FIRST:FIRST + 1], order >= table[LAST:LAST + 1]


def local_part(q, k, v, g, lower, upper, at):
    qh, kh, vh, gh = (ref[:, at] for ref in (q, k, v, g))
    weight_gv = dot(gh, vh, NT).astype(jnp.bfloat16) * lower[...]
    weight_vg = dot(vh, gh, NT).astype(jnp.bfloat16) * upper[...]
    weight_kq = dot(kh, qh, NT).astype(jnp.bfloat16) * upper[...]
    return dot(weight_gv, kh, NN), dot(weight_vg, qh, NN), dot(weight_kq, gh, NN)


def twice(ref, at):
    return jnp.concatenate([ref[:, at]] * 2, axis=1)


def carry_of_state(g, state, first_rows, at):
    return jnp.where(first_rows, dot(twice(g, at), split(state, 1), NT), 0.0)


def carries_of_grad(k, v, grad, last_rows, at):
    carry_k = jnp.where(last_rows, dot(twice(v, at), split(grad, 1), NT), 0.0)
    return carry_k, jnp.where(last_rows, dot(twice(k, at), split(grad, 0), NN), 0.0)


def deal(done, outs, rows, groups):
    part, column = rows // groups, lax.axis_index("head")
    for j in range(groups):
        at = pl.ds(pl.multiple_of(lax.rem(column + j, groups) * part, part), part)
        for i in range(3):
            outs[j][i] = done[i, at, :]


def grad_kernel(table, q, k, v, g, lower, upper, mine, got, *rest, ndocs, rows, offset, heads, groups):
    outs, done = rest[-1 - groups:-1], rest[-1]
    first_core, first_rows, last_rows = own_range(table, rows)
    for h in range(heads):
        cols = slice(h * HEAD_DIM, (h + 1) * HEAD_DIM)
        at = slice(offset + h * HEAD_DIM, offset + (h + 1) * HEAD_DIM)
        state = jnp.where(first_core, got[h], mine[h])
        grad = jnp.where(first_core, mine[h], got[h])
        near = local_part(q, k, v, g, lower, upper, at)
        carries = (carry_of_state(g, state, first_rows, at), *carries_of_grad(k, v, grad, last_rows, at))
        for i in range(3):
            done[i, :, cols] = (near[i] + carries[i]).astype(jnp.bfloat16)
    deal(done, outs, rows, groups)


def local_kernel(table, q, k, v, g, lower, upper, near, token, *, offset, heads):
    token[...] = jnp.zeros_like(token)
    for h in range(heads):
        cols = slice(h * HEAD_DIM, (h + 1) * HEAD_DIM)
        at = slice(offset + h * HEAD_DIM, offset + (h + 1) * HEAD_DIM)
        for i, value in enumerate(local_part(q, k, v, g, lower, upper, at)):
            near[i, :, cols] = value


def carry_kernel(table, k, v, g, near, mine, got, *rest, ndocs, rows, offset, heads, groups):
    outs, done = rest[-1 - groups:-1], rest[-1]
    first_core, first_rows, last_rows = own_range(table, rows)
    for h in range(heads):
        cols = slice(h * HEAD_DIM, (h + 1) * HEAD_DIM)
        at = slice(offset + h * HEAD_DIM, offset + (h + 1) * HEAD_DIM)
        state = jnp.where(first_core, got[h], mine[h])
        grad = jnp.where(first_core, mine[h], got[h])
        carries = (carry_of_state(g, state, first_rows, at), *carries_of_grad(k, v, grad, last_rows, at))
        for i in range(3):
            done[i, :, cols] = (near[i, :, cols] + carries[i]).astype(jnp.bfloat16)
    deal(done, outs, rows, groups)


def carry_rows_kernel(table, k, v, g, near, mine, got, *rest, ndocs, rows, offset, heads, groups, shifts):
    outs = rest[-len(shifts):]
    column, part = lax.axis_index("head"), rows // groups
    for j, out in zip(shifts, outs):
        start = pl.multiple_of(lax.rem(column + j, groups) * part, part)
        lines = pl.ds(start, part)
        first_core, first_rows, last_rows = own_range(table, part, start)
        for h in range(heads):
            cols = slice(h * HEAD_DIM, (h + 1) * HEAD_DIM)
            at = slice(offset + h * HEAD_DIM, offset + (h + 1) * HEAD_DIM)
            state = split(jnp.where(first_core, got[h], mine[h]), 1)
            grad = jnp.where(first_core, mine[h], got[h])
            k2, v2, g2 = (jnp.concatenate([ref[lines, at]] * 2, axis=1) for ref in (k, v, g))
            carry_q = jnp.where(first_rows, dot(g2, state, NT), 0.0)
            carry_k = jnp.where(last_rows, dot(v2, split(grad, 1), NT), 0.0)
            carry_v = jnp.where(last_rows, dot(k2, split(grad, 0), NN), 0.0)
            for i, value in enumerate((carry_q, carry_k, carry_v)):
                out[i, :, cols] = (near[i, lines, cols] + value).astype(jnp.bfloat16)


def place_kernel(*refs, groups, plan, width):
    parts, outs, sems = refs[:len(plan)], refs[-4:-1], refs[-1]
    column = lax.axis_index("head")
    copies = []
    for ref, (j, offset, cw) in zip(parts, plan):
        start = pl.multiple_of(lax.rem(column + groups - j, groups) * width + offset, 128)
        for i in range(3):
            copies.append(pltpu.make_async_copy(ref.at[i], outs[i].at[:, pl.ds(start, cw)], sems.at[len(copies)]))
            copies[-1].start()
    for copy in copies:
        copy.wait()


def cuts_of(width):
    heads = width // HEAD_DIM
    size = CHUNK if heads % (2 * CHUNK) == 0 else 2
    cw, half = size * HEAD_DIM, max(heads // 2, size) * HEAD_DIM
    return [(at, half, [(o, cw) for o in range(at, at + half, cw)]) for at in range(0, width, half)]


def shards(queries, keys, values, out_grad, doc_lengths):
    rows, width = queries.shape
    ndocs = doc_lengths.shape[0]
    seq, groups = lax.axis_size("seq"), lax.axis_size("head")
    pairs = seq // 2
    hops = -(-MOST // (2 * rows))
    halves = cuts_of(width)
    part = rows // groups
    anywhere = pl.BlockSpec(memory_space=pl.ANY)
    in_vmem = pl.BlockSpec(memory_space=pltpu.VMEM)
    in_smem = pl.BlockSpec(memory_space=pltpu.SMEM)
    f32, bf16 = jnp.float32, jnp.bfloat16
    inputs = (queries, keys, values, out_grad)
    sizes = dict(ndocs=ndocs, rows=rows)
    cheap = pl.CostEstimate(flops=0, bytes_accessed=1024, transcendentals=0)

    def shape_of(*dims, dtype=f32):
        return jax.ShapeDtypeStruct(dims, dtype)

    def call(name, kernel, args, outs, scratch=(), after=(), limit=VMEM_LIMIT, known=None):
        known = doc_lengths if known is None else known
        return pl.pallas_call(
            kernel, in_specs=[in_smem if known is doc_lengths else in_vmem] + [in_vmem] * len(args) + [anywhere] * len(after), out_specs=[in_vmem] * len(outs), out_shape=outs,
            scratch_shapes=list(scratch), cost_estimate=cheap,
            compiler_params=pltpu.CompilerParams(vmem_limit_bytes=limit), name=name,
        )(known, *args, *after)

    def swap_cores(a):
        return lax.ppermute(a, "seq", [(b, b ^ 1) for b in range(seq)])

    def swap_pairs(sent):
        came = []
        for hop in range(1, hops + 1):
            perm = [(2 * m, 2 * (m + hop) + 1) for m in range(pairs - hop)]
            came.append(lax.ppermute(sent[hop - 1], "seq", perm + [(b, a) for a, b in perm]))
        return came

    def send_rows(outs):
        arrived = list(outs[:1])
        for j in range(1, groups):
            arrived.append(lax.ppermute(outs[j], "head", [(x, (x + j) % groups) for x in range(groups)]))
        return arrived

    square = (HEAD_DIM, HEAD_DIM)

    def states(kept, offset, half):
        heads = half // HEAD_DIM
        group = GROUP if heads % GROUP == 0 else 2
        outs = [shape_of(heads, *square)] + ([shape_of(rows, rows, dtype=bf16)] * 2 + [shape_of(16, HEAD_DIM)]) * kept
        return pl.pallas_call(
            functools.partial(state_kernel, offset=offset, heads=heads, group=group, kept=kept, hops=hops, **sizes),
            in_specs=[anywhere] * 5, out_specs=[in_vmem] * len(outs), out_shape=outs,
            scratch_shapes=[
                pltpu.VMEM((2, rows, half), bf16), pltpu.SemaphoreType.DMA((heads // group, 2)),
                pltpu.SMEM((ndocs,), jnp.int32), pltpu.SemaphoreType.DMA,
            ],
            cost_estimate=cheap, compiler_params=pltpu.CompilerParams(vmem_limit_bytes=KEPT_LIMIT if kept else FIRST_LIMIT), name="states",
        )(doc_lengths, *inputs)

    def late_states(offset, half, after):
        heads = half // HEAD_DIM
        return call(
            "states", functools.partial(late_state_kernel, offset=offset, heads=heads, **sizes), inputs,
            [shape_of(heads, *square)] * 2, after=after, limit=GRAD_LIMIT, known=table,
        )

    def pair_up(table, kept, got, copies, after):
        lines = kept.shape[0] * HEAD_DIM
        outs = [shape_of(lines + PAD * (hops - hop + 1), HEAD_DIM, dtype=LINK) for hop in range(1, hops + 1)]
        outs += [shape_of(kept.shape[0] // max(copies, 1), *square)] * copies
        made = call(
            "pair", functools.partial(pair_kernel, hops=hops, copies=copies), (kept, got), outs, after=after, known=table
        )
        return made[hops - 1], swap_pairs(made[:hops]), [swap_cores(a) for a in made[hops:]]

    def join(table, spans, others, came, after):
        made = call(
            "join", functools.partial(join_kernel, spans=spans, hops=hops), (*others, *came),
            [shape_of(count, *square) for _, _, count in spans] * 2, after=after, known=table,
        )
        return [(mine, swap_cores(theirs)) for mine, theirs in zip(made[:len(spans)], made[len(spans):])]

    def grads(masks, offset, cw, mine, theirs, after):
        return call(
            "grads", functools.partial(grad_kernel, offset=offset, heads=cw // HEAD_DIM, groups=groups, **sizes),
            (*inputs, *masks, mine, theirs), [shape_of(3, part, cw, dtype=bf16)] * groups,
            [pltpu.VMEM((3, rows, cw), bf16)], after, GRAD_LIMIT, table,
        )

    def local(masks, offset, cw):
        kernel = functools.partial(local_kernel, offset=offset, heads=cw // HEAD_DIM)
        return call(
            "local", kernel, (*inputs, *masks), [shape_of(3, rows, cw), shape_of(8, HEAD_DIM)], limit=GRAD_LIMIT, known=table,
        )

    def carry(near, offset, cw, mine, theirs, after):
        kernel = functools.partial(carry_kernel, offset=offset, heads=cw // HEAD_DIM, groups=groups, **sizes)
        return call(
            "carry", kernel, (*inputs[1:], near, mine, theirs), [shape_of(3, part, cw, dtype=bf16)] * groups,
            [pltpu.VMEM((3, rows, cw), bf16)], after, GRAD_LIMIT, table,
        )

    def carry_rows(shifts, near, offset, cw, mine, theirs, after):
        kernel = functools.partial(
            carry_rows_kernel, offset=offset, heads=cw // HEAD_DIM, groups=groups, shifts=shifts, **sizes
        )
        outs = [shape_of(3, part, cw, dtype=bf16)] * len(shifts)
        return call("carry", kernel, (*inputs[1:], near, mine, theirs), outs, after=after, limit=GRAD_LIMIT, known=table)

    cuts, outs, arrived, totals, masks, table = [], [], [], [], None, None
    for start, half, chunks in halves:
        if not totals:
            (sent,) = states(False, start, half)
            kept, *masks, table = states(True, start, half)
        else:
            kept, sent = late_states(start, half, [token])
        total, came, others = pair_up(
            table, kept, swap_cores(sent), len(chunks), [made[-1] for made in outs[:1]]
        )
        if not totals:
            near = [local(masks, *chunk) for chunk in chunks]
            token = near[0][1]
        count = chunks[0][1] // HEAD_DIM
        if totals:
            spans = [(0, c * count, count) for c in range(len(chunks))]
            joined = join(table, spans, others, came, [arrived[0][1]])
        else:
            joined, after = [], [made[1] for made in near]
            for c in range(len(chunks)):
                joined += join(table, [(0, c * count, count)], others[c:c + 1], came, after)
                after = [joined[-1][0]]
        for c, ((offset, cw), (mine, theirs)) in enumerate(zip(chunks, joined)):
            after = [made[-1] for made in outs[-1:]] + [parts[1] for parts in arrived[1:-1]][-1:]
            if totals:
                outs.append(grads(masks, offset, cw, mine, theirs, after))
            elif c == 0:
                first = (near[0][0], offset, cw, mine, theirs)
                outs.append([None, *carry_rows(range(1, groups), *first, [made for made, _ in joined[1:]])])
            else:
                outs.append(carry(near[c][0], offset, cw, mine, theirs, after))
            arrived.append(send_rows(outs[-1]))
        if not totals:
            arrived[0][0] = carry_rows([0], *first, [outs[-1][-1]])[0]
        totals = [total]
        cuts += chunks

    placed = []
    for c in range(len(cuts)):
        own = [0, 1] if c == 0 else [c + 1]
        plan = [(arrived[n][0], (0, *cuts[n])) for n in own if n < len(cuts)]
        plan += [(arrived[c][j], (j, *cuts[c])) for j in range(1, groups)]
        some = [array for array, _ in plan]
        placed = pl.pallas_call(
            functools.partial(place_kernel, groups=groups, plan=[where for _, where in plan], width=width),
            grid_spec=pl.GridSpec(
                grid=(1,), in_specs=[anywhere] * (len(some) + len(placed)), out_specs=[anywhere] * 3,
                scratch_shapes=[pltpu.SemaphoreType.DMA((3 * len(some),))],
            ),
            out_shape=[shape_of(part, width * groups, dtype=bf16)] * 3,
            input_output_aliases={len(some) + i: i for i in range(len(placed))},
            cost_estimate=cheap,
            compiler_params=pltpu.CompilerParams(vmem_limit_bytes=VMEM_LIMIT), name="place",
        )(*some, *placed)
    return tuple(placed)


def solution(mesh):
    return jax.shard_map(
        shards,
        mesh=mesh,
        in_specs=(P("seq", "head"), P("seq", "head"), P("seq", "head"), P("seq", "head"), P()),
        out_specs=(P(("seq", "head"), None), P(("seq", "head"), None), P(("seq", "head"), None)),
        check_vma=False,
    )
```
